32 devices in a mesh: dp: 8 (over z, y), head: 4 (over x, core).
Axes of the slice: x: 2, y: 2, z: 4, core: 2. Of those that a mesh axis runs over, the one named last changes fastest.
Arguments:
- tokens: bfloat16 [18816, 768], P(('dp', 'head')), may hold values from -6 to 6
- cotangent: bfloat16 [18816, 768], P(('dp', 'head')), may hold values from -6 to 6
- crop_counts: int32 [32], P('dp'), may hold values from 2 to 12, as said below
- pad_mask: int32 [384, 49], P('dp'), may hold values from 0 to 1, as said below
- region_ids: int32 [384, 49], P('dp'), may hold values from 0 to 3, as said below
- rel_index: int32 [49, 49], replicated, may hold values from 0 to 168, as said below
- norm_gain: bfloat16 [2, 2, 768], P(None, None, 'dp'), may hold values from 0.5 to 1.5
- norm_shift: bfloat16 [2, 2, 768], P(None, None, 'dp'), may hold values from -3 to 3
- qkv_weight: bfloat16 [2, 768, 3, 768], P(None, 'dp', None, 'head'), may hold values from -0.21875 to 0.21875
- qv_bias: bfloat16 [2, 2, 768], P(None, None, 'dp'), may hold values from -3 to 3
- bias_table: bfloat16 [2, 24, 169], P(None, 'head'), may hold values from -5 to 5
- proj_weight: bfloat16 [2, 768, 768], P(None, 'head', 'dp'), may hold values from -0.875 to 0.875
- fc1_weight: bfloat16 [2, 768, 3072], P(None, 'dp', 'head'), may hold values from -0.21875 to 0.21875
- fc1_bias: bfloat16 [2, 3072], P(None, 'dp'), may hold values from -3 to 3
- fc2_weight: bfloat16 [2, 3072, 768], P(None, 'head', 'dp'), may hold values from -0.109375 to 0.109375
- out_bias: bfloat16 [2, 2, 768], P(None, None, 'dp'), may hold values from -3 to 3
Outputs:
- output: float32 [18816, 768], P(('dp', 'head'))
- tokens_grad: float32 [18816, 768], P(('dp', 'head'))
- norm_gain_grad: float32 [2, 2, 768], P(None, None, 'dp')
- norm_shift_grad: float32 [2, 2, 768], P(None, None, 'dp')
- qkv_weight_grad: float32 [2, 768, 3, 768], P(None, 'dp', None, 'head')
- qv_bias_grad: float32 [2, 2, 768], P(None, None, 'dp')
- bias_table_grad: float32 [2, 24, 169], P(None, 'head')
- proj_weight_grad: float32 [2, 768, 768], P(None, 'head', 'dp')
- fc1_weight_grad: float32 [2, 768, 3072], P(None, 'dp', 'head')
- fc1_bias_grad: float32 [2, 3072], P(None, 'dp')
- fc2_weight_grad: float32 [2, 3072, 768], P(None, 'head', 'dp')
- out_bias_grad: float32 [2, 2, 768], P(None, None, 'dp')
The draws below stay inside these ranges and needn't reach their ends.
Inputs may be any that keep to these rules, and one draw needn't show every extreme that they name: `crop_counts`: each image has at least 2 crops and one image has exactly 2; among the images of each aligned block of 4 images at least one has 12. `pad_mask`: windows whose slot (window mod 12) is below 2 are all ones; every other window has ones on one square of 3 x 3 positions and zeros elsewhere. `region_ids`: in each window the positions fall into four rectangles, cut by one row boundary and one column boundary. `rel_index`: entry (i, j) depends only on the offset between positions i and j, and different offsets have different entries.
All inputs are finite; a program needn't handle non-finite values.
Results may differ from the reference program's by a relative error of at most 0.022.
Values may be sent and summed in bfloat16 or wider, within the bound.
No kernel may reach another device: no remote copies, remote signals or barrier semaphores. Data moves between devices by JAX's collectives and lax.ppermute only.
A program may use at most 256 MiB of HBM per device.

```python
import jax
import jax.numpy as jnp
from jax import lax

D = 768
HEADS = 24
HEAD_DIM = 32
FF = 3072
WSIDE = 7
SHIFT = 3
GLOBAL = 2
LOCAL_SIDE = 3
CROP_MAX = 12
BLOCKS = 2
IMG_DEV = 4
WTOK = 49
REL = 169
WIN_DEV = 48
IMAGES = 32
WINDOWS = 384
TOKENS = 18816


def draw_crop_counts(key, part):
    key = jax.random.fold_in(key, 11)
    keys = jax.random.split(key, 5)
    first = jax.random.randint(keys[0], (IMAGES,), 0, CROP_MAX - GLOBAL + 1)
    second = jax.random.randint(keys[1], (IMAGES,), 0, CROP_MAX - GLOBAL + 1)
    third = jax.random.randint(keys[2], (IMAGES,), 0, CROP_MAX - GLOBAL + 1)
    extra = jnp.minimum(jnp.minimum(first, second), third)
    full_slot = jax.random.randint(keys[3], (IMAGES // IMG_DEV, 1), 0, IMG_DEV)
    is_full = (jnp.arange(IMG_DEV, dtype=jnp.int32)[None, :] == full_slot).reshape(IMAGES)
    counts = jnp.where(is_full, CROP_MAX, GLOBAL + extra)
    chosen_block = jax.random.randint(keys[4], (), 0, IMAGES // IMG_DEV)
    low_slot = (full_slot[chosen_block, 0] + 1) % IMG_DEV
    low_image = chosen_block * IMG_DEV + low_slot
    counts = jnp.where(jnp.arange(IMAGES, dtype=jnp.int32) == low_image, GLOBAL, counts)
    return counts.astype(jnp.int32)


def draw_pad_mask(key, part):
    key = jax.random.fold_in(key, 12)
    keys = jax.random.split(key, 2)
    top = jax.random.randint(keys[0], (WINDOWS, 1), 0, WSIDE - LOCAL_SIDE + 1)
    left = jax.random.randint(keys[1], (WINDOWS, 1), 0, WSIDE - LOCAL_SIDE + 1)
    places = jnp.arange(WTOK, dtype=jnp.int32)
    row_of = (places // WSIDE)[None, :]
    col_of = (places % WSIDE)[None, :]
    inside = (row_of >= top) & (row_of < top + LOCAL_SIDE) & (col_of >= left) & (col_of < left + LOCAL_SIDE)
    global_window = (jnp.arange(WINDOWS, dtype=jnp.int32) % CROP_MAX < GLOBAL)[:, None]
    return jnp.where(global_window | inside, 1, 0).astype(jnp.int32)


def draw_region_ids(key, part):
    key = jax.random.fold_in(key, 13)
    keys = jax.random.split(key, 2)
    cut_row = jax.random.randint(keys[0], (WINDOWS, 1), 2, WSIDE - 1)
    cut_col = jax.random.randint(keys[1], (WINDOWS, 1), 2, WSIDE - 1)
    places = jnp.arange(WTOK, dtype=jnp.int32)
    row_of = (places // WSIDE)[None, :]
    col_of = (places % WSIDE)[None, :]
    lower = (row_of >= cut_row).astype(jnp.int32)
    right = (col_of >= cut_col).astype(jnp.int32)
    return (2 * lower + right).astype(jnp.int32)


def draw_rel_index(key, part):
    key = jax.random.fold_in(key, 14)
    order = jax.random.permutation(key, REL).astype(jnp.int32)
    places = jnp.arange(WTOK, dtype=jnp.int32)
    row_of = places // WSIDE
    col_of = places % WSIDE
    offset = (row_of[:, None] - row_of[None, :] + WSIDE - 1) * (2 * WSIDE - 1) + (col_of[:, None] - col_of[None, :] + WSIDE - 1)
    return order[offset].astype(jnp.int32)


def with_spikes(drawn, stream_key, source, target, blocks, factor):
    owner, partner = [(jnp.arange(drawn.shape[dim]) // (drawn.shape[dim] // blocks)).reshape([-1 if axis == dim else 1 for axis in range(drawn.ndim)]) for dim in (source, target)]
    chosen = jax.random.permutation(stream_key, blocks)[partner]
    strong = (owner == chosen) | (owner == (partner + blocks // 2) % blocks)
    return jnp.where(strong, factor * drawn, drawn)


def steps_of(rng, extent, cuts, least, high):
    loudness = 1.0
    for axis_at, blocks in cuts:
        draws = jax.random.uniform(jax.random.fold_in(jax.random.fold_in(rng, 6), axis_at), (blocks,), jnp.float32, least / len(cuts), high / len(cuts))
        loudness = loudness * jnp.repeat(jnp.exp(draws), extent[axis_at] // blocks).reshape((-1,) + (1,) * (len(extent) - 1 - axis_at))
    return loudness


def noise(key, dims, scale, limit, shards=(), held_as=jnp.bfloat16):
    level = steps_of(key, dims, shards, -0.22, 0.18) if shards else 1.0
    entries = jax.random.normal(key, dims, jnp.float32) * scale * level
    return jnp.minimum(jnp.maximum(entries, -limit), limit).astype(held_as)


def gaussian_with(key, shape, deviation, limit, pieces, heavy, held_as=jnp.bfloat16):
    values = deviation * jax.random.normal(key, shape, jnp.float32)
    if pieces:
        values = values * steps_of(key, shape, pieces, -0.22, 0.18)
    return jnp.clip(with_spikes(values, jax.random.fold_in(key, 3), *heavy), -limit, limit).astype(held_as)


def setup_inputs(seed: int = 0) -> dict:
    seeds = jax.random.split(jax.random.key(seed), 17)
    return {
        "tokens": noise(seeds[0], (TOKENS, D), 1.0, 6.0, ((0, 32),)),
        "cotangent": gaussian_with(seeds[1], (TOKENS, D), 1.0, 6.0, ((0, 32),), (0, 1, 32, 2.75)),
        "crop_counts": draw_crop_counts(jax.random.fold_in(seeds[16], 71), 0),
        "pad_mask": draw_pad_mask(jax.random.fold_in(seeds[16], 71), 0),
        "region_ids": draw_region_ids(jax.random.fold_in(seeds[16], 71), 0),
        "rel_index": draw_rel_index(jax.random.fold_in(seeds[16], 71), 0),
        "norm_gain": jnp.clip(1.0 + 0.1 * jax.random.normal(seeds[6], (BLOCKS, 2, D), jnp.float32), 0.5, 1.5).astype(jnp.bfloat16),
        "norm_shift": noise(seeds[7], (BLOCKS, 2, D), 0.3, 3.0, ((2, 8),)),
        "qkv_weight": noise(seeds[8], (BLOCKS, D, 3, D), D ** -0.5, 0.21875, ((1, 8), (3, 4))),
        "qv_bias": noise(seeds[9], (BLOCKS, 2, D), 0.3, 3.0, ((2, 8),)),
        "bias_table": noise(seeds[10], (BLOCKS, HEADS, REL), 1.0, 5.0, ((1, 4),)),
        "proj_weight": noise(seeds[11], (BLOCKS, D, D), (D // 16) ** -0.5, 0.875, ((1, 4), (2, 8))),
        "fc1_weight": noise(seeds[12], (BLOCKS, D, FF), D ** -0.5, 0.21875, ((1, 8), (2, 4))),
        "fc1_bias": noise(seeds[13], (BLOCKS, FF), 0.3, 3.0, ((1, 8),)),
        "fc2_weight": noise(seeds[14], (BLOCKS, FF, D), FF ** -0.5, 0.109375, ((1, 4), (2, 8))),
        "out_bias": noise(seeds[15], (BLOCKS, 2, D), 0.3, 3.0, ((2, 8),)),
    }


EPSILON = 1e-05
MASKED = -100.0
HIGHEST = lax.Precision.HIGHEST

@jax.custom_vjp
def low(v):
    return lax.optimization_barrier(v.astype(jnp.bfloat16)).astype(jnp.float32)

@jax.custom_vjp
def low_back(v):
    return v

def low_keep(v):
    return (low(v), None)

def low_pass(kept, grad):
    return (grad,)

def back_keep(v):
    return (v, None)

def back_low(kept, grad):
    return (low(grad),)
low.defvjp(low_keep, low_pass)
low_back.defvjp(back_keep, back_low)

def layer_norm(values, gain, shift):
    centre = lax.optimization_barrier(jnp.mean(values, axis=-1, keepdims=True))
    centred = values - centre
    spread = lax.optimization_barrier(jnp.mean(centred * centred, axis=-1, keepdims=True))
    return centred * lax.rsqrt(spread + EPSILON) * gain + shift

def roll_tokens(values, step):
    shape = values.shape
    grid = values.reshape((shape[0], WSIDE, WSIDE) + shape[2:])
    return jnp.roll(grid, (step, step), axis=(1, 2)).reshape(shape)

def attention_mask(pad_mask, region_ids, shifted):
    valid = pad_mask
    if shifted:
        valid = roll_tokens(pad_mask, -SHIFT)
    allowed = jnp.broadcast_to(valid[:, None, :] == 1, (valid.shape[0], WTOK, WTOK))
    if shifted:
        allowed = allowed & (region_ids[:, :, None] == region_ids[:, None, :])
    return jnp.where(allowed, 0.0, MASKED).astype(jnp.float32)

def attend(query, key, value, position_bias, additive):
    scores = jnp.einsum('wqhd,wkhd->whqk', query, key, precision=HIGHEST)
    scores = low_back(scores + position_bias[None] + additive[:, None])
    peak = lax.optimization_barrier(jnp.max(scores, axis=-1, keepdims=True))
    expo = jnp.exp(scores - peak)
    probs = expo / lax.optimization_barrier(jnp.sum(expo, axis=-1, keepdims=True))
    return jnp.einsum('whqk,wkhd->wqhd', low(probs), value, precision=HIGHEST)

def block_forward(residual, params, live, additive, rel_index, shifted):
    gain, shift, qkv_part, qv_part, table, proj_part, fc1_part, fc1_shift, fc2_part, out_part = params
    count = residual.shape[0]
    groups = count // (WIN_DEV * WTOK)
    normed = low(layer_norm(residual, gain[0], shift[0]))
    query = low(low_back(jnp.dot(normed, qkv_part[:, 0, :], precision=HIGHEST) + qv_part[0]) * HEAD_DIM ** (-0.5))
    key = low(low_back(jnp.dot(normed, qkv_part[:, 1, :], precision=HIGHEST)))
    value = low(low_back(jnp.dot(normed, qkv_part[:, 2, :], precision=HIGHEST) + qv_part[1]))

    def windows(values):
        grid = values.reshape(groups * WIN_DEV, WTOK, HEADS, HEAD_DIM)
        if shifted:
            grid = roll_tokens(grid, -SHIFT)
        return grid.reshape(groups, WIN_DEV, WTOK, HEADS, HEAD_DIM)
    position_bias = table[:, rel_index]
    masks = additive.reshape(groups, WIN_DEV, WTOK, WTOK)
    checked = jax.checkpoint(attend)
    attended = lax.map(lambda parts: checked(parts[0], parts[1], parts[2], position_bias, parts[3]), (windows(query), windows(key), windows(value), masks))
    attended = attended.reshape(groups * WIN_DEV, WTOK, HEADS, HEAD_DIM)
    if shifted:
        attended = roll_tokens(attended, SHIFT)
    attended = low(low_back(attended.reshape(count, D)))
    branch = jnp.dot(attended, proj_part, precision=HIGHEST) + out_part[0]
    mixed = residual + live * low_back(branch)
    normed2 = low(layer_norm(mixed, gain[1], shift[1]))
    pre_hidden = low_back(jnp.dot(normed2, fc1_part, precision=HIGHEST) + fc1_shift)
    hidden = low(jax.nn.gelu(pre_hidden, approximate=False))
    branch2 = jnp.dot(hidden, fc2_part, precision=HIGHEST) + out_part[1]
    return mixed + live * low_back(branch2)

def reference(tokens, cotangent, crop_counts, pad_mask, region_ids, rel_index, norm_gain, norm_shift, qkv_weight, qv_bias, bias_table, proj_weight, fc1_weight, fc1_bias, fc2_weight, out_bias):
    window_ids = jnp.arange(WINDOWS, dtype=jnp.int32)
    live_windows = (window_ids % CROP_MAX < crop_counts[window_ids // CROP_MAX]).astype(jnp.float32)
    live = jnp.repeat(live_windows, WTOK)[:, None]
    masks = (attention_mask(pad_mask, region_ids, False), attention_mask(pad_mask, region_ids, True))
    params = (norm_gain.astype(jnp.float32), norm_shift.astype(jnp.float32), qkv_weight.astype(jnp.float32), qv_bias.astype(jnp.float32), bias_table.astype(jnp.float32), proj_weight.astype(jnp.float32), fc1_weight.astype(jnp.float32), fc1_bias.astype(jnp.float32), fc2_weight.astype(jnp.float32), out_bias.astype(jnp.float32))

    def forward(residual, weights):
        for block in range(BLOCKS):
            chosen = tuple((item[block] for item in weights))
            residual = block_forward(residual, chosen, live, masks[block % 2], rel_index, block % 2 == 1)
        return residual
    output, pullback = jax.vjp(forward, tokens.astype(jnp.float32), params)
    tokens_grad, grads = pullback(cotangent.astype(jnp.float32))
    return (output, tokens_grad, grads[0], grads[1], grads[2], grads[3], grads[4], grads[5], grads[6], grads[7], grads[8], grads[9])
```

```python
import jax
import jax.numpy as jnp
from jax import lax
from jax.sharding import PartitionSpec as P

WSIDE = 7
SHIFT = 3
CROP_MAX = 12
BLOCKS = 2
WTOK = 49

EPSILON = 1e-05
MASKED = -100.0
BF16 = jnp.bfloat16
F32 = jnp.float32


def layer_norm(values, gain, shift):
    centre = jnp.mean(values, axis=-1, keepdims=True)
    centred = values - centre
    spread = jnp.mean(centred * centred, axis=-1, keepdims=True)
    return centred * lax.rsqrt(spread + EPSILON) * gain + shift


def matmul(left, right):
    return jnp.dot(left, right, preferred_element_type=F32)


def matmul_tn(left, right):
    return lax.dot_general(left, right, (((0,), (0,)), ((), ())), preferred_element_type=F32)


def matmul_nt(left, right):
    return lax.dot_general(left, right, (((1,), (1,)), ((), ())), preferred_element_type=F32)


def swap(values, axis, bit):
    size = lax.axis_size(axis)
    return lax.ppermute(values, axis, [(i, i ^ (1 << bit)) for i in range(size)])


def bit_of(axis, bit):
    return (lax.axis_index(axis) >> bit) & 1


def bits_in(axis):
    return lax.axis_size(axis).bit_length() - 1


def join(mine, other, axis, bit, dim):
    upper = bit_of(axis, bit) == 1
    return jnp.where(
        upper, jnp.stack([other, mine], axis=dim), jnp.stack([mine, other], axis=dim)
    )


def pick(values, index, dim):
    return lax.dynamic_index_in_dim(values, index, dim, keepdims=False)


def gather_rows(shard, late):
    rows, width = shard.shape
    held = shard[None]
    for bit in range(1, bits_in("dp")):
        held = join(held, swap(held, "dp", bit), "dp", bit, 0).reshape(-1, rows, width)
    if late:
        pair = [held, swap(held, "head", 1)]
        pair = [join(one, swap(one, "dp", 0), "dp", 0, 1) for one in pair]
    else:
        held = join(held, swap(held, "dp", 0), "dp", 0, 1)
        pair = [held, swap(held, "head", 1)]
    full = [pair[0], swap(pair[0], "head", 0), pair[1], swap(pair[1], "head", 0)]
    return [one.reshape(-1, width) for one in full]


def scatter_rows(pieces, late):
    width = pieces[0].shape[1]
    shards = lax.axis_size("dp")
    rows = pieces[0].shape[0] // shards

    def half(values, bit, dim):
        own = bit_of("dp", bit)
        kept = pick(values, own, dim)
        sent = pick(values, 1 - own, dim)
        return kept.astype(F32) + swap(sent.astype(BF16), "dp", bit).astype(F32)

    near = pieces[0].astype(F32) + swap(pieces[1].astype(BF16), "head", 0).astype(F32)
    far = pieces[2].astype(F32) + swap(pieces[3].astype(BF16), "head", 0).astype(F32)
    if late:
        near, far = [
            half(one.reshape(shards // 2, 2, rows, width), 0, 1) for one in (near, far)
        ]
        held = near + swap(far.astype(BF16), "head", 1).astype(F32)
    else:
        held = near + swap(far.astype(BF16), "head", 1).astype(F32)
        held = half(held.reshape(shards // 2, 2, rows, width), 0, 1)
    for bit in reversed(range(1, bits_in("dp"))):
        held = half(held.reshape(2, -1, rows, width), bit, 0)
    return held.reshape(rows, width)


def sum_all(values):
    for axis in ("head", "dp"):
        for bit in range(bits_in(axis)):
            values = values + swap(values, axis, bit)
    return values


def gather_small(values):
    held = values[None]
    for bit in range(bits_in("head")):
        held = join(held, swap(held, "head", bit), "head", bit, 0).reshape(-1, values.shape[0])
    held = held[None]
    for bit in range(bits_in("dp")):
        other = swap(held, "dp", bit)
        held = join(held, other, "dp", bit, 0).reshape((-1,) + held.shape[1:])
    return held


def attention_mask(pad, region):
    allowed = (pad[:, None, :] == 1) & (region[:, :, None] == region[:, None, :])
    return jnp.where(allowed, 0.0, MASKED).astype(F32)


def unshift(values):
    grid = values.reshape(values.shape[:-1] + (WSIDE, WSIDE))
    return jnp.roll(grid, (SHIFT, SHIFT), axis=(-2, -1)).reshape(values.shape)


def norm_back(values, gain, error):
    centre = jnp.mean(values, axis=-1, keepdims=True)
    centred = values - centre
    scale = lax.rsqrt(jnp.mean(centred * centred, axis=-1, keepdims=True) + EPSILON)
    normal = centred * scale
    flow = error * gain
    grad = (
        flow
        - jnp.mean(flow, axis=-1, keepdims=True)
        - normal * jnp.mean(flow * normal, axis=-1, keepdims=True)
    ) * scale
    return grad, jnp.sum(error * normal, axis=0), jnp.sum(error, axis=0)


def shards(
    tokens,
    cotangent,
    crop_counts,
    pad_mask,
    region_ids,
    rel_index,
    norm_gain,
    norm_shift,
    qkv_weight,
    qv_bias,
    bias_table,
    proj_weight,
    fc1_weight,
    fc1_bias,
    fc2_weight,
    out_bias,
):
    rows = tokens.shape[0]
    width = tokens.shape[1]
    wins = rows // WTOK
    local_width = qkv_weight.shape[3]
    local_heads = bias_table.shape[1]
    rel_count = bias_table.shape[2]
    dp_width = norm_gain.shape[2]
    dp_hidden = fc1_bias.shape[1]
    pieces = lax.axis_size("head")
    heads_total = local_heads * pieces
    head_dim = local_width // local_heads
    scale = head_dim ** (-0.5)
    head_index = lax.axis_index("head")
    dp_index = lax.axis_index("dp")
    relative = [head_index ^ e for e in range(pieces)]

    parts = []
    for block in range(BLOCKS):
        attn = jnp.concatenate(
            [qkv_weight[block].reshape(-1, 3 * local_width), proj_weight[block].T], axis=1
        )
        parts.append((attn, fc1_weight[block], fc2_weight[block].T))
    small = jnp.concatenate(
        [item.reshape(-1) for item in (norm_gain, norm_shift, qv_bias, out_bias, fc1_bias, bias_table)]
    )
    small = jnp.pad(small, (0, -small.shape[0] % 128))
    small_all = gather_small(small)
    weights_all = [
        [gather_rows(parts[block][kind], (block + kind) % 2 == 1) for kind in range(3)]
        for block in range(BLOCKS)
    ]
    offset = 0
    vectors = []
    for item in (norm_gain, norm_shift, qv_bias, out_bias):
        count = item.size
        piece = small_all[:, 0, offset : offset + count].reshape(-1, BLOCKS, 2, dp_width)
        vectors.append(piece.transpose(1, 2, 0, 3).reshape(BLOCKS, 2, width).astype(F32))
        offset += count
    gains, shifts, qv_all, out_all = vectors
    hidden_bias = small_all[:, 0, offset : offset + fc1_bias.size].reshape(-1, BLOCKS, dp_hidden)
    hidden_bias = hidden_bias.transpose(1, 0, 2).reshape(BLOCKS, pieces, -1).astype(F32)
    offset += fc1_bias.size
    tables = small_all[0, :, offset : offset + bias_table.size]
    tables = tables.reshape(pieces, BLOCKS, local_heads, rel_count)
    qv_pieces = qv_all.reshape(BLOCKS, 2, pieces, local_width)

    counts = jnp.repeat(crop_counts, CROP_MAX)
    slots = jnp.arange(pad_mask.shape[0], dtype=jnp.int32) % CROP_MAX
    live_all = (slots < counts).astype(F32)
    live_windows = lax.dynamic_slice_in_dim(live_all, head_index * wins, wins, 0)
    live = jnp.repeat(live_windows, WTOK)[:, None]
    pad = lax.dynamic_slice_in_dim(pad_mask, head_index * wins, wins, 0)
    region = unshift(lax.dynamic_slice_in_dim(region_ids, head_index * wins, wins, 0))
    masks = (attention_mask(pad, jnp.zeros_like(region)), attention_mask(pad, region))
    shifted_index = unshift(unshift(rel_index).T).T
    onehots = [
        (jnp.arange(rel_count, dtype=jnp.int32)[:, None] == index.reshape(1, -1)).astype(BF16)
        for index in (rel_index, shifted_index)
    ]

    kept = []
    residual = tokens.astype(F32)
    for block in range(BLOCKS):
        attn_w, fc1_w, fc2_w = weights_all[block]
        additive = masks[block % 2]
        normed = layer_norm(residual, gains[block, 0], shifts[block, 0]).astype(BF16)
        branch = 0.0
        saved_attn = []
        for e in range(pieces):
            rel = relative[e]
            qkv_w = attn_w[e][:, : 3 * local_width]
            proj_w = attn_w[e][:, 3 * local_width :]
            projected = matmul(normed, qkv_w)
            q_bias = pick(qv_pieces[block, 0], rel, 0)
            v_bias = pick(qv_pieces[block, 1], rel, 0)
            query = ((projected[:, :local_width] + q_bias) * scale).astype(BF16)
            key = projected[:, local_width : 2 * local_width].astype(BF16)
            value = (projected[:, 2 * local_width :] + v_bias).astype(BF16)
            query, key, value = [
                item.reshape(wins, WTOK, local_heads, head_dim) for item in (query, key, value)
            ]
            table = pick(tables[:, block], rel, 0)
            bias = matmul(table, onehots[block % 2]).reshape(local_heads, WTOK, WTOK)
            scores = jnp.einsum("wqhd,wkhd->whqk", query, key, preferred_element_type=F32)
            scores = scores + bias[None] + additive[:, None]
            peak = jnp.max(scores, axis=-1, keepdims=True)
            expo = jnp.exp(scores - peak)
            probs = (expo / jnp.sum(expo, axis=-1, keepdims=True)).astype(BF16)
            attended = jnp.einsum("whqk,wkhd->wqhd", probs, value, preferred_element_type=F32)
            attended = attended.reshape(rows, local_width).astype(BF16)
            branch = branch + matmul_nt(attended, proj_w)
            saved_attn.append((query, key, value, probs, attended))
        mixed = residual + live * (branch + out_all[block, 0])
        normed2 = layer_norm(mixed, gains[block, 1], shifts[block, 1]).astype(BF16)
        saved_mlp = []
        branch2 = 0.0
        for e in range(pieces):
            before = matmul(normed2, fc1_w[e]) + pick(hidden_bias[block], relative[e], 0)
            cdf = 0.5 * (1.0 + lax.erf(before * (0.5**0.5)))
            slope = cdf + before * jnp.exp(-0.5 * before * before) * 0.3989422804014327
            hidden = (before * cdf).astype(BF16)
            branch2 = branch2 + matmul_nt(hidden, fc2_w[e])
            saved_mlp.append((slope.astype(BF16), hidden))
        kept.append((residual, mixed, normed, normed2, saved_attn, saved_mlp))
        residual = mixed + live * (branch2 + out_all[block, 1])

    grad_rows = cotangent.astype(F32)
    shard_grads = [None] * BLOCKS
    small_sums = [None] * BLOCKS
    for block in reversed(range(BLOCKS)):
        attn_w, fc1_w, fc2_w = weights_all[block]
        block_input, mixed, normed, normed2, saved_attn, saved_mlp = kept[block]
        branch_grad = (live * grad_rows).astype(BF16)
        second_bias = jnp.sum(branch_grad, axis=0, dtype=F32)
        fc2_grads, fc1_grads, hidden_grads = [], [], []
        error2 = 0.0
        for e in range(pieces):
            slope, hidden = saved_mlp[e]
            fc2_grads.append(matmul_tn(branch_grad, hidden).astype(BF16))
            pre_grad = (slope * matmul(branch_grad, fc2_w[e])).astype(BF16)
            fc1_grads.append(matmul_tn(normed2, pre_grad).astype(BF16))
            hidden_grads.append(jnp.sum(pre_grad, axis=0, dtype=F32))
            error2 = error2 + matmul_nt(pre_grad, fc1_w[e])
        mixed_part, gain2, shift2 = norm_back(mixed, gains[block, 1], error2)
        mixed_grad = grad_rows + mixed_part
        attn_grad = (live * mixed_grad).astype(BF16)
        first_bias = jnp.sum(attn_grad, axis=0, dtype=F32)
        attn_grads = []
        q_grads, v_grads, table_grads = [], [], []
        error1 = 0.0
        for e in range(pieces):
            query, key, value, probs, attended = saved_attn[e]
            qkv_w = attn_w[e][:, : 3 * local_width]
            proj_w = attn_w[e][:, 3 * local_width :]
            proj_grad = matmul_tn(attn_grad, attended)
            grad_w = matmul(attn_grad, proj_w).astype(BF16)
            grad_w = grad_w.reshape(wins, WTOK, local_heads, head_dim)
            prob_grad = jnp.einsum("wqhd,wkhd->whqk", grad_w, value, preferred_element_type=F32)
            wide = probs.astype(F32)
            row_dot = jnp.sum(wide * prob_grad, axis=-1, keepdims=True)
            score_grad = (wide * (prob_grad - row_dot)).astype(BF16)
            score_total = jnp.sum(score_grad, axis=0, dtype=F32)
            table_grads.append(
                lax.dot_general(
                    score_total.reshape(local_heads, -1),
                    onehots[block % 2].astype(F32),
                    (((1,), (1,)), ((), ())),
                    precision=lax.Precision.HIGHEST,
                    preferred_element_type=F32,
                )
            )
            query_grad = scale * jnp.einsum(
                "whqk,wkhd->wqhd", score_grad, key, preferred_element_type=F32
            )
            key_grad = jnp.einsum(
                "whqk,wqhd->wkhd", score_grad, query, preferred_element_type=F32
            )
            value_grad = jnp.einsum("whqk,wqhd->wkhd", probs, grad_w, preferred_element_type=F32)
            qkv_grad = jnp.concatenate(
                [
                    item.astype(BF16).reshape(rows, local_width)
                    for item in (query_grad, key_grad, value_grad)
                ],
                axis=1,
            )
            sums = jnp.sum(qkv_grad, axis=0, dtype=F32)
            q_grads.append(sums[:local_width])
            v_grads.append(sums[2 * local_width :])
            attn_grads.append(
                jnp.concatenate([matmul_tn(normed, qkv_grad), proj_grad], axis=1).astype(BF16)
            )
            error1 = error1 + matmul_nt(qkv_grad, qkv_w)
        input_part, gain1, shift1 = norm_back(block_input, gains[block, 0], error1)
        grad_rows = mixed_grad + input_part
        shard_grads[block] = [
            scatter_rows(grads, (block + kind) % 2 == 1)
            for kind, grads in enumerate((attn_grads, fc1_grads, fc2_grads))
        ]

        def placed(items):
            whole = jnp.stack(items)
            return jnp.stack([pick(whole, relative[e], 0) for e in range(pieces)]).reshape(-1)

        small_sums[block] = sum_all(
            jnp.concatenate(
                [
                    gain1,
                    gain2,
                    shift1,
                    shift2,
                    placed(q_grads),
                    placed(v_grads),
                    first_bias,
                    second_bias,
                    placed(hidden_grads),
                    placed(table_grads),
                ]
            )
        )

    totals = jnp.stack(small_sums)

    def own(values):
        return lax.dynamic_slice_in_dim(values, dp_index * dp_width, dp_width, 2)

    small_grads = []
    for index in range(4):
        part = totals[:, 2 * index * width : 2 * (index + 1) * width]
        small_grads.append(own(part.reshape(BLOCKS, 2, width)))
    offset = 8 * width
    hidden_total = totals[:, offset : offset + pieces * fc1_weight.shape[2]]
    fc1_bias_grad = lax.dynamic_slice_in_dim(hidden_total, dp_index * dp_hidden, dp_hidden, 1)
    offset += hidden_total.shape[1]
    table_total = totals[:, offset:].reshape(BLOCKS, heads_total, rel_count)
    bias_table_grad = lax.dynamic_slice_in_dim(
        table_total, head_index * local_heads, local_heads, 1
    )
    qkv_weight_grad = jnp.stack(
        [item[0][:, : 3 * local_width].reshape(-1, 3, local_width) for item in shard_grads]
    )
    proj_weight_grad = jnp.stack([item[0][:, 3 * local_width :].T for item in shard_grads])
    fc1_weight_grad = jnp.stack([item[1] for item in shard_grads])
    fc2_weight_grad = jnp.stack([item[2].T for item in shard_grads])
    return (
        residual,
        grad_rows,
        small_grads[0],
        small_grads[1],
        qkv_weight_grad,
        small_grads[2],
        bias_table_grad,
        proj_weight_grad,
        fc1_weight_grad,
        fc1_bias_grad,
        fc2_weight_grad,
        small_grads[3],
    )


def solution(mesh):
    placed = (
        P(("dp", "head"), None),
        P(("dp", "head"), None),
        P("dp"),
        P("dp", None),
        P("dp", None),
        P(),
        P(None, None, "dp"),
        P(None, None, "dp"),
        P(None, "dp", None, "head"),
        P(None, None, "dp"),
        P(None, "head", None),
        P(None, "head", "dp"),
        P(None, "dp", "head"),
        P(None, "dp"),
        P(None, "head", "dp"),
        P(None, None, "dp"),
    )
    return jax.shard_map(
        shards,
        mesh=mesh,
        in_specs=placed,
        out_specs=(
            P(("dp", "head"), None),
            P(("dp", "head"), None),
            P(None, None, "dp"),
            P(None, None, "dp"),
            P(None, "dp", None, "head"),
            P(None, None, "dp"),
            P(None, "head", None),
            P(None, "head", "dp"),
            P(None, "dp", "head"),
            P(None, "dp"),
            P(None, "head", "dp"),
            P(None, None, "dp"),
        ),
        check_vma=False,
    )
```

```python
import functools

import jax
import jax.numpy as jnp
from jax import lax
from jax.experimental import pallas as pl
from jax.experimental.pallas import tpu as pltpu
from jax.sharding import PartitionSpec as P

WSIDE = 7
SHIFT = 3
CROP_MAX = 12
BLOCKS = 2
WTOK = 49
PADDED = 56
PIECES = 4

EPSILON = 1e-05
MASKED = -100.0
ABSENT = -1e30
BF16 = jnp.bfloat16
F32 = jnp.float32


def dot(left, right, left_dim=1, right_dim=0):
    return lax.dot_general(
        left, right, (((left_dim,), (right_dim,)), ((), ())), preferred_element_type=F32
    )


def normalize(values):
    centred = values - jnp.mean(values, axis=-1, keepdims=True)
    scale = lax.rsqrt(jnp.mean(centred * centred, axis=-1, keepdims=True) + EPSILON)
    return centred * scale, scale


def spread_heads(values, heads):
    columns = values.shape[1]
    owner = lax.broadcasted_iota(jnp.int32, values.shape, 1) // (columns // heads)
    return jnp.concatenate(
        [jnp.where(owner == head, values, 0.0) for head in range(heads)], axis=0
    ).astype(BF16)


def merge_heads(values, heads):
    rows = values.shape[0] // heads
    columns = values.shape[1]
    owner = lax.broadcasted_iota(jnp.int32, (rows, columns), 1) // (columns // heads)
    total = values[:rows]
    for head in range(1, heads):
        total = jnp.where(owner == head, values[head * rows : (head + 1) * rows], total)
    return total


def attention_forward_kernel(
    heads,
    scale,
    x_ref,
    w0,
    w1,
    w2,
    w3,
    vec_ref,
    qv_ref,
    bias_ref,
    mask_ref,
    live_ref,
    mixed_ref,
    normed_ref,
    normed2_ref,
    q_ref,
    k_ref,
    v_ref,
    p_ref,
    att_ref,
    qs,
    ks,
    vs,
    atts,
):
    rows = x_ref.shape[0]
    columns = q_ref.shape[2]
    wins = rows // PADDED
    chunk = 2 * PADDED
    weights = (w0, w1, w2, w3)

    def first_norm(step, _):
        span = pl.ds(pl.multiple_of(step * chunk, chunk), chunk)
        normal, _ = normalize(x_ref[span, :])
        normed_ref[span, :] = (normal * vec_ref[0:1, :] + vec_ref[1:2, :]).astype(BF16)
        return 0

    lax.fori_loop(0, rows // chunk, first_norm, 0)
    for e in range(PIECES):
        qkv = dot(normed_ref[...], weights[e][:, : 3 * columns])
        query = ((qkv[:, :columns] + qv_ref[e, 0:1, :]) * scale).astype(BF16)
        key = qkv[:, columns : 2 * columns].astype(BF16)
        value = (qkv[:, 2 * columns :] + qv_ref[e, 1:2, :]).astype(BF16)
        q_ref[e] = query
        k_ref[e] = key
        v_ref[e] = value
        qs[e] = query.astype(F32)
        ks[e] = key.astype(F32)
        vs[e] = value.astype(F32)

    def window(w, _):
        span = pl.ds(pl.multiple_of(w * PADDED, PADDED), PADDED)
        mask = mask_ref[w]
        for e in range(PIECES):
            keys = spread_heads(ks[e, span, :], heads)
            scores = dot(keys, qs[e, span, :].astype(BF16), 1, 1) + bias_ref[e]
            scores = scores.reshape(heads, PADDED, PADDED) + mask[None]
            expo = jnp.exp(scores - jnp.max(scores, axis=1, keepdims=True))
            probs = expo * (1.0 / jnp.sum(expo, axis=1, keepdims=True))
            probs = probs.reshape(heads * PADDED, PADDED)
            p_ref[e, w] = probs.astype(BF16)
            values = spread_heads(vs[e, span, :], heads)
            atts[e, span, :] = dot(probs.T.astype(BF16), values)
        return 0

    lax.fori_loop(0, wins, window, 0)
    branch = None
    for e in range(PIECES):
        attended = atts[e].astype(BF16)
        att_ref[e] = attended
        part = dot(attended, weights[e][:, 3 * columns :], 1, 1)
        branch = part if branch is None else branch + part
    mixed_ref[...] = branch

    def second_norm(step, _):
        span = pl.ds(pl.multiple_of(step * chunk, chunk), chunk)
        mixed = x_ref[span, :] + live_ref[span, :] * (mixed_ref[span, :] + vec_ref[2:3, :])
        mixed_ref[span, :] = mixed
        normal, _ = normalize(mixed)
        normed2_ref[span, :] = (normal * vec_ref[3:4, :] + vec_ref[4:5, :]).astype(BF16)
        return 0

    lax.fori_loop(0, rows // chunk, second_norm, 0)


def attention_forward(x, weights, vectors, qv, bias, mask, live, heads, scale):
    rows, width = x.shape
    columns = qv.shape[2]
    wins = rows // PADDED
    shape = jax.ShapeDtypeStruct
    return pl.pallas_call(
        functools.partial(attention_forward_kernel, heads, scale),
        out_shape=(
            shape((rows, width), F32),
            shape((rows, width), BF16),
            shape((rows, width), BF16),
            shape((PIECES, rows, columns), BF16),
            shape((PIECES, rows, columns), BF16),
            shape((PIECES, rows, columns), BF16),
            shape((PIECES, wins, heads * PADDED, PADDED), BF16),
            shape((PIECES, rows, columns), BF16),
        ),
        scratch_shapes=[pltpu.VMEM((PIECES, rows, columns), F32)] * 4,
        compiler_params=pltpu.CompilerParams(vmem_limit_bytes=60 * 2**20),
        cost_estimate=pl.CostEstimate(
            flops=int(2.5e9 * 1.3), bytes_accessed=30_000_000, transcendentals=2_000_000
        ),
        name="attention_forward",
    )(x, *weights, vectors, qv, bias, mask, live)


def ffn_forward_kernel(
    mixed_ref, normed2_ref, a0, a1, a2, a3, b0, b1, b2, b3, bias_ref, vec_ref, live_ref,
    out_ref, hidden_ref, slope_ref,
):
    rows = mixed_ref.shape[0]
    chunk = 2 * PADDED
    first = (a0, a1, a2, a3)
    second = (b0, b1, b2, b3)
    for e in range(PIECES):
        hidden_ref[e] = jnp.zeros(hidden_ref.shape[1:], BF16)
    total = None
    for e in range(PIECES):
        before = dot(normed2_ref[...], first[e][...]) + bias_ref[e]
        cdf = 0.5 * (1.0 + lax.erf(before * (0.5**0.5)))
        density = jnp.exp(-0.5 * before * before) * 0.3989422804014327
        hidden_ref[e] = (before * cdf).astype(BF16)
        slope_ref[e] = (cdf + before * density).astype(BF16)
        part = dot(hidden_ref[e], second[e][...], 1, 1)
        total = part if total is None else total + part
    out_ref[...] = total

    def finish(step, _):
        span = pl.ds(pl.multiple_of(step * chunk, chunk), chunk)
        out_ref[span, :] = mixed_ref[span, :] + live_ref[span, :] * (
            out_ref[span, :] + vec_ref[5:6, :]
        )
        return 0

    lax.fori_loop(0, rows // chunk, finish, 0)


def ffn_forward(mixed, normed2, first, second, bias, vectors, live):
    rows, width = mixed.shape
    shape = jax.ShapeDtypeStruct
    return pl.pallas_call(
        ffn_forward_kernel,
        out_shape=(
            shape((rows, width), F32),
            shape((PIECES, rows, width), BF16),
            shape((PIECES, rows, width), BF16),
        ),
        compiler_params=pltpu.CompilerParams(vmem_limit_bytes=60 * 2**20),
        name="ffn_forward",
    )(mixed, normed2, *first, *second, bias, vectors, live)


def norm_back_rows(values, gain, error):
    normal, scale = normalize(values)
    flow = error * gain
    grad = (
        flow
        - jnp.mean(flow, axis=-1, keepdims=True)
        - normal * jnp.mean(flow * normal, axis=-1, keepdims=True)
    ) * scale
    return grad, jnp.sum(error * normal, axis=0, keepdims=True), jnp.sum(error, axis=0, keepdims=True)


def ffn_backward_kernel(
    grad_ref, mixed_ref, slope_ref, a0, a1, a2, a3, b0, b1, b2, b3, vec_ref, live_ref,
    branch_ref, pre_ref, mixed_grad_ref, attn_grad_ref, small_ref, hidden_bias_ref,
):
    rows, width = grad_ref.shape
    chunk = 2 * PADDED
    first = (a0, a1, a2, a3)
    second = (b0, b1, b2, b3)

    def start(step, total):
        span = pl.ds(pl.multiple_of(step * chunk, chunk), chunk)
        branch = (live_ref[span, :] * grad_ref[span, :]).astype(BF16)
        branch_ref[span, :] = branch
        return total + jnp.sum(branch.astype(F32), axis=0, keepdims=True)

    zero = jnp.zeros((1, width), F32)
    small_ref[3:4, :] = lax.fori_loop(0, rows // chunk, start, zero)
    error = None
    for e in range(PIECES):
        flow = dot(branch_ref[...], second[e][...])
        pre = (slope_ref[e].astype(F32) * flow).astype(BF16)
        pre_ref[e] = pre
        hidden_bias_ref[e] = jnp.sum(pre.astype(F32), axis=0, keepdims=True)
        part = dot(pre_ref[e], first[e][...], 1, 1)
        error = part if error is None else error + part
    mixed_grad_ref[...] = error

    def finish(step, totals):
        span = pl.ds(pl.multiple_of(step * chunk, chunk), chunk)
        back, gain_part, shift_part = norm_back_rows(
            mixed_ref[span, :], vec_ref[3:4, :], mixed_grad_ref[span, :]
        )
        mixed_grad = grad_ref[span, :] + back
        mixed_grad_ref[span, :] = mixed_grad
        attn_grad = (live_ref[span, :] * mixed_grad).astype(BF16)
        attn_grad_ref[span, :] = attn_grad
        bias_part = jnp.sum(attn_grad.astype(F32), axis=0, keepdims=True)
        return tuple(a + b for a, b in zip(totals, (gain_part, shift_part, bias_part)))

    totals = lax.fori_loop(0, rows // chunk, finish, (zero, zero, zero))
    for index in range(3):
        small_ref[index : index + 1, :] = totals[index]


def ffn_backward(grad, mixed, slope, first, second, vectors, live):
    rows, width = grad.shape
    shape = jax.ShapeDtypeStruct
    return pl.pallas_call(
        ffn_backward_kernel,
        out_shape=(
            shape((rows, width), BF16),
            shape((PIECES, rows, width), BF16),
            shape((rows, width), F32),
            shape((rows, width), BF16),
            shape((8, width), F32),
            shape((PIECES, 1, width), F32),
        ),
        compiler_params=pltpu.CompilerParams(vmem_limit_bytes=60 * 2**20),
        name="ffn_backward",
    )(grad, mixed, slope, *first, *second, vectors, live)


def weight_grad_kernel(picks, left_ref, right_ref, *refs):
    added, outs = refs[: len(refs) - len(picks)], refs[len(refs) - len(picks) :]
    for index, e in enumerate(picks):
        value = dot(left_ref[...], right_ref[e], 0, 0)
        if added:
            value = value + added[index][...].astype(F32)
        outs[index][...] = value.astype(BF16)


def weight_grad(left, right, picks, added=()):
    width = left.shape[1]
    shape = jax.ShapeDtypeStruct
    return pl.pallas_call(
        functools.partial(weight_grad_kernel, picks),
        out_shape=tuple(shape((width, right.shape[2]), BF16) for _ in picks),
        compiler_params=pltpu.CompilerParams(vmem_limit_bytes=60 * 2**20),
        name="weight_grad",
    )(left, right, *added)


def attn_weight_grad_kernel(picks, left_ref, right_ref, left2_ref, right2_ref, *refs):
    added, outs = refs[: len(refs) - len(picks)], refs[len(refs) - len(picks) :]
    for index, e in enumerate(picks):
        value = jnp.concatenate(
            [
                dot(left_ref[...], right_ref[e], 0, 0),
                dot(left2_ref[...], right2_ref[e], 0, 0),
            ],
            axis=1,
        )
        if added:
            value = value + added[index][...].astype(F32)
        outs[index][...] = value.astype(BF16)


def attn_weight_grad(normed, qkv_grad, attn_grad, attended, picks, added=()):
    width = normed.shape[1]
    shape = jax.ShapeDtypeStruct
    return pl.pallas_call(
        functools.partial(attn_weight_grad_kernel, picks),
        out_shape=tuple(shape((width, width), BF16) for _ in picks),
        compiler_params=pltpu.CompilerParams(vmem_limit_bytes=60 * 2**20),
        name="attn_weight_grad",
    )(normed, qkv_grad, attn_grad, attended, *added)


def attention_backward_kernel(
    heads, scale,
    x_ref, mixed_grad_ref, attn_grad_ref, w0, w1, w2, w3, q_ref, k_ref, v_ref, p_ref, vec_ref,
    grad_ref, qkv_grad_ref, bias_grad_ref, small_ref, qv_grad_ref,
    qs, ks, vs, gs, qkvs,
):
    rows, width = x_ref.shape
    columns = q_ref.shape[2]
    wins = rows // PADDED
    chunk = 2 * PADDED
    weights = (w0, w1, w2, w3)
    for e in range(PIECES):
        gs[e] = dot(attn_grad_ref[...], weights[e][:, 3 * columns :]).astype(BF16).astype(F32)
        qs[e] = q_ref[e].astype(F32)
        ks[e] = k_ref[e].astype(F32)
        vs[e] = v_ref[e].astype(F32)
    bias_grad_ref[...] = jnp.zeros(bias_grad_ref.shape, F32)

    def window(w, _):
        span = pl.ds(pl.multiple_of(w * PADDED, PADDED), PADDED)
        for e in range(PIECES):
            keys = spread_heads(ks[e, span, :], heads)
            values = spread_heads(vs[e, span, :], heads)
            query = qs[e, span, :].astype(BF16)
            grads = gs[e, span, :].astype(BF16)
            low = p_ref[e, w]
            probs = low.astype(F32)
            flow = dot(values, grads, 1, 1)
            inner = jnp.sum((probs * flow).reshape(heads, PADDED, PADDED), axis=1, keepdims=True)
            score = probs.reshape(heads, PADDED, PADDED) * (
                flow.reshape(heads, PADDED, PADDED) - inner
            )
            score = score.reshape(heads * PADDED, PADDED).astype(BF16)
            wide = score.astype(F32)
            bias_grad_ref[e] += wide
            qkvs[e, span, :columns] = dot(wide.T.astype(BF16), keys) * scale
            qkvs[e, span, columns : 2 * columns] = merge_heads(dot(score, query), heads)
            qkvs[e, span, 2 * columns :] = merge_heads(dot(low, grads), heads)
        return 0

    lax.fori_loop(0, wins, window, 0)
    error = None
    for e in range(PIECES):
        qkv_grad_ref[e] = qkvs[e].astype(BF16)
        qv_grad_ref[e] = jnp.sum(qkv_grad_ref[e].astype(F32), axis=0, keepdims=True)
        part = dot(qkv_grad_ref[e], weights[e][:, : 3 * columns], 1, 1)
        error = part if error is None else error + part
    grad_ref[...] = error
    zero = jnp.zeros((1, width), F32)

    def finish(step, totals):
        span = pl.ds(pl.multiple_of(step * chunk, chunk), chunk)
        back, gain_part, shift_part = norm_back_rows(
            x_ref[span, :], vec_ref[0:1, :], grad_ref[span, :]
        )
        grad_ref[span, :] = mixed_grad_ref[span, :] + back
        return totals[0] + gain_part, totals[1] + shift_part

    totals = lax.fori_loop(0, rows // chunk, finish, (zero, zero))
    for index in range(2):
        small_ref[index : index + 1, :] = totals[index]


def attention_backward(x, mixed_grad, attn_grad, weights, query, key, value, probs, vectors, heads, scale):
    rows, width = x.shape
    columns = query.shape[2]
    shape = jax.ShapeDtypeStruct
    return pl.pallas_call(
        functools.partial(attention_backward_kernel, heads, scale),
        out_shape=(
            shape((rows, width), F32),
            shape((PIECES, rows, 3 * columns), BF16),
            shape((PIECES, heads * PADDED, PADDED), F32),
            shape((8, width), F32),
            shape((PIECES, 1, 3 * columns), F32),
        ),
        scratch_shapes=[pltpu.VMEM((PIECES, rows, columns), F32)] * 4
        + [pltpu.VMEM((PIECES, rows, 3 * columns), F32)],
        compiler_params=pltpu.CompilerParams(vmem_limit_bytes=60 * 2**20),
        name="attention_backward",
    )(x, mixed_grad, attn_grad, *weights, query, key, value, probs, vectors)


def swap(values, axis, bit):
    size = lax.axis_size(axis)
    return lax.ppermute(values, axis, [(i, i ^ (1 << bit)) for i in range(size)])


def bit_of(axis, bit):
    return (lax.axis_index(axis) >> bit) & 1


def bits_in(axis):
    return lax.axis_size(axis).bit_length() - 1


def join(mine, other, axis, bit, dim):
    upper = bit_of(axis, bit) == 1
    return jnp.where(
        upper, jnp.stack([other, mine], axis=dim), jnp.stack([mine, other], axis=dim)
    )


def pick(values, index, dim):
    return lax.dynamic_index_in_dim(values, index, dim, keepdims=False)


def gather_rows(shard, late):
    rows, width = shard.shape
    held = shard[None]
    for bit in range(1, bits_in("dp")):
        held = join(held, swap(held, "dp", bit), "dp", bit, 0).reshape(-1, rows, width)
    if late:
        pair = [held, swap(held, "head", 1)]
        pair = [join(one, swap(one, "dp", 0), "dp", 0, 1) for one in pair]
    else:
        held = join(held, swap(held, "dp", 0), "dp", 0, 1)
        pair = [held, swap(held, "head", 1)]
    full = [pair[0], swap(pair[0], "head", 0), pair[1], swap(pair[1], "head", 0)]
    return [one.reshape(-1, width) for one in full]


def scatter_rows(make, late):
    shards = lax.axis_size("dp")

    def half(values, bit, dim):
        own = bit_of("dp", bit)
        kept = pick(values, own, dim)
        sent = pick(values, 1 - own, dim)
        return kept.astype(F32) + swap(sent.astype(BF16), "dp", bit).astype(F32)

    away = make((1, 3))
    near, far = make((0, 2), [swap(one, "head", 0) for one in away])
    width = near.shape[1]
    rows = near.shape[0] // shards
    if late:
        near, far = [
            half(one.reshape(shards // 2, 2, rows, width), 0, 1) for one in (near, far)
        ]
        held = near + swap(far.astype(BF16), "head", 1).astype(F32)
    else:
        held = near.astype(F32) + swap(far, "head", 1).astype(F32)
        held = half(held.reshape(shards // 2, 2, rows, width), 0, 1)
    for bit in reversed(range(1, bits_in("dp"))):
        held = half(held.reshape(2, -1, rows, width), bit, 0)
    return held.reshape(rows, width)


def sum_all(values):
    for axis in ("head", "dp"):
        for bit in range(bits_in(axis)):
            values = values + swap(values, axis, bit)
    return values


def gather_small(values):
    held = values[None]
    for bit in range(bits_in("head")):
        held = join(held, swap(held, "head", bit), "head", bit, 0).reshape(-1, values.shape[0])
    held = held[None]
    for bit in range(bits_in("dp")):
        other = swap(held, "dp", bit)
        held = join(held, other, "dp", bit, 0).reshape((-1,) + held.shape[1:])
    return held


def unshift(values):
    grid = values.reshape(values.shape[:-1] + (WSIDE, WSIDE))
    return jnp.roll(grid, (SHIFT, SHIFT), axis=(-2, -1)).reshape(values.shape)


def pad_rows(values):
    grid = values.reshape(-1, WTOK, values.shape[1])
    grid = jnp.pad(grid, ((0, 0), (0, PADDED - WTOK), (0, 0)))
    return grid.reshape(-1, values.shape[1])


def drop_rows(values):
    grid = values.reshape(-1, PADDED, values.shape[1])[:, :WTOK]
    return grid.reshape(-1, values.shape[1])


def attention_mask(pad, region):
    allowed = (pad[:, :, None] == 1) & (region[:, :, None] == region[:, None, :])
    mask = jnp.where(allowed, 0.0, MASKED).astype(F32)
    extra = PADDED - WTOK
    mask = jnp.pad(mask, ((0, 0), (0, 0), (0, extra)))
    return jnp.pad(mask, ((0, 0), (0, extra), (0, 0)), constant_values=ABSENT)


def shards(
    tokens,
    cotangent,
    crop_counts,
    pad_mask,
    region_ids,
    rel_index,
    norm_gain,
    norm_shift,
    qkv_weight,
    qv_bias,
    bias_table,
    proj_weight,
    fc1_weight,
    fc1_bias,
    fc2_weight,
    out_bias,
):
    rows = tokens.shape[0]
    width = tokens.shape[1]
    wins = rows // WTOK
    local_width = qkv_weight.shape[3]
    local_heads = bias_table.shape[1]
    rel_count = bias_table.shape[2]
    dp_width = norm_gain.shape[2]
    dp_hidden = fc1_bias.shape[1]
    pieces = lax.axis_size("head")
    heads_total = local_heads * pieces
    head_dim = local_width // local_heads
    scale = head_dim ** (-0.5)
    head_index = lax.axis_index("head")
    dp_index = lax.axis_index("dp")
    relative = [head_index ^ e for e in range(pieces)]

    parts = []
    for block in range(BLOCKS):
        attn = jnp.concatenate(
            [qkv_weight[block].reshape(-1, 3 * local_width), proj_weight[block].T], axis=1
        )
        parts.append((attn, fc1_weight[block], fc2_weight[block].T))
    small = jnp.concatenate(
        [item.reshape(-1) for item in (norm_gain, norm_shift, qv_bias, out_bias, fc1_bias, bias_table)]
    )
    small = jnp.pad(small, (0, -small.shape[0] % 128))
    small_all = gather_small(small)
    weights_all = [
        [gather_rows(parts[block][kind], (block + kind) % 2 == 1) for kind in range(3)]
        for block in range(BLOCKS)
    ]
    offset = 0
    vectors = []
    for item in (norm_gain, norm_shift, qv_bias, out_bias):
        count = item.size
        piece = small_all[:, 0, offset : offset + count].reshape(-1, BLOCKS, 2, dp_width)
        vectors.append(piece.transpose(1, 2, 0, 3).reshape(BLOCKS, 2, width).astype(F32))
        offset += count
    gains, shifts, qv_all, out_all = vectors
    hidden_bias = small_all[:, 0, offset : offset + fc1_bias.size].reshape(-1, BLOCKS, dp_hidden)
    hidden_bias = hidden_bias.transpose(1, 0, 2).reshape(BLOCKS, pieces, -1).astype(F32)
    offset += fc1_bias.size
    tables = small_all[0, :, offset : offset + bias_table.size]
    tables = tables.reshape(pieces, BLOCKS, local_heads, rel_count)
    qv_pieces = qv_all.reshape(BLOCKS, 2, pieces, local_width)

    counts = jnp.repeat(crop_counts, CROP_MAX)
    slots = jnp.arange(pad_mask.shape[0], dtype=jnp.int32) % CROP_MAX
    live_all = (slots < counts).astype(F32)
    live_windows = lax.dynamic_slice_in_dim(live_all, head_index * wins, wins, 0)
    real = (jnp.arange(PADDED) < WTOK).astype(F32)
    live = (live_windows[:, None] * real[None, :]).reshape(-1, 1)
    pad = lax.dynamic_slice_in_dim(pad_mask, head_index * wins, wins, 0)
    region = unshift(lax.dynamic_slice_in_dim(region_ids, head_index * wins, wins, 0))
    masks = (attention_mask(pad, jnp.zeros_like(region)), attention_mask(pad, region))
    extra = PADDED - WTOK
    onehots = []
    for index in (rel_index, unshift(unshift(rel_index).T).T):
        by_key = jnp.pad(index.T, ((0, extra), (0, extra)), constant_values=-1).reshape(1, -1)
        ids = jnp.arange(rel_count, dtype=jnp.int32)[:, None]
        onehots.append((ids == by_key).astype(BF16))

    def ordered(values, dim):
        return jnp.stack([pick(values, rel, dim) for rel in relative])

    block_rows = local_heads * PADDED
    vectors, qv, biases, hidden_biases = [], [], [], []
    for block in range(BLOCKS):
        rows8 = [
            gains[block, 0],
            shifts[block, 0],
            out_all[block, 0],
            gains[block, 1],
            shifts[block, 1],
            out_all[block, 1],
        ]
        vectors.append(jnp.pad(jnp.stack(rows8), ((0, 2), (0, 0))))
        qv.append(ordered(qv_pieces[block], 1))
        table = ordered(tables[:, block], 0).reshape(heads_total, rel_count)
        bias = jnp.dot(table, onehots[block % 2], preferred_element_type=F32)
        biases.append(bias.reshape(pieces, block_rows, PADDED))
        hidden_biases.append(ordered(hidden_bias[block], 0)[:, None, :])

    kept = []
    residual = pad_rows(tokens).astype(F32)
    for block in range(BLOCKS):
        attn_w, fc1_w, fc2_w = weights_all[block]
        mixed, normed, normed2, query, key, value, probs, attended = attention_forward(
            residual,
            attn_w,
            vectors[block],
            qv[block],
            biases[block],
            masks[block % 2],
            live,
            local_heads,
            scale,
        )
        after, hidden, slope = ffn_forward(
            mixed, normed2, fc1_w, fc2_w, hidden_biases[block], vectors[block], live
        )
        kept.append(
            (residual, mixed, normed, normed2, query, key, value, probs, attended, hidden, slope)
        )
        residual = after

    grad_rows = pad_rows(cotangent).astype(F32)
    shard_grads = [None] * BLOCKS
    small_sums = [None] * BLOCKS
    for block in reversed(range(BLOCKS)):
        attn_w, fc1_w, fc2_w = weights_all[block]
        x, mixed, normed, normed2, query, key, value, probs, attended, hidden, slope = kept[block]
        branch_grad, pre_grad, mixed_grad, attn_grad, small_ffn, hidden_grad = ffn_backward(
            grad_rows, mixed, slope, fc1_w, fc2_w, vectors[block], live
        )
        fc2_grad = scatter_rows(
            lambda picks, added=(): weight_grad(branch_grad, hidden, picks, added), block % 2 == 0
        )
        fc1_grad = scatter_rows(
            lambda picks, added=(): weight_grad(normed2, pre_grad, picks, added), block % 2 == 1
        )
        grad_rows, qkv_grad, score_sum, small_attn, qv_grad = attention_backward(
            x,
            mixed_grad,
            attn_grad,
            attn_w,
            query,
            key,
            value,
            probs,
            vectors[block],
            local_heads,
            scale,
        )
        attn_w_grad = scatter_rows(
            lambda picks, added=(): attn_weight_grad(
                normed, qkv_grad, attn_grad, attended, picks, added
            ),
            block % 2 == 0,
        )
        shard_grads[block] = (attn_w_grad, fc1_grad, fc2_grad)
        table_grad = lax.dot_general(
            score_sum.reshape(heads_total, -1),
            onehots[block % 2].astype(F32),
            (((1,), (1,)), ((), ())),
            precision=lax.Precision.HIGHEST,
            preferred_element_type=F32,
        ).reshape(pieces, -1)
        items = [
            small_attn[0],
            small_ffn[0],
            small_attn[1],
            small_ffn[1],
            ordered(qv_grad[:, 0, :local_width], 0).reshape(-1),
            ordered(qv_grad[:, 0, 2 * local_width :], 0).reshape(-1),
            small_ffn[2],
            small_ffn[3],
            ordered(hidden_grad[:, 0], 0).reshape(-1),
            ordered(table_grad, 0).reshape(-1),
        ]
        small_sums[block] = sum_all(jnp.concatenate(items))

    totals = jnp.stack(small_sums)

    def own(values):
        return lax.dynamic_slice_in_dim(values, dp_index * dp_width, dp_width, 2)

    small_grads = []
    for index in range(4):
        part = totals[:, 2 * index * width : 2 * (index + 1) * width]
        small_grads.append(own(part.reshape(BLOCKS, 2, width)))
    offset = 8 * width
    hidden_total = totals[:, offset : offset + pieces * fc1_weight.shape[2]]
    fc1_bias_grad = lax.dynamic_slice_in_dim(hidden_total, dp_index * dp_hidden, dp_hidden, 1)
    offset += hidden_total.shape[1]
    table_total = totals[:, offset:].reshape(BLOCKS, heads_total, rel_count)
    bias_table_grad = lax.dynamic_slice_in_dim(
        table_total, head_index * local_heads, local_heads, 1
    )
    qkv_weight_grad = jnp.stack(
        [item[0][:, : 3 * local_width].reshape(-1, 3, local_width) for item in shard_grads]
    )
    proj_weight_grad = jnp.stack([item[0][:, 3 * local_width :].T for item in shard_grads])
    fc1_weight_grad = jnp.stack([item[1] for item in shard_grads])
    fc2_weight_grad = jnp.stack([item[2].T for item in shard_grads])
    return (
        drop_rows(residual),
        drop_rows(grad_rows),
        small_grads[0],
        small_grads[1],
        qkv_weight_grad,
        small_grads[2],
        bias_table_grad,
        proj_weight_grad,
        fc1_weight_grad,
        fc1_bias_grad,
        fc2_weight_grad,
        small_grads[3],
    )


def solution(mesh):
    placed = (
        P(("dp", "head"), None),
        P(("dp", "head"), None),
        P("dp"),
        P("dp", None),
        P("dp", None),
        P(),
        P(None, None, "dp"),
        P(None, None, "dp"),
        P(None, "dp", None, "head"),
        P(None, None, "dp"),
        P(None, "head", None),
        P(None, "head", "dp"),
        P(None, "dp", "head"),
        P(None, "dp"),
        P(None, "head", "dp"),
        P(None, None, "dp"),
    )
    return jax.shard_map(
        shards,
        mesh=mesh,
        in_specs=placed,
        out_specs=(
            P(("dp", "head"), None),
            P(("dp", "head"), None),
            P(None, None, "dp"),
            P(None, None, "dp"),
            P(None, "dp", None, "head"),
            P(None, None, "dp"),
            P(None, "head", None),
            P(None, "head", "dp"),
            P(None, "dp", "head"),
            P(None, "dp"),
            P(None, "head", "dp"),
            P(None, None, "dp"),
        ),
        check_vma=False,
    )
```

```python
import functools

import jax
import jax.numpy as jnp
from jax import lax
from jax.experimental import pallas as pl
from jax.experimental.pallas import tpu as pltpu
from jax.sharding import PartitionSpec as P

WSIDE = 7
SHIFT = 3
CROP_MAX = 12
BLOCKS = 2
WTOK = 49
PADDED = 56
PIECES = 4
VMEM_BYTES = 60 * 2**20

EPSILON = 1e-05
MASKED = -100.0
ABSENT = -1e30
BF16 = jnp.bfloat16
F32 = jnp.float32


def cost(micros):
    return pl.CostEstimate(
        flops=int(micros * 1e9), bytes_accessed=int(micros * 3e6), transcendentals=0
    )


def dot(left, right, left_dim=1, right_dim=0):
    return lax.dot_general(
        left, right, (((left_dim,), (right_dim,)), ((), ())), preferred_element_type=F32
    )


def normalize(values):
    centred = values - jnp.mean(values, axis=-1, keepdims=True)
    scale = lax.rsqrt(jnp.mean(centred * centred, axis=-1, keepdims=True) + EPSILON)
    return centred * scale, scale


def norm_back_rows(values, gain, error):
    normal, scale = normalize(values)
    flow = error * gain
    grad = (
        flow
        - jnp.mean(flow, axis=-1, keepdims=True)
        - normal * jnp.mean(flow * normal, axis=-1, keepdims=True)
    ) * scale
    return grad, jnp.sum(error * normal, axis=0, keepdims=True), jnp.sum(error, axis=0, keepdims=True)


def spread_heads(values, heads):
    columns = values.shape[1]
    owner = lax.broadcasted_iota(jnp.int32, values.shape, 1) // (columns // heads)
    return jnp.concatenate(
        [jnp.where(owner == head, values, 0.0) for head in range(heads)], axis=0
    ).astype(BF16)


def merge_heads(values, heads):
    rows = values.shape[0] // heads
    columns = values.shape[1]
    owner = lax.broadcasted_iota(jnp.int32, (rows, columns), 1) // (columns // heads)
    total = values[:rows]
    for head in range(1, heads):
        total = jnp.where(owner == head, values[head * rows : (head + 1) * rows], total)
    return total


class Copies:
    def __init__(self, sems):
        self.sems = sems
        self.used = 0
        self.leaving = []

    def start(self, source, target):
        copy = pltpu.make_async_copy(source, target, self.sems.at[self.used])
        self.used += 1
        copy.start()
        return copy

    def fetch(self, source, target):
        return self.start(source, target)

    def send(self, source, target):
        self.leaving.append(self.start(source, target))

    def finish(self):
        for copy in self.leaving:
            copy.wait()


def choose(weights, picks):
    plan, arrays, rows = weights
    chosen = [index for index, (e, _) in enumerate(plan) if e in picks]
    plan = tuple((picks.index(plan[index][0]), plan[index][1]) for index in chosen)
    return plan, [arrays[index] for index in chosen], rows


def fetch_weights(copies, plan, refs, rows, parts):
    own = lax.axis_index("dp")
    started = {}
    for (slot, rels), ref in sorted(zip(plan, refs), key=lambda item: item[0][0]):
        for place, rel in enumerate(rels):
            start = 0 if rel is None else pl.multiple_of(jnp.bitwise_xor(own, rel) * rows, rows)
            for part, target in enumerate(parts):
                started.setdefault(slot, []).append(
                    copies.fetch(
                        ref.at[place, pl.ds(part * rows, rows), :],
                        target.at[slot, pl.ds(start, rows), :],
                    )
                )
    return started


def wait_all(items):
    for item in items:
        item.wait()


def weight_copies(plan, parts):
    return parts * sum(len(rels) for _, rels in plan)


def in_any(count):
    return [pl.BlockSpec(memory_space=pl.ANY)] * count


def in_vmem(count):
    return [pl.BlockSpec(memory_space=pltpu.VMEM)] * count


def like(array):
    return pltpu.VMEM(array.shape, array.dtype)


def call(kernel, name, micros, small, arrays, outs, scratch, copies):
    return pl.pallas_call(
        kernel,
        in_specs=in_vmem(len(small)) + in_any(len(arrays)),
        out_specs=tuple(in_any(len(outs))),
        out_shape=tuple(outs),
        scratch_shapes=list(scratch) + [pltpu.SemaphoreType.DMA((copies,))],
        compiler_params=pltpu.CompilerParams(vmem_limit_bytes=VMEM_BYTES),
        cost_estimate=cost(micros),
        name=name,
    )(*small, *arrays)


def row_chunks(rows, body, init):
    chunk = 2 * PADDED

    def step(index, carry):
        return body(pl.ds(pl.multiple_of(index * chunk, chunk), chunk), carry)

    return lax.fori_loop(0, rows // chunk, step, init)


def attention_forward_kernel(heads, scale, picks, plan, block_rows, end, *refs):
    count = len(picks)
    vec_ref, qv_ref = refs[:2]
    arrays = refs[2 : 5 + 3 * end]
    x_hbm, bias_hbm, mask_hbm = arrays[:3]
    refs = refs[2 + len(arrays) :]
    weight_refs, refs = refs[: len(plan)], refs[len(plan) :]
    outs, refs = refs[: 5 * count + 2], refs[5 * count + 2 :]
    x, bias, mask, total, normed, normed2, live, weights, qs, ks, vs, ps, atts, sems = refs
    rows = x.shape[0]
    columns = qs.shape[2]
    pairs = rows // (2 * PADDED)
    copies = Copies(sems)
    if end:
        normed_hbm, branch_hbm, live_hbm = arrays[3:]
        arrived_normed = copies.fetch(normed_hbm, normed)
    else:
        arrived_x = copies.fetch(x_hbm, x)
    loads = fetch_weights(copies, plan, weight_refs, block_rows, (weights,))
    arrived = [copies.fetch(mask_hbm, mask)]
    for n, e in enumerate(picks):
        arrived.append(copies.fetch(bias_hbm.at[e], bias.at[n]))
    if end:
        late = [
            copies.fetch(x_hbm, x),
            copies.fetch(branch_hbm, total),
            copies.fetch(live_hbm, live),
        ]
        arrived_normed.wait()
    else:
        arrived_x.wait()

        def first_norm(span, _):
            normal, _ = normalize(x[span, :])
            normed[span, :] = (normal * vec_ref[0:1, :] + vec_ref[1:2, :]).astype(BF16)
            return 0

        row_chunks(rows, first_norm, 0)
        copies.send(normed, outs[-1])
    for n, e in enumerate(picks):
        wait_all(loads[n])
        qkv = dot(normed[...], weights[n, :, : 3 * columns])
        qs[n] = ((qkv[:, :columns] + qv_ref[e, 0:1, :]) * scale).astype(BF16)
        ks[n] = qkv[:, columns : 2 * columns].astype(BF16)
        vs[n] = (qkv[:, 2 * columns :] + qv_ref[e, 1:2, :]).astype(BF16)
        for index, buffer in enumerate((qs, ks, vs)):
            copies.send(buffer.at[n], outs[5 * n + index])
    wait_all(arrived)

    def pair_step(pair, _):
        span = pl.ds(pl.multiple_of(pair * 2 * PADDED, 2 * PADDED), 2 * PADDED)
        for n in range(count):
            query = qs[n, span, :].astype(F32)
            key = ks[n, span, :].astype(F32)
            value = vs[n, span, :].astype(F32)
            results = []
            for side in range(2):
                part = slice(side * PADDED, (side + 1) * PADDED)
                keys = spread_heads(key[part], heads)
                scores = dot(keys, query[part].astype(BF16), 1, 1) + bias[n]
                scores = scores.reshape(heads, PADDED, PADDED) + mask[2 * pair + side][None]
                expo = jnp.exp(scores - jnp.max(scores, axis=1, keepdims=True))
                probs = expo * (1.0 / jnp.sum(expo, axis=1, keepdims=True))
                probs = probs.reshape(heads * PADDED, PADDED).astype(BF16)
                ps[n, 2 * pair + side] = probs
                results.append(dot(probs, spread_heads(value[part], heads), 0, 0))
            atts[n, span, :] = jnp.concatenate(results, axis=0).astype(BF16)
        return 0

    lax.fori_loop(0, pairs, pair_step, 0)
    for n in range(count):
        copies.send(ps.at[n], outs[5 * n + 3])
        copies.send(atts.at[n], outs[5 * n + 4])
    if end:
        wait_all(late)
    branch = total[...] if end else None
    for n in range(count):
        part = dot(atts[n], weights[n, :, 3 * columns :], 1, 1)
        branch = part if branch is None else branch + part
    total[...] = branch
    if end:

        def second_norm(span, _):
            mixed = x[span, :] + live[span, :] * (total[span, :] + vec_ref[2:3, :])
            total[span, :] = mixed
            normal, _ = normalize(mixed)
            normed2[span, :] = (normal * vec_ref[3:4, :] + vec_ref[4:5, :]).astype(BF16)
            return 0

        row_chunks(rows, second_norm, 0)
        copies.send(normed2, outs[-1])
    copies.send(total, outs[-2])
    copies.finish()


def attention_forward(x, weights, picks, vectors, qv, bias, mask, live, heads, scale, earlier=()):
    rows, width = x.shape
    columns = qv.shape[2]
    wins = rows // PADDED
    plan, arrays, block_rows = choose(weights, picks)
    count = len(picks)
    end = bool(earlier)
    shape = jax.ShapeDtypeStruct
    piece = shape((rows, columns), BF16)
    probs = shape((wins, heads * PADDED, PADDED), BF16)
    results = call(
        functools.partial(attention_forward_kernel, heads, scale, picks, plan, block_rows, end),
        "attention_forward",
        4 + 6 * count,
        (vectors, qv),
        [x, bias, mask] + list(earlier) + [live] * end + arrays,
        [piece, piece, piece, probs, piece] * count
        + [shape((rows, width), F32), shape((rows, width), BF16)],
        [
            like(x),
            pltpu.VMEM((count,) + bias.shape[1:], F32),
            like(mask),
            pltpu.VMEM((rows, width), F32),
            pltpu.VMEM((rows, width), BF16),
            pltpu.VMEM((rows, width), BF16),
            like(live),
            pltpu.VMEM((count, width, width), BF16),
        ]
        + [pltpu.VMEM((count, rows, columns), BF16)] * 3
        + [
            pltpu.VMEM((count,) + probs.shape, BF16),
            pltpu.VMEM((count, rows, columns), BF16),
        ],
        weight_copies(plan, 1) + 6 * count + 8,
    )
    saved = {e: results[5 * n : 5 * n + 5] for n, e in enumerate(picks)}
    return saved, results[-2], results[-1]


def ffn_forward_kernel(picks, plan, block_rows, end, *refs):
    count = len(picks)
    bias_ref, vec_ref = refs[:2]
    arrays, refs = refs[2 : 3 + 3 * end], refs[3 + 3 * end :]
    weight_refs, refs = refs[: len(plan)], refs[len(plan) :]
    outs, refs = refs[: 2 * count + 1], refs[2 * count + 1 :]
    normed2, mixed, total, live, first, second, hidden, slope, sems = refs
    rows = normed2.shape[0]
    copies = Copies(sems)
    arrived = copies.fetch(arrays[0], normed2)
    loads = fetch_weights(copies, plan, weight_refs, block_rows, (first, second))
    if end:
        late = [copies.fetch(one, to) for one, to in zip(arrays[1:], (mixed, total, live))]
    arrived.wait()
    branch = None
    for n, e in enumerate(picks):
        wait_all(loads[n])
        before = dot(normed2[...], first[n]) + bias_ref[e]
        cdf = 0.5 * (1.0 + lax.erf(before * (0.5**0.5)))
        density = jnp.exp(-0.5 * before * before) * 0.3989422804014327
        hidden[n] = (before * cdf).astype(BF16)
        copies.send(hidden.at[n], outs[2 * n])
        slope[n] = (cdf + before * density).astype(BF16)
        copies.send(slope.at[n], outs[2 * n + 1])
        part = dot(hidden[n], second[n], 1, 1)
        branch = part if branch is None else branch + part
    if not end:
        total[...] = branch
    else:
        wait_all(late)
        total[...] += branch

        def finish(span, _):
            total[span, :] = mixed[span, :] + live[span, :] * (total[span, :] + vec_ref[5:6, :])
            return 0

        row_chunks(rows, finish, 0)
    copies.send(total, outs[-1])
    copies.finish()


def ffn_forward(normed2, weights, picks, bias, vectors, live, earlier=()):
    rows, width = normed2.shape
    plan, arrays, block_rows = choose(weights, picks)
    count = len(picks)
    end = bool(earlier)
    shape = jax.ShapeDtypeStruct
    piece = shape((rows, width), BF16)
    results = call(
        functools.partial(ffn_forward_kernel, picks, plan, block_rows, end),
        "ffn_forward",
        9,
        (bias, vectors),
        [normed2] + list(earlier) + [live] * end + arrays,
        [piece, piece] * count + [shape((rows, width), F32)],
        [
            like(normed2),
            pltpu.VMEM((rows, width), F32),
            pltpu.VMEM((rows, width), F32),
            like(live),
        ]
        + [pltpu.VMEM((count, width, width), BF16)] * 2
        + [pltpu.VMEM((count, rows, width), BF16)] * 2,
        weight_copies(plan, 2) + 2 * count + 5,
    )
    return {e: results[2 * n : 2 * n + 2] for n, e in enumerate(picks)}, results[-1]


def ffn_backward_kernel(picks, plan, block_rows, end, *refs):
    count = len(picks)
    vec_ref = refs[0]
    given = count + 2 + 3 * end
    arrays, refs = refs[1 : 1 + given], refs[1 + given :]
    weight_refs, refs = refs[: len(plan)], refs[len(plan) :]
    outs, refs = refs[: count + 4], refs[count + 4 :]
    grad, live, mixed, branch, error, attn_grad, slopes, pres, first, second, sums, hidden_sums, sems = refs
    rows, width = grad.shape
    copies = Copies(sems)
    zero = jnp.zeros((1, width), F32)
    slope_hbm = arrays[2 : 2 + count]
    if end:
        mixed_hbm, branch_hbm, error_hbm = arrays[2 + count :]
        copies.fetch(branch_hbm, branch).wait()
    else:
        arrived = [copies.fetch(arrays[0], grad), copies.fetch(arrays[1], live)]
    loads = fetch_weights(copies, plan, weight_refs, block_rows, (first, second))
    slope_loads = [copies.fetch(one, slopes.at[n]) for n, one in enumerate(slope_hbm)]
    if end:
        late = [
            copies.fetch(one, to)
            for one, to in (
                (error_hbm, error),
                (mixed_hbm, mixed),
                (arrays[0], grad),
                (arrays[1], live),
            )
        ]
    else:
        wait_all(arrived)

        def start(span, total):
            part = (live[span, :] * grad[span, :]).astype(BF16)
            branch[span, :] = part
            return total + jnp.sum(part.astype(F32), axis=0, keepdims=True)

        sums[0:1, :] = row_chunks(rows, start, zero)
        copies.send(branch, outs[-3])
    result = None
    for n, e in enumerate(picks):
        wait_all(loads[n])
        flow = dot(branch[...], second[n])
        slope_loads[n].wait()
        pre = (slopes[n].astype(F32) * flow).astype(BF16)
        pres[n] = pre
        copies.send(pres.at[n], outs[n])
        hidden_sums[n] = jnp.sum(pre.astype(F32), axis=0, keepdims=True)
        part = dot(pres[n], first[n], 1, 1)
        result = part if result is None else result + part
    if not end:
        error[...] = result
    else:
        wait_all(late)
        error[...] += result

        def finish(span, totals):
            back, gain_part, shift_part = norm_back_rows(
                mixed[span, :], vec_ref[3:4, :], error[span, :]
            )
            mixed_grad = grad[span, :] + back
            error[span, :] = mixed_grad
            low = (live[span, :] * mixed_grad).astype(BF16)
            attn_grad[span, :] = low
            bias_part = jnp.sum(low.astype(F32), axis=0, keepdims=True)
            return tuple(a + b for a, b in zip(totals, (gain_part, shift_part, bias_part)))

        totals = row_chunks(rows, finish, (zero, zero, zero))
        for index in range(3):
            sums[index : index + 1, :] = totals[index]
        copies.send(attn_grad, outs[-3])
    copies.send(error, outs[-4])
    copies.send(sums, outs[-2])
    copies.send(hidden_sums, outs[-1])
    copies.finish()


def ffn_backward(grad, slopes, weights, picks, vectors, live, earlier=()):
    rows, width = grad.shape
    plan, arrays, block_rows = choose(weights, picks)
    count = len(picks)
    end = bool(earlier)
    shape = jax.ShapeDtypeStruct
    low = shape((rows, width), BF16)
    wide = shape((rows, width), F32)
    results = call(
        functools.partial(ffn_backward_kernel, picks, plan, block_rows, end),
        "ffn_backward",
        9,
        (vectors,),
        [grad, live] + list(slopes) + list(earlier) + arrays,
        [low] * count + [wide, low, shape((8, width), F32), shape((count, 1, width), F32)],
        [like(wide), like(live), like(wide), like(low), like(wide), like(low)]
        + [pltpu.VMEM((count, rows, width), BF16)] * 2
        + [pltpu.VMEM((count, width, width), BF16)] * 2
        + [pltpu.VMEM((8, width), F32), pltpu.VMEM((count, 1, width), F32)],
        weight_copies(plan, 2) + 2 * count + 9,
    )
    return dict(zip(picks, results[:count])), *results[count:]


def weight_grad_kernel(terms, block_rows, plan, count, given, *refs):
    terms_count = sum(len(group) for group in terms)
    lefts_hbm, refs = refs[:terms_count], refs[terms_count:]
    rights_hbm, refs = refs[: terms_count * count], refs[terms_count * count :]
    added_hbm, refs = refs[:given], refs[given:]
    outs, refs = refs[: len(plan)], refs[len(plan) :]
    held, sems = refs[0], refs[-1]
    lefts, refs = refs[1 : 1 + terms_count], refs[1 + terms_count : -1]
    rights, refs = refs[:terms_count], refs[terms_count:]
    added, results = refs[:given], refs[given:]
    own = lax.axis_index("dp")
    blocks = held.shape[0]
    copies = Copies(sems)
    arrived = {}
    for n in range(count):
        for t in range(terms_count):
            waits = arrived.setdefault((n, t), [])
            if n == 0:
                waits.append(copies.fetch(lefts_hbm[t], lefts[t]))
            waits.append(copies.fetch(rights_hbm[t * count + n], rights[t].at[n]))
        if given:
            arrived[n] = copies.fetch(added_hbm[n], added[n])
    for n in range(count):
        for part, group in enumerate(terms):
            columns = []
            for t in group:
                wait_all(arrived[n, t])
                columns.append(dot(lefts[t][...], rights[t][n], 0, 0))
            value = columns[0] if len(columns) == 1 else jnp.concatenate(columns, axis=1)
            held[:, part * block_rows : (part + 1) * block_rows, :] = value.reshape(
                blocks, block_rows, value.shape[1]
            )
        if given:
            arrived[n].wait()
        for (piece, rels), result, out in zip(plan, results, outs):
            if piece != n:
                continue
            for place, rel in enumerate(rels):
                value = held[0 if rel is None else jnp.bitwise_xor(own, rel)]
                if given:
                    value = value + added[n][0 if rel is None else rel].astype(F32)
                result[place] = value.astype(BF16)
            copies.send(result, out)
    copies.finish()


def weight_grad(terms, pairs, plan, block_rows, added, micros):
    lefts = [left for left, _ in pairs]
    count = len(pairs[0][1])
    rights = [one for _, several in pairs for one in several]
    width = lefts[0].shape[1]
    height = len(terms) * block_rows
    outs = [jax.ShapeDtypeStruct((len(rels), height, width), BF16) for _, rels in plan]
    return call(
        functools.partial(weight_grad_kernel, terms, block_rows, plan, count, len(added)),
        "weight_grad",
        micros,
        (),
        lefts + rights + list(added),
        outs,
        [pltpu.VMEM((width // block_rows, height, width), F32)]
        + [like(left) for left in lefts]
        + [pltpu.VMEM((count,) + several[0].shape, BF16) for _, several in pairs]
        + [like(one) for one in added]
        + [like(out) for out in outs],
        len(lefts) + len(rights) + len(added) + len(outs),
    )


def attention_backward_kernel(heads, scale, picks, plan, block_rows, end, *refs):
    count = len(picks)
    vec_ref = refs[0]
    given = 1 + 4 * count + 3 * end
    arrays, refs = refs[1 : 1 + given], refs[1 + given :]
    weight_refs, refs = refs[: len(plan)], refs[len(plan) :]
    outs, refs = refs[: count + 3 + end], refs[count + 3 + end :]
    attn_grad, x, mixed_grad, error, weights, qs, ks, vs, ps, gs, grads, scores_sum, sums, small, sems = refs
    rows, width = attn_grad.shape
    columns = qs.shape[2]
    pairs = rows // (2 * PADDED)
    copies = Copies(sems)
    arrived = copies.fetch(arrays[0], attn_grad)
    loads = fetch_weights(copies, plan, weight_refs, block_rows, (weights,))
    saved = []
    for n in range(count):
        for index, buffer in enumerate((qs, ks, vs, ps)):
            saved.append(copies.fetch(arrays[1 + 4 * n + index], buffer.at[n]))
    if end:
        late = [
            copies.fetch(one, to)
            for one, to in zip(arrays[1 + 4 * count :], (x, mixed_grad, error))
        ]
    scores_sum[...] = jnp.zeros(scores_sum.shape, F32)
    arrived.wait()
    for n in range(count):
        wait_all(loads[n])
        gs[n] = dot(attn_grad[...], weights[n, :, 3 * columns :]).astype(BF16)
    wait_all(saved)

    def pair_step(pair, _):
        span = pl.ds(pl.multiple_of(pair * 2 * PADDED, 2 * PADDED), 2 * PADDED)
        for n in range(count):
            query, key, value, grad = [
                buffer[n, span, :].astype(F32) for buffer in (qs, ks, vs, gs)
            ]
            results = []
            for side in range(2):
                part = slice(side * PADDED, (side + 1) * PADDED)
                keys = spread_heads(key[part], heads)
                values = spread_heads(value[part], heads)
                grad_low = grad[part].astype(BF16)
                low = ps[n, 2 * pair + side]
                probs = low.astype(F32)
                flow = dot(values, grad_low, 1, 1)
                inner = jnp.sum(
                    (probs * flow).reshape(heads, PADDED, PADDED), axis=1, keepdims=True
                )
                score = probs.reshape(heads, PADDED, PADDED) * (
                    flow.reshape(heads, PADDED, PADDED) - inner
                )
                score = score.reshape(heads * PADDED, PADDED).astype(BF16)
                scores_sum[n] += score.astype(F32)
                results.append(
                    jnp.concatenate(
                        [
                            dot(score, keys, 0, 0) * scale,
                            merge_heads(dot(score, query[part].astype(BF16)), heads),
                            merge_heads(dot(low, grad_low), heads),
                        ],
                        axis=1,
                    )
                )
            grads[n, span, :] = jnp.concatenate(results, axis=0).astype(BF16)
        return 0

    lax.fori_loop(0, pairs, pair_step, 0)
    result = None
    for n in range(count):
        copies.send(grads.at[n], outs[n])
        sums[n] = jnp.sum(grads[n].astype(F32), axis=0, keepdims=True)
        part = dot(grads[n], weights[n, :, : 3 * columns], 1, 1)
        result = part if result is None else result + part
    copies.send(scores_sum, outs[count + 1])
    copies.send(sums, outs[count + 2])
    if not end:
        error[...] = result
    else:
        wait_all(late)
        error[...] += result
        zero = jnp.zeros((1, width), F32)

        def finish(span, totals):
            back, gain_part, shift_part = norm_back_rows(
                x[span, :], vec_ref[0:1, :], error[span, :]
            )
            error[span, :] = mixed_grad[span, :] + back
            return totals[0] + gain_part, totals[1] + shift_part

        totals = row_chunks(rows, finish, (zero, zero))
        for index in range(2):
            small[index : index + 1, :] = totals[index]
        copies.send(small, outs[count + 3])
    copies.send(error, outs[count])
    copies.finish()


def attention_backward(attn_grad, saved, weights, picks, vectors, heads, scale, earlier=()):
    rows, width = attn_grad.shape
    columns = saved[picks[0]][0].shape[1]
    plan, arrays, block_rows = choose(weights, picks)
    count = len(picks)
    end = bool(earlier)
    probs = saved[picks[0]][3]
    shape = jax.ShapeDtypeStruct
    wide = shape((rows, width), F32)
    pieces = [item for e in picks for item in saved[e][:4]]
    outs = [shape((rows, 3 * columns), BF16)] * count + [
        wide,
        shape((count, heads * PADDED, PADDED), F32),
        shape((count, 1, 3 * columns), F32),
    ]
    results = call(
        functools.partial(attention_backward_kernel, heads, scale, picks, plan, block_rows, end),
        "attention_backward",
        6 + 8 * count,
        (vectors,),
        [attn_grad] + pieces + list(earlier) + arrays,
        outs + [shape((8, width), F32)] * end,
        [like(attn_grad), like(wide), like(wide), like(wide)]
        + [pltpu.VMEM((count, width, width), BF16)]
        + [pltpu.VMEM((count, rows, columns), BF16)] * 3
        + [pltpu.VMEM((count,) + probs.shape, BF16)]
        + [pltpu.VMEM((count, rows, columns), BF16)]
        + [pltpu.VMEM((count, rows, 3 * columns), BF16)]
        + [like(outs[count + 1]), like(outs[count + 2]), pltpu.VMEM((8, width), F32)],
        weight_copies(plan, 1) + 5 * count + 9,
    )
    return dict(zip(picks, results[:count])), *results[count:]


def swap(values, axis, bit):
    size = lax.axis_size(axis)
    return lax.ppermute(values, axis, [(i, i ^ (1 << bit)) for i in range(size)])


def bits_in(axis):
    return lax.axis_size(axis).bit_length() - 1


def pick(values, index, dim):
    return lax.dynamic_index_in_dim(values, index, dim, keepdims=False)


def tie(values, token):
    if token is None:
        return values
    return lax.optimization_barrier((values, token))[0]


def whole_tiles(rows):
    return rows % 16 == 0


def in_order(values):
    index = jnp.bitwise_xor(jnp.arange(values.shape[0]), lax.axis_index("dp"))
    return jnp.take(values, index, axis=0)


def relatives(halves):
    count = lax.axis_size("dp")
    size = count // halves
    return [
        [tuple(range(part * size + side, (part + 1) * size, 2)) for part in range(halves)]
        for side in range(2)
    ]


class Gather:
    def __init__(self, shard, parts, ways):
        self.shard = shard
        self.parts = parts
        self.ways = ways
        self.bits = list(range(1, bits_in("dp")))
        self.entries = []

    def line(self, after=None):
        held = tie(self.shard, after)[None]
        for bit in self.bits[:-1]:
            held = jnp.concatenate([held, swap(held, "dp", bit)])
        self.held = [held]
        return held

    def last(self, after=None):
        self.moved = swap(tie(self.held[0], after), "dp", self.bits[-1])

    def last_end(self, until=None):
        moved = tie(self.moved, until)
        if len(self.ways) == 2:
            self.held.append(moved)
        else:
            self.held = [jnp.concatenate([self.held[0], moved])]
        return moved

    def sides(self, parts, after=None):
        if parts[0] == 0:
            self.side, self.far = [], []
        for part in parts:
            held = tie(self.held[part], after)
            self.side.append(swap(held, "dp", 0))
            self.far.append(swap(held, "head", 1))

    def sides_end(self, parts, until=None):
        for part in parts:
            self.side[part], self.far[part] = tie((self.side[part], self.far[part]), until)

    def corner(self, part, after=None):
        if part == 0:
            self.corners = []
        if self.ways[part] == "x":
            self.corners.append(swap(tie(self.side[part], after), "head", 1))
        else:
            self.corners.append(swap(tie(self.far[part], after), "dp", 0))

    def corner_end(self, part, until=None):
        self.corners[part] = tie(self.corners[part], until)
        return self.corners[part]

    def core(self, kind):
        own, other = relatives(len(self.ways))
        arrays, e, rels = {
            "held": (self.held, 0, own),
            "side": (self.side, 0, other),
            "far": (self.far, 2, own),
            "corner": (getattr(self, "corners", None), 2, other),
        }[kind]
        for one, several in zip(arrays, rels):
            self.entries.append((e, one, several))
            self.entries.append((e + 1, swap(one, "head", 0), several))

    def result(self):
        rows = self.shard.shape[0] // self.parts
        width = self.shard.shape[1]
        if whole_tiles(rows):
            plan = tuple((e, rels) for e, _, rels in self.entries)
            return plan, [one for _, one, _ in self.entries], rows
        arrays = []
        plan = []
        for e in range(PIECES):
            mine = [(one, rels) for piece, one, rels in self.entries if piece == e]
            if not mine:
                continue
            order = sum((rels for _, rels in mine), ())
            blocks = jnp.concatenate([one for one, _ in mine])
            blocks = in_order(blocks[jnp.argsort(jnp.array(order))])
            blocks = blocks.reshape(-1, self.parts, rows, width).transpose(1, 0, 2, 3)
            arrays.append(blocks.reshape(1, -1, width))
            plan.append((e, (None,)))
        return tuple(plan), arrays, arrays[0].shape[1] // self.parts


def plus(left, right):
    return (left.astype(F32) + right.astype(F32)).astype(BF16)


class Scatter:
    def __init__(self, terms, rows, micros, ways):
        self.terms = terms
        self.rows = rows
        self.micros = micros
        self.ways = ways
        self.blocks = lax.axis_size("dp")
        self.tiled = whole_tiles(rows)
        self.every = tuple(range(self.blocks)) if self.tiled else (None,)
        self.block_rows = rows if self.tiled else rows * self.blocks
        self.bits = list(reversed(range(1, bits_in("dp"))))

    def away(self, pairs):
        plan = ((0, self.every), (1, self.every))
        self.sent = weight_grad(self.terms, pairs, plan, self.block_rows, (), self.micros)
        return self.sent

    def core(self):
        self.added = [swap(one, "head", 0) for one in self.sent]

    def near(self, pairs, until=None):
        added = tie(self.added, until)
        halves = len(self.ways)
        quarters = [rels for side in relatives(halves) for rels in side]
        if self.tiled:
            plan = tuple((n, rels) for n in range(2) for rels in quarters)
        else:
            plan = ((0, self.every), (1, self.every))
        outs = weight_grad(self.terms, pairs, plan, self.block_rows, added, self.micros)
        if not self.tiled:
            parts, rows = len(self.terms), self.rows
            result = []
            for one in outs:
                one = one.reshape(parts, self.blocks, rows, -1).transpose(1, 0, 2, 3)
                one = in_order(one.reshape(self.blocks, parts * rows, -1))
                result += [one[jnp.array(rels)] for rels in quarters]
            outs = result
        self.held, self.side, self.far, self.corners = [
            list(outs[halves * n : halves * (n + 1)]) for n in range(4)
        ]
        return outs

    def corner(self, after=None):
        self.moved = []
        for way, one in zip(self.ways, tie(self.corners, after)):
            self.moved.append(swap(one, "head", 1) if way == "x" else swap(one, "dp", 0))

    def corner_end(self, until=None):
        moved = tie(self.moved, until)
        for part, way in enumerate(self.ways):
            target = self.side if way == "x" else self.far
            target[part] = plus(target[part], moved[part])

    def sides(self, after=None):
        side, far = tie((self.side, self.far), after)
        self.moved = [
            (swap(side[part], "dp", 0), swap(far[part], "head", 1))
            for part in reversed(range(len(self.ways)))
        ][::-1]

    def sides_end(self, until=None):
        moved = tie(self.moved, until)
        for part, (one, other) in enumerate(moved):
            self.held[part] = plus(self.held[part].astype(F32) + one.astype(F32), other)

    def last(self, after=None):
        if len(self.held) == 1:
            cut = self.held[0].shape[0] // 2
            self.held = [self.held[0][:cut], self.held[0][cut:]]
        self.moved = swap(tie(self.held[1], after), "dp", self.bits[0])

    def last_end(self, until=None):
        self.held = plus(self.held[0], tie(self.moved, until))

    def line(self, after=None):
        held = tie(self.held, after)
        for bit in self.bits[1:]:
            cut = held.shape[0] // 2
            moved = swap(held[cut:], "dp", bit)
            held = held[:cut].astype(F32) + moved.astype(F32)
            held = held if bit == self.bits[-1] else held.astype(BF16)
        self.held = held

    def line_end(self, until=None):
        self.result = tie(self.held, until)[0].astype(F32)
        return self.result


class SmallSum:
    def __init__(self, values):
        self.total = values
        self.left = [("head", 0), ("head", 1)]
        self.left += [("dp", bit) for bit in range(bits_in("dp"))]
        self.moved = None

    def step(self, until=None):
        self.result(until)
        axis, bit = self.left.pop(0)
        self.moved = swap(self.total, axis, bit)

    def end(self):
        return not self.left

    def result(self, until=None):
        if self.moved is not None:
            self.total = self.total + tie(self.moved, until)
        self.moved = None
        return self.total


class SmallGather:
    def __init__(self, values):
        self.held = values[None, None]
        self.steps = [("dp", bit) for bit in range(1, bits_in("dp"))]
        self.steps += [("dp", 0), ("head", 1), ("head", 0)]
        self.done = []

    def step(self, after=None):
        axis, bit = self.steps[len(self.done)]
        self.done.append((axis, bit))
        held = tie(self.held, after)
        self.held = jnp.concatenate([held, swap(held, axis, bit)], axis=0 if axis == "dp" else 1)

    def result(self):
        for axis, dim in (("dp", 0), ("head", 1)):
            order = [bit for name, bit in self.done if name == axis]
            index = jnp.arange(lax.axis_size(axis)) ^ lax.axis_index(axis)
            place = sum(((index >> bit) & 1) << n for n, bit in enumerate(order))
            self.held = jnp.take(self.held, place, axis=dim)
        return self.held


def unshift(values):
    grid = values.reshape(values.shape[:-1] + (WSIDE, WSIDE))
    return jnp.roll(grid, (SHIFT, SHIFT), axis=(-2, -1)).reshape(values.shape)


def pad_rows(values):
    grid = values.reshape(-1, WTOK, values.shape[1])
    grid = jnp.pad(grid, ((0, 0), (0, PADDED - WTOK), (0, 0)))
    return grid.reshape(-1, values.shape[1])


def drop_rows(values):
    grid = values.reshape(-1, PADDED, values.shape[1])[:, :WTOK]
    return grid.reshape(-1, values.shape[1])


def attention_mask(pad, region):
    allowed = (pad[:, :, None] == 1) & (region[:, :, None] == region[:, None, :])
    mask = jnp.where(allowed, 0.0, MASKED).astype(F32)
    extra = PADDED - WTOK
    mask = jnp.pad(mask, ((0, 0), (0, 0), (0, extra)))
    return jnp.pad(mask, ((0, 0), (0, extra), (0, 0)), constant_values=ABSENT)


def shards(
    tokens,
    cotangent,
    crop_counts,
    pad_mask,
    region_ids,
    rel_index,
    norm_gain,
    norm_shift,
    qkv_weight,
    qv_bias,
    bias_table,
    proj_weight,
    fc1_weight,
    fc1_bias,
    fc2_weight,
    out_bias,
):
    rows = tokens.shape[0]
    width = tokens.shape[1]
    wins = rows // WTOK
    local_width = qkv_weight.shape[3]
    local_heads = bias_table.shape[1]
    rel_count = bias_table.shape[2]
    dp_width = norm_gain.shape[2]
    dp_hidden = fc1_bias.shape[1]
    pieces = lax.axis_size("head")
    heads_total = local_heads * pieces
    head_dim = local_width // local_heads
    scale = head_dim ** (-0.5)
    head_index = lax.axis_index("head")
    dp_index = lax.axis_index("dp")
    relative = [head_index ^ e for e in range(pieces)]

    shard_rows = qkv_weight.shape[1]
    attn_shards = [
        jnp.concatenate(
            [qkv_weight[block].reshape(-1, 3 * local_width), proj_weight[block].T], axis=1
        )
        for block in range(BLOCKS)
    ]
    ffn_shards = [
        jnp.concatenate([fc1_weight[block], fc2_weight[block].T]) for block in range(BLOCKS)
    ]
    small = jnp.concatenate(
        [item.reshape(-1) for item in (norm_gain, norm_shift, qv_bias, out_bias, fc1_bias, bias_table)]
    )
    small = jnp.pad(small, (0, -small.shape[0] % 128))
    near, away = (0, 2), (1, 3)
    first, second = (0, 1), (2, 3)
    attn_gather = [Gather(shard, 1, "x") for shard in attn_shards]
    ffn_gather = [Gather(shard, 2, "xy") for shard in ffn_shards]
    a0, a1 = attn_gather
    f0, f1 = ffn_gather
    small_gather = SmallGather(small)
    a0.line()
    small_gather.step()
    a0.last()
    f0.line(a0.held)
    for _ in range(bits_in("dp") - 2):
        small_gather.step(a0.held)
    a0.last_end()
    a0.sides((0,))
    a0.core("held")
    small_gather.step(a0.held)
    f0.last(a0.held)
    a0.sides_end((0,))
    a0.core("side")
    small_gather.step(a0.far)
    small_gather.step(a0.far)
    small_all = small_gather.result()
    offset = 0
    vectors = []
    for item in (norm_gain, norm_shift, qv_bias, out_bias):
        count = item.size
        piece = small_all[:, 0, offset : offset + count].reshape(-1, BLOCKS, 2, dp_width)
        vectors.append(piece.transpose(1, 2, 0, 3).reshape(BLOCKS, 2, width).astype(F32))
        offset += count
    gains, shifts, qv_all, out_all = vectors
    hidden_bias = small_all[:, 0, offset : offset + fc1_bias.size].reshape(-1, BLOCKS, dp_hidden)
    hidden_bias = hidden_bias.transpose(1, 0, 2).reshape(BLOCKS, pieces, -1).astype(F32)
    offset += fc1_bias.size
    tables = small_all[0, :, offset : offset + bias_table.size]
    tables = tables.reshape(pieces, BLOCKS, local_heads, rel_count)
    qv_pieces = qv_all.reshape(BLOCKS, 2, pieces, local_width)

    counts = jnp.repeat(crop_counts, CROP_MAX)
    slots = jnp.arange(pad_mask.shape[0], dtype=jnp.int32) % CROP_MAX
    live_all = (slots < counts).astype(F32)
    live_windows = lax.dynamic_slice_in_dim(live_all, head_index * wins, wins, 0)
    real = (jnp.arange(PADDED) < WTOK).astype(F32)
    live = (live_windows[:, None] * real[None, :]).reshape(-1, 1)
    pad = lax.dynamic_slice_in_dim(pad_mask, head_index * wins, wins, 0)
    region = unshift(lax.dynamic_slice_in_dim(region_ids, head_index * wins, wins, 0))
    masks = (attention_mask(pad, jnp.zeros_like(region)), attention_mask(pad, region))
    extra = PADDED - WTOK
    onehots = []
    for index in (rel_index, unshift(unshift(rel_index).T).T):
        by_key = jnp.pad(index.T, ((0, extra), (0, extra)), constant_values=-1).reshape(1, -1)
        ids = jnp.arange(rel_count, dtype=jnp.int32)[:, None]
        onehots.append((ids == by_key).astype(BF16))

    def ordered(values, dim):
        return jnp.stack([pick(values, rel, dim) for rel in relative])

    block_rows = local_heads * PADDED
    vectors, qv, biases, hidden_biases = [], [], [], []
    for block in range(BLOCKS):
        rows8 = [
            gains[block, 0],
            shifts[block, 0],
            out_all[block, 0],
            gains[block, 1],
            shifts[block, 1],
            out_all[block, 1],
        ]
        vectors.append(jnp.pad(jnp.stack(rows8), ((0, 2), (0, 0))))
        qv.append(ordered(qv_pieces[block], 1))
        table = ordered(tables[:, block], 0).reshape(heads_total, rel_count)
        bias = jnp.dot(table, onehots[block % 2], preferred_element_type=F32)
        biases.append(bias.reshape(pieces, block_rows, PADDED))
        hidden_biases.append(ordered(hidden_bias[block], 0)[:, None, :])

    residual = pad_rows(tokens).astype(F32)

    def attend(block, x, picks, token, earlier=()):
        return attention_forward(
            x,
            attn_gather[block].result(),
            picks,
            tie(vectors[block], token),
            qv[block],
            biases[block],
            masks[block % 2],
            live,
            local_heads,
            scale,
            earlier,
        )

    def feed(block, normed2, picks, token, earlier=()):
        return ffn_forward(
            normed2,
            ffn_gather[block].result(),
            picks,
            hidden_biases[block],
            tie(vectors[block], token),
            live,
            earlier,
        )

    x0 = residual
    a0.corner(0)
    f0.sides((0,), a0.far)
    saved_0, branch, normed_0 = attend(0, x0, first, None)
    a0.corner_end(0, branch)
    f0.last_end(branch)
    f0.sides_end((0,), branch)
    a0.core("far")
    a0.core("corner")
    f0.core("held")
    f0.sides((1,))
    f0.corner(0)
    a1.line(f0.held[1])
    more, mixed_0, normed2_0 = attend(0, x0, second, None, (normed_0, branch))
    saved_0.update(more)
    a1.last((a1.held, mixed_0))
    f0.sides_end((1,), mixed_0)
    f0.core("side")
    f0.corner(1)
    f1.line(a1.held)
    f0.core("far")
    hidden_0, branch = feed(0, normed2_0, first, None)
    f0.corner_end(0, branch)
    f0.corner_end(1, branch)
    f0.core("corner")
    a1.last_end(branch)
    a1.sides((0,))
    a1.core("held")
    f1.last((f1.held, a1.held))
    more, x1 = feed(0, normed2_0, second, None, (mixed_0, branch))
    hidden_0.update(more)
    a1.sides_end((0,), x1)
    a1.core("side")
    a1.corner(0)
    f1.sides((0,), x1)
    saved_1, branch, normed_1 = attend(1, x1, first, None)
    a1.corner_end(0, branch)
    a1.core("far")
    a1.core("corner")
    f1.last_end(branch)
    f1.sides_end((0,), branch)
    f1.core("held")
    f1.sides((1,))
    f1.corner(0)
    more, mixed_1, normed2_1 = attend(1, x1, second, None, (normed_1, branch))
    saved_1.update(more)
    f1.sides_end((1,), mixed_1)
    f1.core("side")
    f1.corner(1)
    f1.core("far")
    hidden_1, branch = feed(1, normed2_1, first, None)
    f1.corner_end(0, branch)
    f1.corner_end(1, branch)
    f1.core("corner")
    more, residual = feed(1, normed2_1, second, None, (mixed_1, branch))
    hidden_1.update(more)
    kept = [
        (x0, mixed_0, normed_0, normed2_0, saved_0, hidden_0),
        (x1, mixed_1, normed_1, normed2_1, saved_1, hidden_1),
    ]

    grad_rows = pad_rows(cotangent).astype(F32)
    shard_grads = [None] * BLOCKS
    small_sums = [None] * BLOCKS
    token = residual
    old_f = old_a = None
    for block in reversed(range(BLOCKS)):
        x, mixed, normed, normed2, saved, hidden = kept[block]
        ffn_sum = Scatter(((0,), (1,)), shard_rows, 8, "xy")
        attn_sum = Scatter(((0, 1),), shard_rows, 7, "x" if block else "y")
        ffn_w = ffn_gather[block].result()
        attn_w = attn_gather[block].result()

        def ffn_pairs(picks, pre, token):
            return (
                (tie(normed2, token), [pre[e] for e in picks]),
                (branch_grad, [hidden[e][0] for e in picks]),
            )

        def attn_pairs(picks, qkv, token):
            return (
                (tie(normed, token), [qkv[e] for e in picks]),
                (attn_grad, [saved[e][4] for e in picks]),
            )

        pre_a, error, branch_grad, small_b, hidden_a = ffn_backward(
            grad_rows,
            [hidden[e][1] for e in away],
            ffn_w,
            away,
            tie(vectors[block], token),
            live,
        )
        token = None
        if old_a is not None:
            old_a.corner_end(error)
            token = (old_a.side, old_a.far)
            old_a.sides()
        sent = ffn_sum.away(ffn_pairs(away, pre_a, token))
        ffn_sum.core()
        token = sent
        if old_f is not None:
            old_f.last_end(sent)
            token = (sent, old_f.held)
            old_f.line()
        pre_n, mixed_grad, attn_grad, small_f, hidden_n = ffn_backward(
            grad_rows,
            [hidden[e][1] for e in near],
            ffn_w,
            near,
            tie(vectors[block], token),
            live,
            (mixed, branch_grad, error),
        )
        token = None
        if old_a is not None:
            old_f.line_end(attn_grad)
            old_a.sides_end(attn_grad)
            token = (old_f.result, old_a.held)
            old_a.last()
        ready = ffn_sum.near(ffn_pairs(near, pre_n, token), attn_grad)
        ffn_sum.corner()
        qkv_a, error, scores_a, sums_a = attention_backward(
            attn_grad, saved, attn_w, away, tie(vectors[block], ready), local_heads, scale
        )
        ffn_sum.corner_end(error)
        token = (ffn_sum.side, ffn_sum.far)
        ffn_sum.sides()
        if old_a is not None:
            old_a.last_end(error)
            token = (token, old_a.held)
            old_a.line()
        sent = attn_sum.away(attn_pairs(away, qkv_a, token))
        attn_sum.core()
        token = sent
        if old_a is not None:
            token = (sent, old_a.line_end(sent))
        qkv_n, grad_rows, scores_n, sums_n, small_a = attention_backward(
            attn_grad,
            saved,
            attn_w,
            near,
            tie(vectors[block], token),
            local_heads,
            scale,
            (x, mixed_grad, error),
        )
        ffn_sum.sides_end(grad_rows)
        token = ffn_sum.held
        ffn_sum.last()
        token = attn_sum.near(attn_pairs(near, qkv_n, token), grad_rows)
        attn_sum.corner()
        old_f, old_a = ffn_sum, attn_sum
        shard_grads[block] = (attn_sum, ffn_sum)

        def together(one, other):
            return ordered(jnp.stack([one[0], other[0], one[1], other[1]]), 0)

        table_grad = lax.dot_general(
            together(scores_n, scores_a).reshape(heads_total, -1),
            onehots[block % 2].astype(F32),
            (((1,), (1,)), ((), ())),
            precision=lax.Precision.HIGHEST,
            preferred_element_type=F32,
        )
        qv_sums = together(sums_n, sums_a)[:, 0]
        items = [
            small_a[0],
            small_f[0],
            small_a[1],
            small_f[1],
            qv_sums[:, :local_width].reshape(-1),
            qv_sums[:, 2 * local_width :].reshape(-1),
            small_f[2],
            small_b[0],
            together(hidden_n, hidden_a).reshape(-1),
            table_grad.reshape(-1),
        ]
        small_sums[block] = jnp.concatenate(items)
    small_sum = SmallSum(tie(jnp.stack(small_sums), token))
    small_sum.step()
    old_a.corner_end()
    small_sum.step(until=old_a.side)
    old_a.sides()
    old_f.last_end(token)
    old_f.line()
    old_a.sides_end()
    small_sum.step(until=old_a.held)
    old_a.last()
    old_a.last_end()
    while not small_sum.end():
        small_sum.step(until=old_a.held)
    old_a.line()
    old_a.line_end()
    old_f.line_end()
    shard_grads = [
        (attn.result, ffn.result[:shard_rows], ffn.result[shard_rows:])
        for attn, ffn in shard_grads
    ]

    totals = small_sum.result()

    def own(values):
        return lax.dynamic_slice_in_dim(values, dp_index * dp_width, dp_width, 2)

    small_grads = []
    for index in range(4):
        part = totals[:, 2 * index * width : 2 * (index + 1) * width]
        small_grads.append(own(part.reshape(BLOCKS, 2, width)))
    offset = 8 * width
    hidden_total = totals[:, offset : offset + pieces * fc1_weight.shape[2]]
    fc1_bias_grad = lax.dynamic_slice_in_dim(hidden_total, dp_index * dp_hidden, dp_hidden, 1)
    offset += hidden_total.shape[1]
    table_total = totals[:, offset:].reshape(BLOCKS, heads_total, rel_count)
    bias_table_grad = lax.dynamic_slice_in_dim(
        table_total, head_index * local_heads, local_heads, 1
    )
    qkv_weight_grad = jnp.stack(
        [item[0][:, : 3 * local_width].reshape(-1, 3, local_width) for item in shard_grads]
    )
    proj_weight_grad = jnp.stack([item[0][:, 3 * local_width :].T for item in shard_grads])
    fc1_weight_grad = jnp.stack([item[1] for item in shard_grads])
    fc2_weight_grad = jnp.stack([item[2].T for item in shard_grads])
    return (
        drop_rows(residual),
        drop_rows(grad_rows),
        small_grads[0],
        small_grads[1],
        qkv_weight_grad,
        small_grads[2],
        bias_table_grad,
        proj_weight_grad,
        fc1_weight_grad,
        fc1_bias_grad,
        fc2_weight_grad,
        small_grads[3],
    )


def solution(mesh):
    placed = (
        P(("dp", "head"), None),
        P(("dp", "head"), None),
        P("dp"),
        P("dp", None),
        P("dp", None),
        P(),
        P(None, None, "dp"),
        P(None, None, "dp"),
        P(None, "dp", None, "head"),
        P(None, None, "dp"),
        P(None, "head", None),
        P(None, "head", "dp"),
        P(None, "dp", "head"),
        P(None, "dp"),
        P(None, "head", "dp"),
        P(None, None, "dp"),
    )
    return jax.shard_map(
        shards,
        mesh=mesh,
        in_specs=placed,
        out_specs=(
            P(("dp", "head"), None),
            P(("dp", "head"), None),
            P(None, None, "dp"),
            P(None, None, "dp"),
            P(None, "dp", None, "head"),
            P(None, None, "dp"),
            P(None, "head", None),
            P(None, "head", "dp"),
            P(None, "dp", "head"),
            P(None, "dp"),
            P(None, "head", "dp"),
            P(None, None, "dp"),
        ),
        check_vma=False,
    )
```

```python
import functools

import jax
import jax.numpy as jnp
from jax import lax
from jax.experimental import pallas as pl
from jax.experimental.pallas import tpu as pltpu
from jax.sharding import PartitionSpec as P

WSIDE = 7
SHIFT = 3
CROP_MAX = 12
BLOCKS = 2
WTOK = 49
PADDED = 56
PIECES = 4
VMEM_BYTES = 60 * 2**20

EPSILON = 1e-05
MASKED = -100.0
ABSENT = -1e30
BF16 = jnp.bfloat16
F32 = jnp.float32


def cost(micros):
    return pl.CostEstimate(
        flops=int(micros * 1e8), bytes_accessed=int(micros * 3e5), transcendentals=0
    )


def dot(left, right, left_dim=1, right_dim=0):
    return lax.dot_general(
        left, right, (((left_dim,), (right_dim,)), ((), ())), preferred_element_type=F32
    )


def normalize(values):
    centred = values - jnp.mean(values, axis=-1, keepdims=True)
    scale = lax.rsqrt(jnp.mean(centred * centred, axis=-1, keepdims=True) + EPSILON)
    return centred * scale, scale


def norm_back_rows(values, gain, error):
    normal, scale = normalize(values)
    flow = error * gain
    grad = (
        flow
        - jnp.mean(flow, axis=-1, keepdims=True)
        - normal * jnp.mean(flow * normal, axis=-1, keepdims=True)
    ) * scale
    return grad, jnp.sum(error * normal, axis=0, keepdims=True), jnp.sum(error, axis=0, keepdims=True)


def spread_heads(values, heads):
    columns = values.shape[1]
    owner = lax.broadcasted_iota(jnp.int32, values.shape, 1) // (columns // heads)
    return jnp.concatenate(
        [jnp.where(owner == head, values, 0.0) for head in range(heads)], axis=0
    ).astype(BF16)


def merge_heads(values, heads):
    rows = values.shape[0] // heads
    columns = values.shape[1]
    owner = lax.broadcasted_iota(jnp.int32, (rows, columns), 1) // (columns // heads)
    total = values[:rows]
    for head in range(1, heads):
        total = jnp.where(owner == head, values[head * rows : (head + 1) * rows], total)
    return total


class Copies:
    def __init__(self, sems):
        self.sems = sems
        self.used = 0
        self.leaving = []

    def plan(self, source, target):
        copy = pltpu.make_async_copy(source, target, self.sems.at[self.used])
        self.used += 1
        return copy

    def send(self, source, target):
        copy = self.plan(source, target)
        copy.start()
        self.leaving.append(copy)

    def finish(self):
        wait_all(self.leaving)


def start_all(*groups):
    for group in groups:
        for item in group:
            item.start()


def choose(weights, picks):
    plan, arrays, rows, first = weights
    chosen = [index for index, (e, _) in enumerate(plan) if e in picks]
    plan = tuple((picks.index(plan[index][0]), plan[index][1], first) for index in chosen)
    return plan, [arrays[index] for index in chosen], rows


def weight_plans(copies, plan, refs, rows, parts):
    own = lax.axis_index("dp")
    plans = {}
    for (slot, rels, first), ref in zip(plan, refs):
        for place, rel in enumerate(rels):
            start = 0 if rel is None else pl.multiple_of(jnp.bitwise_xor(own, rel) * rows, rows)
            for part, target in enumerate(parts):
                plans.setdefault((part, slot), []).append(
                    copies.plan(
                        ref.at[place, pl.ds(first + part * rows, rows), :],
                        target.at[slot, pl.ds(start, rows), :],
                    )
                )
    return plans


def wait_all(items):
    for item in items:
        item.wait()


def weight_copies(plan, parts):
    return parts * sum(len(rels) for _, rels, _ in plan)


def in_any(count):
    return [pl.BlockSpec(memory_space=pl.ANY)] * count


def in_vmem(count):
    return [pl.BlockSpec(memory_space=pltpu.VMEM)] * count


def like(array):
    return pltpu.VMEM(array.shape, array.dtype)


def call(kernel, name, micros, live, small, arrays, outs, scratch, copies):
    return pl.pallas_call(
        kernel,
        in_specs=[pl.BlockSpec(memory_space=pltpu.SMEM)] + in_vmem(len(small)) + in_any(len(arrays)),
        out_specs=tuple(in_any(len(outs))),
        out_shape=tuple(outs),
        scratch_shapes=list(scratch) + [pltpu.SemaphoreType.DMA((copies,))],
        compiler_params=pltpu.CompilerParams(vmem_limit_bytes=VMEM_BYTES),
        cost_estimate=cost(micros),
        name=name,
    )(live, *small, *arrays)


def row_chunks(rows, body, init):
    chunk = 2 * PADDED

    def step(index, carry):
        return body(pl.ds(pl.multiple_of(index * chunk, chunk), chunk), index, carry)

    return lax.fori_loop(0, rows // chunk, step, init)


def live_rows(live_ref, index):
    place = lax.broadcasted_iota(jnp.int32, (2 * PADDED, 1), 0)
    value = jnp.where(place < PADDED, live_ref[2 * index], live_ref[2 * index + 1])
    return jnp.where(lax.rem(place, PADDED) < WTOK, value, 0.0)


def attention_forward_kernel(heads, scale, picks, plan, block_rows, end, *refs):
    count = len(picks)
    live_ref, vec_ref, qv_ref = refs[:3]
    arrays = refs[3 : 6 + 2 * end]
    x_hbm, bias_hbm, mask_hbm = arrays[:3]
    refs = refs[3 + len(arrays) :]
    weight_refs, refs = refs[: len(plan)], refs[len(plan) :]
    outs, refs = refs[: 5 * count + 2], refs[5 * count + 2 :]
    x, bias, mask, total, normed, normed2, weights, qs, ks, vs, ps, atts, sems = refs
    rows = x.shape[0]
    columns = qs.shape[2]
    pairs = rows // (2 * PADDED)
    copies = Copies(sems)
    weight = weight_plans(copies, plan, weight_refs, block_rows, (weights,))
    later = [weight[0, n] for n in range(1, count)]
    later.append([copies.plan(mask_hbm, mask)])
    later[-1] += [copies.plan(bias_hbm.at[e], bias.at[n]) for n, e in enumerate(picks)]
    x_copy = copies.plan(x_hbm, x)
    if end:
        normed_copy = copies.plan(arrays[3], normed)
        late = [x_copy, copies.plan(arrays[4], total)]
        start_all([normed_copy], weight[0, 0])
        normed_copy.wait()
        start_all(*later)
    else:
        start_all([x_copy], weight[0, 0])
        x_copy.wait()
        start_all(*later)

        def first_norm(span, index, _):
            normal, _ = normalize(x[span, :])
            normed[span, :] = (normal * vec_ref[0:1, :] + vec_ref[1:2, :]).astype(BF16)
            return 0

        row_chunks(rows, first_norm, 0)
        copies.send(normed, outs[-1])
    for n, e in enumerate(picks):
        wait_all(weight[0, n])
        qkv = dot(normed[...], weights[n, :, : 3 * columns])
        qs[n] = ((qkv[:, :columns] + qv_ref[e, 0:1, :]) * scale).astype(BF16)
        ks[n] = qkv[:, columns : 2 * columns].astype(BF16)
        vs[n] = (qkv[:, 2 * columns :] + qv_ref[e, 1:2, :]).astype(BF16)
        for index, buffer in enumerate((qs, ks, vs)):
            copies.send(buffer.at[n], outs[5 * n + index])
    wait_all(later[-1])
    if end:
        start_all(late)

    def pair_step(pair, _):
        span = pl.ds(pl.multiple_of(pair * 2 * PADDED, 2 * PADDED), 2 * PADDED)
        for n in range(count):
            query = qs[n, span, :].astype(F32)
            key = ks[n, span, :].astype(F32)
            value = vs[n, span, :].astype(F32)
            results = []
            for side in range(2):
                part = slice(side * PADDED, (side + 1) * PADDED)
                keys = spread_heads(key[part], heads)
                scores = dot(keys, query[part].astype(BF16), 1, 1) + bias[n]
                scores = scores.reshape(heads, PADDED, PADDED) + mask[2 * pair + side][None]
                expo = jnp.exp(scores - jnp.max(scores, axis=1, keepdims=True))
                probs = expo * (1.0 / jnp.sum(expo, axis=1, keepdims=True))
                probs = probs.reshape(heads * PADDED, PADDED).astype(BF16)
                ps[n, 2 * pair + side] = probs
                results.append(dot(probs, spread_heads(value[part], heads), 0, 0))
            atts[n, span, :] = jnp.concatenate(results, axis=0).astype(BF16)
        return 0

    lax.fori_loop(0, pairs, pair_step, 0)
    for n in range(count):
        copies.send(ps.at[n], outs[5 * n + 3])
        copies.send(atts.at[n], outs[5 * n + 4])
    if end:
        wait_all(late)
    branch = total[...] if end else None
    for n in range(count):
        part = dot(atts[n], weights[n, :, 3 * columns :], 1, 1)
        branch = part if branch is None else branch + part
    total[...] = branch
    if end:

        def second_norm(span, index, _):
            live = live_rows(live_ref, index)
            mixed = x[span, :] + live * (total[span, :] + vec_ref[2:3, :])
            total[span, :] = mixed
            normal, _ = normalize(mixed)
            normed2[span, :] = (normal * vec_ref[3:4, :] + vec_ref[4:5, :]).astype(BF16)
            return 0

        row_chunks(rows, second_norm, 0)
        copies.send(normed2, outs[-1])
    copies.send(total, outs[-2])
    copies.finish()


def attention_forward(x, weights, picks, vectors, qv, bias, mask, live, heads, scale, earlier=()):
    rows, width = x.shape
    columns = qv.shape[2]
    wins = rows // PADDED
    plan, arrays, block_rows = choose(weights, picks)
    count = len(picks)
    end = bool(earlier)
    shape = jax.ShapeDtypeStruct
    piece = shape((rows, columns), BF16)
    probs = shape((wins, heads * PADDED, PADDED), BF16)
    results = call(
        functools.partial(attention_forward_kernel, heads, scale, picks, plan, block_rows, end),
        "attention_forward",
        4 + 5 * count,
        live,
        (vectors, qv),
        [x, bias, mask] + list(earlier) + arrays,
        [piece, piece, piece, probs, piece] * count
        + [shape((rows, width), F32), shape((rows, width), BF16)],
        [
            like(x),
            pltpu.VMEM((count,) + bias.shape[1:], F32),
            like(mask),
            pltpu.VMEM((rows, width), F32),
            pltpu.VMEM((rows, width), BF16),
            pltpu.VMEM((rows, width), BF16),
            pltpu.VMEM((count, width, width), BF16),
        ]
        + [pltpu.VMEM((count, rows, columns), BF16)] * 3
        + [
            pltpu.VMEM((count,) + probs.shape, BF16),
            pltpu.VMEM((count, rows, columns), BF16),
        ],
        weight_copies(plan, 1) + 6 * count + 8,
    )
    saved = {e: results[5 * n : 5 * n + 5] for n, e in enumerate(picks)}
    return saved, results[-2], results[-1]


def ffn_forward_kernel(picks, plan, block_rows, end, *refs):
    count = len(picks)
    live_ref, bias_ref, vec_ref = refs[:3]
    arrays, refs = refs[3 : 4 + end], refs[4 + end :]
    weight_refs, refs = refs[: len(plan)], refs[len(plan) :]
    outs, refs = refs[: 2 * count + 1], refs[2 * count + 1 :]
    normed2, mixed, earlier, total, first, second, hidden, slope, sems = refs
    rows = normed2.shape[0]
    copies = Copies(sems)
    arrived = copies.plan(arrays[0], normed2)
    weight = weight_plans(copies, plan, weight_refs, block_rows, (first, second))
    late = [copies.plan(one, to) for one, to in zip(arrays[1:], (mixed, earlier))]
    start_all([arrived], weight[0, 0])
    arrived.wait()
    start_all(weight[1, 0])
    for n, e in enumerate(picks):
        wait_all(weight[0, n])
        if n + 1 < count:
            start_all(weight[0, n + 1], weight[1, n + 1])
        else:
            start_all(late)
        before = dot(normed2[...], first[n]) + bias_ref[e]
        cdf = 0.5 * (1.0 + lax.erf(before * (0.5**0.5)))
        density = jnp.exp(-0.5 * before * before) * 0.3989422804014327
        hidden[n] = (before * cdf).astype(BF16)
        copies.send(hidden.at[n], outs[2 * n])
        slope[n] = (cdf + before * density).astype(BF16)
        copies.send(slope.at[n], outs[2 * n + 1])
        wait_all(weight[1, n])
        part = dot(hidden[n], second[n], 1, 1)
        if n == 0:
            total[...] = part
        else:
            total[...] += part
    wait_all(late)
    if end:

        def finish(span, index, _):
            live = live_rows(live_ref, index)
            value = total[span, :] + vec_ref[5:6, :]
            if end == 2:
                value = value + earlier[span, :]
            total[span, :] = mixed[span, :] + live * value
            return 0

        row_chunks(rows, finish, 0)
    copies.send(total, outs[-1])
    copies.finish()


def ffn_forward(normed2, weights, picks, bias, vectors, live, earlier=()):
    rows, width = normed2.shape
    plan, arrays, block_rows = choose(weights, picks)
    count = len(picks)
    end = len(earlier)
    shape = jax.ShapeDtypeStruct
    piece = shape((rows, width), BF16)
    results = call(
        functools.partial(ffn_forward_kernel, picks, plan, block_rows, end),
        "ffn_forward",
        4 * count,
        live,
        (bias, vectors),
        [normed2] + list(earlier) + arrays,
        [piece, piece] * count + [shape((rows, width), F32)],
        [
            like(normed2),
            pltpu.VMEM((rows, width), F32),
            pltpu.VMEM((rows, width), F32),
            pltpu.VMEM((rows, width), F32),
        ]
        + [pltpu.VMEM((count, width, width), BF16)] * 2
        + [pltpu.VMEM((count, rows, width), BF16)] * 2,
        weight_copies(plan, 2) + 2 * count + 5,
    )
    return {e: results[2 * n : 2 * n + 2] for n, e in enumerate(picks)}, results[-1]


def fill_transposed(target, source, block_rows, tiled):
    flipped = source[...].T
    if not tiled:
        target[...] = flipped
        return
    own = lax.axis_index("dp")
    for block in range(flipped.shape[0] // block_rows):
        start = pl.multiple_of(jnp.bitwise_xor(own, block) * block_rows, block_rows)
        target[pl.ds(start, block_rows), :] = flipped[
            block * block_rows : (block + 1) * block_rows
        ]


def put_blocks(buffer, cuts, block_rows, part, value):
    order = [rel for _, _, rels in cuts for rel in rels]
    for place, rel in enumerate(order):
        start = 0 if rel is None else rel * block_rows
        buffer[place, part * block_rows : (part + 1) * block_rows, :] = value[
            start : start + block_rows
        ].astype(BF16)


def send_blocks(copies, buffer, cuts, block_rows, part, outs):
    place = 0
    rows = pl.ds(part * block_rows, block_rows)
    for index, start, rels in cuts:
        copies.send(
            buffer.at[pl.ds(place, len(rels)), rows, :],
            outs[index].at[pl.ds(start, len(rels)), rows, :],
        )
        place += len(rels)


def block_outs(layout, height, width):
    return [jax.ShapeDtypeStruct((size, height, width), BF16) for size in layout[0]]


def ffn_backward_kernel(picks, plan, block_rows, layout, begin, end, *refs):
    count = len(picks)
    sizes, cuts = layout
    tiled = cuts[0][0][2][0] is not None
    live_ref, vec_ref = refs[:2]
    given = 2 * count + 2 + end + 2 * (not begin)
    arrays, refs = refs[2 : 2 + given], refs[2 + given :]
    weight_refs, refs = refs[: len(plan)], refs[len(plan) :]
    outs, refs = refs[: 5 + len(sizes)], refs[5 + len(sizes) :]
    (
        grad, mixed, branch, error, error_here, attn_grad, normed2, slopes, hiddens, pres, first,
        second, normed2_t, branch_t, results, sums, hidden_sums, sems,
    ) = refs
    rows, width = grad.shape
    blocks_out = outs[5:]
    copies = Copies(sems)
    zero = jnp.zeros((1, width), F32)
    weight = weight_plans(copies, plan, weight_refs, block_rows, (first, second))
    grad_copy = copies.plan(arrays[0], grad)
    slope = [copies.plan(one, slopes.at[n]) for n, one in enumerate(arrays[1 : 1 + count])]
    hidden_hbm = arrays[1 + count : 1 + 2 * count]
    hidden = [copies.plan(one, hiddens.at[n]) for n, one in enumerate(hidden_hbm)]
    normed2_copy = copies.plan(arrays[1 + 2 * count], normed2)
    more = list(arrays[2 + 2 * count :])
    late = [copies.plan(more.pop(0), mixed)] if end else []
    if begin:
        arrived = grad_copy
    else:
        arrived = copies.plan(more[0], branch)
        late += [copies.plan(more[1], error), grad_copy]
    start_all([arrived], weight[1, 0], [slope[0]])
    arrived.wait()
    start_all(weight[0, 0], weight[1, 1], [slope[1]])
    if begin:

        def start(span, index, total):
            part = (live_rows(live_ref, index) * grad[span, :]).astype(BF16)
            branch[span, :] = part
            return total + jnp.sum(part.astype(F32), axis=0, keepdims=True)

        sums[3:4, :] = row_chunks(rows, start, zero)
        if not end:
            copies.send(branch, outs[2])
    fill_transposed(branch_t, branch, block_rows, tiled)
    for n, e in enumerate(picks):
        wait_all(weight[1, n])
        flow = dot(branch[...], second[n])
        slope[n].wait()
        pre = (slopes[n].astype(F32) * flow).astype(BF16)
        pres[n] = pre
        if n + 1 < count:
            start_all(weight[0, n + 1])
            if n + 2 < count:
                start_all(weight[1, n + 2], [slope[n + 2]])
        else:
            start_all([normed2_copy, hidden[0]], late)
        hidden_sums[n] = jnp.sum(pre.astype(F32), axis=0, keepdims=True)
        wait_all(weight[0, n])
        part = dot(pres[n], first[n], 1, 1)
        if n == 0:
            error_here[...] = part
        else:
            error_here[...] += part
    wait_all(late)
    if end:

        def finish(span, index, totals):
            if not begin:
                error_here[span, :] += error[span, :]
            back, gain_part, shift_part = norm_back_rows(
                mixed[span, :], vec_ref[3:4, :], error_here[span, :]
            )
            mixed_grad = grad[span, :] + back
            error_here[span, :] = mixed_grad
            low = (live_rows(live_ref, index) * mixed_grad).astype(BF16)
            attn_grad[span, :] = low
            bias_part = jnp.sum(low.astype(F32), axis=0, keepdims=True)
            return tuple(a + b for a, b in zip(totals, (gain_part, shift_part, bias_part)))

        totals = row_chunks(rows, finish, (zero, zero, zero))
        for index in range(3):
            sums[index : index + 1, :] = totals[index]
        copies.send(attn_grad, outs[1])
    copies.send(error_here, outs[0])
    copies.send(sums, outs[3])
    copies.send(hidden_sums, outs[4])
    normed2_copy.wait()
    fill_transposed(normed2_t, normed2, block_rows, tiled)
    for n in range(count):
        if n + 1 < count:
            hidden[n + 1].start()
        put_blocks(results.at[n], cuts[n], block_rows, 0, dot(normed2_t[...], pres[n]))
        send_blocks(copies, results.at[n], cuts[n], block_rows, 0, blocks_out)
        hidden[n].wait()
        put_blocks(results.at[n], cuts[n], block_rows, 1, dot(branch_t[...], hiddens[n]))
        send_blocks(copies, results.at[n], cuts[n], block_rows, 1, blocks_out)
    copies.finish()


def ffn_backward(
    grad, hidden, normed2, weights, picks, layout, vectors, live, mixed=None, earlier=()
):
    rows, width = grad.shape
    plan, arrays, block_rows = choose(weights, picks)
    count = len(picks)
    end = mixed is not None
    shape = jax.ShapeDtypeStruct
    low = shape((rows, width), BF16)
    wide = shape((rows, width), F32)
    tiny = shape((8, width), F32)
    blocks = block_outs(layout, 2 * block_rows, width)
    results = call(
        functools.partial(
            ffn_backward_kernel, picks, plan, block_rows, layout, not earlier, end
        ),
        "ffn_backward",
        7 * count,
        live,
        (vectors,),
        [grad]
        + [hidden[e][1] for e in picks]
        + [hidden[e][0] for e in picks]
        + [normed2]
        + [mixed] * end
        + list(earlier)
        + arrays,
        [wide, low if end else tiny, tiny if end else low, tiny, shape((count, 1, width), F32)]
        + blocks,
        [like(wide), like(wide), like(low), like(wide), like(wide), like(low), like(low)]
        + [pltpu.VMEM((count, rows, width), BF16)] * 3
        + [pltpu.VMEM((count, width, width), BF16)] * 2
        + [pltpu.VMEM((width, rows), BF16)] * 2
        + [pltpu.VMEM((count, width // block_rows, 2 * block_rows, width), BF16)]
        + [pltpu.VMEM((8, width), F32), pltpu.VMEM((count, 1, width), F32)],
        weight_copies(plan, 2) + 2 * count + 9 + 4 * len(blocks) + 4,
    )
    return *results[:5], results[5:]


def attention_backward_kernel(heads, scale, picks, plan, block_rows, layout, end, *refs):
    count = len(picks)
    sizes, cuts = layout
    tiled = cuts[0][0][2][0] is not None
    live_ref, vec_ref = refs[:2]
    given = 2 + 5 * count + 3 * end
    arrays, refs = refs[2 : 2 + given], refs[2 + given :]
    weight_refs, refs = refs[: len(plan)], refs[len(plan) :]
    outs_count = 3 + end + len(sizes)
    outs, refs = refs[:outs_count], refs[outs_count:]
    (
        attn_grad, normed, x, mixed_grad, error, weights, qs, ks, vs, atts, ps, gs, grads,
        normed_t, attn_grad_t, results, scores_sum, sums, small, sems,
    ) = refs
    rows, width = attn_grad.shape
    columns = qs.shape[2]
    pairs = rows // (2 * PADDED)
    copies = Copies(sems)
    weight = weight_plans(copies, plan, weight_refs, block_rows, (weights,))
    arrived = copies.plan(arrays[0], attn_grad)
    saved = [
        copies.plan(arrays[2 + 5 * n + index], buffer.at[n])
        for n in range(count)
        for index, buffer in ((0, qs), (1, ks), (2, vs), (3, ps))
    ]
    late = [copies.plan(arrays[1], normed)]
    for n in range(count):
        late.append(copies.plan(arrays[2 + 5 * n + 4], atts.at[n]))
    if end:
        for one, to in zip(arrays[2 + 5 * count :], (x, mixed_grad, error)):
            late.append(copies.plan(one, to))
    start_all([arrived], weight[0, 0])
    arrived.wait()
    start_all(*[weight[0, n] for n in range(1, count)], saved)
    scores_sum[...] = jnp.zeros(scores_sum.shape, F32)
    fill_transposed(attn_grad_t, attn_grad, block_rows, tiled)
    for n in range(count):
        wait_all(weight[0, n])
        gs[n] = dot(attn_grad[...], weights[n, :, 3 * columns :]).astype(BF16)
    wait_all(saved)
    start_all(late)

    def pair_step(pair, _):
        span = pl.ds(pl.multiple_of(pair * 2 * PADDED, 2 * PADDED), 2 * PADDED)
        for n in range(count):
            query, key, value, grad = [
                buffer[n, span, :].astype(F32) for buffer in (qs, ks, vs, gs)
            ]
            rows_out = []
            for side in range(2):
                part = slice(side * PADDED, (side + 1) * PADDED)
                keys = spread_heads(key[part], heads)
                values = spread_heads(value[part], heads)
                grad_low = grad[part].astype(BF16)
                low = ps[n, 2 * pair + side]
                probs = low.astype(F32)
                flow = dot(values, grad_low, 1, 1)
                inner = jnp.sum(
                    (probs * flow).reshape(heads, PADDED, PADDED), axis=1, keepdims=True
                )
                score = probs.reshape(heads, PADDED, PADDED) * (
                    flow.reshape(heads, PADDED, PADDED) - inner
                )
                score = score.reshape(heads * PADDED, PADDED).astype(BF16)
                scores_sum[n] += score.astype(F32)
                rows_out.append(
                    jnp.concatenate(
                        [
                            dot(score, keys, 0, 0) * scale,
                            merge_heads(dot(score, query[part].astype(BF16)), heads),
                            merge_heads(dot(low, grad_low), heads),
                        ],
                        axis=1,
                    )
                )
            grads[n, span, :] = jnp.concatenate(rows_out, axis=0).astype(BF16)
        return 0

    lax.fori_loop(0, pairs, pair_step, 0)
    copies.send(scores_sum, outs[1])
    wait_all(late)
    for n in range(count):
        sums[n] = jnp.sum(grads[n].astype(F32), axis=0, keepdims=True)
        part = dot(grads[n], weights[n, :, : 3 * columns], 1, 1)
        if n == 0 and not end:
            error[...] = part
        else:
            error[...] += part
    copies.send(sums, outs[2])
    if end:
        zero = jnp.zeros((1, width), F32)

        def finish(span, index, totals):
            back, gain_part, shift_part = norm_back_rows(
                x[span, :], vec_ref[0:1, :], error[span, :]
            )
            error[span, :] = mixed_grad[span, :] + back
            return totals[0] + gain_part, totals[1] + shift_part

        totals = row_chunks(rows, finish, (zero, zero))
        for index in range(2):
            small[index : index + 1, :] = totals[index]
        copies.send(small, outs[3])
    copies.send(error, outs[0])
    fill_transposed(normed_t, normed, block_rows, tiled)
    for n in range(count):
        value = jnp.concatenate(
            [dot(normed_t[...], grads[n]), dot(attn_grad_t[...], atts[n])], axis=1
        )
        put_blocks(results.at[n], cuts[n], block_rows, 0, value)
        send_blocks(copies, results.at[n], cuts[n], block_rows, 0, outs[3 + end :])
    copies.finish()


def attention_backward(
    attn_grad, normed, saved, weights, picks, layout, vectors, live, heads, scale, earlier=()
):
    rows, width = attn_grad.shape
    columns = saved[picks[0]][0].shape[1]
    plan, arrays, block_rows = choose(weights, picks)
    count = len(picks)
    end = bool(earlier)
    probs = saved[picks[0]][3]
    shape = jax.ShapeDtypeStruct
    wide = shape((rows, width), F32)
    pieces = [item for e in picks for item in saved[e]]
    outs = [
        wide,
        shape((count, heads * PADDED, PADDED), F32),
        shape((count, 1, 3 * columns), F32),
    ]
    blocks = block_outs(layout, block_rows, width)
    results = call(
        functools.partial(
            attention_backward_kernel, heads, scale, picks, plan, block_rows, layout, end
        ),
        "attention_backward",
        19,
        live,
        (vectors,),
        [attn_grad, normed] + pieces + list(earlier) + arrays,
        outs + [shape((8, width), F32)] * end + blocks,
        [like(attn_grad), like(normed), like(wide), like(wide), like(wide)]
        + [pltpu.VMEM((count, width, width), BF16)]
        + [pltpu.VMEM((count, rows, columns), BF16)] * 4
        + [pltpu.VMEM((count,) + probs.shape, BF16)]
        + [pltpu.VMEM((count, rows, columns), BF16)]
        + [pltpu.VMEM((count, rows, 3 * columns), BF16)]
        + [pltpu.VMEM((width, rows), BF16)] * 2
        + [pltpu.VMEM((count, width // block_rows, block_rows, width), BF16)]
        + [like(outs[1]), like(outs[2]), pltpu.VMEM((8, width), F32)],
        weight_copies(plan, 1) + 5 * count + 11 + 4 * len(blocks),
    )
    return *results[: 3 + end], results[3 + end :]


def swap(values, axis, bit):
    size = lax.axis_size(axis)
    return lax.ppermute(values, axis, [(i, i ^ (1 << bit)) for i in range(size)])


def bits_in(axis):
    return lax.axis_size(axis).bit_length() - 1


def pick(values, index, dim):
    return lax.dynamic_index_in_dim(values, index, dim, keepdims=False)


def tie(values, token):
    if token is None:
        return values
    return lax.optimization_barrier((values, token))[0]


def whole_tiles(rows):
    return rows % 16 == 0


def in_order(values):
    index = jnp.bitwise_xor(jnp.arange(values.shape[0]), lax.axis_index("dp"))
    return jnp.take(values, index, axis=0)


def relatives(halves):
    count = lax.axis_size("dp")
    size = count // halves
    return [
        [tuple(range(part * size + side, (part + 1) * size, 2)) for part in range(halves)]
        for side in range(2)
    ]


def line_bits():
    return list(range(1, bits_in("dp")))


def straight(values):
    size = lax.axis_size("dp")
    low, high = [1 << bit for bit in line_bits()[-2:]]
    return [
        lax.ppermute(values(n), "dp", [(i, i ^ shift) for i in range(size)])
        for n, shift in ((1, low), (2, high), (3, low | high))
    ]


class Gather:
    def __init__(self, shard, parts, rows, ways):
        self.shard = shard
        self.parts = parts
        self.rows = rows
        self.ways = ways
        self.entries = []

    def line(self, after=None, at_once=False):
        held = tie(self.shard, after)[None]
        bits = line_bits()
        for bit in bits[:-2]:
            held = jnp.concatenate([held, swap(held, "dp", bit)])
        self.moved = straight(lambda n: held) if at_once else [swap(held, "dp", bits[-2])]
        self.held = [held]

    def line_end(self, until=None):
        moved = tie(self.moved, until)
        self.held = [jnp.concatenate(self.held + moved)]
        return self.held[0]

    def last(self, after=None):
        self.moved = swap(tie(self.held[0], after), "dp", line_bits()[-1])

    def last_end(self, until=None):
        moved = tie(self.moved, until)
        self.held.append(moved)
        if len(self.ways) == 1:
            self.held = [jnp.concatenate(self.held)]
        return self.held[-1]

    def sides(self, part, after=None):
        if part == 0:
            self.side, self.far = [], []
        held = tie(self.held[part], after)
        self.side.append(swap(held, "dp", 0))
        self.far.append(swap(held, "head", 1))

    def sides_end(self, part, until=None):
        self.side[part], self.far[part] = tie((self.side[part], self.far[part]), until)
        return self.side[part], self.far[part]

    def corner(self, part, after=None):
        if part == 0:
            self.corners = []
        if self.ways[part] == "x":
            self.corners.append(swap(tie(self.side[part], after), "head", 1))
        else:
            self.corners.append(swap(tie(self.far[part], after), "dp", 0))

    def corner_end(self, part, until=None):
        self.corners[part] = tie(self.corners[part], until)
        return self.corners[part]

    def core(self, kind, part=None):
        own, other = relatives(len(self.ways))
        arrays, e, rels = {
            "held": (self.held, 0, own),
            "side": (self.side, 0, other),
            "far": (self.far, 2, own),
            "corner": (getattr(self, "corners", None), 2, other),
        }[kind]
        for n, (one, several) in enumerate(zip(arrays, rels)):
            if part is None or part == n:
                self.entries.append((e, one, several))
                self.entries.append((e + 1, swap(one, "head", 0), several))

    def result(self, first=0):
        rows, parts = self.rows, self.parts
        width = self.shard.shape[1]
        if whole_tiles(rows):
            plan = tuple((e, rels) for e, _, rels in self.entries)
            return plan, [one for _, one, _ in self.entries], rows, first * rows
        arrays = []
        plan = []
        for e in range(PIECES):
            mine = [(one, rels) for piece, one, rels in self.entries if piece == e]
            if not mine:
                continue
            order = sum((rels for _, rels in mine), ())
            if len(order) < lax.axis_size("dp"):
                continue
            blocks = jnp.concatenate([one[:, : parts * rows] for one, _ in mine])
            blocks = in_order(blocks[jnp.argsort(jnp.array(order))])
            blocks = blocks.reshape(-1, parts, rows, width).transpose(1, 0, 2, 3)
            arrays.append(blocks.reshape(1, -1, width))
            plan.append((e, (None,)))
        rows = arrays[0].shape[1] // parts
        return tuple(plan), arrays, rows, first * rows


def wide(*values):
    total = values[0].astype(F32)
    for value in values[1:]:
        total = total + value.astype(F32)
    return total


def plus(*values):
    return wide(*values).astype(BF16)


class Scatter:
    def __init__(self, parts, rows, ways):
        self.parts = parts
        self.rows = rows
        self.ways = ways
        self.tiled = whole_tiles(rows)
        blocks = lax.axis_size("dp")
        half = blocks // 2
        even = tuple(range(0, blocks, 2))
        odd = tuple(range(1, blocks, 2))
        cut = half // len(ways)
        corners = [odd[n * cut : (n + 1) * cut] for n in range(len(ways))]
        self.order = even + odd
        if self.tiled:
            self.away_layout = (
                (2 * blocks,),
                (((0, 0, self.order),), ((0, blocks, self.order),)),
            )
            last = tuple((3 + n, 0, rels) for n, rels in enumerate(corners))
            self.near_layout = (
                (half,) * 3 + (cut,) * len(ways),
                (((0, 0, even), (1, 0, odd)), ((2, 0, even),) + last),
            )
        else:
            one = ((0, 0, (None,)),)
            two = ((0, 1, (None,)),)
            self.away_layout = self.near_layout = ((2,), (one, two))

    def both_layouts(self):
        sizes, cuts = self.near_layout
        first = len(self.away_layout[0])
        moved = tuple(
            tuple((first + index, start, rels) for index, start, rels in one) for one in cuts
        )
        return self.away_layout[0] + sizes, self.away_layout[1] + moved

    def arrange(self, outs):
        one = outs[0].reshape(2, self.parts, -1, self.rows, outs[0].shape[-1])
        one = one.transpose(0, 2, 1, 3, 4)
        one = one.reshape(one.shape[:2] + (-1, one.shape[-1]))
        return jnp.concatenate([in_order(item)[jnp.array(self.order)] for item in one])

    def away(self, outs):
        self.moved = swap(outs[0] if self.tiled else self.arrange(outs), "head", 0)

    def near(self, outs, until=None):
        moved = tie(self.moved, until)
        half = moved.shape[0] // 4
        if self.tiled:
            own = list(outs)
        else:
            one = self.arrange(outs)
            own = [one[n * half : (n + 1) * half] for n in range(3)]
            cut = half // len(self.ways)
            own += [one[3 * half + n * cut :][:cut] for n in range(len(self.ways))]
        cut = half // len(self.ways)
        self.held = [own[0], moved[:half]]
        self.side = [own[1], moved[half : 2 * half]]
        self.far = [own[2], moved[2 * half : 3 * half]]
        self.corners = [
            plus(own[3 + n], moved[3 * half + n * cut :][:cut]) for n in range(len(self.ways))
        ]
        return self.corners

    def corner(self, after=None):
        self.moved = []
        for way, one in zip(self.ways, tie(self.corners, after)):
            self.moved.append(swap(one, "head", 1) if way == "x" else swap(one, "dp", 0))

    def corner_end(self, until=None):
        moved = tie(self.moved, until)
        half = self.side[0].shape[0]
        for part, (way, one) in enumerate(zip(self.ways, moved)):
            size = one.shape[0]
            around = (part * size, half - (part + 1) * size)
            one = jnp.pad(one, (around,) + ((0, 0),) * 2) if size < half else one
            (self.side if way == "x" else self.far).append(one)
        self.side, self.far = plus(*self.side), plus(*self.far)
        return self.side, self.far

    def sides(self, after=None):
        side, far = tie((self.side, self.far), after)
        self.moved = [swap(side, "dp", 0), swap(far, "head", 1)]

    def sides_end(self, until=None, at_once=False):
        terms = self.held + list(tie(self.moved, until))
        count = 4 if at_once else 2
        size = terms[0].shape[0] // count
        self.held = [
            plus(*[one[n * size : (n + 1) * size] for one in terms]) for n in range(count)
        ]
        return self.held

    def last(self, after=None):
        self.moved = swap(tie(self.held[1], after), "dp", line_bits()[-1])

    def last_end(self, until=None):
        moved = tie(self.moved, until)
        size = moved.shape[0] // 2
        terms = [self.held[0], moved]
        self.held = [plus(*[one[n * size :][:size] for one in terms]) for n in range(2)]
        return self.held

    def line(self, after=None):
        held = tie(self.held, after)
        if len(held) == 4:
            self.moved = straight(lambda n: held[n])
        else:
            self.moved = [swap(held[1], "dp", line_bits()[-2])]

    def line_end(self, until=None):
        held = wide(self.held[0], *tie(self.moved, until))
        for bit in reversed(line_bits()[:-2]):
            cut = held.shape[0] // 2
            moved = swap(held[cut:].astype(BF16), "dp", bit)
            held = wide(held[:cut], moved)
        self.result = held[0]
        return self.result


class SmallSum:
    def __init__(self, values):
        self.total = values
        self.left = [("head", 0), ("head", 1)]
        self.left += [("dp", bit) for bit in range(bits_in("dp"))]
        self.moved = None

    def step(self, until=None):
        self.result(until)
        axis, bit = self.left.pop(0)
        self.moved = swap(self.total, axis, bit)

    def end(self):
        return not self.left

    def result(self, until=None):
        if self.moved is not None:
            self.total = self.total + tie(self.moved, until)
        self.moved = None
        return self.total


def unshift(values):
    grid = values.reshape(values.shape[:-1] + (WSIDE, WSIDE))
    return jnp.roll(grid, (SHIFT, SHIFT), axis=(-2, -1)).reshape(values.shape)


def pad_rows(values):
    grid = values.reshape(-1, WTOK, values.shape[1])
    grid = jnp.pad(grid, ((0, 0), (0, PADDED - WTOK), (0, 0)))
    return grid.reshape(-1, values.shape[1])


def drop_rows(values):
    grid = values.reshape(-1, PADDED, values.shape[1])[:, :WTOK]
    return grid.reshape(-1, values.shape[1])


def attention_mask(pad, region):
    allowed = (pad[:, :, None] == 1) & (region[:, :, None] == region[:, None, :])
    mask = jnp.where(allowed, 0.0, MASKED).astype(F32)
    extra = PADDED - WTOK
    mask = jnp.pad(mask, ((0, 0), (0, 0), (0, extra)))
    return jnp.pad(mask, ((0, 0), (0, extra), (0, 0)), constant_values=ABSENT)


def shards(
    tokens,
    cotangent,
    crop_counts,
    pad_mask,
    region_ids,
    rel_index,
    norm_gain,
    norm_shift,
    qkv_weight,
    qv_bias,
    bias_table,
    proj_weight,
    fc1_weight,
    fc1_bias,
    fc2_weight,
    out_bias,
):
    rows = tokens.shape[0]
    width = tokens.shape[1]
    wins = rows // WTOK
    local_width = qkv_weight.shape[3]
    local_heads = bias_table.shape[1]
    rel_count = bias_table.shape[2]
    dp_width = norm_gain.shape[2]
    dp_hidden = fc1_bias.shape[1]
    pieces = lax.axis_size("head")
    heads_total = local_heads * pieces
    head_dim = local_width // local_heads
    scale = head_dim ** (-0.5)
    head_index = lax.axis_index("head")
    dp_index = lax.axis_index("dp")
    relative = [head_index ^ e for e in range(pieces)]

    shard_rows = qkv_weight.shape[1]
    attn_shards = [
        jnp.concatenate(
            [qkv_weight[block].reshape(-1, 3 * local_width), proj_weight[block].T], axis=1
        )
        for block in range(BLOCKS)
    ]
    ffn_shards = [
        jnp.concatenate([fc1_weight[block], fc2_weight[block].T]) for block in range(BLOCKS)
    ]
    small = jnp.concatenate([norm_gain, norm_shift, qv_bias, out_bias]).reshape(-1, dp_width)
    small_rows = small.shape[0]
    beside = -(-dp_width // 128) * 128
    small = jnp.pad(small, ((0, 0), (0, width - dp_width)))
    small = small + jnp.pad(
        fc1_bias, ((0, small_rows - BLOCKS), (beside, width - beside - dp_hidden))
    )
    attn_shards[0] = jnp.concatenate([attn_shards[0], small])
    near, away = (0, 2), (1, 3)
    first, second = (0, 1), (2, 3)
    a0 = Gather(attn_shards[0], 1, shard_rows, "x")
    middle = Gather(jnp.concatenate([ffn_shards[0], attn_shards[1]]), 3, shard_rows, "xy")
    f1 = Gather(ffn_shards[1], 2, shard_rows, "xy")

    def attn_weights(block):
        return middle.result(2) if block else a0.result()

    def ffn_weights(block):
        return f1.result() if block else middle.result()

    a0.line(at_once=True)
    far_table = swap(bias_table, "head", 1)
    near_table = swap(bias_table, "head", 0)
    a0.line_end()
    a0.sides(0)
    middle.line(a0.held)
    a0.core("held")
    middle.line_end()
    middle.last()
    a0.sides_end(0)
    a0.core("side")
    a0.core("far")
    a0.corner(0)
    middle.sides(0, a0.far)
    table_pieces = [bias_table, near_table, far_table, swap(far_table, "head", 0)]
    small_all = jnp.stack([a0.held[0][:, shard_rows:], a0.side[0][:, shard_rows:]], axis=1)
    small_all = in_order(small_all.reshape((-1,) + small.shape)).transpose(1, 0, 2).astype(F32)
    every = small_all[:, :, :dp_width].reshape(4, BLOCKS, 2, width)
    gains, shifts, qv_all, out_all = every[0], every[1], every[2], every[3]
    hidden_bias = small_all[:BLOCKS, :, beside : beside + dp_hidden].reshape(BLOCKS, pieces, -1)
    qv_pieces = qv_all.reshape(BLOCKS, 2, pieces, local_width)

    counts = jnp.repeat(crop_counts, CROP_MAX)
    slots = jnp.arange(pad_mask.shape[0], dtype=jnp.int32) % CROP_MAX
    live_all = (slots < counts).astype(F32)
    live_windows = lax.dynamic_slice_in_dim(live_all, head_index * wins, wins, 0)
    live = live_windows
    pad = lax.dynamic_slice_in_dim(pad_mask, head_index * wins, wins, 0)
    region = unshift(lax.dynamic_slice_in_dim(region_ids, head_index * wins, wins, 0))
    masks = (attention_mask(pad, jnp.zeros_like(region)), attention_mask(pad, region))
    extra = PADDED - WTOK
    onehots = []
    for index in (rel_index, unshift(unshift(rel_index).T).T):
        by_key = jnp.pad(index.T, ((0, extra), (0, extra)), constant_values=-1).reshape(1, -1)
        ids = jnp.arange(rel_count, dtype=jnp.int32)[:, None]
        onehots.append((ids == by_key).astype(BF16))

    def ordered(values, dim):
        return jnp.stack([pick(values, rel, dim) for rel in relative])

    block_rows = local_heads * PADDED
    vectors, qv, biases, hidden_biases = [], [], [], []
    for block in range(BLOCKS):
        rows8 = [
            gains[block, 0],
            shifts[block, 0],
            out_all[block, 0],
            gains[block, 1],
            shifts[block, 1],
            out_all[block, 1],
        ]
        vectors.append(jnp.pad(jnp.stack(rows8), ((0, 2), (0, 0))))
        qv.append(ordered(qv_pieces[block], 1))
        table = jnp.concatenate([one[block] for one in table_pieces])
        bias = jnp.dot(table, onehots[block % 2], preferred_element_type=F32)
        biases.append(bias.reshape(pieces, block_rows, PADDED))
        hidden_biases.append(ordered(hidden_bias[block], 0)[:, None, :])

    residual = pad_rows(tokens).astype(F32)

    def attend(block, x, picks, token, earlier=()):
        return attention_forward(
            x,
            attn_weights(block),
            picks,
            tie(vectors[block], token),
            qv[block],
            biases[block],
            masks[block % 2],
            live,
            local_heads,
            scale,
            earlier,
        )

    def feed(block, normed2, picks, token, earlier=()):
        return ffn_forward(
            normed2,
            ffn_weights(block),
            picks,
            hidden_biases[block],
            tie(vectors[block], token),
            live,
            earlier,
        )

    x0 = residual
    saved_0, branch, normed_0 = attend(0, x0, first, middle.held[0])
    a0.corner_end(0, branch)
    a0.core("corner")
    middle.sides_end(0, branch)
    middle.corner(0)
    middle.last_end(branch)
    middle.sides(1)
    f1.line(middle.held[1])
    f1.line_end()
    f1.last()
    token = (middle.held[1], f1.held[0])
    more, mixed_0, normed2_0 = attend(0, x0, second, token, (normed_0, branch))
    saved_0.update(more)
    middle.core("held")
    middle.sides_end(1, mixed_0)
    middle.corner(1)
    middle.core("side")
    middle.core("far")
    middle.corner_end(0, mixed_0)
    middle.corner_end(1, mixed_0)
    middle.core("corner")
    f1.sides(0, middle.corners)
    hidden_0, x1 = feed(0, normed2_0, first + second, f1.held, (mixed_0,))
    f1.sides_end(0, x1)
    f1.last_end(x1)
    f1.core("held")
    f1.core("side", 0)
    f1.sides(1)
    f1.corner(0)
    saved_1, branch, normed_1 = attend(1, x1, first, f1.held)
    f1.sides_end(1, branch)
    f1.corner_end(0, branch)
    f1.corner(1)
    f1.core("side", 1)
    f1.core("far")
    f1.core("corner", 0)
    token = (f1.side, f1.far)
    more, mixed_1, normed2_1 = attend(1, x1, second, token, (normed_1, branch))
    saved_1.update(more)
    f1.corner_end(1, mixed_1)
    f1.core("corner", 1)
    hidden_1, residual = feed(1, normed2_1, first + second, f1.corners, (mixed_1,))
    kept = [
        (x0, mixed_0, normed_0, normed2_0, saved_0, hidden_0),
        (x1, mixed_1, normed_1, normed2_1, saved_1, hidden_1),
    ]

    def feed_back(block, picks, layout, grad, token, mixed=None, earlier=()):
        _, _, _, normed2, _, hidden = kept[block]
        return ffn_backward(
            grad,
            hidden,
            normed2,
            ffn_weights(block),
            picks,
            layout,
            tie(vectors[block], token),
            live,
            mixed,
            earlier,
        )

    def attend_back(block, picks, layout, attn_grad, token, earlier=()):
        _, _, normed, _, saved, _ = kept[block]
        return attention_backward(
            attn_grad,
            normed,
            saved,
            attn_weights(block),
            picks,
            layout,
            tie(vectors[block], token),
            live,
            local_heads,
            scale,
            earlier,
        )

    def small_terms(block, attn, small_f, hidden_terms):
        scores_a, sums_a, scores_n, sums_n, small_a = attn

        def together(one, other):
            return ordered(jnp.stack([one[0], other[0], one[1], other[1]]), 0)

        table_grad = lax.dot_general(
            together(scores_n, scores_a).reshape(heads_total, -1),
            onehots[block % 2].astype(F32),
            (((1,), (1,)), ((), ())),
            precision=lax.Precision.HIGHEST,
            preferred_element_type=F32,
        )
        qv_sums = together(sums_n, sums_a)[:, 0]
        items = [
            small_a[0],
            small_f[0],
            small_a[1],
            small_f[1],
            qv_sums[:, :local_width].reshape(-1),
            qv_sums[:, 2 * local_width :].reshape(-1),
            small_f[2],
            small_f[3],
            together(*hidden_terms).reshape(-1),
            table_grad.reshape(-1),
        ]
        return jnp.concatenate(items)

    f1_sum, f0_sum = [Scatter(2, shard_rows, "xy") for _ in range(2)]
    a1_sum, a0_sum = [Scatter(1, shard_rows, "xy") for _ in range(2)]
    grad_rows = pad_rows(cotangent).astype(F32)
    mixed_grad, attn_grad, _, small_f, hidden_sums, outs = feed_back(
        1, away + near, f1_sum.both_layouts(), grad_rows, residual, mixed_1
    )
    count = len(f1_sum.away_layout[0])
    f1_sum.away(outs[:count])
    error, scores_a, sums_a, sent = attend_back(1, away, a1_sum.away_layout, attn_grad, None)
    f1_sum.near(outs[count:], error)
    f1_sum.corner()
    a1_sum.away(sent)
    grad_rows, scores_n, sums_n, small_a, outs = attend_back(
        1, near, a1_sum.near_layout, attn_grad, f1_sum.corners, (x1, mixed_grad, error)
    )
    attn_terms = (scores_a, sums_a, scores_n, sums_n, small_a)
    small_1 = small_terms(1, attn_terms, small_f, (hidden_sums[2:], hidden_sums[:2]))
    token = f1_sum.corner_end(grad_rows)
    f1_sum.sides()
    a1_sum.near(outs, grad_rows)
    a1_sum.corner()
    error, _, branch_grad, small_b, hidden_a, sent = feed_back(
        0, away, f0_sum.away_layout, grad_rows, (token, a1_sum.corners)
    )
    f0_sum.away(sent)
    token = a1_sum.corner_end(error)
    mixed_grad, attn_grad, _, small_f, hidden_n, outs = feed_back(
        0,
        near,
        f0_sum.near_layout,
        grad_rows,
        (error, token),
        mixed_0,
        (branch_grad, error),
    )
    small_f = jnp.concatenate([small_f[:3], small_b[3:4]])
    token = f1_sum.sides_end(attn_grad)
    f1_sum.last()
    a1_sum.sides(attn_grad)
    f0_sum.near(outs, attn_grad)
    f0_sum.corner()
    error, scores_a, sums_a, sent = attend_back(
        0, away, a0_sum.away_layout, attn_grad, (token, f0_sum.corners)
    )
    a0_sum.away(sent)
    token = (f0_sum.corner_end(error), a1_sum.sides_end(error), f1_sum.last_end(error))
    f0_sum.sides()
    a1_sum.last()
    f1_sum.line()
    grad_rows, scores_n, sums_n, small_a, outs = attend_back(
        0, near, a0_sum.near_layout, attn_grad, token, (x0, mixed_grad, error)
    )
    f0_sum.sides_end(grad_rows)
    f0_sum.last()
    a0_sum.near(outs, (grad_rows, f0_sum.held))
    a0_sum.corner()
    a1_sum.last_end(grad_rows)
    a1_sum.line()
    attn_terms = tie((scores_a, sums_a, scores_n, sums_n, small_a), a0_sum.corners)
    small_0 = small_terms(0, attn_terms, small_f, (hidden_n, hidden_a))
    small_sum = SmallSum(jnp.stack([small_0, small_1]))
    small_sum.step()
    small_sum.step()
    token = a0_sum.corner_end()
    a0_sum.sides()
    small_sum.step(token)
    token = a0_sum.sides_end(at_once=True)
    f0_sum.last_end((a0_sum.side, a0_sum.far))
    a0_sum.line(f0_sum.held)
    f0_sum.line()
    small_sum.step(token)
    while not small_sum.end():
        small_sum.step()
    shard_grads = [(a0_sum, f0_sum), (a1_sum, f1_sum)]
    for several in shard_grads:
        for one in several:
            one.line_end()
    shard_grads = [
        (attn.result, ffn.result[:shard_rows], ffn.result[shard_rows:])
        for attn, ffn in shard_grads
    ]

    totals = small_sum.result()

    def own(values):
        return lax.dynamic_slice_in_dim(values, dp_index * dp_width, dp_width, 2)

    small_grads = []
    for index in range(4):
        part = totals[:, 2 * index * width : 2 * (index + 1) * width]
        small_grads.append(own(part.reshape(BLOCKS, 2, width)))
    offset = 8 * width
    hidden_total = totals[:, offset : offset + pieces * fc1_weight.shape[2]]
    fc1_bias_grad = lax.dynamic_slice_in_dim(hidden_total, dp_index * dp_hidden, dp_hidden, 1)
    offset += hidden_total.shape[1]
    table_total = totals[:, offset:].reshape(BLOCKS, heads_total, rel_count)
    bias_table_grad = lax.dynamic_slice_in_dim(
        table_total, head_index * local_heads, local_heads, 1
    )
    qkv_weight_grad = jnp.stack(
        [item[0][:, : 3 * local_width].reshape(-1, 3, local_width) for item in shard_grads]
    )
    proj_weight_grad = jnp.stack([item[0][:, 3 * local_width :].T for item in shard_grads])
    fc1_weight_grad = jnp.stack([item[1] for item in shard_grads])
    fc2_weight_grad = jnp.stack([item[2].T for item in shard_grads])
    return (
        drop_rows(residual),
        drop_rows(grad_rows),
        small_grads[0],
        small_grads[1],
        qkv_weight_grad,
        small_grads[2],
        bias_table_grad,
        proj_weight_grad,
        fc1_weight_grad,
        fc1_bias_grad,
        fc2_weight_grad,
        small_grads[3],
    )


def solution(mesh):
    placed = (
        P(("dp", "head"), None),
        P(("dp", "head"), None),
        P("dp"),
        P("dp", None),
        P("dp", None),
        P(),
        P(None, None, "dp"),
        P(None, None, "dp"),
        P(None, "dp", None, "head"),
        P(None, None, "dp"),
        P(None, "head", None),
        P(None, "head", "dp"),
        P(None, "dp", "head"),
        P(None, "dp"),
        P(None, "head", "dp"),
        P(None, None, "dp"),
    )
    return jax.shard_map(
        shards,
        mesh=mesh,
        in_specs=placed,
        out_specs=(
            P(("dp", "head"), None),
            P(("dp", "head"), None),
            P(None, None, "dp"),
            P(None, None, "dp"),
            P(None, "dp", None, "head"),
            P(None, None, "dp"),
            P(None, "head", None),
            P(None, "head", "dp"),
            P(None, "dp", "head"),
            P(None, "dp"),
            P(None, "head", "dp"),
            P(None, None, "dp"),
        ),
        check_vma=False,
    )
```

```python
import functools

import jax
import jax.numpy as jnp
from jax import lax
from jax.experimental import pallas as pl
from jax.experimental.pallas import tpu as pltpu
from jax.sharding import PartitionSpec as P

WSIDE = 7
SHIFT = 3
CROP_MAX = 12
BLOCKS = 2
WTOK = 49
PADDED = 56
PIECES = 4
VMEM_BYTES = 60 * 2**20

EPSILON = 1e-05
MASKED = -100.0
ABSENT = -1e30
BF16 = jnp.bfloat16
F32 = jnp.float32


def cost(micros):
    return pl.CostEstimate(
        flops=int(micros * 5e9), bytes_accessed=int(micros * 2e7), transcendentals=0
    )


def dot(left, right, left_dim=1, right_dim=0):
    return lax.dot_general(
        left, right, (((left_dim,), (right_dim,)), ((), ())), preferred_element_type=F32
    )


def normalize(values):
    centred = values - jnp.mean(values, axis=-1, keepdims=True)
    scale = lax.rsqrt(jnp.mean(centred * centred, axis=-1, keepdims=True) + EPSILON)
    return centred * scale, scale


def norm_back_rows(values, gain, error):
    normal, scale = normalize(values)
    flow = error * gain
    grad = (
        flow
        - jnp.mean(flow, axis=-1, keepdims=True)
        - normal * jnp.mean(flow * normal, axis=-1, keepdims=True)
    ) * scale
    return grad, jnp.sum(error * normal, axis=0, keepdims=True), jnp.sum(error, axis=0, keepdims=True)


def spread_heads(values, heads):
    columns = values.shape[1]
    owner = lax.broadcasted_iota(jnp.int32, values.shape, 1) // (columns // heads)
    return jnp.concatenate(
        [jnp.where(owner == head, values, 0.0) for head in range(heads)], axis=0
    ).astype(BF16)


def merge_heads(values, heads):
    rows = values.shape[0] // heads
    columns = values.shape[1]
    owner = lax.broadcasted_iota(jnp.int32, (rows, columns), 1) // (columns // heads)
    total = values[:rows]
    for head in range(1, heads):
        total = jnp.where(owner == head, values[head * rows : (head + 1) * rows], total)
    return total


class Copies:
    def __init__(self, sems):
        self.sems = sems
        self.used = 0
        self.leaving = []

    def plan(self, source, target):
        copy = pltpu.make_async_copy(source, target, self.sems.at[self.used])
        self.used += 1
        return copy

    def send(self, source, target):
        copy = self.plan(source, target)
        copy.start()
        self.leaving.append(copy)

    def finish(self):
        wait_all(self.leaving)


def start_all(*groups):
    for group in groups:
        for item in group:
            item.start()


def choose(weights, picks):
    plan, arrays, rows, first = weights
    chosen = [index for index, (e, _) in enumerate(plan) if e in picks]
    plan = tuple((picks.index(plan[index][0]), plan[index][1], first) for index in chosen)
    return plan, [arrays[index] for index in chosen], rows


def weight_plans(copies, plan, refs, rows, parts):
    own = lax.axis_index("dp")
    plans = {}
    for (slot, rels, first), ref in zip(plan, refs):
        for place, rel in enumerate(rels):
            start = 0 if rel is None else pl.multiple_of(jnp.bitwise_xor(own, rel) * rows, rows)
            for part, target in enumerate(parts):
                plans.setdefault((part, slot), []).append(
                    copies.plan(
                        ref.at[place, pl.ds(first + part * rows, rows), :],
                        target.at[slot, pl.ds(start, rows), :],
                    )
                )
    return plans


def wait_all(items):
    for item in items:
        item.wait()


def weight_copies(plan, parts):
    return parts * sum(len(rels) for _, rels, _ in plan)


def in_any(count):
    return [pl.BlockSpec(memory_space=pl.ANY)] * count


def in_vmem(count):
    return [pl.BlockSpec(memory_space=pltpu.VMEM)] * count


def like(array):
    return pltpu.VMEM(array.shape, array.dtype)


def call(kernel, name, micros, live, small, arrays, outs, scratch, copies):
    return pl.pallas_call(
        kernel,
        in_specs=[pl.BlockSpec(memory_space=pltpu.SMEM)] + in_vmem(len(small)) + in_any(len(arrays)),
        out_specs=tuple(in_any(len(outs))),
        out_shape=tuple(outs),
        scratch_shapes=list(scratch) + [pltpu.SemaphoreType.DMA((copies,))],
        compiler_params=pltpu.CompilerParams(vmem_limit_bytes=VMEM_BYTES),
        cost_estimate=cost(micros),
        name=name,
    )(live, *small, *arrays)


def row_chunks(rows, body, init):
    chunk = 2 * PADDED

    def step(index, carry):
        return body(pl.ds(pl.multiple_of(index * chunk, chunk), chunk), index, carry)

    return lax.fori_loop(0, rows // chunk, step, init)


def live_rows(live_ref, index):
    place = lax.broadcasted_iota(jnp.int32, (2 * PADDED, 1), 0)
    value = jnp.where(place < PADDED, live_ref[2 * index], live_ref[2 * index + 1])
    return jnp.where(lax.rem(place, PADDED) < WTOK, value, 0.0)


def attention_forward_kernel(heads, scale, picks, plan, block_rows, end, *refs):
    count = len(picks)
    live_ref, vec_ref, qv_ref = refs[:3]
    arrays = refs[3 : 6 + 2 * end]
    x_hbm, bias_hbm, mask_hbm = arrays[:3]
    refs = refs[3 + len(arrays) :]
    weight_refs, refs = refs[: len(plan)], refs[len(plan) :]
    outs, refs = refs[: 5 * count + 2], refs[5 * count + 2 :]
    x, bias, mask, total, normed, normed2, weights, qs, ks, vs, ps, atts, sems = refs
    rows = x.shape[0]
    columns = qs.shape[2]
    pairs = rows // (2 * PADDED)
    copies = Copies(sems)
    weight = weight_plans(copies, plan, weight_refs, block_rows, (weights,))
    later = [weight[0, n] for n in range(1, count)]
    later.append([copies.plan(mask_hbm, mask)])
    later[-1] += [copies.plan(bias_hbm.at[e], bias.at[n]) for n, e in enumerate(picks)]
    x_copy = copies.plan(x_hbm, x)
    if end:
        normed_copy = copies.plan(arrays[3], normed)
        late = [x_copy, copies.plan(arrays[4], total)]
        start_all([normed_copy], weight[0, 0])
        normed_copy.wait()
        start_all(*later)
    else:
        start_all([x_copy], weight[0, 0])
        x_copy.wait()
        start_all(*later)

        def first_norm(span, index, _):
            normal, _ = normalize(x[span, :])
            normed[span, :] = (normal * vec_ref[0:1, :] + vec_ref[1:2, :]).astype(BF16)
            return 0

        row_chunks(rows, first_norm, 0)
        copies.send(normed, outs[-1])
    for n, e in enumerate(picks):
        wait_all(weight[0, n])
        qkv = dot(normed[...], weights[n, :, : 3 * columns])
        qs[n] = ((qkv[:, :columns] + qv_ref[e, 0:1, :]) * scale).astype(BF16)
        ks[n] = qkv[:, columns : 2 * columns].astype(BF16)
        vs[n] = (qkv[:, 2 * columns :] + qv_ref[e, 1:2, :]).astype(BF16)
        for index, buffer in enumerate((qs, ks, vs)):
            copies.send(buffer.at[n], outs[5 * n + index])
    wait_all(later[-1])
    if end:
        start_all(late)

    def pair_step(pair, _):
        span = pl.ds(pl.multiple_of(pair * 2 * PADDED, 2 * PADDED), 2 * PADDED)
        for n in range(count):
            query = qs[n, span, :].astype(F32)
            key = ks[n, span, :].astype(F32)
            value = vs[n, span, :].astype(F32)
            results = []
            for side in range(2):
                part = slice(side * PADDED, (side + 1) * PADDED)
                keys = spread_heads(key[part], heads)
                scores = dot(keys, query[part].astype(BF16), 1, 1) + bias[n]
                scores = scores.reshape(heads, PADDED, PADDED) + mask[2 * pair + side][None]
                expo = jnp.exp(scores - jnp.max(scores, axis=1, keepdims=True))
                probs = expo * (1.0 / jnp.sum(expo, axis=1, keepdims=True))
                probs = probs.reshape(heads * PADDED, PADDED).astype(BF16)
                ps[n, 2 * pair + side] = probs
                results.append(dot(probs, spread_heads(value[part], heads), 0, 0))
            atts[n, span, :] = jnp.concatenate(results, axis=0).astype(BF16)
        return 0

    lax.fori_loop(0, pairs, pair_step, 0)
    for n in range(count):
        copies.send(ps.at[n], outs[5 * n + 3])
        copies.send(atts.at[n], outs[5 * n + 4])
    if end:
        wait_all(late)
    branch = total[...] if end else None
    for n in range(count):
        part = dot(atts[n], weights[n, :, 3 * columns :], 1, 1)
        branch = part if branch is None else branch + part
    total[...] = branch
    if end:

        def second_norm(span, index, _):
            live = live_rows(live_ref, index)
            mixed = x[span, :] + live * (total[span, :] + vec_ref[2:3, :])
            total[span, :] = mixed
            normal, _ = normalize(mixed)
            normed2[span, :] = (normal * vec_ref[3:4, :] + vec_ref[4:5, :]).astype(BF16)
            return 0

        row_chunks(rows, second_norm, 0)
        copies.send(normed2, outs[-1])
    copies.send(total, outs[-2])
    copies.finish()


def attention_forward(
    x, weights, picks, vectors, qv, bias, mask, live, heads, scale, earlier=()
):
    rows, width = x.shape
    columns = qv.shape[2]
    wins = rows // PADDED
    plan, arrays, block_rows = choose(weights, picks)
    count = len(picks)
    end = bool(earlier)
    shape = jax.ShapeDtypeStruct
    piece = shape((rows, columns), BF16)
    probs = shape((wins, heads * PADDED, PADDED), BF16)
    results = call(
        functools.partial(attention_forward_kernel, heads, scale, picks, plan, block_rows, end),
        "attention_forward",
        4 + 5 * count,
        live,
        (vectors, qv),
        [x, bias, mask] + list(earlier) + arrays,
        [piece, piece, piece, probs, piece] * count
        + [shape((rows, width), F32), shape((rows, width), BF16)],
        [
            like(x),
            pltpu.VMEM((count,) + bias.shape[1:], F32),
            like(mask),
            pltpu.VMEM((rows, width), F32),
            pltpu.VMEM((rows, width), BF16),
            pltpu.VMEM((rows, width), BF16),
            pltpu.VMEM((count, width, width), BF16),
        ]
        + [pltpu.VMEM((count, rows, columns), BF16)] * 3
        + [
            pltpu.VMEM((count,) + probs.shape, BF16),
            pltpu.VMEM((count, rows, columns), BF16),
        ],
        weight_copies(plan, 1) + 6 * count + 8,
    )
    saved = {e: results[5 * n : 5 * n + 5] for n, e in enumerate(picks)}
    return saved, results[-2], results[-1]


def ffn_forward_kernel(picks, plan, block_rows, end, *refs):
    count = len(picks)
    live_ref, bias_ref, vec_ref = refs[:3]
    arrays, refs = refs[3 : 4 + end], refs[4 + end :]
    weight_refs, refs = refs[: len(plan)], refs[len(plan) :]
    outs, refs = refs[: 2 * count + 1], refs[2 * count + 1 :]
    normed2, mixed, earlier, total, first, second, hidden, slope, sems = refs
    rows = normed2.shape[0]
    copies = Copies(sems)
    arrived = copies.plan(arrays[0], normed2)
    weight = weight_plans(copies, plan, weight_refs, block_rows, (first, second))
    late = [copies.plan(one, to) for one, to in zip(arrays[1:], (mixed, earlier))]
    start_all([arrived], weight[0, 0])
    arrived.wait()
    start_all(weight[1, 0])
    for n, e in enumerate(picks):
        wait_all(weight[0, n])
        if n + 1 < count:
            start_all(weight[0, n + 1], weight[1, n + 1])
        else:
            start_all(late)
        before = dot(normed2[...], first[n]) + bias_ref[e]
        cdf = 0.5 * (1.0 + lax.erf(before * (0.5**0.5)))
        density = jnp.exp(-0.5 * before * before) * 0.3989422804014327
        hidden[n] = (before * cdf).astype(BF16)
        copies.send(hidden.at[n], outs[2 * n])
        slope[n] = (cdf + before * density).astype(BF16)
        copies.send(slope.at[n], outs[2 * n + 1])
        wait_all(weight[1, n])
        part = dot(hidden[n], second[n], 1, 1)
        if n == 0:
            total[...] = part
        else:
            total[...] += part
    wait_all(late)
    if end:

        def finish(span, index, _):
            live = live_rows(live_ref, index)
            value = total[span, :] + vec_ref[5:6, :]
            if end == 2:
                value = value + earlier[span, :]
            total[span, :] = mixed[span, :] + live * value
            return 0

        row_chunks(rows, finish, 0)
    copies.send(total, outs[-1])
    copies.finish()


def ffn_forward(normed2, weights, picks, bias, vectors, live, earlier=()):
    rows, width = normed2.shape
    plan, arrays, block_rows = choose(weights, picks)
    count = len(picks)
    end = len(earlier)
    shape = jax.ShapeDtypeStruct
    piece = shape((rows, width), BF16)
    results = call(
        functools.partial(ffn_forward_kernel, picks, plan, block_rows, end),
        "ffn_forward",
        4 * count,
        live,
        (bias, vectors),
        [normed2] + list(earlier) + arrays,
        [piece, piece] * count + [shape((rows, width), F32)],
        [
            like(normed2),
            pltpu.VMEM((rows, width), F32),
            pltpu.VMEM((rows, width), F32),
            pltpu.VMEM((rows, width), F32),
        ]
        + [pltpu.VMEM((count, width, width), BF16)] * 2
        + [pltpu.VMEM((count, rows, width), BF16)] * 2,
        weight_copies(plan, 2) + 2 * count + 5,
    )
    return {e: results[2 * n : 2 * n + 2] for n, e in enumerate(picks)}, results[-1]


def fill_transposed(target, source, block_rows, tiled):
    flipped = source[...].T
    if not tiled:
        target[...] = flipped
        return
    own = lax.axis_index("dp")
    for block in range(flipped.shape[0] // block_rows):
        start = pl.multiple_of(jnp.bitwise_xor(own, block) * block_rows, block_rows)
        target[pl.ds(start, block_rows), :] = flipped[
            block * block_rows : (block + 1) * block_rows
        ]


def put_blocks(buffer, cuts, block_rows, part, value):
    order = [rel for _, _, rels in cuts for rel in rels]
    for place, rel in enumerate(order):
        start = 0 if rel is None else rel * block_rows
        buffer[place, part * block_rows : (part + 1) * block_rows, :] = value[
            start : start + block_rows
        ].astype(BF16)


def send_blocks(copies, buffer, cuts, block_rows, part, outs):
    place = 0
    rows = pl.ds(part * block_rows, block_rows)
    for index, start, rels in cuts:
        copies.send(
            buffer.at[pl.ds(place, len(rels)), rows, :],
            outs[index].at[pl.ds(start, len(rels)), rows, :],
        )
        place += len(rels)


def block_outs(layout, height, width):
    return [jax.ShapeDtypeStruct((size, height, width), BF16) for size in layout[0]]


def ffn_backward_kernel(picks, plan, block_rows, layout, begin, end, *refs):
    count = len(picks)
    sizes, cuts = layout
    tiled = cuts[0][0][2][0] is not None
    live_ref, vec_ref = refs[:2]
    given = 2 * count + 2 + end + 2 * (not begin)
    arrays, refs = refs[2 : 2 + given], refs[2 + given :]
    weight_refs, refs = refs[: len(plan)], refs[len(plan) :]
    outs, refs = refs[: 5 + len(sizes)], refs[5 + len(sizes) :]
    (
        grad, mixed, branch, error, error_here, attn_grad, normed2, slopes, hiddens, pres, first,
        second, normed2_t, branch_t, results, sums, hidden_sums, sems,
    ) = refs
    rows, width = grad.shape
    blocks_out = outs[5:]
    copies = Copies(sems)
    zero = jnp.zeros((1, width), F32)
    weight = weight_plans(copies, plan, weight_refs, block_rows, (first, second))
    grad_copy = copies.plan(arrays[0], grad)
    slope = [copies.plan(one, slopes.at[n]) for n, one in enumerate(arrays[1 : 1 + count])]
    hidden_hbm = arrays[1 + count : 1 + 2 * count]
    hidden = [copies.plan(one, hiddens.at[n]) for n, one in enumerate(hidden_hbm)]
    normed2_copy = copies.plan(arrays[1 + 2 * count], normed2)
    more = list(arrays[2 + 2 * count :])
    late = [copies.plan(more.pop(0), mixed)] if end else []
    if begin:
        arrived = grad_copy
    else:
        arrived = copies.plan(more[0], branch)
        late += [copies.plan(more[1], error), grad_copy]
    start_all([arrived], weight[1, 0], [slope[0]])
    arrived.wait()
    start_all(weight[0, 0], weight[1, 1], [slope[1]])
    if begin:

        def start(span, index, total):
            part = (live_rows(live_ref, index) * grad[span, :]).astype(BF16)
            branch[span, :] = part
            return total + jnp.sum(part.astype(F32), axis=0, keepdims=True)

        sums[3:4, :] = row_chunks(rows, start, zero)
        if not end:
            copies.send(branch, outs[2])
    fill_transposed(branch_t, branch, block_rows, tiled)
    for n, e in enumerate(picks):
        wait_all(weight[1, n])
        flow = dot(branch[...], second[n])
        slope[n].wait()
        pre = (slopes[n].astype(F32) * flow).astype(BF16)
        pres[n] = pre
        if n + 1 < count:
            start_all(weight[0, n + 1])
            if n + 2 < count:
                start_all(weight[1, n + 2], [slope[n + 2]])
        else:
            start_all([normed2_copy, hidden[0]], late)
        hidden_sums[n] = jnp.sum(pre.astype(F32), axis=0, keepdims=True)
        wait_all(weight[0, n])
        part = dot(pres[n], first[n], 1, 1)
        if n == 0:
            error_here[...] = part
        else:
            error_here[...] += part
    wait_all(late)
    if end:

        def finish(span, index, totals):
            if not begin:
                error_here[span, :] += error[span, :]
            back, gain_part, shift_part = norm_back_rows(
                mixed[span, :], vec_ref[3:4, :], error_here[span, :]
            )
            mixed_grad = grad[span, :] + back
            error_here[span, :] = mixed_grad
            low = (live_rows(live_ref, index) * mixed_grad).astype(BF16)
            attn_grad[span, :] = low
            bias_part = jnp.sum(low.astype(F32), axis=0, keepdims=True)
            return tuple(a + b for a, b in zip(totals, (gain_part, shift_part, bias_part)))

        totals = row_chunks(rows, finish, (zero, zero, zero))
        for index in range(3):
            sums[index : index + 1, :] = totals[index]
        copies.send(attn_grad, outs[1])
    copies.send(error_here, outs[0])
    copies.send(sums, outs[3])
    copies.send(hidden_sums, outs[4])
    normed2_copy.wait()
    fill_transposed(normed2_t, normed2, block_rows, tiled)
    for n in range(count):
        if n + 1 < count:
            hidden[n + 1].start()
        put_blocks(results.at[n], cuts[n], block_rows, 0, dot(normed2_t[...], pres[n]))
        send_blocks(copies, results.at[n], cuts[n], block_rows, 0, blocks_out)
        hidden[n].wait()
        put_blocks(results.at[n], cuts[n], block_rows, 1, dot(branch_t[...], hiddens[n]))
        send_blocks(copies, results.at[n], cuts[n], block_rows, 1, blocks_out)
    copies.finish()


def ffn_backward(
    grad, hidden, normed2, weights, picks, layout, vectors, live, mixed=None, earlier=()
):
    rows, width = grad.shape
    plan, arrays, block_rows = choose(weights, picks)
    count = len(picks)
    end = mixed is not None
    shape = jax.ShapeDtypeStruct
    low = shape((rows, width), BF16)
    wide = shape((rows, width), F32)
    tiny = shape((8, width), F32)
    blocks = block_outs(layout, 2 * block_rows, width)
    results = call(
        functools.partial(
            ffn_backward_kernel, picks, plan, block_rows, layout, not earlier, end
        ),
        "ffn_backward",
        7 * count,
        live,
        (vectors,),
        [grad]
        + [hidden[e][1] for e in picks]
        + [hidden[e][0] for e in picks]
        + [normed2]
        + [mixed] * end
        + list(earlier)
        + arrays,
        [wide, low if end else tiny, tiny if end else low, tiny, shape((count, 1, width), F32)]
        + blocks,
        [like(wide), like(wide), like(low), like(wide), like(wide), like(low), like(low)]
        + [pltpu.VMEM((count, rows, width), BF16)] * 3
        + [pltpu.VMEM((count, width, width), BF16)] * 2
        + [pltpu.VMEM((width, rows), BF16)] * 2
        + [pltpu.VMEM((count, width // block_rows, 2 * block_rows, width), BF16)]
        + [pltpu.VMEM((8, width), F32), pltpu.VMEM((count, 1, width), F32)],
        weight_copies(plan, 2) + 2 * count + 9 + 4 * len(blocks) + 4,
    )
    return *results[:5], results[5:]


def ffn_both_kernel(picks, plan, block_rows, layout, *refs):
    count = len(picks)
    sizes, cuts = layout
    tiled = cuts[0][0][2][0] is not None
    live_ref, bias_ref, vec_ref = refs[:3]
    normed2_hbm, mixed_hbm, grad_hbm = refs[3:6]
    refs = refs[6:]
    weight_refs, refs = refs[: len(plan)], refs[len(plan) :]
    outs, refs = refs[:5], refs[5:]
    blocks_out, refs = refs[: len(sizes)], refs[len(sizes) :]
    (
        normed2, mixed, grad, total, error, branch, attn_grad, hiddens, pres, first, second,
        normed2_t, branch_t, results, sums, hidden_sums, sems,
    ) = refs
    rows, width = grad.shape
    copies = Copies(sems)
    zero = jnp.zeros((1, width), F32)
    weight = weight_plans(copies, plan, weight_refs, block_rows, (first, second))
    grad_copy = copies.plan(grad_hbm, grad)
    normed2_copy = copies.plan(normed2_hbm, normed2)
    mixed_copy = copies.plan(mixed_hbm, mixed)
    start_all([normed2_copy], weight[0, 0])
    normed2_copy.wait()
    start_all([grad_copy], weight[1, 0])
    fill_transposed(normed2_t, normed2, block_rows, tiled)
    for n, e in enumerate(picks):
        wait_all(weight[0, n])
        before = dot(normed2[...], first[n]) + bias_ref[e]
        if n + 1 < count:
            start_all(weight[0, n + 1], weight[1, n + 1])
        else:
            start_all([mixed_copy])
        cdf = 0.5 * (1.0 + lax.erf(before * (0.5**0.5)))
        density = jnp.exp(-0.5 * before * before) * 0.3989422804014327
        hiddens[n] = (before * cdf).astype(BF16)
        slope = cdf + before * density
        if n == 0:
            grad_copy.wait()

            def start(span, index, carry):
                part = (live_rows(live_ref, index) * grad[span, :]).astype(BF16)
                branch[span, :] = part
                return carry + jnp.sum(part.astype(F32), axis=0, keepdims=True)

            sums[3:4, :] = row_chunks(rows, start, zero)
            fill_transposed(branch_t, branch, block_rows, tiled)
        wait_all(weight[1, n])
        pre = (slope * dot(branch[...], second[n])).astype(BF16)
        pres[n] = pre
        hidden_sums[n] = jnp.sum(pre.astype(F32), axis=0, keepdims=True)
        part = dot(hiddens[n], second[n], 1, 1)
        back = dot(pres[n], first[n], 1, 1)
        if n == 0:
            total[...] = part
            error[...] = back
        else:
            total[...] += part
            error[...] += back
    mixed_copy.wait()

    def finish(span, index, totals):
        live = live_rows(live_ref, index)
        values = mixed[span, :]
        total[span, :] = values + live * (total[span, :] + vec_ref[5:6, :])
        back, gain_part, shift_part = norm_back_rows(values, vec_ref[3:4, :], error[span, :])
        mixed_grad = grad[span, :] + back
        error[span, :] = mixed_grad
        low = (live * mixed_grad).astype(BF16)
        attn_grad[span, :] = low
        bias_part = jnp.sum(low.astype(F32), axis=0, keepdims=True)
        return tuple(a + b for a, b in zip(totals, (gain_part, shift_part, bias_part)))

    totals = row_chunks(rows, finish, (zero, zero, zero))
    for index in range(3):
        sums[index : index + 1, :] = totals[index]
    for buffer, out in zip((total, error, attn_grad, sums, hidden_sums), outs):
        copies.send(buffer, out)
    for n in range(count):
        put_blocks(results.at[n], cuts[n], block_rows, 0, dot(normed2_t[...], pres[n]))
        send_blocks(copies, results.at[n], cuts[n], block_rows, 0, blocks_out)
        put_blocks(results.at[n], cuts[n], block_rows, 1, dot(branch_t[...], hiddens[n]))
        send_blocks(copies, results.at[n], cuts[n], block_rows, 1, blocks_out)
    copies.finish()


def ffn_both(normed2, mixed, grad, weights, picks, layout, bias, vectors, live):
    rows, width = grad.shape
    plan, arrays, block_rows = choose(weights, picks)
    count = len(picks)
    shape = jax.ShapeDtypeStruct
    low = shape((rows, width), BF16)
    wide = shape((rows, width), F32)
    blocks = block_outs(layout, 2 * block_rows, width)
    results = call(
        functools.partial(ffn_both_kernel, picks, plan, block_rows, layout),
        "ffn_both",
        30,
        live,
        (bias, vectors),
        [normed2, mixed, grad] + arrays,
        [wide, wide, low, shape((8, width), F32), shape((count, 1, width), F32)] + blocks,
        [like(low), like(wide), like(wide), like(wide), like(wide), like(low), like(low)]
        + [pltpu.VMEM((count, rows, width), BF16)] * 2
        + [pltpu.VMEM((count, width, width), BF16)] * 2
        + [pltpu.VMEM((width, rows), BF16)] * 2
        + [pltpu.VMEM((count, width // block_rows, 2 * block_rows, width), BF16)]
        + [pltpu.VMEM((8, width), F32), pltpu.VMEM((count, 1, width), F32)],
        weight_copies(plan, 2) + 8 + 4 * len(blocks) + 4,
    )
    return *results[:5], results[5:]


def attention_backward_kernel(heads, scale, picks, plan, block_rows, layout, end, *refs):
    count = len(picks)
    sizes, cuts = layout
    tiled = cuts[0][0][2][0] is not None
    live_ref, vec_ref = refs[:2]
    given = 2 + 5 * count + 3 * end
    arrays, refs = refs[2 : 2 + given], refs[2 + given :]
    weight_refs, refs = refs[: len(plan)], refs[len(plan) :]
    outs_count = 3 + end + len(sizes)
    outs, refs = refs[:outs_count], refs[outs_count:]
    (
        attn_grad, normed, x, mixed_grad, error, weights, qs, ks, vs, atts, ps, gs, grads,
        normed_t, attn_grad_t, results, scores_sum, sums, small, sems,
    ) = refs
    rows, width = attn_grad.shape
    columns = qs.shape[2]
    pairs = rows // (2 * PADDED)
    copies = Copies(sems)
    weight = weight_plans(copies, plan, weight_refs, block_rows, (weights,))
    arrived = copies.plan(arrays[0], attn_grad)
    saved = [
        copies.plan(arrays[2 + 5 * n + index], buffer.at[n])
        for n in range(count)
        for index, buffer in ((0, qs), (1, ks), (2, vs), (3, ps))
    ]
    late = [copies.plan(arrays[1], normed)]
    for n in range(count):
        late.append(copies.plan(arrays[2 + 5 * n + 4], atts.at[n]))
    if end:
        for one, to in zip(arrays[2 + 5 * count :], (x, mixed_grad, error)):
            late.append(copies.plan(one, to))
    start_all([arrived], weight[0, 0])
    arrived.wait()
    start_all(*[weight[0, n] for n in range(1, count)], saved)
    scores_sum[...] = jnp.zeros(scores_sum.shape, F32)
    fill_transposed(attn_grad_t, attn_grad, block_rows, tiled)
    for n in range(count):
        wait_all(weight[0, n])
        gs[n] = dot(attn_grad[...], weights[n, :, 3 * columns :]).astype(BF16)
    wait_all(saved)
    start_all(late)

    def pair_step(pair, _):
        span = pl.ds(pl.multiple_of(pair * 2 * PADDED, 2 * PADDED), 2 * PADDED)
        for n in range(count):
            query, key, value, grad = [
                buffer[n, span, :].astype(F32) for buffer in (qs, ks, vs, gs)
            ]
            rows_out = []
            for side in range(2):
                part = slice(side * PADDED, (side + 1) * PADDED)
                keys = spread_heads(key[part], heads)
                values = spread_heads(value[part], heads)
                grad_low = grad[part].astype(BF16)
                low = ps[n, 2 * pair + side]
                probs = low.astype(F32)
                flow = dot(values, grad_low, 1, 1)
                inner = jnp.sum(
                    (probs * flow).reshape(heads, PADDED, PADDED), axis=1, keepdims=True
                )
                score = probs.reshape(heads, PADDED, PADDED) * (
                    flow.reshape(heads, PADDED, PADDED) - inner
                )
                score = score.reshape(heads * PADDED, PADDED).astype(BF16)
                scores_sum[n] += score.astype(F32)
                rows_out.append(
                    jnp.concatenate(
                        [
                            dot(score, keys, 0, 0) * scale,
                            merge_heads(dot(score, query[part].astype(BF16)), heads),
                            merge_heads(dot(low, grad_low), heads),
                        ],
                        axis=1,
                    )
                )
            grads[n, span, :] = jnp.concatenate(rows_out, axis=0).astype(BF16)
        return 0

    lax.fori_loop(0, pairs, pair_step, 0)
    copies.send(scores_sum, outs[1])
    wait_all(late)
    for n in range(count):
        sums[n] = jnp.sum(grads[n].astype(F32), axis=0, keepdims=True)
        part = dot(grads[n], weights[n, :, : 3 * columns], 1, 1)
        if n == 0 and not end:
            error[...] = part
        else:
            error[...] += part
    copies.send(sums, outs[2])
    if end:
        zero = jnp.zeros((1, width), F32)

        def finish(span, index, totals):
            back, gain_part, shift_part = norm_back_rows(
                x[span, :], vec_ref[0:1, :], error[span, :]
            )
            error[span, :] = mixed_grad[span, :] + back
            return totals[0] + gain_part, totals[1] + shift_part

        totals = row_chunks(rows, finish, (zero, zero))
        for index in range(2):
            small[index : index + 1, :] = totals[index]
        copies.send(small, outs[3])
    copies.send(error, outs[0])
    fill_transposed(normed_t, normed, block_rows, tiled)
    for n in range(count):
        value = jnp.concatenate(
            [dot(normed_t[...], grads[n]), dot(attn_grad_t[...], atts[n])], axis=1
        )
        put_blocks(results.at[n], cuts[n], block_rows, 0, value)
        send_blocks(copies, results.at[n], cuts[n], block_rows, 0, outs[3 + end :])
    copies.finish()


def attention_backward(
    attn_grad, normed, saved, weights, picks, layout, vectors, live, heads, scale, earlier=()
):
    rows, width = attn_grad.shape
    columns = saved[picks[0]][0].shape[1]
    plan, arrays, block_rows = choose(weights, picks)
    count = len(picks)
    end = bool(earlier)
    probs = saved[picks[0]][3]
    shape = jax.ShapeDtypeStruct
    wide = shape((rows, width), F32)
    pieces = [item for e in picks for item in saved[e]]
    outs = [
        wide,
        shape((count, heads * PADDED, PADDED), F32),
        shape((count, 1, 3 * columns), F32),
    ]
    blocks = block_outs(layout, block_rows, width)
    results = call(
        functools.partial(
            attention_backward_kernel, heads, scale, picks, plan, block_rows, layout, end
        ),
        "attention_backward",
        19,
        live,
        (vectors,),
        [attn_grad, normed] + pieces + list(earlier) + arrays,
        outs + [shape((8, width), F32)] * end + blocks,
        [like(attn_grad), like(normed), like(wide), like(wide), like(wide)]
        + [pltpu.VMEM((count, width, width), BF16)]
        + [pltpu.VMEM((count, rows, columns), BF16)] * 4
        + [pltpu.VMEM((count,) + probs.shape, BF16)]
        + [pltpu.VMEM((count, rows, columns), BF16)]
        + [pltpu.VMEM((count, rows, 3 * columns), BF16)]
        + [pltpu.VMEM((width, rows), BF16)] * 2
        + [pltpu.VMEM((count, width // block_rows, block_rows, width), BF16)]
        + [like(outs[1]), like(outs[2]), pltpu.VMEM((8, width), F32)],
        weight_copies(plan, 1) + 5 * count + 11 + 4 * len(blocks),
    )
    return *results[: 3 + end], results[3 + end :]


def swap(values, axis, bit):
    size = lax.axis_size(axis)
    return lax.ppermute(values, axis, [(i, i ^ (1 << bit)) for i in range(size)])


def bits_in(axis):
    return lax.axis_size(axis).bit_length() - 1


def pick(values, index, dim):
    return lax.dynamic_index_in_dim(values, index, dim, keepdims=False)


def tie(values, token):
    if token is None:
        return values
    return lax.optimization_barrier((values, token))[0]


def whole_tiles(rows):
    return rows % 16 == 0


def in_order(values):
    index = jnp.bitwise_xor(jnp.arange(values.shape[0]), lax.axis_index("dp"))
    return jnp.take(values, index, axis=0)


def relatives(halves):
    count = lax.axis_size("dp")
    size = count // halves
    return [
        [tuple(range(part * size + side, (part + 1) * size, 2)) for part in range(halves)]
        for side in range(2)
    ]


def line_bits():
    return list(range(1, bits_in("dp")))


def straight(values):
    size = lax.axis_size("dp")
    low, high = [1 << bit for bit in line_bits()[-2:]]
    return [
        lax.ppermute(values(n), "dp", [(i, i ^ shift) for i in range(size)])
        for n, shift in ((1, low), (2, high), (3, low | high))
    ]


class Gather:
    def __init__(self, shard, parts, rows, ways):
        self.shard = shard
        self.parts = parts
        self.rows = rows
        self.ways = ways
        self.entries = []

    def line(self, after=None, at_once=False):
        held = tie(self.shard, after)[None]
        bits = line_bits()
        for bit in bits[:-2]:
            held = jnp.concatenate([held, swap(held, "dp", bit)])
        self.moved = straight(lambda n: held) if at_once else [swap(held, "dp", bits[-2])]
        self.held = [held]

    def line_end(self, until=None):
        moved = tie(self.moved, until)
        self.held = [jnp.concatenate(self.held + moved)]
        return self.held[0]

    def last(self, after=None):
        self.moved = swap(tie(self.held[0], after), "dp", line_bits()[-1])

    def last_end(self, until=None):
        moved = tie(self.moved, until)
        self.held.append(moved)
        if len(self.ways) == 1:
            self.held = [jnp.concatenate(self.held)]
        return self.held[-1]

    def sides(self, part, after=None):
        if part == 0:
            self.side, self.far = [], []
        held = tie(self.held[part], after)
        self.side.append(swap(held, "dp", 0))
        self.far.append(swap(held, "head", 1))

    def sides_end(self, part, until=None):
        self.side[part], self.far[part] = tie((self.side[part], self.far[part]), until)
        return self.side[part], self.far[part]

    def corner(self, part, after=None):
        if part == 0:
            self.corners = []
        if self.ways[part] == "x":
            self.corners.append(swap(tie(self.side[part], after), "head", 1))
        else:
            self.corners.append(swap(tie(self.far[part], after), "dp", 0))

    def corner_end(self, part, until=None):
        self.corners[part] = tie(self.corners[part], until)
        return self.corners[part]

    def core(self, kind, part=None):
        own, other = relatives(len(self.ways))
        arrays, e, rels = {
            "held": (self.held, 0, own),
            "side": (self.side, 0, other),
            "far": (self.far, 2, own),
            "corner": (getattr(self, "corners", None), 2, other),
        }[kind]
        for n, (one, several) in enumerate(zip(arrays, rels)):
            if part is None or part == n:
                self.entries.append((e, one, several))
                self.entries.append((e + 1, swap(one, "head", 0), several))

    def result(self, first=0):
        rows, parts = self.rows, self.parts
        width = self.shard.shape[1]
        if whole_tiles(rows):
            plan = tuple((e, rels) for e, _, rels in self.entries)
            return plan, [one for _, one, _ in self.entries], rows, first * rows
        arrays = []
        plan = []
        for e in range(PIECES):
            mine = [(one, rels) for piece, one, rels in self.entries if piece == e]
            if not mine:
                continue
            order = sum((rels for _, rels in mine), ())
            if len(order) < lax.axis_size("dp"):
                continue
            blocks = jnp.concatenate([one[:, : parts * rows] for one, _ in mine])
            blocks = in_order(blocks[jnp.argsort(jnp.array(order))])
            blocks = blocks.reshape(-1, parts, rows, width).transpose(1, 0, 2, 3)
            arrays.append(blocks.reshape(1, -1, width))
            plan.append((e, (None,)))
        rows = arrays[0].shape[1] // parts
        return tuple(plan), arrays, rows, first * rows


def wide(*values):
    total = values[0].astype(F32)
    for value in values[1:]:
        total = total + value.astype(F32)
    return total


def plus(*values):
    return wide(*values).astype(BF16)


class Scatter:
    def __init__(self, parts, rows, ways):
        self.parts = parts
        self.rows = rows
        self.ways = ways
        self.tiled = whole_tiles(rows)
        blocks = lax.axis_size("dp")
        half = blocks // 2
        even = tuple(range(0, blocks, 2))
        odd = tuple(range(1, blocks, 2))
        cut = half // len(ways)
        corners = [odd[n * cut : (n + 1) * cut] for n in range(len(ways))]
        self.order = even + odd
        if self.tiled:
            self.away_layout = (
                (2 * blocks,),
                (((0, 0, self.order),), ((0, blocks, self.order),)),
            )
            last = tuple((3 + n, 0, rels) for n, rels in enumerate(corners))
            self.near_layout = (
                (half,) * 3 + (cut,) * len(ways),
                (((0, 0, even), (1, 0, odd)), ((2, 0, even),) + last),
            )
        else:
            one = ((0, 0, (None,)),)
            two = ((0, 1, (None,)),)
            self.away_layout = self.near_layout = ((2,), (one, two))

    def both_layouts(self):
        sizes, cuts = self.near_layout
        first = len(self.away_layout[0])
        moved = tuple(
            tuple((first + index, start, rels) for index, start, rels in one) for one in cuts
        )
        return self.away_layout[0] + sizes, self.away_layout[1] + moved

    def arrange(self, outs):
        one = outs[0].reshape(2, self.parts, -1, self.rows, outs[0].shape[-1])
        one = one.transpose(0, 2, 1, 3, 4)
        one = one.reshape(one.shape[:2] + (-1, one.shape[-1]))
        return jnp.concatenate([in_order(item)[jnp.array(self.order)] for item in one])

    def away(self, outs):
        self.moved = swap(outs[0] if self.tiled else self.arrange(outs), "head", 0)

    def near(self, outs, until=None):
        moved = tie(self.moved, until)
        half = moved.shape[0] // 4
        if self.tiled:
            own = list(outs)
        else:
            one = self.arrange(outs)
            own = [one[n * half : (n + 1) * half] for n in range(3)]
            cut = half // len(self.ways)
            own += [one[3 * half + n * cut :][:cut] for n in range(len(self.ways))]
        cut = half // len(self.ways)
        self.held = [own[0], moved[:half]]
        self.side = [own[1], moved[half : 2 * half]]
        self.far = [own[2], moved[2 * half : 3 * half]]
        self.corners = [
            plus(own[3 + n], moved[3 * half + n * cut :][:cut]) for n in range(len(self.ways))
        ]
        return self.corners

    def corner(self, after=None):
        self.moved = []
        for way, one in zip(self.ways, tie(self.corners, after)):
            self.moved.append(swap(one, "head", 1) if way == "x" else swap(one, "dp", 0))

    def corner_end(self, until=None):
        moved = tie(self.moved, until)
        half = self.side[0].shape[0]
        for part, (way, one) in enumerate(zip(self.ways, moved)):
            size = one.shape[0]
            around = (part * size, half - (part + 1) * size)
            one = jnp.pad(one, (around,) + ((0, 0),) * 2) if size < half else one
            (self.side if way == "x" else self.far).append(one)
        self.side, self.far = plus(*self.side), plus(*self.far)
        return self.side, self.far

    def sides(self, after=None, part=None):
        side, far = tie((self.side, self.far), after)
        if part is not None:
            size = side.shape[0] // 2
            side, far = [one[part * size : (part + 1) * size] for one in (side, far)]
        self.moved = [swap(side, "dp", 0), swap(far, "head", 1)]

    def sides_end(self, until=None, at_once=False, part=None):
        terms = self.held + list(tie(self.moved, until))
        if part is not None:
            size = terms[-1].shape[0]
            terms[:2] = [one[part * size : (part + 1) * size] for one in terms[:2]]
            if part == 0:
                self.lower = plus(*terms)
                return self.lower
            self.held = [self.lower, plus(*terms)]
            return self.held
        count = 4 if at_once else 2
        size = terms[0].shape[0] // count
        self.held = [
            plus(*[one[n * size : (n + 1) * size] for one in terms]) for n in range(count)
        ]
        return self.held

    def last(self, after=None):
        self.moved = swap(tie(self.held[1], after), "dp", line_bits()[-1])

    def last_end(self, until=None):
        moved = tie(self.moved, until)
        size = moved.shape[0] // 2
        terms = [self.held[0], moved]
        self.held = [plus(*[one[n * size :][:size] for one in terms]) for n in range(2)]
        return self.held

    def line(self, after=None):
        held = tie(self.held, after)
        if len(held) == 4:
            self.moved = straight(lambda n: held[n])
        else:
            self.moved = [swap(held[1], "dp", line_bits()[-2])]

    def line_end(self, until=None):
        held = wide(self.held[0], *tie(self.moved, until))
        for bit in reversed(line_bits()[:-2]):
            cut = held.shape[0] // 2
            moved = swap(held[cut:].astype(BF16), "dp", bit)
            held = wide(held[:cut], moved)
        self.result = held[0]
        return self.result


class SmallSum:
    def __init__(self, values):
        self.total = values
        self.left = [("head", 0), ("head", 1)]
        self.left += [("dp", bit) for bit in range(bits_in("dp"))]
        self.moved = None

    def step(self, until=None):
        self.result(until)
        axis, bit = self.left.pop(0)
        self.moved = swap(self.total, axis, bit)

    def end(self):
        return not self.left

    def result(self, until=None):
        if self.moved is not None:
            self.total = self.total + tie(self.moved, until)
        self.moved = None
        return self.total


def unshift(values):
    grid = values.reshape(values.shape[:-1] + (WSIDE, WSIDE))
    return jnp.roll(grid, (SHIFT, SHIFT), axis=(-2, -1)).reshape(values.shape)


def pad_rows(values):
    grid = values.reshape(-1, WTOK, values.shape[1])
    grid = jnp.pad(grid, ((0, 0), (0, PADDED - WTOK), (0, 0)))
    return grid.reshape(-1, values.shape[1])


def drop_rows(values):
    grid = values.reshape(-1, PADDED, values.shape[1])[:, :WTOK]
    return grid.reshape(-1, values.shape[1])


def attention_mask(pad, region):
    allowed = (pad[:, :, None] == 1) & (region[:, :, None] == region[:, None, :])
    mask = jnp.where(allowed, 0.0, MASKED).astype(F32)
    extra = PADDED - WTOK
    mask = jnp.pad(mask, ((0, 0), (0, 0), (0, extra)))
    return jnp.pad(mask, ((0, 0), (0, extra), (0, 0)), constant_values=ABSENT)


def shards(
    tokens,
    cotangent,
    crop_counts,
    pad_mask,
    region_ids,
    rel_index,
    norm_gain,
    norm_shift,
    qkv_weight,
    qv_bias,
    bias_table,
    proj_weight,
    fc1_weight,
    fc1_bias,
    fc2_weight,
    out_bias,
):
    rows = tokens.shape[0]
    width = tokens.shape[1]
    wins = rows // WTOK
    local_width = qkv_weight.shape[3]
    local_heads = bias_table.shape[1]
    rel_count = bias_table.shape[2]
    dp_width = norm_gain.shape[2]
    dp_hidden = fc1_bias.shape[1]
    pieces = lax.axis_size("head")
    heads_total = local_heads * pieces
    head_dim = local_width // local_heads
    scale = head_dim ** (-0.5)
    head_index = lax.axis_index("head")
    dp_index = lax.axis_index("dp")
    relative = [head_index ^ e for e in range(pieces)]

    shard_rows = qkv_weight.shape[1]
    attn_shards = [
        jnp.concatenate(
            [qkv_weight[block].reshape(-1, 3 * local_width), proj_weight[block].T], axis=1
        )
        for block in range(BLOCKS)
    ]
    ffn_shards = [
        jnp.concatenate([fc1_weight[block], fc2_weight[block].T]) for block in range(BLOCKS)
    ]
    small = jnp.concatenate([norm_gain, norm_shift, qv_bias, out_bias]).reshape(-1, dp_width)
    small_rows = small.shape[0]
    beside = -(-dp_width // 128) * 128
    small = jnp.pad(small, ((0, 0), (0, width - dp_width)))
    small = small + jnp.pad(
        fc1_bias, ((0, small_rows - BLOCKS), (beside, width - beside - dp_hidden))
    )
    attn_shards[0] = jnp.concatenate([attn_shards[0], small])
    near, away = (0, 2), (1, 3)
    first, second = (0, 1), (2, 3)
    a0 = Gather(attn_shards[0], 1, shard_rows, "x")
    middle = Gather(jnp.concatenate([ffn_shards[0], attn_shards[1]]), 3, shard_rows, "xy")
    f1 = Gather(ffn_shards[1], 2, shard_rows, "xy")

    def attn_weights(block):
        return middle.result(2) if block else a0.result()

    def ffn_weights(block):
        return f1.result() if block else middle.result()

    a0.line(at_once=True)
    far_table = swap(bias_table, "head", 1)
    near_table = swap(bias_table, "head", 0)
    a0.line_end()
    a0.sides(0)
    middle.line(a0.held)
    a0.core("held")
    middle.line_end()
    middle.last()
    a0.sides_end(0)
    a0.core("side")
    a0.core("far")
    a0.corner(0)
    middle.sides(0, a0.far)
    table_pieces = [bias_table, near_table, far_table, swap(far_table, "head", 0)]
    small_all = jnp.stack([a0.held[0][:, shard_rows:], a0.side[0][:, shard_rows:]], axis=1)
    small_all = in_order(small_all.reshape((-1,) + small.shape)).transpose(1, 0, 2).astype(F32)
    every = small_all[:, :, :dp_width].reshape(4, BLOCKS, 2, width)
    gains, shifts, qv_all, out_all = every[0], every[1], every[2], every[3]
    hidden_bias = small_all[:BLOCKS, :, beside : beside + dp_hidden].reshape(BLOCKS, pieces, -1)
    qv_pieces = qv_all.reshape(BLOCKS, 2, pieces, local_width)

    counts = jnp.repeat(crop_counts, CROP_MAX)
    slots = jnp.arange(pad_mask.shape[0], dtype=jnp.int32) % CROP_MAX
    live_all = (slots < counts).astype(F32)
    live_windows = lax.dynamic_slice_in_dim(live_all, head_index * wins, wins, 0)
    live = live_windows
    pad = lax.dynamic_slice_in_dim(pad_mask, head_index * wins, wins, 0)
    region = unshift(lax.dynamic_slice_in_dim(region_ids, head_index * wins, wins, 0))
    masks = (attention_mask(pad, jnp.zeros_like(region)), attention_mask(pad, region))
    extra = PADDED - WTOK
    onehots = []
    for index in (rel_index, unshift(unshift(rel_index).T).T):
        by_key = jnp.pad(index.T, ((0, extra), (0, extra)), constant_values=-1).reshape(1, -1)
        ids = jnp.arange(rel_count, dtype=jnp.int32)[:, None]
        onehots.append((ids == by_key).astype(BF16))

    def ordered(values, dim):
        return jnp.stack([pick(values, rel, dim) for rel in relative])

    block_rows = local_heads * PADDED
    vectors, qv, biases, hidden_biases = [], [], [], []
    for block in range(BLOCKS):
        rows8 = [
            gains[block, 0],
            shifts[block, 0],
            out_all[block, 0],
            gains[block, 1],
            shifts[block, 1],
            out_all[block, 1],
        ]
        vectors.append(jnp.pad(jnp.stack(rows8), ((0, 2), (0, 0))))
        qv.append(ordered(qv_pieces[block], 1))
        table = jnp.concatenate([one[block] for one in table_pieces])
        bias = jnp.dot(table, onehots[block % 2], preferred_element_type=F32)
        biases.append(bias.reshape(pieces, block_rows, PADDED))
        hidden_biases.append(ordered(hidden_bias[block], 0)[:, None, :])

    residual = pad_rows(tokens).astype(F32)

    def attend(block, x, picks, token, earlier=()):
        return attention_forward(
            x,
            attn_weights(block),
            picks,
            tie(vectors[block], token),
            qv[block],
            biases[block],
            masks[block % 2],
            live,
            local_heads,
            scale,
            earlier,
        )

    def feed(block, normed2, picks, token, earlier=()):
        return ffn_forward(
            normed2,
            ffn_weights(block),
            picks,
            hidden_biases[block],
            tie(vectors[block], token),
            live,
            earlier,
        )

    x0 = residual
    grad_rows = pad_rows(cotangent).astype(F32)
    token = (middle.held[0], biases[1], masks[1], grad_rows)
    saved_0, branch, normed_0 = attend(0, x0, first, token)
    a0.corner_end(0, branch)
    a0.core("corner")
    middle.sides_end(0, branch)
    middle.corner(0)
    middle.last_end(branch)
    middle.sides(1)
    f1.line(middle.held[1])
    f1.line_end()
    token = (middle.held[1], f1.held[0])
    more, mixed_0, normed2_0 = attend(0, x0, second, token, (normed_0, branch))
    saved_0.update(more)
    f1.last()
    middle.core("held")
    middle.sides_end(1, mixed_0)
    middle.corner(1)
    middle.core("side")
    middle.core("far")
    middle.corner_end(0, mixed_0)
    middle.corner_end(1, mixed_0)
    middle.core("corner")
    f1.sides(0, middle.corners)
    hidden_0, x1 = feed(0, normed2_0, first + second, middle.corners, (mixed_0,))
    f1.sides_end(0, x1)
    f1.last_end(x1)
    f1.core("held")
    f1.core("side", 0)
    f1.sides(1)
    saved_1, branch, normed_1 = attend(1, x1, first, f1.held)
    f1.sides_end(1, branch)
    f1.corner(0)
    f1.corner(1)
    f1.core("side", 1)
    f1.core("far")
    token = (f1.side, f1.far)
    more, mixed_1, normed2_1 = attend(1, x1, second, token, (normed_1, branch))
    saved_1.update(more)
    f1.corner_end(0, mixed_1)
    f1.corner_end(1, mixed_1)
    f1.core("corner")
    kept = [
        (x0, mixed_0, normed_0, normed2_0, saved_0, hidden_0),
        (x1, mixed_1, normed_1, normed2_1, saved_1, None),
    ]

    def feed_back(block, picks, layout, grad, token, mixed=None, earlier=()):
        _, _, _, normed2, _, hidden = kept[block]
        return ffn_backward(
            grad,
            hidden,
            normed2,
            ffn_weights(block),
            picks,
            layout,
            tie(vectors[block], token),
            live,
            mixed,
            earlier,
        )

    def attend_back(block, picks, layout, attn_grad, token, earlier=()):
        _, _, normed, _, saved, _ = kept[block]
        return attention_backward(
            attn_grad,
            normed,
            saved,
            attn_weights(block),
            picks,
            layout,
            tie(vectors[block], token),
            live,
            local_heads,
            scale,
            earlier,
        )

    def small_terms(block, attn, small_f, hidden_terms):
        scores_a, sums_a, scores_n, sums_n, small_a = attn

        def together(one, other):
            return ordered(jnp.stack([one[0], other[0], one[1], other[1]]), 0)

        table_grad = lax.dot_general(
            together(scores_n, scores_a).reshape(heads_total, -1),
            onehots[block % 2].astype(F32),
            (((1,), (1,)), ((), ())),
            precision=lax.Precision.HIGHEST,
            preferred_element_type=F32,
        )
        table_grad = jnp.pad(table_grad, ((0, 0), (0, table_lanes - rel_count)))
        qv_sums = together(sums_n, sums_a)[:, 0]
        items = [
            small_a[0:1],
            small_f[0:1],
            small_a[1:2],
            small_f[1:2],
            qv_sums[:, :local_width].reshape(1, width),
            qv_sums[:, 2 * local_width :].reshape(1, width),
            small_f[2:4],
            together(*hidden_terms)[:, 0],
            table_grad.reshape(-1, width),
        ]
        return jnp.concatenate(items)

    table_lanes = 2 * 128
    f1_sum, f0_sum = [Scatter(2, shard_rows, "xy") for _ in range(2)]
    a1_sum, a0_sum = [Scatter(1, shard_rows, "xy") for _ in range(2)]
    residual, mixed_grad, attn_grad, small_f, hidden_sums, outs = ffn_both(
        normed2_1,
        mixed_1,
        grad_rows,
        ffn_weights(1),
        away + near,
        f1_sum.both_layouts(),
        hidden_biases[1],
        tie(vectors[1], mixed_1),
        live,
    )
    count = len(f1_sum.away_layout[0])
    f1_sum.away(outs[:count])
    error, scores_a, sums_a, sent = attend_back(1, away, a1_sum.away_layout, attn_grad, None)
    f1_sum.near(outs[count:], error)
    f1_sum.corner()
    a1_sum.away(sent)
    grad_rows, scores_n, sums_n, small_a, outs = attend_back(
        1, near, a1_sum.near_layout, attn_grad, f1_sum.corners, (x1, mixed_grad, error)
    )
    late_terms = (scores_a, sums_a, scores_n, sums_n, small_a), small_f, hidden_sums
    token = f1_sum.corner_end(grad_rows)
    f1_sum.sides(part=0)
    a1_sum.near(outs, grad_rows)
    error, _, branch_grad, small_b, hidden_a, sent = feed_back(
        0, away, f0_sum.away_layout, grad_rows, (token, a1_sum.corners)
    )
    f0_sum.away(sent)
    token = f1_sum.sides_end(error, part=0)
    f1_sum.sides(token, part=1)
    a1_sum.corner(token)
    mixed_grad, attn_grad, _, small_f, hidden_n, outs = feed_back(
        0,
        near,
        f0_sum.near_layout,
        grad_rows,
        (error, token),
        mixed_0,
        (branch_grad, error),
    )
    small_f = jnp.concatenate([small_f[:3], small_b[3:4]])
    token = (f1_sum.sides_end(attn_grad, part=1), a1_sum.corner_end(attn_grad))
    f1_sum.last()
    a1_sum.sides()
    f0_sum.near(outs, attn_grad)
    f0_sum.corner()
    error, scores_a, sums_a, sent = attend_back(
        0, away, a0_sum.away_layout, attn_grad, (token, f0_sum.corners)
    )
    a0_sum.away(sent)
    token = (f0_sum.corner_end(error), a1_sum.sides_end(error), f1_sum.last_end(error))
    f0_sum.sides()
    a1_sum.last()
    f1_sum.line()
    grad_rows, scores_n, sums_n, small_a, outs = attend_back(
        0, near, a0_sum.near_layout, attn_grad, token, (x0, mixed_grad, error)
    )
    f0_sum.sides_end(grad_rows)
    f0_sum.last()
    a1_sum.last_end(grad_rows)
    a0_sum.near(outs, (grad_rows, f0_sum.held, a1_sum.held))
    a0_sum.corner()
    a1_sum.line()
    token = a0_sum.corner_end()
    a0_sum.sides()
    attn_terms = tie((scores_a, sums_a, scores_n, sums_n, small_a), token)
    small_0 = small_terms(0, attn_terms, small_f, (hidden_n, hidden_a))
    attn_terms, small_f, hidden_sums = tie(late_terms, token)
    small_1 = small_terms(1, attn_terms, small_f, (hidden_sums[2:], hidden_sums[:2]))
    small_sum = SmallSum(jnp.stack([small_0, small_1]))
    residual, grad_rows = tie((residual, grad_rows), token)
    f0_sum.last_end(token)
    token = a0_sum.sides_end(at_once=True)
    a0_sum.line((f0_sum.held, small_sum.total))
    f0_sum.line()
    a1_sum.line_end(token)
    f1_sum.line_end(token)
    small_sum.step()
    small_sum.step(token)
    while not small_sum.end():
        small_sum.step()
    a0_sum.line_end()
    f0_sum.line_end()
    shard_grads = [(a0_sum, f0_sum), (a1_sum, f1_sum)]
    shard_grads = [
        (attn.result, ffn.result[:shard_rows], ffn.result[shard_rows:])
        for attn, ffn in shard_grads
    ]

    totals = small_sum.result()

    def own(values):
        return lax.dynamic_slice_in_dim(values, dp_index * dp_width, dp_width, 2)

    small_grads = [own(totals[:, 2 * index : 2 * index + 2]) for index in range(4)]
    hidden_total = totals[:, 8 : 8 + pieces].reshape(BLOCKS, -1)
    fc1_bias_grad = lax.dynamic_slice_in_dim(hidden_total, dp_index * dp_hidden, dp_hidden, 1)
    table_total = totals[:, 8 + pieces :].reshape(BLOCKS, heads_total, table_lanes)
    bias_table_grad = lax.dynamic_slice_in_dim(
        table_total[:, :, :rel_count], head_index * local_heads, local_heads, 1
    )
    qkv_weight_grad = jnp.stack(
        [item[0][:, : 3 * local_width].reshape(-1, 3, local_width) for item in shard_grads]
    )
    proj_weight_grad = jnp.stack([item[0][:, 3 * local_width :].T for item in shard_grads])
    fc1_weight_grad = jnp.stack([item[1] for item in shard_grads])
    fc2_weight_grad = jnp.stack([item[2].T for item in shard_grads])
    return (
        drop_rows(residual),
        drop_rows(grad_rows),
        small_grads[0],
        small_grads[1],
        qkv_weight_grad,
        small_grads[2],
        bias_table_grad,
        proj_weight_grad,
        fc1_weight_grad,
        fc1_bias_grad,
        fc2_weight_grad,
        small_grads[3],
    )


def solution(mesh):
    placed = (
        P(("dp", "head"), None),
        P(("dp", "head"), None),
        P("dp"),
        P("dp", None),
        P("dp", None),
        P(),
        P(None, None, "dp"),
        P(None, None, "dp"),
        P(None, "dp", None, "head"),
        P(None, None, "dp"),
        P(None, "head", None),
        P(None, "head", "dp"),
        P(None, "dp", "head"),
        P(None, "dp"),
        P(None, "head", "dp"),
        P(None, None, "dp"),
    )
    return jax.shard_map(
        shards,
        mesh=mesh,
        in_specs=placed,
        out_specs=(
            P(("dp", "head"), None),
            P(("dp", "head"), None),
            P(None, None, "dp"),
            P(None, None, "dp"),
            P(None, "dp", None, "head"),
            P(None, None, "dp"),
            P(None, "head", None),
            P(None, "head", "dp"),
            P(None, "dp", "head"),
            P(None, "dp"),
            P(None, "head", "dp"),
            P(None, None, "dp"),
        ),
        check_vma=False,
    )
```

```python
import functools

import jax
import jax.numpy as jnp
from jax import lax
from jax.experimental import pallas as pl
from jax.experimental.pallas import tpu as pltpu
from jax.sharding import PartitionSpec as P

WSIDE = 7
SHIFT = 3
CROP_MAX = 12
BLOCKS = 2
WTOK = 49
PADDED = 56
STORED = 64
PIECES = 4
VMEM_BYTES = 60 * 2**20

EPSILON = 1e-05
MASKED = -100.0
ABSENT = -1e30
BF16 = jnp.bfloat16
F32 = jnp.float32


def cost(micros):
    return pl.CostEstimate(
        flops=int(micros * 5e9), bytes_accessed=int(micros * 2e7), transcendentals=0
    )


def dot(left, right, left_dim=1, right_dim=0):
    return lax.dot_general(
        left, right, (((left_dim,), (right_dim,)), ((), ())), preferred_element_type=F32
    )


def normalize(values):
    centred = values - jnp.mean(values, axis=-1, keepdims=True)
    scale = lax.rsqrt(jnp.mean(centred * centred, axis=-1, keepdims=True) + EPSILON)
    return centred * scale, scale


def norm_back_rows(values, gain, error):
    normal, scale = normalize(values)
    flow = error * gain
    grad = (
        flow
        - jnp.mean(flow, axis=-1, keepdims=True)
        - normal * jnp.mean(flow * normal, axis=-1, keepdims=True)
    ) * scale
    return grad, jnp.sum(error * normal, axis=0, keepdims=True), jnp.sum(error, axis=0, keepdims=True)


def spread_heads(values, heads):
    columns = values.shape[1]
    owner = lax.broadcasted_iota(jnp.int32, values.shape, 1) // (columns // heads)
    return jnp.concatenate(
        [jnp.where(owner == head, values, 0.0) for head in range(heads)], axis=0
    ).astype(BF16)


def beside_heads(values, heads):
    rows = values.shape[0] // heads
    return jnp.concatenate([values[h * rows : (h + 1) * rows] for h in range(heads)], axis=1)


def below_heads(values, heads):
    columns = values.shape[1] // heads
    parts = [values[:, h * columns : (h + 1) * columns] for h in range(heads)]
    return jnp.concatenate(parts, axis=0)


def stored_rows(values):
    extra = jnp.zeros((STORED - values.shape[0], values.shape[1]), F32)
    return jnp.concatenate([values, extra], axis=0).astype(BF16)


def merge_heads(values, heads):
    rows = values.shape[0] // heads
    columns = values.shape[1]
    owner = lax.broadcasted_iota(jnp.int32, (rows, columns), 1) // (columns // heads)
    total = values[:rows]
    for head in range(1, heads):
        total = jnp.where(owner == head, values[head * rows : (head + 1) * rows], total)
    return total


class Copies:
    def __init__(self, sems):
        self.sems = sems
        self.used = 0
        self.leaving = []

    def plan(self, source, target):
        copy = pltpu.make_async_copy(source, target, self.sems.at[self.used])
        self.used += 1
        return copy

    def send(self, source, target):
        copy = self.plan(source, target)
        copy.start()
        self.leaving.append(copy)

    def finish(self):
        wait_all(self.leaving)


def start_all(*groups):
    for group in groups:
        for item in group:
            item.start()


def choose(weights, picks):
    plan, arrays, rows, first = weights
    chosen = [index for index, (e, _) in enumerate(plan) if e in picks]
    plan = tuple((picks.index(plan[index][0]), plan[index][1], first) for index in chosen)
    return plan, [arrays[index] for index in chosen], rows


def weight_plans(copies, plan, refs, rows, parts):
    own = lax.axis_index("dp")
    plans = {}
    for (slot, rels, first), ref in zip(plan, refs):
        for place, rel in enumerate(rels):
            start = 0 if rel is None else pl.multiple_of(jnp.bitwise_xor(own, rel) * rows, rows)
            for part, target in enumerate(parts):
                plans.setdefault((part, slot), []).append(
                    copies.plan(
                        ref.at[place, pl.ds(first + part * rows, rows), :],
                        target.at[slot, pl.ds(start, rows), :],
                    )
                )
    return plans


def wait_all(items):
    for item in items:
        item.wait()


def weight_copies(plan, parts):
    return parts * sum(len(rels) for _, rels, _ in plan)


def in_any(count):
    return [pl.BlockSpec(memory_space=pl.ANY)] * count


def in_vmem(count):
    return [pl.BlockSpec(memory_space=pltpu.VMEM)] * count


def like(array):
    return pltpu.VMEM(array.shape, array.dtype)


def call(kernel, name, micros, live, small, arrays, outs, scratch, copies):
    return pl.pallas_call(
        kernel,
        in_specs=[pl.BlockSpec(memory_space=pltpu.SMEM)] + in_vmem(len(small)) + in_any(len(arrays)),
        out_specs=tuple(in_any(len(outs))),
        out_shape=tuple(outs),
        scratch_shapes=list(scratch) + [pltpu.SemaphoreType.DMA((copies,))],
        compiler_params=pltpu.CompilerParams(vmem_limit_bytes=VMEM_BYTES),
        cost_estimate=cost(micros),
        name=name,
    )(live, *small, *arrays)


def row_chunks(rows, body, init):
    chunk = 2 * PADDED

    def step(index, carry):
        return body(pl.ds(pl.multiple_of(index * chunk, chunk), chunk), index, carry)

    return lax.fori_loop(0, rows // chunk, step, init)


def live_rows(live_ref, index):
    place = lax.broadcasted_iota(jnp.int32, (2 * PADDED, 1), 0)
    value = jnp.where(place < PADDED, live_ref[2 * index], live_ref[2 * index + 1])
    return jnp.where(lax.rem(place, PADDED) < WTOK, value, 0.0)


def attention_forward_kernel(heads, scale, picks, plan, block_rows, end, *refs):
    count = len(picks)
    live_ref, vec_ref, qv_ref = refs[:3]
    arrays = refs[3 : 6 + 2 * end]
    x_hbm, bias_hbm, mask_hbm = arrays[:3]
    refs = refs[3 + len(arrays) :]
    weight_refs, refs = refs[: len(plan)], refs[len(plan) :]
    outs, refs = refs[: 5 * count + 2], refs[5 * count + 2 :]
    x, bias, mask, total, normed, normed2, weights, qs, ks, vs, ps, atts, sems = refs
    rows = x.shape[0]
    columns = qs.shape[2]
    pairs = rows // (2 * PADDED)
    copies = Copies(sems)
    weight = weight_plans(copies, plan, weight_refs, block_rows, (weights,))
    later = [weight[0, n] for n in range(1, count)]
    later.append([copies.plan(mask_hbm, mask)])
    later[-1] += [copies.plan(bias_hbm.at[e], bias.at[n]) for n, e in enumerate(picks)]
    x_copy = copies.plan(x_hbm, x)
    if end:
        normed_copy = copies.plan(arrays[3], normed)
        late = [x_copy, copies.plan(arrays[4], total)]
        start_all([normed_copy], weight[0, 0])
        normed_copy.wait()
        start_all(*later)
    else:
        start_all([x_copy], weight[0, 0])
        x_copy.wait()
        start_all(*later)

        def first_norm(span, index, _):
            normal, _ = normalize(x[span, :])
            normed[span, :] = (normal * vec_ref[0:1, :] + vec_ref[1:2, :]).astype(BF16)
            return 0

        row_chunks(rows, first_norm, 0)
        copies.send(normed, outs[-1])
    for n, e in enumerate(picks):
        wait_all(weight[0, n])
        qkv = dot(normed[...], weights[n, :, : 3 * columns])
        qs[n] = ((qkv[:, :columns] + qv_ref[e, 0:1, :]) * scale).astype(BF16)
        ks[n] = qkv[:, columns : 2 * columns].astype(BF16)
        vs[n] = (qkv[:, 2 * columns :] + qv_ref[e, 1:2, :]).astype(BF16)
        for index, buffer in enumerate((qs, ks, vs)):
            copies.send(buffer.at[n], outs[5 * n + index])
    wait_all(later[-1])
    if end:
        start_all(late)

    def pair_step(pair, _):
        span = pl.ds(pl.multiple_of(pair * 2 * PADDED, 2 * PADDED), 2 * PADDED)
        for n in range(count):
            query = qs[n, span, :].astype(F32)
            key = ks[n, span, :].astype(F32)
            value = vs[n, span, :].astype(F32)
            results = []
            for side in range(2):
                part = slice(side * PADDED, (side + 1) * PADDED)
                keys = spread_heads(key[part], heads)
                scores = dot(keys, query[part].astype(BF16), 1, 1) + bias[n]
                scores = scores.reshape(heads, PADDED, PADDED) + mask[2 * pair + side][None]
                expo = jnp.exp(scores - jnp.max(scores, axis=1, keepdims=True))
                probs = expo * (1.0 / jnp.sum(expo, axis=1, keepdims=True))
                probs = probs.reshape(heads * PADDED, PADDED)
                ps[n, 2 * pair + side] = stored_rows(beside_heads(probs, heads))
                values = spread_heads(value[part], heads)
                results.append(dot(probs.astype(BF16), values, 0, 0))
            atts[n, span, :] = jnp.concatenate(results, axis=0).astype(BF16)
        return 0

    lax.fori_loop(0, pairs, pair_step, 0)
    for n in range(count):
        copies.send(ps.at[n], outs[5 * n + 3])
        copies.send(atts.at[n], outs[5 * n + 4])
    if end:
        wait_all(late)
    branch = total[...] if end else None
    for n in range(count):
        part = dot(atts[n], weights[n, :, 3 * columns :], 1, 1)
        branch = part if branch is None else branch + part
    total[...] = branch
    if end:

        def second_norm(span, index, _):
            live = live_rows(live_ref, index)
            mixed = x[span, :] + live * (total[span, :] + vec_ref[2:3, :])
            total[span, :] = mixed
            normal, _ = normalize(mixed)
            normed2[span, :] = (normal * vec_ref[3:4, :] + vec_ref[4:5, :]).astype(BF16)
            return 0

        row_chunks(rows, second_norm, 0)
        copies.send(normed2, outs[-1])
    copies.send(total, outs[-2])
    copies.finish()


def attention_forward(
    x, weights, picks, vectors, qv, bias, mask, live, heads, scale, earlier=()
):
    rows, width = x.shape
    columns = qv.shape[2]
    wins = rows // PADDED
    plan, arrays, block_rows = choose(weights, picks)
    count = len(picks)
    end = bool(earlier)
    shape = jax.ShapeDtypeStruct
    piece = shape((rows, columns), BF16)
    probs = shape((wins, STORED, heads * PADDED), BF16)
    results = call(
        functools.partial(attention_forward_kernel, heads, scale, picks, plan, block_rows, end),
        "attention_forward",
        4 + 5 * count,
        live,
        (vectors, qv),
        [x, bias, mask] + list(earlier) + arrays,
        [piece, piece, piece, probs, piece] * count
        + [shape((rows, width), F32), shape((rows, width), BF16)],
        [
            like(x),
            pltpu.VMEM((count,) + bias.shape[1:], F32),
            like(mask),
            pltpu.VMEM((rows, width), F32),
            pltpu.VMEM((rows, width), BF16),
            pltpu.VMEM((rows, width), BF16),
            pltpu.VMEM((count, width, width), BF16),
        ]
        + [pltpu.VMEM((count, rows, columns), BF16)] * 3
        + [
            pltpu.VMEM((count,) + probs.shape, BF16),
            pltpu.VMEM((count, rows, columns), BF16),
        ],
        weight_copies(plan, 1) + 6 * count + 8,
    )
    saved = {e: results[5 * n : 5 * n + 5] for n, e in enumerate(picks)}
    return saved, results[-2], results[-1]


def ffn_forward_kernel(picks, plan, block_rows, end, *refs):
    count = len(picks)
    live_ref, bias_ref, vec_ref = refs[:3]
    arrays, refs = refs[3 : 4 + end], refs[4 + end :]
    weight_refs, refs = refs[: len(plan)], refs[len(plan) :]
    outs, refs = refs[: 2 * count + 1], refs[2 * count + 1 :]
    normed2, mixed, earlier, total, first, second, hidden, slope, sems = refs
    rows = normed2.shape[0]
    copies = Copies(sems)
    arrived = copies.plan(arrays[0], normed2)
    weight = weight_plans(copies, plan, weight_refs, block_rows, (first, second))
    late = [copies.plan(one, to) for one, to in zip(arrays[1:], (mixed, earlier))]
    start_all([arrived], weight[0, 0])
    arrived.wait()
    start_all(weight[1, 0])
    for n, e in enumerate(picks):
        wait_all(weight[0, n])
        if n + 1 < count:
            start_all(weight[0, n + 1], weight[1, n + 1])
        else:
            start_all(late)
        before = dot(normed2[...], first[n]) + bias_ref[e]
        cdf = 0.5 * (1.0 + lax.erf(before * (0.5**0.5)))
        density = jnp.exp(-0.5 * before * before) * 0.3989422804014327
        hidden[n] = (before * cdf).astype(BF16)
        copies.send(hidden.at[n], outs[2 * n])
        slope[n] = (cdf + before * density).astype(BF16)
        copies.send(slope.at[n], outs[2 * n + 1])
        wait_all(weight[1, n])
        part = dot(hidden[n], second[n], 1, 1)
        if n == 0:
            total[...] = part
        else:
            total[...] += part
    wait_all(late)
    if end:

        def finish(span, index, _):
            live = live_rows(live_ref, index)
            value = total[span, :] + vec_ref[5:6, :]
            if end == 2:
                value = value + earlier[span, :]
            total[span, :] = mixed[span, :] + live * value
            return 0

        row_chunks(rows, finish, 0)
    copies.send(total, outs[-1])
    copies.finish()


def ffn_forward(normed2, weights, picks, bias, vectors, live, earlier=()):
    rows, width = normed2.shape
    plan, arrays, block_rows = choose(weights, picks)
    count = len(picks)
    end = len(earlier)
    shape = jax.ShapeDtypeStruct
    piece = shape((rows, width), BF16)
    results = call(
        functools.partial(ffn_forward_kernel, picks, plan, block_rows, end),
        "ffn_forward",
        4 * count,
        live,
        (bias, vectors),
        [normed2] + list(earlier) + arrays,
        [piece, piece] * count + [shape((rows, width), F32)],
        [
            like(normed2),
            pltpu.VMEM((rows, width), F32),
            pltpu.VMEM((rows, width), F32),
            pltpu.VMEM((rows, width), F32),
        ]
        + [pltpu.VMEM((count, width, width), BF16)] * 2
        + [pltpu.VMEM((count, rows, width), BF16)] * 2,
        weight_copies(plan, 2) + 2 * count + 5,
    )
    return {e: results[2 * n : 2 * n + 2] for n, e in enumerate(picks)}, results[-1]


def fill_transposed(target, source, block_rows, tiled):
    flipped = source[...].T
    if not tiled:
        target[...] = flipped
        return
    own = lax.axis_index("dp")
    for block in range(flipped.shape[0] // block_rows):
        start = pl.multiple_of(jnp.bitwise_xor(own, block) * block_rows, block_rows)
        target[pl.ds(start, block_rows), :] = flipped[
            block * block_rows : (block + 1) * block_rows
        ]


def put_blocks(buffer, cuts, block_rows, part, value):
    order = [rel for _, _, rels in cuts for rel in rels]
    for place, rel in enumerate(order):
        start = 0 if rel is None else rel * block_rows
        buffer[place, part * block_rows : (part + 1) * block_rows, :] = value[
            start : start + block_rows
        ].astype(BF16)


def send_blocks(copies, buffer, cuts, block_rows, part, outs):
    place = 0
    rows = pl.ds(part * block_rows, block_rows)
    for index, start, rels in cuts:
        copies.send(
            buffer.at[pl.ds(place, len(rels)), rows, :],
            outs[index].at[pl.ds(start, len(rels)), rows, :],
        )
        place += len(rels)


def block_outs(layout, height, width):
    return [jax.ShapeDtypeStruct((size, height, width), BF16) for size in layout[0]]


def ffn_backward_kernel(picks, plan, block_rows, layout, begin, end, *refs):
    count = len(picks)
    sizes, cuts = layout
    tiled = cuts[0][0][2][0] is not None
    live_ref, vec_ref = refs[:2]
    given = 2 * count + 2 + end + 2 * (not begin)
    arrays, refs = refs[2 : 2 + given], refs[2 + given :]
    weight_refs, refs = refs[: len(plan)], refs[len(plan) :]
    outs, refs = refs[: 5 + len(sizes)], refs[5 + len(sizes) :]
    (
        grad, mixed, branch, error, error_here, attn_grad, normed2, slopes, hiddens, pres, first,
        second, normed2_t, branch_t, results, sums, hidden_sums, sems,
    ) = refs
    rows, width = grad.shape
    blocks_out = outs[5:]
    copies = Copies(sems)
    zero = jnp.zeros((1, width), F32)
    weight = weight_plans(copies, plan, weight_refs, block_rows, (first, second))
    grad_copy = copies.plan(arrays[0], grad)
    slope = [copies.plan(one, slopes.at[n]) for n, one in enumerate(arrays[1 : 1 + count])]
    hidden_hbm = arrays[1 + count : 1 + 2 * count]
    hidden = [copies.plan(one, hiddens.at[n]) for n, one in enumerate(hidden_hbm)]
    normed2_copy = copies.plan(arrays[1 + 2 * count], normed2)
    more = list(arrays[2 + 2 * count :])
    late = [copies.plan(more.pop(0), mixed)] if end else []
    if begin:
        arrived = grad_copy
    else:
        arrived = copies.plan(more[0], branch)
        late += [copies.plan(more[1], error), grad_copy]
    start_all([arrived], weight[1, 0], [slope[0]])
    arrived.wait()
    start_all(weight[0, 0], weight[1, 1], [slope[1]])
    if begin:

        def start(span, index, total):
            part = (live_rows(live_ref, index) * grad[span, :]).astype(BF16)
            branch[span, :] = part
            return total + jnp.sum(part.astype(F32), axis=0, keepdims=True)

        sums[3:4, :] = row_chunks(rows, start, zero)
        if not end:
            copies.send(branch, outs[2])
    fill_transposed(branch_t, branch, block_rows, tiled)
    for n, e in enumerate(picks):
        wait_all(weight[1, n])
        flow = dot(branch[...], second[n])
        slope[n].wait()
        pre = (slopes[n].astype(F32) * flow).astype(BF16)
        pres[n] = pre
        if n + 1 < count:
            start_all(weight[0, n + 1])
            if n + 2 < count:
                start_all(weight[1, n + 2], [slope[n + 2]])
        else:
            start_all([normed2_copy, hidden[0]], late)
        hidden_sums[n] = jnp.sum(pre.astype(F32), axis=0, keepdims=True)
        wait_all(weight[0, n])
        part = dot(pres[n], first[n], 1, 1)
        if n == 0:
            error_here[...] = part
        else:
            error_here[...] += part
    wait_all(late)
    if end:

        def finish(span, index, totals):
            if not begin:
                error_here[span, :] += error[span, :]
            back, gain_part, shift_part = norm_back_rows(
                mixed[span, :], vec_ref[3:4, :], error_here[span, :]
            )
            mixed_grad = grad[span, :] + back
            error_here[span, :] = mixed_grad
            low = (live_rows(live_ref, index) * mixed_grad).astype(BF16)
            attn_grad[span, :] = low
            bias_part = jnp.sum(low.astype(F32), axis=0, keepdims=True)
            return tuple(a + b for a, b in zip(totals, (gain_part, shift_part, bias_part)))

        totals = row_chunks(rows, finish, (zero, zero, zero))
        for index in range(3):
            sums[index : index + 1, :] = totals[index]
        copies.send(attn_grad, outs[1])
    copies.send(error_here, outs[0])
    copies.send(sums, outs[3])
    copies.send(hidden_sums, outs[4])
    normed2_copy.wait()
    fill_transposed(normed2_t, normed2, block_rows, tiled)
    for n in range(count):
        if n + 1 < count:
            hidden[n + 1].start()
        put_blocks(results.at[n], cuts[n], block_rows, 0, dot(normed2_t[...], pres[n]))
        send_blocks(copies, results.at[n], cuts[n], block_rows, 0, blocks_out)
        hidden[n].wait()
        put_blocks(results.at[n], cuts[n], block_rows, 1, dot(branch_t[...], hiddens[n]))
        send_blocks(copies, results.at[n], cuts[n], block_rows, 1, blocks_out)
    copies.finish()


def ffn_backward(
    grad, hidden, normed2, weights, picks, layout, vectors, live, mixed=None, earlier=()
):
    rows, width = grad.shape
    plan, arrays, block_rows = choose(weights, picks)
    count = len(picks)
    end = mixed is not None
    shape = jax.ShapeDtypeStruct
    low = shape((rows, width), BF16)
    wide = shape((rows, width), F32)
    tiny = shape((8, width), F32)
    blocks = block_outs(layout, 2 * block_rows, width)
    results = call(
        functools.partial(
            ffn_backward_kernel, picks, plan, block_rows, layout, not earlier, end
        ),
        "ffn_backward",
        7 * count,
        live,
        (vectors,),
        [grad]
        + [hidden[e][1] for e in picks]
        + [hidden[e][0] for e in picks]
        + [normed2]
        + [mixed] * end
        + list(earlier)
        + arrays,
        [wide, low if end else tiny, tiny if end else low, tiny, shape((count, 1, width), F32)]
        + blocks,
        [like(wide), like(wide), like(low), like(wide), like(wide), like(low), like(low)]
        + [pltpu.VMEM((count, rows, width), BF16)] * 3
        + [pltpu.VMEM((count, width, width), BF16)] * 2
        + [pltpu.VMEM((width, rows), BF16)] * 2
        + [pltpu.VMEM((count, width // block_rows, 2 * block_rows, width), BF16)]
        + [pltpu.VMEM((8, width), F32), pltpu.VMEM((count, 1, width), F32)],
        weight_copies(plan, 2) + 2 * count + 9 + 4 * len(blocks) + 4,
    )
    return *results[:5], results[5:]


def ffn_both_kernel(picks, plan, block_rows, layout, *refs):
    count = len(picks)
    sizes, cuts = layout
    tiled = cuts[0][0][2][0] is not None
    live_ref, bias_ref, vec_ref = refs[:3]
    normed2_hbm, mixed_hbm, grad_hbm = refs[3:6]
    refs = refs[6:]
    weight_refs, refs = refs[: len(plan)], refs[len(plan) :]
    outs, refs = refs[:5], refs[5:]
    blocks_out, refs = refs[: len(sizes)], refs[len(sizes) :]
    (
        normed2, mixed, grad, total, error, branch, attn_grad, hiddens, pres, first, second,
        normed2_t, branch_t, results, sums, hidden_sums, sems,
    ) = refs
    rows, width = grad.shape
    copies = Copies(sems)
    zero = jnp.zeros((1, width), F32)
    weight = weight_plans(copies, plan, weight_refs, block_rows, (first, second))
    grad_copy = copies.plan(grad_hbm, grad)
    normed2_copy = copies.plan(normed2_hbm, normed2)
    mixed_copy = copies.plan(mixed_hbm, mixed)
    start_all([normed2_copy], weight[0, 0])
    normed2_copy.wait()
    start_all([grad_copy], weight[1, 0])
    fill_transposed(normed2_t, normed2, block_rows, tiled)
    for n, e in enumerate(picks):
        wait_all(weight[0, n])
        before = dot(normed2[...], first[n]) + bias_ref[e]
        if n + 1 < count:
            start_all(weight[0, n + 1], weight[1, n + 1])
        else:
            start_all([mixed_copy])
        cdf = 0.5 * (1.0 + lax.erf(before * (0.5**0.5)))
        density = jnp.exp(-0.5 * before * before) * 0.3989422804014327
        hiddens[n] = (before * cdf).astype(BF16)
        slope = cdf + before * density
        if n == 0:
            grad_copy.wait()

            def start(span, index, carry):
                part = (live_rows(live_ref, index) * grad[span, :]).astype(BF16)
                branch[span, :] = part
                return carry + jnp.sum(part.astype(F32), axis=0, keepdims=True)

            sums[3:4, :] = row_chunks(rows, start, zero)
            fill_transposed(branch_t, branch, block_rows, tiled)
        wait_all(weight[1, n])
        pre = (slope * dot(branch[...], second[n])).astype(BF16)
        pres[n] = pre
        hidden_sums[n] = jnp.sum(pre.astype(F32), axis=0, keepdims=True)
        part = dot(hiddens[n], second[n], 1, 1)
        back = dot(pres[n], first[n], 1, 1)
        if n == 0:
            total[...] = part
            error[...] = back
        else:
            total[...] += part
            error[...] += back
    mixed_copy.wait()

    def finish(span, index, totals):
        live = live_rows(live_ref, index)
        values = mixed[span, :]
        total[span, :] = values + live * (total[span, :] + vec_ref[5:6, :])
        back, gain_part, shift_part = norm_back_rows(values, vec_ref[3:4, :], error[span, :])
        mixed_grad = grad[span, :] + back
        error[span, :] = mixed_grad
        low = (live * mixed_grad).astype(BF16)
        attn_grad[span, :] = low
        bias_part = jnp.sum(low.astype(F32), axis=0, keepdims=True)
        return tuple(a + b for a, b in zip(totals, (gain_part, shift_part, bias_part)))

    totals = row_chunks(rows, finish, (zero, zero, zero))
    for index in range(3):
        sums[index : index + 1, :] = totals[index]
    for buffer, out in zip((total, error, attn_grad, sums, hidden_sums), outs):
        copies.send(buffer, out)
    for n in range(count):
        put_blocks(results.at[n], cuts[n], block_rows, 0, dot(normed2_t[...], pres[n]))
        send_blocks(copies, results.at[n], cuts[n], block_rows, 0, blocks_out)
        put_blocks(results.at[n], cuts[n], block_rows, 1, dot(branch_t[...], hiddens[n]))
        send_blocks(copies, results.at[n], cuts[n], block_rows, 1, blocks_out)
    copies.finish()


def ffn_both(normed2, mixed, grad, weights, picks, layout, bias, vectors, live):
    rows, width = grad.shape
    plan, arrays, block_rows = choose(weights, picks)
    count = len(picks)
    shape = jax.ShapeDtypeStruct
    low = shape((rows, width), BF16)
    wide = shape((rows, width), F32)
    blocks = block_outs(layout, 2 * block_rows, width)
    results = call(
        functools.partial(ffn_both_kernel, picks, plan, block_rows, layout),
        "ffn_both",
        30,
        live,
        (bias, vectors),
        [normed2, mixed, grad] + arrays,
        [wide, wide, low, shape((8, width), F32), shape((count, 1, width), F32)] + blocks,
        [like(low), like(wide), like(wide), like(wide), like(wide), like(low), like(low)]
        + [pltpu.VMEM((count, rows, width), BF16)] * 2
        + [pltpu.VMEM((count, width, width), BF16)] * 2
        + [pltpu.VMEM((width, rows), BF16)] * 2
        + [pltpu.VMEM((count, width // block_rows, 2 * block_rows, width), BF16)]
        + [pltpu.VMEM((8, width), F32), pltpu.VMEM((count, 1, width), F32)],
        weight_copies(plan, 2) + 8 + 4 * len(blocks) + 4,
    )
    return *results[:5], results[5:]


def attention_backward_kernel(heads, scale, picks, plan, block_rows, layout, end, *refs):
    count = len(picks)
    sizes, cuts = layout
    tiled = cuts[0][0][2][0] is not None
    live_ref, vec_ref = refs[:2]
    given = 2 + 5 * count + 3 * end
    arrays, refs = refs[2 : 2 + given], refs[2 + given :]
    weight_refs, refs = refs[: len(plan)], refs[len(plan) :]
    outs_count = 3 + end + len(sizes)
    outs, refs = refs[:outs_count], refs[outs_count:]
    (
        attn_grad, normed, x, mixed_grad, error, weights, qs, ks, vs, atts, ps, gs, grads,
        normed_t, attn_grad_t, results, scores_sum, scores_out, sums, small, sems,
    ) = refs
    rows, width = attn_grad.shape
    columns = qs.shape[2]
    pairs = rows // (2 * PADDED)
    copies = Copies(sems)
    weight = weight_plans(copies, plan, weight_refs, block_rows, (weights,))
    arrived = copies.plan(arrays[0], attn_grad)
    saved = [
        copies.plan(arrays[2 + 5 * n + index], buffer.at[n])
        for n in range(count)
        for index, buffer in ((0, qs), (1, ks), (2, vs), (3, ps))
    ]
    late = [copies.plan(arrays[1], normed)]
    for n in range(count):
        late.append(copies.plan(arrays[2 + 5 * n + 4], atts.at[n]))
    if end:
        for one, to in zip(arrays[2 + 5 * count :], (x, mixed_grad, error)):
            late.append(copies.plan(one, to))
    start_all([arrived], weight[0, 0])
    arrived.wait()
    start_all(*[weight[0, n] for n in range(1, count)], saved)
    scores_sum[...] = jnp.zeros(scores_sum.shape, F32)
    fill_transposed(attn_grad_t, attn_grad, block_rows, tiled)
    for n in range(count):
        wait_all(weight[0, n])
        gs[n] = dot(attn_grad[...], weights[n, :, 3 * columns :]).astype(BF16)
    wait_all(saved)
    start_all(late)

    def pair_step(pair, _):
        span = pl.ds(pl.multiple_of(pair * 2 * PADDED, 2 * PADDED), 2 * PADDED)
        for n in range(count):
            query, key, value, grad = [
                buffer[n, span, :].astype(F32) for buffer in (qs, ks, vs, gs)
            ]
            rows_out = []
            for side in range(2):
                part = slice(side * PADDED, (side + 1) * PADDED)
                queries = spread_heads(query[part], heads)
                grads_out = spread_heads(grad[part], heads)
                probs = ps[n, 2 * pair + side].astype(F32)[:PADDED]
                flow = dot(value[part].astype(BF16), grads_out, 1, 1)
                inner = jnp.sum(probs * flow, axis=0, keepdims=True)
                score = (probs * (flow - inner)).astype(BF16)
                scores_sum[n] += score.astype(F32)
                query_part = dot(score, key[part].astype(BF16), 0, 0)
                rows_out.append(
                    jnp.concatenate(
                        [
                            merge_heads(query_part, heads) * scale,
                            dot(score, queries),
                            dot(probs.astype(BF16), grads_out),
                        ],
                        axis=1,
                    )
                )
            grads[n, span, :] = jnp.concatenate(rows_out, axis=0).astype(BF16)
        return 0

    lax.fori_loop(0, pairs, pair_step, 0)
    for n in range(count):
        scores_out[n] = below_heads(scores_sum[n], heads)
    copies.send(scores_out, outs[1])
    wait_all(late)
    for n in range(count):
        sums[n] = jnp.sum(grads[n].astype(F32), axis=0, keepdims=True)
        part = dot(grads[n], weights[n, :, : 3 * columns], 1, 1)
        if n == 0 and not end:
            error[...] = part
        else:
            error[...] += part
    copies.send(sums, outs[2])
    if end:
        zero = jnp.zeros((1, width), F32)

        def finish(span, index, totals):
            back, gain_part, shift_part = norm_back_rows(
                x[span, :], vec_ref[0:1, :], error[span, :]
            )
            error[span, :] = mixed_grad[span, :] + back
            return totals[0] + gain_part, totals[1] + shift_part

        totals = row_chunks(rows, finish, (zero, zero))
        for index in range(2):
            small[index : index + 1, :] = totals[index]
        copies.send(small, outs[3])
    copies.send(error, outs[0])
    fill_transposed(normed_t, normed, block_rows, tiled)
    for n in range(count):
        value = jnp.concatenate(
            [dot(normed_t[...], grads[n]), dot(attn_grad_t[...], atts[n])], axis=1
        )
        put_blocks(results.at[n], cuts[n], block_rows, 0, value)
        send_blocks(copies, results.at[n], cuts[n], block_rows, 0, outs[3 + end :])
    copies.finish()


def attention_backward(
    attn_grad, normed, saved, weights, picks, layout, vectors, live, heads, scale, earlier=()
):
    rows, width = attn_grad.shape
    columns = saved[picks[0]][0].shape[1]
    plan, arrays, block_rows = choose(weights, picks)
    count = len(picks)
    end = bool(earlier)
    probs = saved[picks[0]][3]
    shape = jax.ShapeDtypeStruct
    wide = shape((rows, width), F32)
    pieces = [item for e in picks for item in saved[e]]
    outs = [
        wide,
        shape((count, heads * PADDED, PADDED), F32),
        shape((count, 1, 3 * columns), F32),
    ]
    blocks = block_outs(layout, block_rows, width)
    results = call(
        functools.partial(
            attention_backward_kernel, heads, scale, picks, plan, block_rows, layout, end
        ),
        "attention_backward",
        19,
        live,
        (vectors,),
        [attn_grad, normed] + pieces + list(earlier) + arrays,
        outs + [shape((8, width), F32)] * end + blocks,
        [like(attn_grad), like(normed), like(wide), like(wide), like(wide)]
        + [pltpu.VMEM((count, width, width), BF16)]
        + [pltpu.VMEM((count, rows, columns), BF16)] * 4
        + [pltpu.VMEM((count,) + probs.shape, BF16)]
        + [pltpu.VMEM((count, rows, columns), BF16)]
        + [pltpu.VMEM((count, rows, 3 * columns), BF16)]
        + [pltpu.VMEM((width, rows), BF16)] * 2
        + [pltpu.VMEM((count, width // block_rows, block_rows, width), BF16)]
        + [pltpu.VMEM((count, PADDED, heads * PADDED), F32), like(outs[1]), like(outs[2])]
        + [pltpu.VMEM((8, width), F32)],
        weight_copies(plan, 1) + 5 * count + 11 + 4 * len(blocks),
    )
    return *results[: 3 + end], results[3 + end :]


def swap(values, axis, bit):
    size = lax.axis_size(axis)
    return lax.ppermute(values, axis, [(i, i ^ (1 << bit)) for i in range(size)])


def bits_in(axis):
    return lax.axis_size(axis).bit_length() - 1


def pick(values, index, dim):
    return lax.dynamic_index_in_dim(values, index, dim, keepdims=False)


def tie(values, token):
    if token is None:
        return values
    return lax.optimization_barrier((values, token))[0]


def whole_tiles(rows):
    return rows % 16 == 0


def in_order(values):
    index = jnp.bitwise_xor(jnp.arange(values.shape[0]), lax.axis_index("dp"))
    return jnp.take(values, index, axis=0)


def relatives(halves):
    count = lax.axis_size("dp")
    size = count // halves
    return [
        [tuple(range(part * size + side, (part + 1) * size, 2)) for part in range(halves)]
        for side in range(2)
    ]


def line_bits():
    return list(range(1, bits_in("dp")))


def straight(values):
    size = lax.axis_size("dp")
    low, high = [1 << bit for bit in line_bits()[-2:]]
    return [
        lax.ppermute(values(n), "dp", [(i, i ^ shift) for i in range(size)])
        for n, shift in ((1, low), (2, high), (3, low | high))
    ]


class Gather:
    def __init__(self, shard, parts, rows, ways):
        self.shard = shard
        self.parts = parts
        self.rows = rows
        self.ways = ways
        self.entries = []

    def line(self, after=None, at_once=False):
        held = tie(self.shard, after)[None]
        bits = line_bits()
        for bit in bits[:-2]:
            held = jnp.concatenate([held, swap(held, "dp", bit)])
        self.moved = straight(lambda n: held) if at_once else [swap(held, "dp", bits[-2])]
        self.held = [held]

    def line_end(self, until=None):
        moved = tie(self.moved, until)
        self.held = [jnp.concatenate(self.held + moved)]
        return self.held[0]

    def last(self, after=None):
        self.moved = swap(tie(self.held[0], after), "dp", line_bits()[-1])

    def last_end(self, until=None):
        moved = tie(self.moved, until)
        self.held.append(moved)
        if len(self.ways) == 1:
            self.held = [jnp.concatenate(self.held)]
        return self.held[-1]

    def sides(self, part, after=None):
        if part == 0:
            self.side, self.far = [], []
        held = tie(self.held[part], after)
        self.side.append(swap(held, "dp", 0))
        self.far.append(swap(held, "head", 1))

    def sides_end(self, part, until=None):
        self.side[part], self.far[part] = tie((self.side[part], self.far[part]), until)
        return self.side[part], self.far[part]

    def corner(self, part, after=None):
        if part == 0:
            self.corners = []
        if self.ways[part] == "x":
            self.corners.append(swap(tie(self.side[part], after), "head", 1))
        else:
            self.corners.append(swap(tie(self.far[part], after), "dp", 0))

    def corner_end(self, part, until=None):
        self.corners[part] = tie(self.corners[part], until)
        return self.corners[part]

    def core(self, kind, part=None):
        own, other = relatives(len(self.ways))
        arrays, e, rels = {
            "held": (self.held, 0, own),
            "side": (self.side, 0, other),
            "far": (self.far, 2, own),
            "corner": (getattr(self, "corners", None), 2, other),
        }[kind]
        for n, (one, several) in enumerate(zip(arrays, rels)):
            if part is None or part == n:
                self.entries.append((e, one, several))
                self.entries.append((e + 1, swap(one, "head", 0), several))

    def result(self, first=0):
        rows, parts = self.rows, self.parts
        width = self.shard.shape[1]
        if whole_tiles(rows):
            plan = tuple((e, rels) for e, _, rels in self.entries)
            return plan, [one for _, one, _ in self.entries], rows, first * rows
        arrays = []
        plan = []
        for e in range(PIECES):
            mine = [(one, rels) for piece, one, rels in self.entries if piece == e]
            if not mine:
                continue
            order = sum((rels for _, rels in mine), ())
            if len(order) < lax.axis_size("dp"):
                continue
            blocks = jnp.concatenate([one[:, : parts * rows] for one, _ in mine])
            blocks = in_order(blocks[jnp.argsort(jnp.array(order))])
            blocks = blocks.reshape(-1, parts, rows, width).transpose(1, 0, 2, 3)
            arrays.append(blocks.reshape(1, -1, width))
            plan.append((e, (None,)))
        rows = arrays[0].shape[1] // parts
        return tuple(plan), arrays, rows, first * rows


def wide(*values):
    total = values[0].astype(F32)
    for value in values[1:]:
        total = total + value.astype(F32)
    return total


def plus(*values):
    return wide(*values).astype(BF16)


class Scatter:
    def __init__(self, parts, rows, ways):
        self.parts = parts
        self.rows = rows
        self.ways = ways
        self.tiled = whole_tiles(rows)
        blocks = lax.axis_size("dp")
        half = blocks // 2
        even = tuple(range(0, blocks, 2))
        odd = tuple(range(1, blocks, 2))
        cut = half // len(ways)
        corners = [odd[n * cut : (n + 1) * cut] for n in range(len(ways))]
        self.order = even + odd
        if self.tiled:
            self.away_layout = (
                (2 * blocks,),
                (((0, 0, self.order),), ((0, blocks, self.order),)),
            )
            last = tuple((3 + n, 0, rels) for n, rels in enumerate(corners))
            self.near_layout = (
                (half,) * 3 + (cut,) * len(ways),
                (((0, 0, even), (1, 0, odd)), ((2, 0, even),) + last),
            )
        else:
            one = ((0, 0, (None,)),)
            two = ((0, 1, (None,)),)
            self.away_layout = self.near_layout = ((2,), (one, two))

    def both_layouts(self):
        sizes, cuts = self.near_layout
        first = len(self.away_layout[0])
        moved = tuple(
            tuple((first + index, start, rels) for index, start, rels in one) for one in cuts
        )
        return self.away_layout[0] + sizes, self.away_layout[1] + moved

    def arrange(self, outs):
        one = outs[0].reshape(2, self.parts, -1, self.rows, outs[0].shape[-1])
        one = one.transpose(0, 2, 1, 3, 4)
        one = one.reshape(one.shape[:2] + (-1, one.shape[-1]))
        return jnp.concatenate([in_order(item)[jnp.array(self.order)] for item in one])

    def away(self, outs):
        self.moved = swap(outs[0] if self.tiled else self.arrange(outs), "head", 0)

    def near(self, outs, until=None):
        moved = tie(self.moved, until)
        half = moved.shape[0] // 4
        if self.tiled:
            own = list(outs)
        else:
            one = self.arrange(outs)
            own = [one[n * half : (n + 1) * half] for n in range(3)]
            cut = half // len(self.ways)
            own += [one[3 * half + n * cut :][:cut] for n in range(len(self.ways))]
        cut = half // len(self.ways)
        self.held = [own[0], moved[:half]]
        self.side = [own[1], moved[half : 2 * half]]
        self.far = [own[2], moved[2 * half : 3 * half]]
        self.corners = [
            plus(own[3 + n], moved[3 * half + n * cut :][:cut]) for n in range(len(self.ways))
        ]
        return self.corners

    def corner(self, after=None):
        self.moved = []
        for way, one in zip(self.ways, tie(self.corners, after)):
            self.moved.append(swap(one, "head", 1) if way == "x" else swap(one, "dp", 0))

    def corner_end(self, until=None):
        moved = tie(self.moved, until)
        half = self.side[0].shape[0]
        for part, (way, one) in enumerate(zip(self.ways, moved)):
            size = one.shape[0]
            around = (part * size, half - (part + 1) * size)
            one = jnp.pad(one, (around,) + ((0, 0),) * 2) if size < half else one
            (self.side if way == "x" else self.far).append(one)
        self.side, self.far = plus(*self.side), plus(*self.far)
        return self.side, self.far

    def sides(self, after=None, part=None):
        side, far = tie((self.side, self.far), after)
        if part is not None:
            size = side.shape[0] // 2
            side, far = [one[part * size : (part + 1) * size] for one in (side, far)]
        self.moved = [swap(side, "dp", 0), swap(far, "head", 1)]

    def sides_end(self, until=None, at_once=False, part=None):
        terms = self.held + list(tie(self.moved, until))
        if part is not None:
            size = terms[-1].shape[0]
            terms[:2] = [one[part * size : (part + 1) * size] for one in terms[:2]]
            if part == 0:
                self.lower = plus(*terms)
                return self.lower
            self.held = [self.lower, plus(*terms)]
            return self.held
        count = 4 if at_once else 2
        size = terms[0].shape[0] // count
        self.held = [
            plus(*[one[n * size : (n + 1) * size] for one in terms]) for n in range(count)
        ]
        return self.held

    def last(self, after=None):
        self.moved = swap(tie(self.held[1], after), "dp", line_bits()[-1])

    def last_end(self, until=None):
        moved = tie(self.moved, until)
        size = moved.shape[0] // 2
        terms = [self.held[0], moved]
        self.held = [plus(*[one[n * size :][:size] for one in terms]) for n in range(2)]
        return self.held

    def line(self, after=None):
        held = tie(self.held, after)
        if len(held) == 4:
            self.moved = straight(lambda n: held[n])
        else:
            self.moved = [swap(held[1], "dp", line_bits()[-2])]

    def line_end(self, until=None):
        held = wide(self.held[0], *tie(self.moved, until))
        for bit in reversed(line_bits()[:-2]):
            cut = held.shape[0] // 2
            moved = swap(held[cut:].astype(BF16), "dp", bit)
            held = wide(held[:cut], moved)
        self.result = held[0]
        return self.result


class SmallSum:
    def __init__(self, values):
        self.total = values
        self.left = [("head", 0), ("head", 1)]
        self.left += [("dp", bit) for bit in range(bits_in("dp"))]
        self.moved = None

    def step(self, until=None):
        self.result(until)
        axis, bit = self.left.pop(0)
        self.moved = swap(self.total, axis, bit)

    def end(self):
        return not self.left

    def result(self, until=None):
        if self.moved is not None:
            self.total = self.total + tie(self.moved, until)
        self.moved = None
        return self.total


def unshift(values):
    grid = values.reshape(values.shape[:-1] + (WSIDE, WSIDE))
    return jnp.roll(grid, (SHIFT, SHIFT), axis=(-2, -1)).reshape(values.shape)


def pad_rows(values):
    grid = values.reshape(-1, WTOK, values.shape[1])
    grid = jnp.pad(grid, ((0, 0), (0, PADDED - WTOK), (0, 0)))
    return grid.reshape(-1, values.shape[1])


def drop_rows(values):
    grid = values.reshape(-1, PADDED, values.shape[1])[:, :WTOK]
    return grid.reshape(-1, values.shape[1])


def attention_mask(pad, region):
    allowed = (pad[:, :, None] == 1) & (region[:, :, None] == region[:, None, :])
    mask = jnp.where(allowed, 0.0, MASKED).astype(F32)
    extra = PADDED - WTOK
    mask = jnp.pad(mask, ((0, 0), (0, 0), (0, extra)))
    return jnp.pad(mask, ((0, 0), (0, extra), (0, 0)), constant_values=ABSENT)


def shards(
    tokens,
    cotangent,
    crop_counts,
    pad_mask,
    region_ids,
    rel_index,
    norm_gain,
    norm_shift,
    qkv_weight,
    qv_bias,
    bias_table,
    proj_weight,
    fc1_weight,
    fc1_bias,
    fc2_weight,
    out_bias,
):
    rows = tokens.shape[0]
    width = tokens.shape[1]
    wins = rows // WTOK
    local_width = qkv_weight.shape[3]
    local_heads = bias_table.shape[1]
    rel_count = bias_table.shape[2]
    dp_width = norm_gain.shape[2]
    dp_hidden = fc1_bias.shape[1]
    pieces = lax.axis_size("head")
    heads_total = local_heads * pieces
    head_dim = local_width // local_heads
    scale = head_dim ** (-0.5)
    head_index = lax.axis_index("head")
    dp_index = lax.axis_index("dp")
    relative = [head_index ^ e for e in range(pieces)]

    shard_rows = qkv_weight.shape[1]
    attn_shards = [
        jnp.concatenate(
            [qkv_weight[block].reshape(-1, 3 * local_width), proj_weight[block].T], axis=1
        )
        for block in range(BLOCKS)
    ]
    ffn_shards = [
        jnp.concatenate([fc1_weight[block], fc2_weight[block].T]) for block in range(BLOCKS)
    ]
    small = jnp.concatenate([norm_gain, norm_shift, qv_bias, out_bias]).reshape(-1, dp_width)
    small_rows = small.shape[0]
    beside = -(-dp_width // 128) * 128
    small = jnp.pad(small, ((0, 0), (0, width - dp_width)))
    small = small + jnp.pad(
        fc1_bias, ((0, small_rows - BLOCKS), (beside, width - beside - dp_hidden))
    )
    attn_shards[0] = jnp.concatenate([attn_shards[0], small])
    near, away = (0, 2), (1, 3)
    first, second = (0, 1), (2, 3)
    a0 = Gather(attn_shards[0], 1, shard_rows, "y")
    middle = Gather(jnp.concatenate([ffn_shards[0], attn_shards[1]]), 3, shard_rows, "xy")
    f1 = Gather(ffn_shards[1], 2, shard_rows, "xy")

    def attn_weights(block):
        return middle.result(2) if block else a0.result()

    def ffn_weights(block):
        return f1.result() if block else middle.result()

    a0.line(at_once=True)
    far_table = swap(bias_table, "head", 1)
    near_table = swap(bias_table, "head", 0)
    a0.line_end()
    a0.sides(0)
    middle.line(a0.held)
    a0.core("held")
    middle.line_end()
    middle.last()
    a0.sides_end(0)
    a0.core("side")
    a0.core("far")
    a0.corner(0)
    middle.sides(0, a0.far)
    table_pieces = [bias_table, near_table, far_table, swap(far_table, "head", 0)]
    small_all = jnp.stack([a0.held[0][:, shard_rows:], a0.side[0][:, shard_rows:]], axis=1)
    small_all = in_order(small_all.reshape((-1,) + small.shape)).transpose(1, 0, 2).astype(F32)
    every = small_all[:, :, :dp_width].reshape(4, BLOCKS, 2, width)
    gains, shifts, qv_all, out_all = every[0], every[1], every[2], every[3]
    hidden_bias = small_all[:BLOCKS, :, beside : beside + dp_hidden].reshape(BLOCKS, pieces, -1)
    qv_pieces = qv_all.reshape(BLOCKS, 2, pieces, local_width)

    counts = jnp.repeat(crop_counts, CROP_MAX)
    slots = jnp.arange(pad_mask.shape[0], dtype=jnp.int32) % CROP_MAX
    live_all = (slots < counts).astype(F32)
    live_windows = lax.dynamic_slice_in_dim(live_all, head_index * wins, wins, 0)
    live = live_windows
    pad = lax.dynamic_slice_in_dim(pad_mask, head_index * wins, wins, 0)
    region = unshift(lax.dynamic_slice_in_dim(region_ids, head_index * wins, wins, 0))
    masks = (attention_mask(pad, jnp.zeros_like(region)), attention_mask(pad, region))
    extra = PADDED - WTOK
    onehots = []
    for index in (rel_index, unshift(unshift(rel_index).T).T):
        by_key = jnp.pad(index.T, ((0, extra), (0, extra)), constant_values=-1).reshape(1, -1)
        ids = jnp.arange(rel_count, dtype=jnp.int32)[:, None]
        onehots.append((ids == by_key).astype(BF16))

    def ordered(values, dim):
        return jnp.stack([pick(values, rel, dim) for rel in relative])

    block_rows = local_heads * PADDED
    vectors, qv, biases, hidden_biases = [], [], [], []
    for block in range(BLOCKS):
        rows8 = [
            gains[block, 0],
            shifts[block, 0],
            out_all[block, 0],
            gains[block, 1],
            shifts[block, 1],
            out_all[block, 1],
        ]
        vectors.append(jnp.pad(jnp.stack(rows8), ((0, 2), (0, 0))))
        qv.append(ordered(qv_pieces[block], 1))
        table = jnp.concatenate([one[block] for one in table_pieces])
        bias = jnp.dot(table, onehots[block % 2], preferred_element_type=F32)
        biases.append(bias.reshape(pieces, block_rows, PADDED))
        hidden_biases.append(ordered(hidden_bias[block], 0)[:, None, :])

    residual = pad_rows(tokens).astype(F32)

    def attend(block, x, picks, token, earlier=()):
        return attention_forward(
            x,
            attn_weights(block),
            picks,
            tie(vectors[block], token),
            qv[block],
            biases[block],
            masks[block % 2],
            live,
            local_heads,
            scale,
            earlier,
        )

    def feed(block, normed2, picks, token, earlier=()):
        return ffn_forward(
            normed2,
            ffn_weights(block),
            picks,
            hidden_biases[block],
            tie(vectors[block], token),
            live,
            earlier,
        )

    x0 = residual
    grad_rows = pad_rows(cotangent).astype(F32)
    token = (middle.held[0], biases[1], masks[1], grad_rows)
    saved_0, branch, normed_0 = attend(0, x0, first, token)
    a0.corner_end(0, branch)
    a0.core("corner")
    middle.sides_end(0, branch)
    middle.corner(0)
    middle.last_end(branch)
    middle.sides(1)
    f1.line(middle.held[1])
    f1.line_end()
    token = (middle.held[1], f1.held[0])
    more, mixed_0, normed2_0 = attend(0, x0, second, token, (normed_0, branch))
    saved_0.update(more)
    f1.last()
    middle.core("held")
    middle.sides_end(1, mixed_0)
    middle.corner(1)
    middle.core("side")
    middle.core("far")
    middle.corner_end(0, mixed_0)
    middle.corner_end(1, mixed_0)
    middle.core("corner")
    f1.sides(0, middle.corners)
    hidden_0, x1 = feed(0, normed2_0, first + second, middle.corners, (mixed_0,))
    f1.sides_end(0, x1)
    f1.last_end(x1)
    f1.core("held")
    f1.core("side", 0)
    f1.sides(1)
    saved_1, branch, normed_1 = attend(1, x1, first, f1.held)
    f1.sides_end(1, branch)
    f1.corner(0)
    f1.corner(1)
    f1.core("side", 1)
    f1.core("far")
    token = (f1.side, f1.far)
    more, mixed_1, normed2_1 = attend(1, x1, second, token, (normed_1, branch))
    saved_1.update(more)
    f1.corner_end(0, mixed_1)
    f1.corner_end(1, mixed_1)
    f1.core("corner")
    kept = [
        (x0, mixed_0, normed_0, normed2_0, saved_0, hidden_0),
        (x1, mixed_1, normed_1, normed2_1, saved_1, None),
    ]

    def feed_back(block, picks, layout, grad, token, mixed=None, earlier=()):
        _, _, _, normed2, _, hidden = kept[block]
        return ffn_backward(
            grad,
            hidden,
            normed2,
            ffn_weights(block),
            picks,
            layout,
            tie(vectors[block], token),
            live,
            mixed,
            earlier,
        )

    def attend_back(block, picks, layout, attn_grad, token, earlier=()):
        _, _, normed, _, saved, _ = kept[block]
        return attention_backward(
            attn_grad,
            normed,
            saved,
            attn_weights(block),
            picks,
            layout,
            tie(vectors[block], token),
            live,
            local_heads,
            scale,
            earlier,
        )

    def small_terms(block, attn, small_f, hidden_terms):
        scores_a, sums_a, scores_n, sums_n, small_a = attn

        def together(one, other):
            return ordered(jnp.stack([one[0], other[0], one[1], other[1]]), 0)

        table_grad = lax.dot_general(
            together(scores_n, scores_a).reshape(heads_total, -1),
            onehots[block % 2].astype(F32),
            (((1,), (1,)), ((), ())),
            precision=lax.Precision.HIGHEST,
            preferred_element_type=F32,
        )
        table_grad = jnp.pad(table_grad, ((0, 0), (0, table_lanes - rel_count)))
        qv_sums = together(sums_n, sums_a)[:, 0]
        items = [
            small_a[0:1],
            small_f[0:1],
            small_a[1:2],
            small_f[1:2],
            qv_sums[:, :local_width].reshape(1, width),
            qv_sums[:, 2 * local_width :].reshape(1, width),
            small_f[2:4],
            together(*hidden_terms)[:, 0],
            table_grad.reshape(-1, width),
        ]
        return jnp.concatenate(items)

    table_lanes = 2 * 128
    f1_sum, f0_sum = [Scatter(2, shard_rows, "xy") for _ in range(2)]
    a1_sum, a0_sum = [Scatter(1, shard_rows, "xy") for _ in range(2)]
    residual, mixed_grad, attn_grad, small_f, hidden_sums, outs = ffn_both(
        normed2_1,
        mixed_1,
        grad_rows,
        ffn_weights(1),
        away + near,
        f1_sum.both_layouts(),
        hidden_biases[1],
        tie(vectors[1], mixed_1),
        live,
    )
    count = len(f1_sum.away_layout[0])
    f1_sum.away(outs[:count])
    error, scores_a, sums_a, sent = attend_back(1, away, a1_sum.away_layout, attn_grad, None)
    f1_sum.near(outs[count:], error)
    f1_sum.corner()
    a1_sum.away(sent)
    grad_rows, scores_n, sums_n, small_a, outs = attend_back(
        1, near, a1_sum.near_layout, attn_grad, f1_sum.corners, (x1, mixed_grad, error)
    )
    late_terms = (scores_a, sums_a, scores_n, sums_n, small_a), small_f, hidden_sums
    token = f1_sum.corner_end(grad_rows)
    f1_sum.sides(part=0)
    a1_sum.near(outs, grad_rows)
    error, _, branch_grad, small_b, hidden_a, sent = feed_back(
        0, away, f0_sum.away_layout, grad_rows, (token, a1_sum.corners)
    )
    f0_sum.away(sent)
    token = f1_sum.sides_end(error, part=0)
    f1_sum.sides(token, part=1)
    a1_sum.corner(token)
    mixed_grad, attn_grad, _, small_f, hidden_n, outs = feed_back(
        0,
        near,
        f0_sum.near_layout,
        grad_rows,
        (error, token),
        mixed_0,
        (branch_grad, error),
    )
    small_f = jnp.concatenate([small_f[:3], small_b[3:4]])
    token = (f1_sum.sides_end(attn_grad, part=1), a1_sum.corner_end(attn_grad))
    f1_sum.last()
    a1_sum.sides()
    f0_sum.near(outs, attn_grad)
    f0_sum.corner()
    error, scores_a, sums_a, sent = attend_back(
        0, away, a0_sum.away_layout, attn_grad, (token, f0_sum.corners)
    )
    a0_sum.away(sent)
    token = (f0_sum.corner_end(error), a1_sum.sides_end(error), f1_sum.last_end(error))
    f0_sum.sides()
    a1_sum.last()
    f1_sum.line()
    grad_rows, scores_n, sums_n, small_a, outs = attend_back(
        0, near, a0_sum.near_layout, attn_grad, token, (x0, mixed_grad, error)
    )
    f0_sum.sides_end(grad_rows)
    f0_sum.last()
    a1_sum.last_end(grad_rows)
    a0_sum.near(outs, (grad_rows, f0_sum.held, a1_sum.held))
    a0_sum.corner()
    a1_sum.line()
    token = a0_sum.corner_end()
    a0_sum.sides()
    attn_terms = tie((scores_a, sums_a, scores_n, sums_n, small_a), token)
    small_0 = small_terms(0, attn_terms, small_f, (hidden_n, hidden_a))
    attn_terms, small_f, hidden_sums = tie(late_terms, token)
    small_1 = small_terms(1, attn_terms, small_f, (hidden_sums[2:], hidden_sums[:2]))
    small_sum = SmallSum(jnp.stack([small_0, small_1]))
    token = a0_sum.sides_end(at_once=True)
    residual, grad_rows = tie((residual, grad_rows), token)
    f0_sum.last_end(token)
    a0_sum.line((f0_sum.held, small_sum.total))
    f0_sum.line()
    a1_sum.line_end(token)
    f1_sum.line_end(token)
    small_sum.step()
    small_sum.step(token)
    while not small_sum.end():
        small_sum.step()
    a0_sum.line_end()
    f0_sum.line_end()
    shard_grads = [(a0_sum, f0_sum), (a1_sum, f1_sum)]
    shard_grads = [
        (attn.result, ffn.result[:shard_rows], ffn.result[shard_rows:])
        for attn, ffn in shard_grads
    ]

    totals = small_sum.result()

    def own(values):
        return lax.dynamic_slice_in_dim(values, dp_index * dp_width, dp_width, 2)

    small_grads = [own(totals[:, 2 * index : 2 * index + 2]) for index in range(4)]
    hidden_total = totals[:, 8 : 8 + pieces].reshape(BLOCKS, -1)
    fc1_bias_grad = lax.dynamic_slice_in_dim(hidden_total, dp_index * dp_hidden, dp_hidden, 1)
    table_total = totals[:, 8 + pieces :].reshape(BLOCKS, heads_total, table_lanes)
    bias_table_grad = lax.dynamic_slice_in_dim(
        table_total[:, :, :rel_count], head_index * local_heads, local_heads, 1
    )
    qkv_weight_grad = jnp.stack(
        [item[0][:, : 3 * local_width].reshape(-1, 3, local_width) for item in shard_grads]
    )
    proj_weight_grad = jnp.stack([item[0][:, 3 * local_width :].T for item in shard_grads])
    fc1_weight_grad = jnp.stack([item[1] for item in shard_grads])
    fc2_weight_grad = jnp.stack([item[2].T for item in shard_grads])
    return (
        drop_rows(residual),
        drop_rows(grad_rows),
        small_grads[0],
        small_grads[1],
        qkv_weight_grad,
        small_grads[2],
        bias_table_grad,
        proj_weight_grad,
        fc1_weight_grad,
        fc1_bias_grad,
        fc2_weight_grad,
        small_grads[3],
    )


def solution(mesh):
    placed = (
        P(("dp", "head"), None),
        P(("dp", "head"), None),
        P("dp"),
        P("dp", None),
        P("dp", None),
        P(),
        P(None, None, "dp"),
        P(None, None, "dp"),
        P(None, "dp", None, "head"),
        P(None, None, "dp"),
        P(None, "head", None),
        P(None, "head", "dp"),
        P(None, "dp", "head"),
        P(None, "dp"),
        P(None, "head", "dp"),
        P(None, None, "dp"),
    )
    return jax.shard_map(
        shards,
        mesh=mesh,
        in_specs=placed,
        out_specs=(
            P(("dp", "head"), None),
            P(("dp", "head"), None),
            P(None, None, "dp"),
            P(None, None, "dp"),
            P(None, "dp", None, "head"),
            P(None, None, "dp"),
            P(None, "head", None),
            P(None, "head", "dp"),
            P(None, "dp", "head"),
            P(None, "dp"),
            P(None, "head", "dp"),
            P(None, None, "dp"),
        ),
        check_vma=False,
    )
```

```python
import functools

import jax
import jax.numpy as jnp
from jax import lax
from jax.experimental import pallas as pl
from jax.experimental.pallas import tpu as pltpu
from jax.sharding import PartitionSpec as P

WSIDE = 7
SHIFT = 3
CROP_MAX = 12
BLOCKS = 2
WTOK = 49
PADDED = 56
STORED = 64
PIECES = 4
VMEM_BYTES = 60 * 2**20

EPSILON = 1e-05
MASKED = -100.0
ABSENT = -1e30
BF16 = jnp.bfloat16
F32 = jnp.float32


def cost(micros):
    return pl.CostEstimate(
        flops=int(micros * 5e9), bytes_accessed=int(micros * 2e7), transcendentals=0
    )


def dot(left, right, left_dim=1, right_dim=0):
    return lax.dot_general(
        left, right, (((left_dim,), (right_dim,)), ((), ())), preferred_element_type=F32
    )


def normalize(values):
    centred = values - jnp.mean(values, axis=-1, keepdims=True)
    scale = lax.rsqrt(jnp.mean(centred * centred, axis=-1, keepdims=True) + EPSILON)
    return centred * scale, scale


def norm_back_rows(values, gain, error):
    normal, scale = normalize(values)
    flow = error * gain
    grad = (
        flow
        - jnp.mean(flow, axis=-1, keepdims=True)
        - normal * jnp.mean(flow * normal, axis=-1, keepdims=True)
    ) * scale
    return grad, jnp.sum(error * normal, axis=0, keepdims=True), jnp.sum(error, axis=0, keepdims=True)


def spread_heads(values, heads):
    columns = values.shape[1]
    owner = lax.broadcasted_iota(jnp.int32, values.shape, 1) // (columns // heads)
    return jnp.concatenate(
        [jnp.where(owner == head, values, 0.0) for head in range(heads)], axis=0
    ).astype(BF16)


def beside_heads(values, heads):
    rows = values.shape[0] // heads
    return jnp.concatenate([values[h * rows : (h + 1) * rows] for h in range(heads)], axis=1)


def below_heads(values, heads):
    columns = values.shape[1] // heads
    parts = [values[:, h * columns : (h + 1) * columns] for h in range(heads)]
    return jnp.concatenate(parts, axis=0)


def stored_rows(values):
    extra = jnp.zeros((STORED - values.shape[0], values.shape[1]), F32)
    return jnp.concatenate([values, extra], axis=0).astype(BF16)


def merge_heads(values, heads):
    rows = values.shape[0] // heads
    columns = values.shape[1]
    owner = lax.broadcasted_iota(jnp.int32, (rows, columns), 1) // (columns // heads)
    total = values[:rows]
    for head in range(1, heads):
        total = jnp.where(owner == head, values[head * rows : (head + 1) * rows], total)
    return total


class Copies:
    def __init__(self, sems):
        self.sems = sems
        self.used = 0
        self.leaving = []

    def plan(self, source, target):
        copy = pltpu.make_async_copy(source, target, self.sems.at[self.used])
        self.used += 1
        return copy

    def send(self, source, target):
        copy = self.plan(source, target)
        copy.start()
        self.leaving.append(copy)

    def finish(self):
        wait_all(self.leaving)


def start_all(*groups):
    for group in groups:
        for item in group:
            item.start()


def choose(weights, picks):
    plan, arrays, rows, first = weights
    chosen = [index for index, (e, _) in enumerate(plan) if e in picks]
    plan = tuple((picks.index(plan[index][0]), plan[index][1], first) for index in chosen)
    return plan, [arrays[index] for index in chosen], rows


def weight_plans(copies, plan, refs, rows, parts):
    own = lax.axis_index("dp")
    plans = {}
    for (slot, rels, first), ref in zip(plan, refs):
        for place, rel in enumerate(rels):
            start = 0 if rel is None else pl.multiple_of(jnp.bitwise_xor(own, rel) * rows, rows)
            for part, target in enumerate(parts):
                plans.setdefault((part, slot), []).append(
                    copies.plan(
                        ref.at[place, pl.ds(first + part * rows, rows), :],
                        target.at[slot, pl.ds(start, rows), :],
                    )
                )
    return plans


def wait_all(items):
    for item in items:
        item.wait()


def weight_copies(plan, parts):
    return parts * sum(len(rels) for _, rels, _ in plan)


def in_any(count):
    return [pl.BlockSpec(memory_space=pl.ANY)] * count


def in_vmem(count):
    return [pl.BlockSpec(memory_space=pltpu.VMEM)] * count


def like(array):
    return pltpu.VMEM(array.shape, array.dtype)


def call(kernel, name, micros, live, small, arrays, outs, scratch, copies):
    return pl.pallas_call(
        kernel,
        in_specs=[pl.BlockSpec(memory_space=pltpu.SMEM)] + in_vmem(len(small)) + in_any(len(arrays)),
        out_specs=tuple(in_any(len(outs))),
        out_shape=tuple(outs),
        scratch_shapes=list(scratch) + [pltpu.SemaphoreType.DMA((copies,))],
        compiler_params=pltpu.CompilerParams(vmem_limit_bytes=VMEM_BYTES),
        cost_estimate=cost(micros),
        name=name,
    )(live, *small, *arrays)


def row_chunks(rows, body, init):
    chunk = 2 * PADDED

    def step(index, carry):
        return body(pl.ds(pl.multiple_of(index * chunk, chunk), chunk), index, carry)

    return lax.fori_loop(0, rows // chunk, step, init)


def live_rows(live_ref, index):
    place = lax.broadcasted_iota(jnp.int32, (2 * PADDED, 1), 0)
    value = jnp.where(place < PADDED, live_ref[2 * index], live_ref[2 * index + 1])
    return jnp.where(lax.rem(place, PADDED) < WTOK, value, 0.0)


def attention_forward_kernel(heads, scale, picks, plan, block_rows, end, *refs):
    count = len(picks)
    live_ref, vec_ref, qv_ref = refs[:3]
    arrays = refs[3 : 6 + 2 * end]
    x_hbm, bias_hbm, mask_hbm = arrays[:3]
    refs = refs[3 + len(arrays) :]
    weight_refs, refs = refs[: len(plan)], refs[len(plan) :]
    outs, refs = refs[: 5 * count + 2], refs[5 * count + 2 :]
    x, bias, mask, total, normed, normed2, weights, qs, ks, vs, ps, atts, sems = refs
    rows = x.shape[0]
    columns = qs.shape[2]
    pairs = rows // (2 * PADDED)
    copies = Copies(sems)
    weight = weight_plans(copies, plan, weight_refs, block_rows, (weights,))
    later = [weight[0, n] for n in range(1, count)]
    later.append([copies.plan(mask_hbm, mask)])
    later[-1] += [copies.plan(bias_hbm.at[e], bias.at[n]) for n, e in enumerate(picks)]
    x_copy = copies.plan(x_hbm, x)
    if end:
        normed_copy = copies.plan(arrays[3], normed)
        late = [x_copy, copies.plan(arrays[4], total)]
        start_all([normed_copy], weight[0, 0])
        normed_copy.wait()
        start_all(*later)
    else:
        start_all([x_copy], weight[0, 0])
        x_copy.wait()
        start_all(*later)

        def first_norm(span, index, _):
            normal, _ = normalize(x[span, :])
            normed[span, :] = (normal * vec_ref[0:1, :] + vec_ref[1:2, :]).astype(BF16)
            return 0

        row_chunks(rows, first_norm, 0)
        copies.send(normed, outs[-1])
    for n, e in enumerate(picks):
        wait_all(weight[0, n])
        qkv = dot(normed[...], weights[n, :, : 3 * columns])
        qs[n] = ((qkv[:, :columns] + qv_ref[e, 0:1, :]) * scale).astype(BF16)
        ks[n] = qkv[:, columns : 2 * columns].astype(BF16)
        vs[n] = (qkv[:, 2 * columns :] + qv_ref[e, 1:2, :]).astype(BF16)
        for index, buffer in enumerate((qs, ks, vs)):
            copies.send(buffer.at[n], outs[5 * n + index])
    wait_all(later[-1])
    if end:
        start_all(late)

    def pair_step(pair, _):
        span = pl.ds(pl.multiple_of(pair * 2 * PADDED, 2 * PADDED), 2 * PADDED)
        for n in range(count):
            query = qs[n, span, :].astype(F32)
            key = ks[n, span, :].astype(F32)
            value = vs[n, span, :].astype(F32)
            results = []
            for side in range(2):
                part = slice(side * PADDED, (side + 1) * PADDED)
                keys = spread_heads(key[part], heads)
                scores = dot(keys, query[part].astype(BF16), 1, 1) + bias[n]
                scores = scores.reshape(heads, PADDED, PADDED) + mask[2 * pair + side][None]
                expo = jnp.exp(scores - jnp.max(scores, axis=1, keepdims=True))
                probs = expo * (1.0 / jnp.sum(expo, axis=1, keepdims=True))
                probs = probs.reshape(heads * PADDED, PADDED)
                ps[n, 2 * pair + side] = stored_rows(beside_heads(probs, heads))
                values = spread_heads(value[part], heads)
                results.append(dot(probs.astype(BF16), values, 0, 0))
            atts[n, span, :] = jnp.concatenate(results, axis=0).astype(BF16)
        return 0

    lax.fori_loop(0, pairs, pair_step, 0)
    for n in range(count):
        copies.send(ps.at[n], outs[5 * n + 3])
        copies.send(atts.at[n], outs[5 * n + 4])
    if end:
        wait_all(late)
    branch = total[...] if end else None
    for n in range(count):
        part = dot(atts[n], weights[n, :, 3 * columns :], 1, 1)
        branch = part if branch is None else branch + part
    total[...] = branch
    if end:

        def second_norm(span, index, _):
            live = live_rows(live_ref, index)
            mixed = x[span, :] + live * (total[span, :] + vec_ref[2:3, :])
            total[span, :] = mixed
            normal, _ = normalize(mixed)
            normed2[span, :] = (normal * vec_ref[3:4, :] + vec_ref[4:5, :]).astype(BF16)
            return 0

        row_chunks(rows, second_norm, 0)
        copies.send(normed2, outs[-1])
    copies.send(total, outs[-2])
    copies.finish()


def attention_forward(
    x, weights, picks, vectors, qv, bias, mask, live, heads, scale, earlier=()
):
    rows, width = x.shape
    columns = qv.shape[2]
    wins = rows // PADDED
    plan, arrays, block_rows = choose(weights, picks)
    count = len(picks)
    end = bool(earlier)
    shape = jax.ShapeDtypeStruct
    piece = shape((rows, columns), BF16)
    probs = shape((wins, STORED, heads * PADDED), BF16)
    results = call(
        functools.partial(attention_forward_kernel, heads, scale, picks, plan, block_rows, end),
        "attention_forward",
        4 + 5 * count,
        live,
        (vectors, qv),
        [x, bias, mask] + list(earlier) + arrays,
        [piece, piece, piece, probs, piece] * count
        + [shape((rows, width), F32), shape((rows, width), BF16)],
        [
            like(x),
            pltpu.VMEM((count,) + bias.shape[1:], F32),
            like(mask),
            pltpu.VMEM((rows, width), F32),
            pltpu.VMEM((rows, width), BF16),
            pltpu.VMEM((rows, width), BF16),
            pltpu.VMEM((count, width, width), BF16),
        ]
        + [pltpu.VMEM((count, rows, columns), BF16)] * 3
        + [
            pltpu.VMEM((count,) + probs.shape, BF16),
            pltpu.VMEM((count, rows, columns), BF16),
        ],
        weight_copies(plan, 1) + 6 * count + 8,
    )
    saved = {e: results[5 * n : 5 * n + 5] for n, e in enumerate(picks)}
    return saved, results[-2], results[-1]


def ffn_forward_kernel(picks, plan, block_rows, end, *refs):
    count = len(picks)
    live_ref, bias_ref, vec_ref = refs[:3]
    arrays, refs = refs[3 : 4 + end], refs[4 + end :]
    weight_refs, refs = refs[: len(plan)], refs[len(plan) :]
    outs, refs = refs[: 2 * count + 1], refs[2 * count + 1 :]
    normed2, mixed, earlier, total, first, second, hidden, slope, sems = refs
    rows = normed2.shape[0]
    copies = Copies(sems)
    arrived = copies.plan(arrays[0], normed2)
    weight = weight_plans(copies, plan, weight_refs, block_rows, (first, second))
    late = [copies.plan(one, to) for one, to in zip(arrays[1:], (mixed, earlier))]
    start_all([arrived], weight[0, 0])
    arrived.wait()
    start_all(weight[1, 0])
    for n, e in enumerate(picks):
        wait_all(weight[0, n])
        if n + 1 < count:
            start_all(weight[0, n + 1], weight[1, n + 1])
        else:
            start_all(late)
        before = dot(normed2[...], first[n]) + bias_ref[e]
        cdf = 0.5 * (1.0 + lax.erf(before * (0.5**0.5)))
        density = jnp.exp(-0.5 * before * before) * 0.3989422804014327
        hidden[n] = (before * cdf).astype(BF16)
        copies.send(hidden.at[n], outs[2 * n])
        slope[n] = (cdf + before * density).astype(BF16)
        copies.send(slope.at[n], outs[2 * n + 1])
        wait_all(weight[1, n])
        part = dot(hidden[n], second[n], 1, 1)
        if n == 0:
            total[...] = part
        else:
            total[...] += part
    wait_all(late)
    if end:

        def finish(span, index, _):
            live = live_rows(live_ref, index)
            value = total[span, :] + vec_ref[5:6, :]
            if end == 2:
                value = value + earlier[span, :]
            total[span, :] = mixed[span, :] + live * value
            return 0

        row_chunks(rows, finish, 0)
    copies.send(total, outs[-1])
    copies.finish()


def ffn_forward(normed2, weights, picks, bias, vectors, live, earlier=()):
    rows, width = normed2.shape
    plan, arrays, block_rows = choose(weights, picks)
    count = len(picks)
    end = len(earlier)
    shape = jax.ShapeDtypeStruct
    piece = shape((rows, width), BF16)
    results = call(
        functools.partial(ffn_forward_kernel, picks, plan, block_rows, end),
        "ffn_forward",
        4 * count,
        live,
        (bias, vectors),
        [normed2] + list(earlier) + arrays,
        [piece, piece] * count + [shape((rows, width), F32)],
        [
            like(normed2),
            pltpu.VMEM((rows, width), F32),
            pltpu.VMEM((rows, width), F32),
            pltpu.VMEM((rows, width), F32),
        ]
        + [pltpu.VMEM((count, width, width), BF16)] * 2
        + [pltpu.VMEM((count, rows, width), BF16)] * 2,
        weight_copies(plan, 2) + 2 * count + 5,
    )
    return {e: results[2 * n : 2 * n + 2] for n, e in enumerate(picks)}, results[-1]


def fill_transposed(target, source, block_rows, tiled):
    flipped = source[...].T
    if not tiled:
        target[...] = flipped
        return
    own = lax.axis_index("dp")
    for block in range(flipped.shape[0] // block_rows):
        start = pl.multiple_of(jnp.bitwise_xor(own, block) * block_rows, block_rows)
        target[pl.ds(start, block_rows), :] = flipped[
            block * block_rows : (block + 1) * block_rows
        ]


def put_blocks(buffer, cuts, block_rows, part, value):
    order = [rel for _, _, rels in cuts for rel in rels]
    for place, rel in enumerate(order):
        start = 0 if rel is None else rel * block_rows
        buffer[place, part * block_rows : (part + 1) * block_rows, :] = value[
            start : start + block_rows
        ].astype(BF16)


def send_blocks(copies, buffer, cuts, block_rows, part, outs):
    place = 0
    rows = pl.ds(part * block_rows, block_rows)
    for index, start, rels in cuts:
        copies.send(
            buffer.at[pl.ds(place, len(rels)), rows, :],
            outs[index].at[pl.ds(start, len(rels)), rows, :],
        )
        place += len(rels)


def block_outs(layout, height, width):
    return [jax.ShapeDtypeStruct((size, height, width), BF16) for size in layout[0]]


def ffn_backward_kernel(picks, plan, block_rows, layout, begin, end, *refs):
    count = len(picks)
    sizes, cuts = layout
    tiled = cuts[0][0][2][0] is not None
    live_ref, vec_ref = refs[:2]
    given = 2 * count + 2 + end + 2 * (not begin)
    arrays, refs = refs[2 : 2 + given], refs[2 + given :]
    weight_refs, refs = refs[: len(plan)], refs[len(plan) :]
    outs, refs = refs[: 5 + len(sizes)], refs[5 + len(sizes) :]
    (
        grad, mixed, branch, error, error_here, attn_grad, normed2, slopes, hiddens, pres, first,
        second, normed2_t, branch_t, results, sums, hidden_sums, sems,
    ) = refs
    rows, width = grad.shape
    blocks_out = outs[5:]
    copies = Copies(sems)
    zero = jnp.zeros((1, width), F32)
    weight = weight_plans(copies, plan, weight_refs, block_rows, (first, second))
    grad_copy = copies.plan(arrays[0], grad)
    slope = [copies.plan(one, slopes.at[n]) for n, one in enumerate(arrays[1 : 1 + count])]
    hidden_hbm = arrays[1 + count : 1 + 2 * count]
    hidden = [copies.plan(one, hiddens.at[n]) for n, one in enumerate(hidden_hbm)]
    normed2_copy = copies.plan(arrays[1 + 2 * count], normed2)
    more = list(arrays[2 + 2 * count :])
    late = [copies.plan(more.pop(0), mixed)] if end else []
    if begin:
        arrived = grad_copy
    else:
        arrived = copies.plan(more[0], branch)
        late += [copies.plan(more[1], error), grad_copy]
    start_all([arrived], weight[1, 0], [slope[0]])
    arrived.wait()
    start_all(weight[0, 0], weight[1, 1], [slope[1]])
    if begin:

        def start(span, index, total):
            part = (live_rows(live_ref, index) * grad[span, :]).astype(BF16)
            branch[span, :] = part
            return total + jnp.sum(part.astype(F32), axis=0, keepdims=True)

        sums[3:4, :] = row_chunks(rows, start, zero)
        if not end:
            copies.send(branch, outs[2])
    fill_transposed(branch_t, branch, block_rows, tiled)
    for n, e in enumerate(picks):
        wait_all(weight[1, n])
        flow = dot(branch[...], second[n])
        slope[n].wait()
        pre = (slopes[n].astype(F32) * flow).astype(BF16)
        pres[n] = pre
        if n + 1 < count:
            start_all(weight[0, n + 1])
            if n + 2 < count:
                start_all(weight[1, n + 2], [slope[n + 2]])
        else:
            start_all([normed2_copy, hidden[0]], late)
        hidden_sums[n] = jnp.sum(pre.astype(F32), axis=0, keepdims=True)
        wait_all(weight[0, n])
        part = dot(pres[n], first[n], 1, 1)
        if n == 0:
            error_here[...] = part
        else:
            error_here[...] += part
    wait_all(late)
    if end:

        def finish(span, index, totals):
            if not begin:
                error_here[span, :] += error[span, :]
            back, gain_part, shift_part = norm_back_rows(
                mixed[span, :], vec_ref[3:4, :], error_here[span, :]
            )
            mixed_grad = grad[span, :] + back
            error_here[span, :] = mixed_grad
            low = (live_rows(live_ref, index) * mixed_grad).astype(BF16)
            attn_grad[span, :] = low
            bias_part = jnp.sum(low.astype(F32), axis=0, keepdims=True)
            return tuple(a + b for a, b in zip(totals, (gain_part, shift_part, bias_part)))

        totals = row_chunks(rows, finish, (zero, zero, zero))
        for index in range(3):
            sums[index : index + 1, :] = totals[index]
        copies.send(attn_grad, outs[1])
    copies.send(error_here, outs[0])
    copies.send(sums, outs[3])
    copies.send(hidden_sums, outs[4])
    normed2_copy.wait()
    fill_transposed(normed2_t, normed2, block_rows, tiled)
    for n in range(count):
        if n + 1 < count:
            hidden[n + 1].start()
        put_blocks(results.at[n], cuts[n], block_rows, 0, dot(normed2_t[...], pres[n]))
        send_blocks(copies, results.at[n], cuts[n], block_rows, 0, blocks_out)
        hidden[n].wait()
        put_blocks(results.at[n], cuts[n], block_rows, 1, dot(branch_t[...], hiddens[n]))
        send_blocks(copies, results.at[n], cuts[n], block_rows, 1, blocks_out)
    copies.finish()


def ffn_backward(
    grad, hidden, normed2, weights, picks, layout, vectors, live, mixed=None, earlier=()
):
    rows, width = grad.shape
    plan, arrays, block_rows = choose(weights, picks)
    count = len(picks)
    end = mixed is not None
    shape = jax.ShapeDtypeStruct
    low = shape((rows, width), BF16)
    wide = shape((rows, width), F32)
    tiny = shape((8, width), F32)
    blocks = block_outs(layout, 2 * block_rows, width)
    results = call(
        functools.partial(
            ffn_backward_kernel, picks, plan, block_rows, layout, not earlier, end
        ),
        "ffn_backward",
        7 * count,
        live,
        (vectors,),
        [grad]
        + [hidden[e][1] for e in picks]
        + [hidden[e][0] for e in picks]
        + [normed2]
        + [mixed] * end
        + list(earlier)
        + arrays,
        [wide, low if end else tiny, tiny if end else low, tiny, shape((count, 1, width), F32)]
        + blocks,
        [like(wide), like(wide), like(low), like(wide), like(wide), like(low), like(low)]
        + [pltpu.VMEM((count, rows, width), BF16)] * 3
        + [pltpu.VMEM((count, width, width), BF16)] * 2
        + [pltpu.VMEM((width, rows), BF16)] * 2
        + [pltpu.VMEM((count, width // block_rows, 2 * block_rows, width), BF16)]
        + [pltpu.VMEM((8, width), F32), pltpu.VMEM((count, 1, width), F32)],
        weight_copies(plan, 2) + 2 * count + 9 + 4 * len(blocks) + 4,
    )
    return *results[:5], results[5:]


def ffn_both_kernel(picks, plan, block_rows, layout, *refs):
    count = len(picks)
    sizes, cuts = layout
    tiled = cuts[0][0][2][0] is not None
    live_ref, bias_ref, vec_ref = refs[:3]
    normed2_hbm, mixed_hbm, grad_hbm = refs[3:6]
    refs = refs[6:]
    weight_refs, refs = refs[: len(plan)], refs[len(plan) :]
    outs, refs = refs[:5], refs[5:]
    blocks_out, refs = refs[: len(sizes)], refs[len(sizes) :]
    (
        normed2, mixed, grad, total, error, branch, attn_grad, hiddens, pres, first, second,
        normed2_t, branch_t, results, sums, hidden_sums, sems,
    ) = refs
    rows, width = grad.shape
    copies = Copies(sems)
    zero = jnp.zeros((1, width), F32)
    weight = weight_plans(copies, plan, weight_refs, block_rows, (first, second))
    grad_copy = copies.plan(grad_hbm, grad)
    normed2_copy = copies.plan(normed2_hbm, normed2)
    mixed_copy = copies.plan(mixed_hbm, mixed)
    start_all([normed2_copy], weight[0, 0])
    normed2_copy.wait()
    start_all([grad_copy], weight[1, 0])
    fill_transposed(normed2_t, normed2, block_rows, tiled)
    for n, e in enumerate(picks):
        wait_all(weight[0, n])
        before = dot(normed2[...], first[n]) + bias_ref[e]
        if n + 1 < count:
            start_all(weight[0, n + 1], weight[1, n + 1])
        else:
            start_all([mixed_copy])
        cdf = 0.5 * (1.0 + lax.erf(before * (0.5**0.5)))
        density = jnp.exp(-0.5 * before * before) * 0.3989422804014327
        hiddens[n] = (before * cdf).astype(BF16)
        slope = cdf + before * density
        if n == 0:
            grad_copy.wait()

            def start(span, index, carry):
                part = (live_rows(live_ref, index) * grad[span, :]).astype(BF16)
                branch[span, :] = part
                return carry + jnp.sum(part.astype(F32), axis=0, keepdims=True)

            sums[3:4, :] = row_chunks(rows, start, zero)
            fill_transposed(branch_t, branch, block_rows, tiled)
        wait_all(weight[1, n])
        pre = (slope * dot(branch[...], second[n])).astype(BF16)
        pres[n] = pre
        hidden_sums[n] = jnp.sum(pre.astype(F32), axis=0, keepdims=True)
        part = dot(hiddens[n], second[n], 1, 1)
        back = dot(pres[n], first[n], 1, 1)
        if n == 0:
            total[...] = part
            error[...] = back
        else:
            total[...] += part
            error[...] += back
    mixed_copy.wait()

    def finish(span, index, totals):
        live = live_rows(live_ref, index)
        values = mixed[span, :]
        total[span, :] = values + live * (total[span, :] + vec_ref[5:6, :])
        back, gain_part, shift_part = norm_back_rows(values, vec_ref[3:4, :], error[span, :])
        mixed_grad = grad[span, :] + back
        error[span, :] = mixed_grad
        low = (live * mixed_grad).astype(BF16)
        attn_grad[span, :] = low
        bias_part = jnp.sum(low.astype(F32), axis=0, keepdims=True)
        return tuple(a + b for a, b in zip(totals, (gain_part, shift_part, bias_part)))

    totals = row_chunks(rows, finish, (zero, zero, zero))
    for index in range(3):
        sums[index : index + 1, :] = totals[index]
    for buffer, out in zip((total, error, attn_grad, sums, hidden_sums), outs):
        copies.send(buffer, out)
    for n in range(count):
        put_blocks(results.at[n], cuts[n], block_rows, 0, dot(normed2_t[...], pres[n]))
        send_blocks(copies, results.at[n], cuts[n], block_rows, 0, blocks_out)
        put_blocks(results.at[n], cuts[n], block_rows, 1, dot(branch_t[...], hiddens[n]))
        send_blocks(copies, results.at[n], cuts[n], block_rows, 1, blocks_out)
    copies.finish()


def ffn_both(normed2, mixed, grad, weights, picks, layout, bias, vectors, live):
    rows, width = grad.shape
    plan, arrays, block_rows = choose(weights, picks)
    count = len(picks)
    shape = jax.ShapeDtypeStruct
    low = shape((rows, width), BF16)
    wide = shape((rows, width), F32)
    blocks = block_outs(layout, 2 * block_rows, width)
    results = call(
        functools.partial(ffn_both_kernel, picks, plan, block_rows, layout),
        "ffn_both",
        30,
        live,
        (bias, vectors),
        [normed2, mixed, grad] + arrays,
        [wide, wide, low, shape((8, width), F32), shape((count, 1, width), F32)] + blocks,
        [like(low), like(wide), like(wide), like(wide), like(wide), like(low), like(low)]
        + [pltpu.VMEM((count, rows, width), BF16)] * 2
        + [pltpu.VMEM((count, width, width), BF16)] * 2
        + [pltpu.VMEM((width, rows), BF16)] * 2
        + [pltpu.VMEM((count, width // block_rows, 2 * block_rows, width), BF16)]
        + [pltpu.VMEM((8, width), F32), pltpu.VMEM((count, 1, width), F32)],
        weight_copies(plan, 2) + 8 + 4 * len(blocks) + 4,
    )
    return *results[:5], results[5:]


def attention_backward_kernel(heads, scale, picks, plan, block_rows, layout, end, *refs):
    count = len(picks)
    sizes, cuts = layout
    tiled = cuts[0][0][2][0] is not None
    live_ref, vec_ref = refs[:2]
    given = 2 + 5 * count + 3 * end
    arrays, refs = refs[2 : 2 + given], refs[2 + given :]
    weight_refs, refs = refs[: len(plan)], refs[len(plan) :]
    outs_count = 3 + end + len(sizes)
    outs, refs = refs[:outs_count], refs[outs_count:]
    (
        attn_grad, normed, x, mixed_grad, error, weights, qs, ks, vs, atts, ps, gs, grads,
        normed_t, attn_grad_t, results, scores_sum, scores_out, sums, small, sems,
    ) = refs
    rows, width = attn_grad.shape
    columns = qs.shape[2]
    pairs = rows // (2 * PADDED)
    copies = Copies(sems)
    weight = weight_plans(copies, plan, weight_refs, block_rows, (weights,))
    arrived = copies.plan(arrays[0], attn_grad)
    saved = [
        copies.plan(arrays[2 + 5 * n + index], buffer.at[n])
        for n in range(count)
        for index, buffer in ((0, qs), (1, ks), (2, vs), (3, ps))
    ]
    late = [copies.plan(arrays[1], normed)]
    for n in range(count):
        late.append(copies.plan(arrays[2 + 5 * n + 4], atts.at[n]))
    if end:
        for one, to in zip(arrays[2 + 5 * count :], (x, mixed_grad, error)):
            late.append(copies.plan(one, to))
    start_all([arrived], weight[0, 0])
    arrived.wait()
    start_all(*[weight[0, n] for n in range(1, count)], saved)
    scores_sum[...] = jnp.zeros(scores_sum.shape, F32)
    fill_transposed(attn_grad_t, attn_grad, block_rows, tiled)
    for n in range(count):
        wait_all(weight[0, n])
        gs[n] = dot(attn_grad[...], weights[n, :, 3 * columns :]).astype(BF16)
    wait_all(saved)
    start_all(late)

    def pair_step(pair, _):
        span = pl.ds(pl.multiple_of(pair * 2 * PADDED, 2 * PADDED), 2 * PADDED)
        for n in range(count):
            query, key, value, grad = [
                buffer[n, span, :].astype(F32) for buffer in (qs, ks, vs, gs)
            ]
            rows_out = []
            for side in range(2):
                part = slice(side * PADDED, (side + 1) * PADDED)
                queries = spread_heads(query[part], heads)
                grads_out = spread_heads(grad[part], heads)
                probs = ps[n, 2 * pair + side].astype(F32)[:PADDED]
                flow = dot(value[part].astype(BF16), grads_out, 1, 1)
                inner = jnp.sum(probs * flow, axis=0, keepdims=True)
                score = (probs * (flow - inner)).astype(BF16)
                scores_sum[n] += score.astype(F32)
                query_part = dot(score, key[part].astype(BF16), 0, 0)
                rows_out.append(
                    jnp.concatenate(
                        [
                            merge_heads(query_part, heads) * scale,
                            dot(score, queries),
                            dot(probs.astype(BF16), grads_out),
                        ],
                        axis=1,
                    )
                )
            grads[n, span, :] = jnp.concatenate(rows_out, axis=0).astype(BF16)
        return 0

    lax.fori_loop(0, pairs, pair_step, 0)
    for n in range(count):
        scores_out[n] = below_heads(scores_sum[n], heads)
    copies.send(scores_out, outs[1])
    wait_all(late)
    for n in range(count):
        sums[n] = jnp.sum(grads[n].astype(F32), axis=0, keepdims=True)
        part = dot(grads[n], weights[n, :, : 3 * columns], 1, 1)
        if n == 0 and not end:
            error[...] = part
        else:
            error[...] += part
    copies.send(sums, outs[2])
    if end:
        zero = jnp.zeros((1, width), F32)

        def finish(span, index, totals):
            back, gain_part, shift_part = norm_back_rows(
                x[span, :], vec_ref[0:1, :], error[span, :]
            )
            error[span, :] = mixed_grad[span, :] + back
            return totals[0] + gain_part, totals[1] + shift_part

        totals = row_chunks(rows, finish, (zero, zero))
        for index in range(2):
            small[index : index + 1, :] = totals[index]
        copies.send(small, outs[3])
    copies.send(error, outs[0])
    fill_transposed(normed_t, normed, block_rows, tiled)
    for n in range(count):
        value = jnp.concatenate(
            [dot(normed_t[...], grads[n]), dot(attn_grad_t[...], atts[n])], axis=1
        )
        put_blocks(results.at[n], cuts[n], block_rows, 0, value)
        send_blocks(copies, results.at[n], cuts[n], block_rows, 0, outs[3 + end :])
    copies.finish()


def attention_backward(
    attn_grad, normed, saved, weights, picks, layout, vectors, live, heads, scale, earlier=()
):
    rows, width = attn_grad.shape
    columns = saved[picks[0]][0].shape[1]
    plan, arrays, block_rows = choose(weights, picks)
    count = len(picks)
    end = bool(earlier)
    probs = saved[picks[0]][3]
    shape = jax.ShapeDtypeStruct
    wide = shape((rows, width), F32)
    pieces = [item for e in picks for item in saved[e]]
    outs = [
        wide,
        shape((count, heads * PADDED, PADDED), F32),
        shape((count, 1, 3 * columns), F32),
    ]
    blocks = block_outs(layout, block_rows, width)
    results = call(
        functools.partial(
            attention_backward_kernel, heads, scale, picks, plan, block_rows, layout, end
        ),
        "attention_backward",
        19,
        live,
        (vectors,),
        [attn_grad, normed] + pieces + list(earlier) + arrays,
        outs + [shape((8, width), F32)] * end + blocks,
        [like(attn_grad), like(normed), like(wide), like(wide), like(wide)]
        + [pltpu.VMEM((count, width, width), BF16)]
        + [pltpu.VMEM((count, rows, columns), BF16)] * 4
        + [pltpu.VMEM((count,) + probs.shape, BF16)]
        + [pltpu.VMEM((count, rows, columns), BF16)]
        + [pltpu.VMEM((count, rows, 3 * columns), BF16)]
        + [pltpu.VMEM((width, rows), BF16)] * 2
        + [pltpu.VMEM((count, width // block_rows, block_rows, width), BF16)]
        + [pltpu.VMEM((count, PADDED, heads * PADDED), F32), like(outs[1]), like(outs[2])]
        + [pltpu.VMEM((8, width), F32)],
        weight_copies(plan, 1) + 5 * count + 11 + 4 * len(blocks),
    )
    return *results[: 3 + end], results[3 + end :]


def swap(values, axis, bit):
    size = lax.axis_size(axis)
    return lax.ppermute(values, axis, [(i, i ^ (1 << bit)) for i in range(size)])


def bits_in(axis):
    return lax.axis_size(axis).bit_length() - 1


def pick(values, index, dim):
    return lax.dynamic_index_in_dim(values, index, dim, keepdims=False)


def tie(values, token):
    if token is None:
        return values
    return lax.optimization_barrier((values, token))[0]


def whole_tiles(rows):
    return rows % 16 == 0


def in_order(values):
    index = jnp.bitwise_xor(jnp.arange(values.shape[0]), lax.axis_index("dp"))
    return jnp.take(values, index, axis=0)


def relatives(halves):
    count = lax.axis_size("dp")
    size = count // halves
    return [
        [tuple(range(part * size + side, (part + 1) * size, 2)) for part in range(halves)]
        for side in range(2)
    ]


def line_bits():
    return list(range(1, bits_in("dp")))


def straight(values):
    size = lax.axis_size("dp")
    low, high = [1 << bit for bit in line_bits()[-2:]]
    return [
        lax.ppermute(values(n), "dp", [(i, i ^ shift) for i in range(size)])
        for n, shift in ((1, low), (2, high), (3, low | high))
    ]


class Gather:
    def __init__(self, shard, parts, rows, ways):
        self.shard = shard
        self.parts = parts
        self.rows = rows
        self.ways = ways
        self.entries = []

    def line(self, after=None, at_once=False):
        held = tie(self.shard, after)[None]
        bits = line_bits()
        for bit in bits[:-2]:
            held = jnp.concatenate([held, swap(held, "dp", bit)])
        self.moved = straight(lambda n: held) if at_once else [swap(held, "dp", bits[-2])]
        self.held = [held]

    def line_end(self, until=None):
        moved = tie(self.moved, until)
        self.held = [jnp.concatenate(self.held + moved)]
        return self.held[0]

    def last(self, after=None):
        self.moved = swap(tie(self.held[0], after), "dp", line_bits()[-1])

    def last_end(self, until=None):
        moved = tie(self.moved, until)
        self.held.append(moved)
        if len(self.ways) == 1:
            self.held = [jnp.concatenate(self.held)]
        return self.held[-1]

    def sides(self, part, after=None):
        if part == 0:
            self.side, self.far = [], []
        held = tie(self.held[part], after)
        self.side.append(swap(held, "dp", 0))
        self.far.append(swap(held, "head", 1))

    def sides_end(self, part, until=None):
        self.side[part], self.far[part] = tie((self.side[part], self.far[part]), until)
        return self.side[part], self.far[part]

    def corner(self, part, after=None):
        if part == 0:
            self.corners = []
        if self.ways[part] == "x":
            self.corners.append(swap(tie(self.side[part], after), "head", 1))
        else:
            self.corners.append(swap(tie(self.far[part], after), "dp", 0))

    def corner_end(self, part, until=None):
        self.corners[part] = tie(self.corners[part], until)
        return self.corners[part]

    def core(self, kind, part=None):
        own, other = relatives(len(self.ways))
        arrays, e, rels = {
            "held": (self.held, 0, own),
            "side": (getattr(self, "side", None), 0, other),
            "far": (getattr(self, "far", None), 2, own),
            "corner": (getattr(self, "corners", None), 2, other),
        }[kind]
        for n, (one, several) in enumerate(zip(arrays, rels)):
            if part is None or part == n:
                self.entries.append((e, one, several))
                self.entries.append((e + 1, swap(one, "head", 0), several))

    def result(self, first=0):
        rows, parts = self.rows, self.parts
        width = self.shard.shape[1]
        if whole_tiles(rows):
            plan = tuple((e, rels) for e, _, rels in self.entries)
            return plan, [one for _, one, _ in self.entries], rows, first * rows
        arrays = []
        plan = []
        for e in range(PIECES):
            mine = [(one, rels) for piece, one, rels in self.entries if piece == e]
            if not mine:
                continue
            order = sum((rels for _, rels in mine), ())
            if len(order) < lax.axis_size("dp"):
                continue
            blocks = jnp.concatenate([one[:, : parts * rows] for one, _ in mine])
            blocks = in_order(blocks[jnp.argsort(jnp.array(order))])
            blocks = blocks.reshape(-1, parts, rows, width).transpose(1, 0, 2, 3)
            arrays.append(blocks.reshape(1, -1, width))
            plan.append((e, (None,)))
        rows = arrays[0].shape[1] // parts
        return tuple(plan), arrays, rows, first * rows


def wide(*values):
    total = values[0].astype(F32)
    for value in values[1:]:
        total = total + value.astype(F32)
    return total


def plus(*values):
    return wide(*values).astype(BF16)


class Scatter:
    def __init__(self, parts, rows, ways):
        self.parts = parts
        self.rows = rows
        self.ways = ways
        self.tiled = whole_tiles(rows)
        blocks = lax.axis_size("dp")
        half = blocks // 2
        even = tuple(range(0, blocks, 2))
        odd = tuple(range(1, blocks, 2))
        cut = half // len(ways)
        corners = [odd[n * cut : (n + 1) * cut] for n in range(len(ways))]
        self.order = even + odd
        if self.tiled:
            self.away_layout = (
                (2 * blocks,),
                (((0, 0, self.order),), ((0, blocks, self.order),)),
            )
            last = tuple((3 + n, 0, rels) for n, rels in enumerate(corners))
            self.near_layout = (
                (half,) * 3 + (cut,) * len(ways),
                (((0, 0, even), (1, 0, odd)), ((2, 0, even),) + last),
            )
        else:
            one = ((0, 0, (None,)),)
            two = ((0, 1, (None,)),)
            self.away_layout = self.near_layout = ((2,), (one, two))

    def both_layouts(self):
        sizes, cuts = self.near_layout
        first = len(self.away_layout[0])
        moved = tuple(
            tuple((first + index, start, rels) for index, start, rels in one) for one in cuts
        )
        return self.away_layout[0] + sizes, self.away_layout[1] + moved

    def arrange(self, outs):
        one = outs[0].reshape(2, self.parts, -1, self.rows, outs[0].shape[-1])
        one = one.transpose(0, 2, 1, 3, 4)
        one = one.reshape(one.shape[:2] + (-1, one.shape[-1]))
        return jnp.concatenate([in_order(item)[jnp.array(self.order)] for item in one])

    def away(self, outs):
        self.moved = swap(outs[0] if self.tiled else self.arrange(outs), "head", 0)

    def near(self, outs, until=None):
        moved = tie(self.moved, until)
        half = moved.shape[0] // 4
        if self.tiled:
            own = list(outs)
        else:
            one = self.arrange(outs)
            own = [one[n * half : (n + 1) * half] for n in range(3)]
            cut = half // len(self.ways)
            own += [one[3 * half + n * cut :][:cut] for n in range(len(self.ways))]
        cut = half // len(self.ways)
        self.held = [own[0], moved[:half]]
        self.side = [own[1], moved[half : 2 * half]]
        self.far = [own[2], moved[2 * half : 3 * half]]
        self.corners = [
            plus(own[3 + n], moved[3 * half + n * cut :][:cut]) for n in range(len(self.ways))
        ]
        return self.corners

    def corner(self, after=None):
        self.moved = []
        for way, one in zip(self.ways, tie(self.corners, after)):
            self.moved.append(swap(one, "head", 1) if way == "x" else swap(one, "dp", 0))

    def corner_end(self, until=None):
        moved = tie(self.moved, until)
        half = self.side[0].shape[0]
        for part, (way, one) in enumerate(zip(self.ways, moved)):
            size = one.shape[0]
            around = (part * size, half - (part + 1) * size)
            one = jnp.pad(one, (around,) + ((0, 0),) * 2) if size < half else one
            (self.side if way == "x" else self.far).append(one)
        self.side, self.far = plus(*self.side), plus(*self.far)
        return self.side, self.far

    def sides(self, after=None, part=None):
        side, far = tie((self.side, self.far), after)
        if part is not None:
            size = side.shape[0] // 2
            side, far = [one[part * size : (part + 1) * size] for one in (side, far)]
        self.moved = [swap(side, "dp", 0), swap(far, "head", 1)]

    def sides_end(self, until=None, at_once=False, part=None):
        terms = self.held + list(tie(self.moved, until))
        if part is not None:
            size = terms[-1].shape[0]
            terms[:2] = [one[part * size : (part + 1) * size] for one in terms[:2]]
            if part == 0:
                self.lower = plus(*terms)
                return self.lower
            self.held = [self.lower, plus(*terms)]
            return self.held
        count = 4 if at_once else 2
        size = terms[0].shape[0] // count
        self.held = [
            plus(*[one[n * size : (n + 1) * size] for one in terms]) for n in range(count)
        ]
        return self.held

    def last(self, after=None):
        self.moved = swap(tie(self.held[1], after), "dp", line_bits()[-1])

    def last_end(self, until=None):
        moved = tie(self.moved, until)
        size = moved.shape[0] // 2
        terms = [self.held[0], moved]
        self.held = [plus(*[one[n * size :][:size] for one in terms]) for n in range(2)]
        return self.held

    def line(self, after=None):
        held = tie(self.held, after)
        if len(held) == 4:
            self.moved = straight(lambda n: held[n])
        else:
            self.moved = [swap(held[1], "dp", line_bits()[-2])]

    def line_end(self, until=None):
        held = wide(self.held[0], *tie(self.moved, until))
        for bit in reversed(line_bits()[:-2]):
            cut = held.shape[0] // 2
            moved = swap(held[cut:].astype(BF16), "dp", bit)
            held = wide(held[:cut], moved)
        self.result = held[0]
        return self.result


class SmallSum:
    def __init__(self, values):
        self.total = values
        self.left = [("head", 0), ("head", 1)]
        self.left += [("dp", bit) for bit in range(bits_in("dp"))]
        self.moved = None

    def step(self, until=None):
        self.result(until)
        axis, bit = self.left.pop(0)
        self.moved = swap(self.total, axis, bit)

    def end(self):
        return not self.left

    def result(self, until=None):
        if self.moved is not None:
            self.total = self.total + tie(self.moved, until)
        self.moved = None
        return self.total


def unshift(values):
    grid = values.reshape(values.shape[:-1] + (WSIDE, WSIDE))
    return jnp.roll(grid, (SHIFT, SHIFT), axis=(-2, -1)).reshape(values.shape)


def pad_rows(values):
    grid = values.reshape(-1, WTOK, values.shape[1])
    grid = jnp.pad(grid, ((0, 0), (0, PADDED - WTOK), (0, 0)))
    return grid.reshape(-1, values.shape[1])


def drop_rows(values):
    grid = values.reshape(-1, PADDED, values.shape[1])[:, :WTOK]
    return grid.reshape(-1, values.shape[1])


def attention_mask(pad, region):
    allowed = (pad[:, :, None] == 1) & (region[:, :, None] == region[:, None, :])
    mask = jnp.where(allowed, 0.0, MASKED).astype(F32)
    extra = PADDED - WTOK
    mask = jnp.pad(mask, ((0, 0), (0, 0), (0, extra)))
    return jnp.pad(mask, ((0, 0), (0, extra), (0, 0)), constant_values=ABSENT)


def shards(
    tokens,
    cotangent,
    crop_counts,
    pad_mask,
    region_ids,
    rel_index,
    norm_gain,
    norm_shift,
    qkv_weight,
    qv_bias,
    bias_table,
    proj_weight,
    fc1_weight,
    fc1_bias,
    fc2_weight,
    out_bias,
):
    rows = tokens.shape[0]
    width = tokens.shape[1]
    wins = rows // WTOK
    local_width = qkv_weight.shape[3]
    local_heads = bias_table.shape[1]
    rel_count = bias_table.shape[2]
    dp_width = norm_gain.shape[2]
    dp_hidden = fc1_bias.shape[1]
    pieces = lax.axis_size("head")
    heads_total = local_heads * pieces
    head_dim = local_width // local_heads
    scale = head_dim ** (-0.5)
    head_index = lax.axis_index("head")
    dp_index = lax.axis_index("dp")
    relative = [head_index ^ e for e in range(pieces)]

    shard_rows = qkv_weight.shape[1]
    attn_shards = [
        jnp.concatenate(
            [qkv_weight[block].reshape(-1, 3 * local_width), proj_weight[block].T], axis=1
        )
        for block in range(BLOCKS)
    ]
    ffn_shards = [
        jnp.concatenate([fc1_weight[block], fc2_weight[block].T]) for block in range(BLOCKS)
    ]
    small = jnp.concatenate([norm_gain, norm_shift, qv_bias, out_bias]).reshape(-1, dp_width)
    small_rows = small.shape[0]
    beside = -(-dp_width // 128) * 128
    small = jnp.pad(small, ((0, 0), (0, width - dp_width)))
    small = small + jnp.pad(
        fc1_bias, ((0, small_rows - BLOCKS), (beside, width - beside - dp_hidden))
    )
    attn_shards[0] = jnp.concatenate([attn_shards[0], small])
    near, away = (0, 2), (1, 3)
    first, second = (0, 1), (2, 3)
    a0 = Gather(attn_shards[0], 1, shard_rows, "y")
    middle = Gather(jnp.concatenate([ffn_shards[0], attn_shards[1]]), 3, shard_rows, "xy")
    f1 = Gather(ffn_shards[1], 2, shard_rows, "xy")

    def attn_weights(block):
        return middle.result(2) if block else a0.result()

    def ffn_weights(block):
        return f1.result() if block else middle.result()

    a0.line(at_once=True)
    far_table = swap(bias_table, "head", 1)
    near_table = swap(bias_table, "head", 0)
    a0.line_end()
    a0.sides(0)
    middle.line(a0.held)
    a0.core("held")
    middle.line_end()
    middle.core("held", 0)
    middle.last()
    a0.sides_end(0)
    a0.core("side")
    a0.core("far")
    a0.corner(0)
    middle.sides(0, a0.far)
    table_pieces = [bias_table, near_table, far_table, swap(far_table, "head", 0)]
    small_all = jnp.stack([a0.held[0][:, shard_rows:], a0.side[0][:, shard_rows:]], axis=1)
    small_all = in_order(small_all.reshape((-1,) + small.shape)).transpose(1, 0, 2).astype(F32)
    every = small_all[:, :, :dp_width].reshape(4, BLOCKS, 2, width)
    gains, shifts, qv_all, out_all = every[0], every[1], every[2], every[3]
    hidden_bias = small_all[:BLOCKS, :, beside : beside + dp_hidden].reshape(BLOCKS, pieces, -1)
    qv_pieces = qv_all.reshape(BLOCKS, 2, pieces, local_width)

    counts = jnp.repeat(crop_counts, CROP_MAX)
    slots = jnp.arange(pad_mask.shape[0], dtype=jnp.int32) % CROP_MAX
    live_all = (slots < counts).astype(F32)
    live_windows = lax.dynamic_slice_in_dim(live_all, head_index * wins, wins, 0)
    live = live_windows
    pad = lax.dynamic_slice_in_dim(pad_mask, head_index * wins, wins, 0)
    region = unshift(lax.dynamic_slice_in_dim(region_ids, head_index * wins, wins, 0))
    masks = (attention_mask(pad, jnp.zeros_like(region)), attention_mask(pad, region))
    extra = PADDED - WTOK
    onehots = []
    for index in (rel_index, unshift(unshift(rel_index).T).T):
        by_key = jnp.pad(index.T, ((0, extra), (0, extra)), constant_values=-1).reshape(1, -1)
        ids = jnp.arange(rel_count, dtype=jnp.int32)[:, None]
        onehots.append((ids == by_key).astype(BF16))

    def ordered(values, dim):
        return jnp.stack([pick(values, rel, dim) for rel in relative])

    block_rows = local_heads * PADDED
    vectors, qv, biases, hidden_biases = [], [], [], []
    for block in range(BLOCKS):
        rows8 = [
            gains[block, 0],
            shifts[block, 0],
            out_all[block, 0],
            gains[block, 1],
            shifts[block, 1],
            out_all[block, 1],
        ]
        vectors.append(jnp.pad(jnp.stack(rows8), ((0, 2), (0, 0))))
        qv.append(ordered(qv_pieces[block], 1))
        table = jnp.concatenate([one[block] for one in table_pieces])
        bias = jnp.dot(table, onehots[block % 2], preferred_element_type=F32)
        biases.append(bias.reshape(pieces, block_rows, PADDED))
        hidden_biases.append(ordered(hidden_bias[block], 0)[:, None, :])

    residual = pad_rows(tokens).astype(F32)

    def attend(block, x, picks, token, earlier=()):
        return attention_forward(
            x,
            attn_weights(block),
            picks,
            tie(vectors[block], token),
            qv[block],
            biases[block],
            masks[block % 2],
            live,
            local_heads,
            scale,
            earlier,
        )

    def feed(block, normed2, picks, token, earlier=()):
        return ffn_forward(
            normed2,
            ffn_weights(block),
            picks,
            hidden_biases[block],
            tie(vectors[block], token),
            live,
            earlier,
        )

    x0 = residual
    grad_rows = pad_rows(cotangent).astype(F32)
    token = (middle.held[0], biases[1], masks[1], grad_rows)
    saved_0, branch, normed_0 = attend(0, x0, first, token)
    a0.corner_end(0, branch)
    a0.core("corner")
    middle.sides_end(0, branch)
    middle.core("side", 0)
    middle.core("far", 0)
    middle.corner(0)
    middle.last_end(branch)
    middle.sides(1)
    f1.line(middle.held[1])
    f1.line_end()
    f1.last()
    token = (middle.held[1], f1.held[0])
    more, mixed_0, normed2_0 = attend(0, x0, second, token, (normed_0, branch))
    saved_0.update(more)
    middle.sides_end(1, mixed_0)
    middle.corner(1)
    f1.last_end(mixed_0)
    middle.held[1] = tie(middle.held[1], f1.held[1])
    middle.core("held", 1)
    middle.core("side", 1)
    middle.core("far", 1)
    middle.corner_end(0, mixed_0)
    middle.corner_end(1, mixed_0)
    middle.core("corner")
    f1.sides(0, middle.corners)
    f1.sides(1, middle.corners)
    hidden_0, x1 = feed(0, normed2_0, first + second, middle.corners, (mixed_0,))
    f1.sides_end(0, x1)
    f1.core("held")
    f1.core("side", 0)
    saved_1, branch, normed_1 = attend(1, x1, first, (f1.side[0], f1.far[0]))
    f1.sides_end(1, branch)
    f1.corner(0)
    f1.corner(1)
    f1.core("side", 1)
    f1.core("far")
    token = (f1.side, f1.far)
    more, mixed_1, normed2_1 = attend(1, x1, second, token, (normed_1, branch))
    saved_1.update(more)
    f1.corner_end(0, mixed_1)
    f1.corner_end(1, mixed_1)
    f1.core("corner")
    kept = [
        (x0, mixed_0, normed_0, normed2_0, saved_0, hidden_0),
        (x1, mixed_1, normed_1, normed2_1, saved_1, None),
    ]

    def feed_back(block, picks, layout, grad, token, mixed=None, earlier=()):
        _, _, _, normed2, _, hidden = kept[block]
        return ffn_backward(
            grad,
            hidden,
            normed2,
            ffn_weights(block),
            picks,
            layout,
            tie(vectors[block], token),
            live,
            mixed,
            earlier,
        )

    def attend_back(block, picks, layout, attn_grad, token, earlier=()):
        _, _, normed, _, saved, _ = kept[block]
        return attention_backward(
            attn_grad,
            normed,
            saved,
            attn_weights(block),
            picks,
            layout,
            tie(vectors[block], token),
            live,
            local_heads,
            scale,
            earlier,
        )

    def small_terms(block, attn, small_f, hidden_terms):
        scores_a, sums_a, scores_n, sums_n, small_a = attn

        def together(one, other):
            return ordered(jnp.stack([one[0], other[0], one[1], other[1]]), 0)

        table_grad = lax.dot_general(
            together(scores_n, scores_a).reshape(heads_total, -1),
            onehots[block % 2].astype(F32),
            (((1,), (1,)), ((), ())),
            precision=lax.Precision.HIGHEST,
            preferred_element_type=F32,
        )
        table_grad = jnp.pad(table_grad, ((0, 0), (0, table_lanes - rel_count)))
        qv_sums = together(sums_n, sums_a)[:, 0]
        items = [
            small_a[0:1],
            small_f[0:1],
            small_a[1:2],
            small_f[1:2],
            qv_sums[:, :local_width].reshape(1, width),
            qv_sums[:, 2 * local_width :].reshape(1, width),
            small_f[2:4],
            together(*hidden_terms)[:, 0],
            table_grad.reshape(-1, width),
        ]
        return jnp.concatenate(items)

    table_lanes = 2 * 128
    f1_sum, f0_sum = [Scatter(2, shard_rows, "xy") for _ in range(2)]
    a1_sum, a0_sum = [Scatter(1, shard_rows, "xy") for _ in range(2)]
    residual, mixed_grad, attn_grad, small_f, hidden_sums, outs = ffn_both(
        normed2_1,
        mixed_1,
        grad_rows,
        ffn_weights(1),
        away + near,
        f1_sum.both_layouts(),
        hidden_biases[1],
        tie(vectors[1], mixed_1),
        live,
    )
    count = len(f1_sum.away_layout[0])
    f1_sum.away(outs[:count])
    error, scores_a, sums_a, sent = attend_back(1, away, a1_sum.away_layout, attn_grad, None)
    f1_sum.near(outs[count:], error)
    f1_sum.corner()
    a1_sum.away(sent)
    grad_rows, scores_n, sums_n, small_a, outs = attend_back(
        1, near, a1_sum.near_layout, attn_grad, f1_sum.corners, (x1, mixed_grad, error)
    )
    late_terms = (scores_a, sums_a, scores_n, sums_n, small_a), small_f, hidden_sums
    token = f1_sum.corner_end(grad_rows)
    f1_sum.sides(part=0)
    a1_sum.near(outs, grad_rows)
    error, _, branch_grad, small_b, hidden_a, sent = feed_back(
        0, away, f0_sum.away_layout, grad_rows, (token, a1_sum.corners)
    )
    f0_sum.away(sent)
    token = f1_sum.sides_end(error, part=0)
    f1_sum.sides(token, part=1)
    a1_sum.corner(token)
    mixed_grad, attn_grad, _, small_f, hidden_n, outs = feed_back(
        0,
        near,
        f0_sum.near_layout,
        grad_rows,
        (error, token),
        mixed_0,
        (branch_grad, error),
    )
    small_f = jnp.concatenate([small_f[:3], small_b[3:4]])
    token = (f1_sum.sides_end(attn_grad, part=1), a1_sum.corner_end(attn_grad))
    f1_sum.last()
    a1_sum.sides()
    f0_sum.near(outs, attn_grad)
    f0_sum.corner()
    error, scores_a, sums_a, sent = attend_back(
        0, away, a0_sum.away_layout, attn_grad, (token, f0_sum.corners)
    )
    a0_sum.away(sent)
    token = (f0_sum.corner_end(error), a1_sum.sides_end(error), f1_sum.last_end(error))
    f0_sum.sides()
    a1_sum.last()
    f1_sum.line()
    grad_rows, scores_n, sums_n, small_a, outs = attend_back(
        0, near, a0_sum.near_layout, attn_grad, token, (x0, mixed_grad, error)
    )
    f0_sum.sides_end(grad_rows)
    f0_sum.last()
    a1_sum.last_end(grad_rows)
    a0_sum.near(outs, (grad_rows, f0_sum.held, a1_sum.held))
    a0_sum.corner()
    a1_sum.line()
    token = a0_sum.corner_end()
    a0_sum.sides()
    attn_terms = tie((scores_a, sums_a, scores_n, sums_n, small_a), token)
    small_0 = small_terms(0, attn_terms, small_f, (hidden_n, hidden_a))
    attn_terms, small_f, hidden_sums = tie(late_terms, token)
    small_1 = small_terms(1, attn_terms, small_f, (hidden_sums[2:], hidden_sums[:2]))
    small_sum = SmallSum(jnp.stack([small_0, small_1]))
    token = a0_sum.sides_end(at_once=True)
    residual, grad_rows = tie((residual, grad_rows), token)
    f0_sum.last_end(token)
    a0_sum.line((f0_sum.held, small_sum.total))
    f0_sum.line()
    a1_sum.line_end(token)
    f1_sum.line_end(token)
    small_sum.step()
    small_sum.step(token)
    while not small_sum.end():
        small_sum.step()
    a0_sum.line_end()
    f0_sum.line_end()
    shard_grads = [(a0_sum, f0_sum), (a1_sum, f1_sum)]
    shard_grads = [
        (attn.result, ffn.result[:shard_rows], ffn.result[shard_rows:])
        for attn, ffn in shard_grads
    ]

    totals = small_sum.result()

    def own(values):
        return lax.dynamic_slice_in_dim(values, dp_index * dp_width, dp_width, 2)

    small_grads = [own(totals[:, 2 * index : 2 * index + 2]) for index in range(4)]
    hidden_total = totals[:, 8 : 8 + pieces].reshape(BLOCKS, -1)
    fc1_bias_grad = lax.dynamic_slice_in_dim(hidden_total, dp_index * dp_hidden, dp_hidden, 1)
    table_total = totals[:, 8 + pieces :].reshape(BLOCKS, heads_total, table_lanes)
    bias_table_grad = lax.dynamic_slice_in_dim(
        table_total[:, :, :rel_count], head_index * local_heads, local_heads, 1
    )
    qkv_weight_grad = jnp.stack(
        [item[0][:, : 3 * local_width].reshape(-1, 3, local_width) for item in shard_grads]
    )
    proj_weight_grad = jnp.stack([item[0][:, 3 * local_width :].T for item in shard_grads])
    fc1_weight_grad = jnp.stack([item[1] for item in shard_grads])
    fc2_weight_grad = jnp.stack([item[2].T for item in shard_grads])
    return (
        drop_rows(residual),
        drop_rows(grad_rows),
        small_grads[0],
        small_grads[1],
        qkv_weight_grad,
        small_grads[2],
        bias_table_grad,
        proj_weight_grad,
        fc1_weight_grad,
        fc1_bias_grad,
        fc2_weight_grad,
        small_grads[3],
    )


def solution(mesh):
    placed = (
        P(("dp", "head"), None),
        P(("dp", "head"), None),
        P("dp"),
        P("dp", None),
        P("dp", None),
        P(),
        P(None, None, "dp"),
        P(None, None, "dp"),
        P(None, "dp", None, "head"),
        P(None, None, "dp"),
        P(None, "head", None),
        P(None, "head", "dp"),
        P(None, "dp", "head"),
        P(None, "dp"),
        P(None, "head", "dp"),
        P(None, None, "dp"),
    )
    return jax.shard_map(
        shards,
        mesh=mesh,
        in_specs=placed,
        out_specs=(
            P(("dp", "head"), None),
            P(("dp", "head"), None),
            P(None, None, "dp"),
            P(None, None, "dp"),
            P(None, "dp", None, "head"),
            P(None, None, "dp"),
            P(None, "head", None),
            P(None, "head", "dp"),
            P(None, "dp", "head"),
            P(None, "dp"),
            P(None, "head", "dp"),
            P(None, None, "dp"),
        ),
        check_vma=False,
    )
```

```python
import functools

import jax
import jax.numpy as jnp
from jax import lax
from jax.experimental import pallas as pl
from jax.experimental.pallas import tpu as pltpu
from jax.sharding import PartitionSpec as P

WSIDE = 7
SHIFT = 3
CROP_MAX = 12
BLOCKS = 2
WTOK = 49
PADDED = 56
STORED = 64
PIECES = 4
VMEM_BYTES = 60 * 2**20

EPSILON = 1e-05
MASKED = -100.0
ABSENT = -1e30
BF16 = jnp.bfloat16
F32 = jnp.float32


def cost(micros):
    return pl.CostEstimate(
        flops=int(micros * 5e9), bytes_accessed=int(micros * 2e7), transcendentals=0
    )


def dot(left, right, left_dim=1, right_dim=0):
    return lax.dot_general(
        left, right, (((left_dim,), (right_dim,)), ((), ())), preferred_element_type=F32
    )


def normalize(values):
    centred = values - jnp.mean(values, axis=-1, keepdims=True)
    scale = lax.rsqrt(jnp.mean(centred * centred, axis=-1, keepdims=True) + EPSILON)
    return centred * scale, scale


def norm_back_rows(values, gain, error):
    normal, scale = normalize(values)
    flow = error * gain
    grad = (
        flow
        - jnp.mean(flow, axis=-1, keepdims=True)
        - normal * jnp.mean(flow * normal, axis=-1, keepdims=True)
    ) * scale
    return grad, jnp.sum(error * normal, axis=0, keepdims=True), jnp.sum(error, axis=0, keepdims=True)


def spread_heads(values, heads):
    columns = values.shape[1]
    owner = lax.broadcasted_iota(jnp.int32, values.shape, 1) // (columns // heads)
    return jnp.concatenate(
        [jnp.where(owner == head, values, 0.0) for head in range(heads)], axis=0
    ).astype(BF16)


def beside_heads(values, heads):
    rows = values.shape[0] // heads
    return jnp.concatenate([values[h * rows : (h + 1) * rows] for h in range(heads)], axis=1)


def below_heads(values, heads):
    columns = values.shape[1] // heads
    parts = [values[:, h * columns : (h + 1) * columns] for h in range(heads)]
    return jnp.concatenate(parts, axis=0)


def stored_rows(values):
    extra = jnp.zeros((STORED - values.shape[0], values.shape[1]), F32)
    return jnp.concatenate([values, extra], axis=0).astype(BF16)


def merge_heads(values, heads):
    rows = values.shape[0] // heads
    columns = values.shape[1]
    owner = lax.broadcasted_iota(jnp.int32, (rows, columns), 1) // (columns // heads)
    total = values[:rows]
    for head in range(1, heads):
        total = jnp.where(owner == head, values[head * rows : (head + 1) * rows], total)
    return total


class Copies:
    def __init__(self, sems):
        self.sems = sems
        self.used = 0
        self.leaving = []

    def plan(self, source, target):
        copy = pltpu.make_async_copy(source, target, self.sems.at[self.used])
        self.used += 1
        return copy

    def send(self, source, target):
        copy = self.plan(source, target)
        copy.start()
        self.leaving.append(copy)

    def finish(self):
        wait_all(self.leaving)


def start_all(*groups):
    for group in groups:
        for item in group:
            item.start()


def choose(weights, picks):
    plan, arrays, rows, first = weights
    chosen = [index for index, (e, _) in enumerate(plan) if e in picks]
    plan = tuple((picks.index(plan[index][0]), plan[index][1], first) for index in chosen)
    return plan, [arrays[index] for index in chosen], rows


def weight_plans(copies, plan, refs, rows, parts):
    own = lax.axis_index("dp")
    plans = {}
    for (slot, rels, first), ref in zip(plan, refs):
        for place, rel in enumerate(rels):
            start = 0 if rel is None else pl.multiple_of(jnp.bitwise_xor(own, rel) * rows, rows)
            for part, target in enumerate(parts):
                plans.setdefault((part, slot), []).append(
                    copies.plan(
                        ref.at[place, pl.ds(first + part * rows, rows), :],
                        target.at[slot, pl.ds(start, rows), :],
                    )
                )
    return plans


def wait_all(items):
    for item in items:
        item.wait()


def weight_copies(plan, parts):
    return parts * sum(len(rels) for _, rels, _ in plan)


def in_any(count):
    return [pl.BlockSpec(memory_space=pl.ANY)] * count


def in_vmem(count):
    return [pl.BlockSpec(memory_space=pltpu.VMEM)] * count


def like(array):
    return pltpu.VMEM(array.shape, array.dtype)


def call(kernel, name, micros, live, small, arrays, outs, scratch, copies):
    return pl.pallas_call(
        kernel,
        in_specs=[pl.BlockSpec(memory_space=pltpu.SMEM)] + in_vmem(len(small)) + in_any(len(arrays)),
        out_specs=tuple(in_any(len(outs))),
        out_shape=tuple(outs),
        scratch_shapes=list(scratch) + [pltpu.SemaphoreType.DMA((copies,))],
        compiler_params=pltpu.CompilerParams(vmem_limit_bytes=VMEM_BYTES),
        cost_estimate=cost(micros),
        name=name,
    )(live, *small, *arrays)


def row_chunks(rows, body, init):
    chunk = 2 * PADDED

    def step(index, carry):
        return body(pl.ds(pl.multiple_of(index * chunk, chunk), chunk), index, carry)

    return lax.fori_loop(0, rows // chunk, step, init)


def live_rows(live_ref, index):
    place = lax.broadcasted_iota(jnp.int32, (2 * PADDED, 1), 0)
    value = jnp.where(place < PADDED, live_ref[2 * index], live_ref[2 * index + 1])
    return jnp.where(lax.rem(place, PADDED) < WTOK, value, 0.0)


def attention_forward_kernel(heads, scale, picks, plan, block_rows, end, *refs):
    count = len(picks)
    live_ref, vec_ref, qv_ref = refs[:3]
    arrays = refs[3 : 6 + 2 * end]
    x_hbm, bias_hbm, mask_hbm = arrays[:3]
    refs = refs[3 + len(arrays) :]
    weight_refs, refs = refs[: len(plan)], refs[len(plan) :]
    outs, refs = refs[: 5 * count + 2], refs[5 * count + 2 :]
    x, bias, mask, total, normed, normed2, weights, qs, ks, vs, ps, atts, sems = refs
    rows = x.shape[0]
    columns = qs.shape[2]
    pairs = rows // (2 * PADDED)
    copies = Copies(sems)
    weight = weight_plans(copies, plan, weight_refs, block_rows, (weights,))
    later = [weight[0, n] for n in range(1, count)]
    later.append([copies.plan(mask_hbm, mask)])
    later[-1] += [copies.plan(bias_hbm.at[e], bias.at[n]) for n, e in enumerate(picks)]
    x_copy = copies.plan(x_hbm, x)
    if end:
        normed_copy = copies.plan(arrays[3], normed)
        late = [x_copy, copies.plan(arrays[4], total)]
        start_all([normed_copy], weight[0, 0])
        normed_copy.wait()
        start_all(*later)
    else:
        start_all([x_copy], weight[0, 0])
        x_copy.wait()
        start_all(*later)

        def first_norm(span, index, _):
            normal, _ = normalize(x[span, :])
            normed[span, :] = (normal * vec_ref[0:1, :] + vec_ref[1:2, :]).astype(BF16)
            return 0

        row_chunks(rows, first_norm, 0)
        copies.send(normed, outs[-1])
    for n, e in enumerate(picks):
        wait_all(weight[0, n])
        qkv = dot(normed[...], weights[n, :, : 3 * columns])
        qs[n] = ((qkv[:, :columns] + qv_ref[e, 0:1, :]) * scale).astype(BF16)
        ks[n] = qkv[:, columns : 2 * columns].astype(BF16)
        vs[n] = (qkv[:, 2 * columns :] + qv_ref[e, 1:2, :]).astype(BF16)
        for index, buffer in enumerate((qs, ks, vs)):
            copies.send(buffer.at[n], outs[5 * n + index])
    wait_all(later[-1])
    if end:
        start_all(late)

    def pair_step(pair, _):
        span = pl.ds(pl.multiple_of(pair * 2 * PADDED, 2 * PADDED), 2 * PADDED)
        for n in range(count):
            query = qs[n, span, :].astype(F32)
            key = ks[n, span, :].astype(F32)
            value = vs[n, span, :].astype(F32)
            results = []
            for side in range(2):
                part = slice(side * PADDED, (side + 1) * PADDED)
                keys = spread_heads(key[part], heads)
                scores = dot(keys, query[part].astype(BF16), 1, 1) + bias[n]
                scores = scores.reshape(heads, PADDED, PADDED) + mask[2 * pair + side][None]
                expo = jnp.exp(scores - jnp.max(scores, axis=1, keepdims=True))
                probs = expo * (1.0 / jnp.sum(expo, axis=1, keepdims=True))
                probs = probs.reshape(heads * PADDED, PADDED)
                ps[n, 2 * pair + side] = stored_rows(beside_heads(probs, heads))
                values = spread_heads(value[part], heads)
                results.append(dot(probs.astype(BF16), values, 0, 0))
            atts[n, span, :] = jnp.concatenate(results, axis=0).astype(BF16)
        return 0

    lax.fori_loop(0, pairs, pair_step, 0)
    for n in range(count):
        copies.send(ps.at[n], outs[5 * n + 3])
        copies.send(atts.at[n], outs[5 * n + 4])
    if end:
        wait_all(late)
    branch = total[...] if end else None
    for n in range(count):
        part = dot(atts[n], weights[n, :, 3 * columns :], 1, 1)
        branch = part if branch is None else branch + part
    total[...] = branch
    if end:

        def second_norm(span, index, _):
            live = live_rows(live_ref, index)
            mixed = x[span, :] + live * (total[span, :] + vec_ref[2:3, :])
            total[span, :] = mixed
            normal, _ = normalize(mixed)
            normed2[span, :] = (normal * vec_ref[3:4, :] + vec_ref[4:5, :]).astype(BF16)
            return 0

        row_chunks(rows, second_norm, 0)
        copies.send(normed2, outs[-1])
    copies.send(total, outs[-2])
    copies.finish()


def attention_forward(
    x, weights, picks, vectors, qv, bias, mask, live, heads, scale, earlier=()
):
    rows, width = x.shape
    columns = qv.shape[2]
    wins = rows // PADDED
    plan, arrays, block_rows = choose(weights, picks)
    count = len(picks)
    end = bool(earlier)
    shape = jax.ShapeDtypeStruct
    piece = shape((rows, columns), BF16)
    probs = shape((wins, STORED, heads * PADDED), BF16)
    results = call(
        functools.partial(attention_forward_kernel, heads, scale, picks, plan, block_rows, end),
        "attention_forward",
        4 + 5 * count,
        live,
        (vectors, qv),
        [x, bias, mask] + list(earlier) + arrays,
        [piece, piece, piece, probs, piece] * count
        + [shape((rows, width), F32), shape((rows, width), BF16)],
        [
            like(x),
            pltpu.VMEM((count,) + bias.shape[1:], F32),
            like(mask),
            pltpu.VMEM((rows, width), F32),
            pltpu.VMEM((rows, width), BF16),
            pltpu.VMEM((rows, width), BF16),
            pltpu.VMEM((count, width, width), BF16),
        ]
        + [pltpu.VMEM((count, rows, columns), BF16)] * 3
        + [
            pltpu.VMEM((count,) + probs.shape, BF16),
            pltpu.VMEM((count, rows, columns), BF16),
        ],
        weight_copies(plan, 1) + 6 * count + 8,
    )
    saved = {e: results[5 * n : 5 * n + 5] for n, e in enumerate(picks)}
    return saved, results[-2], results[-1]


def ffn_forward_kernel(picks, plan, block_rows, end, *refs):
    count = len(picks)
    live_ref, bias_ref, vec_ref = refs[:3]
    arrays, refs = refs[3 : 4 + end], refs[4 + end :]
    weight_refs, refs = refs[: len(plan)], refs[len(plan) :]
    outs, refs = refs[: 2 * count + 1], refs[2 * count + 1 :]
    normed2, mixed, earlier, total, first, second, hidden, slope, sems = refs
    rows = normed2.shape[0]
    copies = Copies(sems)
    arrived = copies.plan(arrays[0], normed2)
    weight = weight_plans(copies, plan, weight_refs, block_rows, (first, second))
    late = [copies.plan(one, to) for one, to in zip(arrays[1:], (mixed, earlier))]
    start_all([arrived], weight[0, 0])
    arrived.wait()
    start_all(weight[1, 0])
    for n, e in enumerate(picks):
        wait_all(weight[0, n])
        if n + 1 < count:
            start_all(weight[0, n + 1], weight[1, n + 1])
        else:
            start_all(late)
        before = dot(normed2[...], first[n]) + bias_ref[e]
        cdf = 0.5 * (1.0 + lax.erf(before * (0.5**0.5)))
        density = jnp.exp(-0.5 * before * before) * 0.3989422804014327
        hidden[n] = (before * cdf).astype(BF16)
        copies.send(hidden.at[n], outs[2 * n])
        slope[n] = (cdf + before * density).astype(BF16)
        copies.send(slope.at[n], outs[2 * n + 1])
        wait_all(weight[1, n])
        part = dot(hidden[n], second[n], 1, 1)
        if n == 0:
            total[...] = part
        else:
            total[...] += part
    wait_all(late)
    if end:

        def finish(span, index, _):
            live = live_rows(live_ref, index)
            value = total[span, :] + vec_ref[5:6, :]
            if end == 2:
                value = value + earlier[span, :]
            total[span, :] = mixed[span, :] + live * value
            return 0

        row_chunks(rows, finish, 0)
    copies.send(total, outs[-1])
    copies.finish()


def ffn_forward(normed2, weights, picks, bias, vectors, live, earlier=()):
    rows, width = normed2.shape
    plan, arrays, block_rows = choose(weights, picks)
    count = len(picks)
    end = len(earlier)
    shape = jax.ShapeDtypeStruct
    piece = shape((rows, width), BF16)
    results = call(
        functools.partial(ffn_forward_kernel, picks, plan, block_rows, end),
        "ffn_forward",
        4 * count,
        live,
        (bias, vectors),
        [normed2] + list(earlier) + arrays,
        [piece, piece] * count + [shape((rows, width), F32)],
        [
            like(normed2),
            pltpu.VMEM((rows, width), F32),
            pltpu.VMEM((rows, width), F32),
            pltpu.VMEM((rows, width), F32),
        ]
        + [pltpu.VMEM((count, width, width), BF16)] * 2
        + [pltpu.VMEM((count, rows, width), BF16)] * 2,
        weight_copies(plan, 2) + 2 * count + 5,
    )
    return {e: results[2 * n : 2 * n + 2] for n, e in enumerate(picks)}, results[-1]


def fill_transposed(target, source, block_rows, tiled):
    flipped = source[...].T
    if not tiled:
        target[...] = flipped
        return
    own = lax.axis_index("dp")
    for block in range(flipped.shape[0] // block_rows):
        start = pl.multiple_of(jnp.bitwise_xor(own, block) * block_rows, block_rows)
        target[pl.ds(start, block_rows), :] = flipped[
            block * block_rows : (block + 1) * block_rows
        ]


def put_blocks(buffer, cuts, block_rows, part, value):
    order = [rel for _, _, rels in cuts for rel in rels]
    for place, rel in enumerate(order):
        start = 0 if rel is None else rel * block_rows
        buffer[place, part * block_rows : (part + 1) * block_rows, :] = value[
            start : start + block_rows
        ].astype(BF16)


def send_blocks(copies, buffer, cuts, block_rows, part, outs):
    place = 0
    rows = pl.ds(part * block_rows, block_rows)
    for index, start, rels in cuts:
        copies.send(
            buffer.at[pl.ds(place, len(rels)), rows, :],
            outs[index].at[pl.ds(start, len(rels)), rows, :],
        )
        place += len(rels)


def block_outs(layout, height, width):
    return [jax.ShapeDtypeStruct((size, height, width), BF16) for size in layout[0]]


def ffn_backward_kernel(picks, plan, block_rows, layout, begin, end, *refs):
    count = len(picks)
    sizes, cuts = layout
    tiled = cuts[0][0][2][0] is not None
    live_ref, vec_ref = refs[:2]
    given = 2 * count + 2 + end + 2 * (not begin)
    arrays, refs = refs[2 : 2 + given], refs[2 + given :]
    weight_refs, refs = refs[: len(plan)], refs[len(plan) :]
    outs, refs = refs[: 5 + len(sizes)], refs[5 + len(sizes) :]
    (
        grad, mixed, branch, error, error_here, attn_grad, normed2, slopes, hiddens, pres, first,
        second, normed2_t, branch_t, results, sums, hidden_sums, sems,
    ) = refs
    rows, width = grad.shape
    blocks_out = outs[5:]
    copies = Copies(sems)
    zero = jnp.zeros((1, width), F32)
    weight = weight_plans(copies, plan, weight_refs, block_rows, (first, second))
    grad_copy = copies.plan(arrays[0], grad)
    slope = [copies.plan(one, slopes.at[n]) for n, one in enumerate(arrays[1 : 1 + count])]
    hidden_hbm = arrays[1 + count : 1 + 2 * count]
    hidden = [copies.plan(one, hiddens.at[n]) for n, one in enumerate(hidden_hbm)]
    normed2_copy = copies.plan(arrays[1 + 2 * count], normed2)
    more = list(arrays[2 + 2 * count :])
    late = [copies.plan(more.pop(0), mixed)] if end else []
    if begin:
        arrived = grad_copy
    else:
        arrived = copies.plan(more[0], branch)
        late += [copies.plan(more[1], error), grad_copy]
    start_all([arrived], weight[1, 0], [slope[0]])
    arrived.wait()
    start_all(weight[0, 0], weight[1, 1], [slope[1]])
    if begin:

        def start(span, index, total):
            part = (live_rows(live_ref, index) * grad[span, :]).astype(BF16)
            branch[span, :] = part
            return total + jnp.sum(part.astype(F32), axis=0, keepdims=True)

        sums[3:4, :] = row_chunks(rows, start, zero)
        if not end:
            copies.send(branch, outs[2])
    fill_transposed(branch_t, branch, block_rows, tiled)
    for n, e in enumerate(picks):
        wait_all(weight[1, n])
        flow = dot(branch[...], second[n])
        slope[n].wait()
        pre = (slopes[n].astype(F32) * flow).astype(BF16)
        pres[n] = pre
        if n + 1 < count:
            start_all(weight[0, n + 1])
            if n + 2 < count:
                start_all(weight[1, n + 2], [slope[n + 2]])
        else:
            start_all([normed2_copy, hidden[0]], late)
        hidden_sums[n] = jnp.sum(pre.astype(F32), axis=0, keepdims=True)
        wait_all(weight[0, n])
        part = dot(pres[n], first[n], 1, 1)
        if n == 0:
            error_here[...] = part
        else:
            error_here[...] += part
    wait_all(late)
    if end:

        def finish(span, index, totals):
            if not begin:
                error_here[span, :] += error[span, :]
            back, gain_part, shift_part = norm_back_rows(
                mixed[span, :], vec_ref[3:4, :], error_here[span, :]
            )
            mixed_grad = grad[span, :] + back
            error_here[span, :] = mixed_grad
            low = (live_rows(live_ref, index) * mixed_grad).astype(BF16)
            attn_grad[span, :] = low
            bias_part = jnp.sum(low.astype(F32), axis=0, keepdims=True)
            return tuple(a + b for a, b in zip(totals, (gain_part, shift_part, bias_part)))

        totals = row_chunks(rows, finish, (zero, zero, zero))
        for index in range(3):
            sums[index : index + 1, :] = totals[index]
        copies.send(attn_grad, outs[1])
    copies.send(error_here, outs[0])
    copies.send(sums, outs[3])
    copies.send(hidden_sums, outs[4])
    normed2_copy.wait()
    fill_transposed(normed2_t, normed2, block_rows, tiled)
    for n in range(count):
        if n + 1 < count:
            hidden[n + 1].start()
        put_blocks(results.at[n], cuts[n], block_rows, 0, dot(normed2_t[...], pres[n]))
        send_blocks(copies, results.at[n], cuts[n], block_rows, 0, blocks_out)
        hidden[n].wait()
        put_blocks(results.at[n], cuts[n], block_rows, 1, dot(branch_t[...], hiddens[n]))
        send_blocks(copies, results.at[n], cuts[n], block_rows, 1, blocks_out)
    copies.finish()


def ffn_backward(
    grad, hidden, normed2, weights, picks, layout, vectors, live, mixed=None, earlier=()
):
    rows, width = grad.shape
    plan, arrays, block_rows = choose(weights, picks)
    count = len(picks)
    end = mixed is not None
    shape = jax.ShapeDtypeStruct
    low = shape((rows, width), BF16)
    wide = shape((rows, width), F32)
    tiny = shape((8, width), F32)
    blocks = block_outs(layout, 2 * block_rows, width)
    results = call(
        functools.partial(
            ffn_backward_kernel, picks, plan, block_rows, layout, not earlier, end
        ),
        "ffn_backward",
        7 * count,
        live,
        (vectors,),
        [grad]
        + [hidden[e][1] for e in picks]
        + [hidden[e][0] for e in picks]
        + [normed2]
        + [mixed] * end
        + list(earlier)
        + arrays,
        [wide, low if end else tiny, tiny if end else low, tiny, shape((count, 1, width), F32)]
        + blocks,
        [like(wide), like(wide), like(low), like(wide), like(wide), like(low), like(low)]
        + [pltpu.VMEM((count, rows, width), BF16)] * 3
        + [pltpu.VMEM((count, width, width), BF16)] * 2
        + [pltpu.VMEM((width, rows), BF16)] * 2
        + [pltpu.VMEM((count, width // block_rows, 2 * block_rows, width), BF16)]
        + [pltpu.VMEM((8, width), F32), pltpu.VMEM((count, 1, width), F32)],
        weight_copies(plan, 2) + 2 * count + 9 + 4 * len(blocks) + 4,
    )
    return *results[:5], results[5:]


def ffn_both_kernel(picks, plan, block_rows, layout, *refs):
    count = len(picks)
    sizes, cuts = layout
    tiled = cuts[0][0][2][0] is not None
    live_ref, bias_ref, vec_ref = refs[:3]
    normed2_hbm, mixed_hbm, grad_hbm = refs[3:6]
    refs = refs[6:]
    weight_refs, refs = refs[: len(plan)], refs[len(plan) :]
    outs, refs = refs[:5], refs[5:]
    blocks_out, refs = refs[: len(sizes)], refs[len(sizes) :]
    (
        normed2, mixed, grad, total, error, branch, attn_grad, hiddens, pres, first, second,
        normed2_t, branch_t, results, sums, hidden_sums, sems,
    ) = refs
    rows, width = grad.shape
    copies = Copies(sems)
    zero = jnp.zeros((1, width), F32)
    weight = weight_plans(copies, plan, weight_refs, block_rows, (first, second))
    grad_copy = copies.plan(grad_hbm, grad)
    normed2_copy = copies.plan(normed2_hbm, normed2)
    mixed_copy = copies.plan(mixed_hbm, mixed)
    start_all([normed2_copy], weight[0, 0])
    normed2_copy.wait()
    start_all([grad_copy], weight[1, 0])
    fill_transposed(normed2_t, normed2, block_rows, tiled)
    for n, e in enumerate(picks):
        wait_all(weight[0, n])
        before = dot(normed2[...], first[n]) + bias_ref[e]
        if n + 1 < count:
            start_all(weight[0, n + 1], weight[1, n + 1])
        else:
            start_all([mixed_copy])
        cdf = 0.5 * (1.0 + lax.erf(before * (0.5**0.5)))
        density = jnp.exp(-0.5 * before * before) * 0.3989422804014327
        hiddens[n] = (before * cdf).astype(BF16)
        slope = cdf + before * density
        if n == 0:
            grad_copy.wait()

            def start(span, index, carry):
                part = (live_rows(live_ref, index) * grad[span, :]).astype(BF16)
                branch[span, :] = part
                return carry + jnp.sum(part.astype(F32), axis=0, keepdims=True)

            sums[3:4, :] = row_chunks(rows, start, zero)
            fill_transposed(branch_t, branch, block_rows, tiled)
        wait_all(weight[1, n])
        pre = (slope * dot(branch[...], second[n])).astype(BF16)
        pres[n] = pre
        hidden_sums[n] = jnp.sum(pre.astype(F32), axis=0, keepdims=True)
        part = dot(hiddens[n], second[n], 1, 1)
        back = dot(pres[n], first[n], 1, 1)
        if n == 0:
            total[...] = part
            error[...] = back
        else:
            total[...] += part
            error[...] += back
    mixed_copy.wait()

    def finish(span, index, totals):
        live = live_rows(live_ref, index)
        values = mixed[span, :]
        total[span, :] = values + live * (total[span, :] + vec_ref[5:6, :])
        back, gain_part, shift_part = norm_back_rows(values, vec_ref[3:4, :], error[span, :])
        mixed_grad = grad[span, :] + back
        error[span, :] = mixed_grad
        low = (live * mixed_grad).astype(BF16)
        attn_grad[span, :] = low
        bias_part = jnp.sum(low.astype(F32), axis=0, keepdims=True)
        return tuple(a + b for a, b in zip(totals, (gain_part, shift_part, bias_part)))

    totals = row_chunks(rows, finish, (zero, zero, zero))
    for index in range(3):
        sums[index : index + 1, :] = totals[index]
    for buffer, out in zip((total, error, attn_grad, sums, hidden_sums), outs):
        copies.send(buffer, out)
    for n in range(count):
        put_blocks(results.at[n], cuts[n], block_rows, 0, dot(normed2_t[...], pres[n]))
        send_blocks(copies, results.at[n], cuts[n], block_rows, 0, blocks_out)
        put_blocks(results.at[n], cuts[n], block_rows, 1, dot(branch_t[...], hiddens[n]))
        send_blocks(copies, results.at[n], cuts[n], block_rows, 1, blocks_out)
    copies.finish()


def ffn_both(normed2, mixed, grad, weights, picks, layout, bias, vectors, live):
    rows, width = grad.shape
    plan, arrays, block_rows = choose(weights, picks)
    count = len(picks)
    shape = jax.ShapeDtypeStruct
    low = shape((rows, width), BF16)
    wide = shape((rows, width), F32)
    blocks = block_outs(layout, 2 * block_rows, width)
    results = call(
        functools.partial(ffn_both_kernel, picks, plan, block_rows, layout),
        "ffn_both",
        30,
        live,
        (bias, vectors),
        [normed2, mixed, grad] + arrays,
        [wide, wide, low, shape((8, width), F32), shape((count, 1, width), F32)] + blocks,
        [like(low), like(wide), like(wide), like(wide), like(wide), like(low), like(low)]
        + [pltpu.VMEM((count, rows, width), BF16)] * 2
        + [pltpu.VMEM((count, width, width), BF16)] * 2
        + [pltpu.VMEM((width, rows), BF16)] * 2
        + [pltpu.VMEM((count, width // block_rows, 2 * block_rows, width), BF16)]
        + [pltpu.VMEM((8, width), F32), pltpu.VMEM((count, 1, width), F32)],
        weight_copies(plan, 2) + 8 + 4 * len(blocks) + 4,
    )
    return *results[:5], results[5:]


def attention_backward_kernel(heads, scale, picks, plan, block_rows, layout, end, *refs):
    count = len(picks)
    sizes, cuts = layout
    tiled = cuts[0][0][2][0] is not None
    live_ref, vec_ref = refs[:2]
    given = 2 + 5 * count + 3 * end
    arrays, refs = refs[2 : 2 + given], refs[2 + given :]
    weight_refs, refs = refs[: len(plan)], refs[len(plan) :]
    outs_count = 3 + end + len(sizes)
    outs, refs = refs[:outs_count], refs[outs_count:]
    (
        attn_grad, normed, x, mixed_grad, error, weights, qs, ks, vs, atts, ps, gs, grads,
        normed_t, attn_grad_t, results, scores_sum, scores_out, sums, small, sems,
    ) = refs
    rows, width = attn_grad.shape
    columns = qs.shape[2]
    pairs = rows // (2 * PADDED)
    copies = Copies(sems)
    weight = weight_plans(copies, plan, weight_refs, block_rows, (weights,))
    arrived = copies.plan(arrays[0], attn_grad)
    saved = [
        copies.plan(arrays[2 + 5 * n + index], buffer.at[n])
        for n in range(count)
        for index, buffer in ((0, qs), (1, ks), (2, vs), (3, ps))
    ]
    late = [copies.plan(arrays[1], normed)]
    for n in range(count):
        late.append(copies.plan(arrays[2 + 5 * n + 4], atts.at[n]))
    if end:
        for one, to in zip(arrays[2 + 5 * count :], (x, mixed_grad, error)):
            late.append(copies.plan(one, to))
    start_all([arrived], weight[0, 0])
    arrived.wait()
    start_all(*[weight[0, n] for n in range(1, count)], saved)
    scores_sum[...] = jnp.zeros(scores_sum.shape, F32)
    fill_transposed(attn_grad_t, attn_grad, block_rows, tiled)
    for n in range(count):
        wait_all(weight[0, n])
        gs[n] = dot(attn_grad[...], weights[n, :, 3 * columns :]).astype(BF16)
    wait_all(saved)
    start_all(late)

    def pair_step(pair, _):
        span = pl.ds(pl.multiple_of(pair * 2 * PADDED, 2 * PADDED), 2 * PADDED)
        for n in range(count):
            query, key, value, grad = [
                buffer[n, span, :].astype(F32) for buffer in (qs, ks, vs, gs)
            ]
            rows_out = []
            for side in range(2):
                part = slice(side * PADDED, (side + 1) * PADDED)
                queries = spread_heads(query[part], heads)
                grads_out = spread_heads(grad[part], heads)
                probs = ps[n, 2 * pair + side].astype(F32)[:PADDED]
                flow = dot(value[part].astype(BF16), grads_out, 1, 1)
                inner = jnp.sum(probs * flow, axis=0, keepdims=True)
                score = (probs * (flow - inner)).astype(BF16)
                scores_sum[n] += score.astype(F32)
                query_part = dot(score, key[part].astype(BF16), 0, 0)
                rows_out.append(
                    jnp.concatenate(
                        [
                            merge_heads(query_part, heads) * scale,
                            dot(score, queries),
                            dot(probs.astype(BF16), grads_out),
                        ],
                        axis=1,
                    )
                )
            grads[n, span, :] = jnp.concatenate(rows_out, axis=0).astype(BF16)
        return 0

    lax.fori_loop(0, pairs, pair_step, 0)
    for n in range(count):
        scores_out[n] = below_heads(scores_sum[n], heads)
    copies.send(scores_out, outs[1])
    wait_all(late)
    for n in range(count):
        sums[n] = jnp.sum(grads[n].astype(F32), axis=0, keepdims=True)
        part = dot(grads[n], weights[n, :, : 3 * columns], 1, 1)
        if n == 0 and not end:
            error[...] = part
        else:
            error[...] += part
    copies.send(sums, outs[2])
    if end:
        zero = jnp.zeros((1, width), F32)

        def finish(span, index, totals):
            back, gain_part, shift_part = norm_back_rows(
                x[span, :], vec_ref[0:1, :], error[span, :]
            )
            error[span, :] = mixed_grad[span, :] + back
            return totals[0] + gain_part, totals[1] + shift_part

        totals = row_chunks(rows, finish, (zero, zero))
        for index in range(2):
            small[index : index + 1, :] = totals[index]
        copies.send(small, outs[3])
    copies.send(error, outs[0])
    fill_transposed(normed_t, normed, block_rows, tiled)
    for n in range(count):
        value = jnp.concatenate(
            [dot(normed_t[...], grads[n]), dot(attn_grad_t[...], atts[n])], axis=1
        )
        put_blocks(results.at[n], cuts[n], block_rows, 0, value)
        send_blocks(copies, results.at[n], cuts[n], block_rows, 0, outs[3 + end :])
    copies.finish()


def attention_backward(
    attn_grad, normed, saved, weights, picks, layout, vectors, live, heads, scale, earlier=()
):
    rows, width = attn_grad.shape
    columns = saved[picks[0]][0].shape[1]
    plan, arrays, block_rows = choose(weights, picks)
    count = len(picks)
    end = bool(earlier)
    probs = saved[picks[0]][3]
    shape = jax.ShapeDtypeStruct
    wide = shape((rows, width), F32)
    pieces = [item for e in picks for item in saved[e]]
    outs = [
        wide,
        shape((count, heads * PADDED, PADDED), F32),
        shape((count, 1, 3 * columns), F32),
    ]
    blocks = block_outs(layout, block_rows, width)
    results = call(
        functools.partial(
            attention_backward_kernel, heads, scale, picks, plan, block_rows, layout, end
        ),
        "attention_backward",
        19,
        live,
        (vectors,),
        [attn_grad, normed] + pieces + list(earlier) + arrays,
        outs + [shape((8, width), F32)] * end + blocks,
        [like(attn_grad), like(normed), like(wide), like(wide), like(wide)]
        + [pltpu.VMEM((count, width, width), BF16)]
        + [pltpu.VMEM((count, rows, columns), BF16)] * 4
        + [pltpu.VMEM((count,) + probs.shape, BF16)]
        + [pltpu.VMEM((count, rows, columns), BF16)]
        + [pltpu.VMEM((count, rows, 3 * columns), BF16)]
        + [pltpu.VMEM((width, rows), BF16)] * 2
        + [pltpu.VMEM((count, width // block_rows, block_rows, width), BF16)]
        + [pltpu.VMEM((count, PADDED, heads * PADDED), F32), like(outs[1]), like(outs[2])]
        + [pltpu.VMEM((8, width), F32)],
        weight_copies(plan, 1) + 5 * count + 11 + 4 * len(blocks),
    )
    return *results[: 3 + end], results[3 + end :]


def swap(values, axis, bit):
    size = lax.axis_size(axis)
    return lax.ppermute(values, axis, [(i, i ^ (1 << bit)) for i in range(size)])


def bits_in(axis):
    return lax.axis_size(axis).bit_length() - 1


def pick(values, index, dim):
    return lax.dynamic_index_in_dim(values, index, dim, keepdims=False)


def tie(values, token):
    if token is None:
        return values
    return lax.optimization_barrier((values, token))[0]


def whole_tiles(rows):
    return rows % 16 == 0


def in_order(values):
    index = jnp.bitwise_xor(jnp.arange(values.shape[0]), lax.axis_index("dp"))
    return jnp.take(values, index, axis=0)


def relatives(halves):
    count = lax.axis_size("dp")
    size = count // halves
    return [
        [tuple(range(part * size + side, (part + 1) * size, 2)) for part in range(halves)]
        for side in range(2)
    ]


def line_bits():
    return list(range(1, bits_in("dp")))


def straight(values):
    size = lax.axis_size("dp")
    low, high = [1 << bit for bit in line_bits()[-2:]]
    return [
        lax.ppermute(values(n), "dp", [(i, i ^ shift) for i in range(size)])
        for n, shift in ((1, low), (2, high), (3, low | high))
    ]


class Gather:
    def __init__(self, shard, parts, rows, ways):
        self.shard = shard
        self.parts = parts
        self.rows = rows
        self.ways = ways
        self.entries = []

    def line(self, after=None, at_once=False):
        held = tie(self.shard, after)[None]
        bits = line_bits()
        for bit in bits[:-2]:
            held = jnp.concatenate([held, swap(held, "dp", bit)])
        self.moved = straight(lambda n: held) if at_once else [swap(held, "dp", bits[-2])]
        self.held = [held]

    def line_end(self, until=None):
        moved = tie(self.moved, until)
        self.held = [jnp.concatenate(self.held + moved)]
        return self.held[0]

    def last(self, after=None):
        self.moved = swap(tie(self.held[0], after), "dp", line_bits()[-1])

    def last_end(self, until=None):
        moved = tie(self.moved, until)
        self.held.append(moved)
        if len(self.ways) == 1:
            self.held = [jnp.concatenate(self.held)]
        return self.held[-1]

    def sides(self, part, after=None):
        if part == 0:
            self.side, self.far = [], []
        held = tie(self.held[part], after)
        self.side.append(swap(held, "dp", 0))
        self.far.append(swap(held, "head", 1))

    def sides_end(self, part, until=None):
        self.side[part], self.far[part] = tie((self.side[part], self.far[part]), until)
        return self.side[part], self.far[part]

    def corner(self, part, after=None):
        if part == 0:
            self.corners = []
        if self.ways[part] == "x":
            self.corners.append(swap(tie(self.side[part], after), "head", 1))
        else:
            self.corners.append(swap(tie(self.far[part], after), "dp", 0))

    def corner_end(self, part, until=None):
        self.corners[part] = tie(self.corners[part], until)
        return self.corners[part]

    def core(self, kind, part=None):
        own, other = relatives(len(self.ways))
        arrays, e, rels = {
            "held": (self.held, 0, own),
            "side": (getattr(self, "side", None), 0, other),
            "far": (getattr(self, "far", None), 2, own),
            "corner": (getattr(self, "corners", None), 2, other),
        }[kind]
        for n, (one, several) in enumerate(zip(arrays, rels)):
            if part is None or part == n:
                self.entries.append((e, one, several))
                self.entries.append((e + 1, swap(one, "head", 0), several))

    def result(self, first=0):
        rows, parts = self.rows, self.parts
        width = self.shard.shape[1]
        if whole_tiles(rows):
            plan = tuple((e, rels) for e, _, rels in self.entries)
            return plan, [one for _, one, _ in self.entries], rows, first * rows
        arrays = []
        plan = []
        for e in range(PIECES):
            mine = [(one, rels) for piece, one, rels in self.entries if piece == e]
            if not mine:
                continue
            order = sum((rels for _, rels in mine), ())
            if len(order) < lax.axis_size("dp"):
                continue
            blocks = jnp.concatenate([one[:, : parts * rows] for one, _ in mine])
            blocks = in_order(blocks[jnp.argsort(jnp.array(order))])
            blocks = blocks.reshape(-1, parts, rows, width).transpose(1, 0, 2, 3)
            arrays.append(blocks.reshape(1, -1, width))
            plan.append((e, (None,)))
        rows = arrays[0].shape[1] // parts
        return tuple(plan), arrays, rows, first * rows


def wide(*values):
    total = values[0].astype(F32)
    for value in values[1:]:
        total = total + value.astype(F32)
    return total


def plus(*values):
    return wide(*values).astype(BF16)


class Scatter:
    def __init__(self, parts, rows, ways):
        self.parts = parts
        self.rows = rows
        self.ways = ways
        self.tiled = whole_tiles(rows)
        blocks = lax.axis_size("dp")
        half = blocks // 2
        even = tuple(range(0, blocks, 2))
        odd = tuple(range(1, blocks, 2))
        cut = half // len(ways)
        corners = [odd[n * cut : (n + 1) * cut] for n in range(len(ways))]
        self.order = even + odd
        if self.tiled:
            self.away_layout = (
                (2 * blocks,),
                (((0, 0, self.order),), ((0, blocks, self.order),)),
            )
            last = tuple((3 + n, 0, rels) for n, rels in enumerate(corners))
            self.near_layout = (
                (half,) * 3 + (cut,) * len(ways),
                (((0, 0, even), (1, 0, odd)), ((2, 0, even),) + last),
            )
        else:
            one = ((0, 0, (None,)),)
            two = ((0, 1, (None,)),)
            self.away_layout = self.near_layout = ((2,), (one, two))

    def both_layouts(self):
        sizes, cuts = self.near_layout
        first = len(self.away_layout[0])
        moved = tuple(
            tuple((first + index, start, rels) for index, start, rels in one) for one in cuts
        )
        return self.away_layout[0] + sizes, self.away_layout[1] + moved

    def arrange(self, outs):
        one = outs[0].reshape(2, self.parts, -1, self.rows, outs[0].shape[-1])
        one = one.transpose(0, 2, 1, 3, 4)
        one = one.reshape(one.shape[:2] + (-1, one.shape[-1]))
        return jnp.concatenate([in_order(item)[jnp.array(self.order)] for item in one])

    def away(self, outs):
        self.moved = swap(outs[0] if self.tiled else self.arrange(outs), "head", 0)

    def near(self, outs, until=None):
        moved = tie(self.moved, until)
        half = moved.shape[0] // 4
        if self.tiled:
            own = list(outs)
        else:
            one = self.arrange(outs)
            own = [one[n * half : (n + 1) * half] for n in range(3)]
            cut = half // len(self.ways)
            own += [one[3 * half + n * cut :][:cut] for n in range(len(self.ways))]
        cut = half // len(self.ways)
        self.held = [own[0], moved[:half]]
        self.side = [own[1], moved[half : 2 * half]]
        self.far = [own[2], moved[2 * half : 3 * half]]
        self.corners = [
            plus(own[3 + n], moved[3 * half + n * cut :][:cut]) for n in range(len(self.ways))
        ]
        return self.corners

    def corner(self, after=None):
        self.moved = []
        for way, one in zip(self.ways, tie(self.corners, after)):
            self.moved.append(swap(one, "head", 1) if way == "x" else swap(one, "dp", 0))

    def corner_end(self, until=None):
        moved = tie(self.moved, until)
        half = self.side[0].shape[0]
        for part, (way, one) in enumerate(zip(self.ways, moved)):
            size = one.shape[0]
            around = (part * size, half - (part + 1) * size)
            one = jnp.pad(one, (around,) + ((0, 0),) * 2) if size < half else one
            (self.side if way == "x" else self.far).append(one)
        self.side, self.far = plus(*self.side), plus(*self.far)
        return self.side, self.far

    def sides(self, after=None, part=None):
        side, far = tie((self.side, self.far), after)
        if part is not None:
            size = side.shape[0] // 2
            side, far = [one[part * size : (part + 1) * size] for one in (side, far)]
        self.moved = [swap(side, "dp", 0), swap(far, "head", 1)]

    def sides_end(self, until=None, at_once=False, part=None):
        moved = list(tie(self.moved, until))
        if part == 0:
            self.lower = moved
            return moved
        if part == 1:
            size = moved[0].shape[0]
            self.held = [
                plus(*[one[n * size : (n + 1) * size] for one in self.held], *several)
                for n, several in enumerate((self.lower, moved))
            ]
            return self.held
        terms = self.held + moved
        count = 4 if at_once else 2
        size = terms[0].shape[0] // count
        self.held = [
            plus(*[one[n * size : (n + 1) * size] for one in terms]) for n in range(count)
        ]
        return self.held

    def last(self, after=None):
        self.moved = swap(tie(self.held[1], after), "dp", line_bits()[-1])

    def last_end(self, until=None):
        moved = tie(self.moved, until)
        size = moved.shape[0] // 2
        terms = [self.held[0], moved]
        self.held = [plus(*[one[n * size :][:size] for one in terms]) for n in range(2)]
        return self.held

    def line(self, after=None):
        held = tie(self.held, after)
        if len(held) == 4:
            self.moved = straight(lambda n: held[n])
        else:
            self.moved = [swap(held[1], "dp", line_bits()[-2])]

    def line_end(self, until=None):
        held = wide(self.held[0], *tie(self.moved, until))
        for bit in reversed(line_bits()[:-2]):
            cut = held.shape[0] // 2
            moved = swap(held[cut:].astype(BF16), "dp", bit)
            held = wide(held[:cut], moved)
        self.result = held[0]
        return self.result


class SmallSum:
    def __init__(self, values):
        self.total = values
        self.left = [("head", 0), ("head", 1)]
        self.left += [("dp", bit) for bit in range(bits_in("dp"))]
        self.moved = None

    def step(self, until=None):
        self.result(until)
        axis, bit = self.left.pop(0)
        self.moved = swap(self.total, axis, bit)

    def end(self):
        return not self.left

    def result(self, until=None):
        if self.moved is not None:
            self.total = self.total + tie(self.moved, until)
        self.moved = None
        return self.total


def unshift(values):
    grid = values.reshape(values.shape[:-1] + (WSIDE, WSIDE))
    return jnp.roll(grid, (SHIFT, SHIFT), axis=(-2, -1)).reshape(values.shape)


def pad_rows(values):
    grid = values.reshape(-1, WTOK, values.shape[1])
    grid = jnp.pad(grid, ((0, 0), (0, PADDED - WTOK), (0, 0)))
    return grid.reshape(-1, values.shape[1])


def drop_rows(values):
    grid = values.reshape(-1, PADDED, values.shape[1])[:, :WTOK]
    return grid.reshape(-1, values.shape[1])


def attention_mask(pad, region):
    allowed = (pad[:, :, None] == 1) & (region[:, :, None] == region[:, None, :])
    mask = jnp.where(allowed, 0.0, MASKED).astype(F32)
    extra = PADDED - WTOK
    mask = jnp.pad(mask, ((0, 0), (0, 0), (0, extra)))
    return jnp.pad(mask, ((0, 0), (0, extra), (0, 0)), constant_values=ABSENT)


def shards(
    tokens,
    cotangent,
    crop_counts,
    pad_mask,
    region_ids,
    rel_index,
    norm_gain,
    norm_shift,
    qkv_weight,
    qv_bias,
    bias_table,
    proj_weight,
    fc1_weight,
    fc1_bias,
    fc2_weight,
    out_bias,
):
    rows = tokens.shape[0]
    width = tokens.shape[1]
    wins = rows // WTOK
    local_width = qkv_weight.shape[3]
    local_heads = bias_table.shape[1]
    rel_count = bias_table.shape[2]
    dp_width = norm_gain.shape[2]
    dp_hidden = fc1_bias.shape[1]
    pieces = lax.axis_size("head")
    heads_total = local_heads * pieces
    head_dim = local_width // local_heads
    scale = head_dim ** (-0.5)
    head_index = lax.axis_index("head")
    dp_index = lax.axis_index("dp")
    relative = [head_index ^ e for e in range(pieces)]

    shard_rows = qkv_weight.shape[1]
    attn_shards = [
        jnp.concatenate(
            [qkv_weight[block].reshape(-1, 3 * local_width), proj_weight[block].T], axis=1
        )
        for block in range(BLOCKS)
    ]
    ffn_shards = [
        jnp.concatenate([fc1_weight[block], fc2_weight[block].T]) for block in range(BLOCKS)
    ]
    small = jnp.concatenate([norm_gain, norm_shift, qv_bias, out_bias]).reshape(-1, dp_width)
    small_rows = small.shape[0]
    beside = -(-dp_width // 128) * 128
    small = jnp.pad(small, ((0, 0), (0, width - dp_width)))
    small = small + jnp.pad(
        fc1_bias, ((0, small_rows - BLOCKS), (beside, width - beside - dp_hidden))
    )
    attn_shards[0] = jnp.concatenate([attn_shards[0], small])
    near, away = (0, 2), (1, 3)
    first, second = (0, 1), (2, 3)
    a0 = Gather(attn_shards[0], 1, shard_rows, "y")
    middle = Gather(jnp.concatenate([ffn_shards[0], attn_shards[1]]), 3, shard_rows, "xy")
    f1 = Gather(ffn_shards[1], 2, shard_rows, "xy")

    def attn_weights(block):
        return middle.result(2) if block else a0.result()

    def ffn_weights(block):
        return f1.result() if block else middle.result()

    a0.line(at_once=True)
    far_table = swap(bias_table, "head", 1)
    near_table = swap(bias_table, "head", 0)
    a0.line_end()
    a0.sides(0)
    middle.line(a0.held)
    a0.core("held")
    middle.line_end()
    middle.core("held", 0)
    middle.last()
    a0.sides_end(0)
    a0.core("side")
    a0.core("far")
    a0.corner(0)
    middle.sides(0, a0.far)
    table_pieces = [bias_table, near_table, far_table, swap(far_table, "head", 0)]
    small_all = jnp.stack([a0.held[0][:, shard_rows:], a0.side[0][:, shard_rows:]], axis=1)
    small_all = in_order(small_all.reshape((-1,) + small.shape)).transpose(1, 0, 2).astype(F32)
    every = small_all[:, :, :dp_width].reshape(4, BLOCKS, 2, width)
    gains, shifts, qv_all, out_all = every[0], every[1], every[2], every[3]
    hidden_bias = small_all[:BLOCKS, :, beside : beside + dp_hidden].reshape(BLOCKS, pieces, -1)
    qv_pieces = qv_all.reshape(BLOCKS, 2, pieces, local_width)

    counts = jnp.repeat(crop_counts, CROP_MAX)
    slots = jnp.arange(pad_mask.shape[0], dtype=jnp.int32) % CROP_MAX
    live_all = (slots < counts).astype(F32)
    live_windows = lax.dynamic_slice_in_dim(live_all, head_index * wins, wins, 0)
    live = live_windows
    pad = lax.dynamic_slice_in_dim(pad_mask, head_index * wins, wins, 0)
    region = unshift(lax.dynamic_slice_in_dim(region_ids, head_index * wins, wins, 0))
    masks = (attention_mask(pad, jnp.zeros_like(region)), attention_mask(pad, region))
    extra = PADDED - WTOK
    onehots = []
    for index in (rel_index, unshift(unshift(rel_index).T).T):
        by_key = jnp.pad(index.T, ((0, extra), (0, extra)), constant_values=-1).reshape(1, -1)
        ids = jnp.arange(rel_count, dtype=jnp.int32)[:, None]
        onehots.append((ids == by_key).astype(BF16))

    def ordered(values, dim):
        return jnp.stack([pick(values, rel, dim) for rel in relative])

    block_rows = local_heads * PADDED
    vectors, qv, biases, hidden_biases = [], [], [], []
    for block in range(BLOCKS):
        rows8 = [
            gains[block, 0],
            shifts[block, 0],
            out_all[block, 0],
            gains[block, 1],
            shifts[block, 1],
            out_all[block, 1],
        ]
        vectors.append(jnp.pad(jnp.stack(rows8), ((0, 2), (0, 0))))
        qv.append(ordered(qv_pieces[block], 1))
        table = jnp.concatenate([one[block] for one in table_pieces])
        bias = jnp.dot(table, onehots[block % 2], preferred_element_type=F32)
        biases.append(bias.reshape(pieces, block_rows, PADDED))
        hidden_biases.append(ordered(hidden_bias[block], 0)[:, None, :])

    residual = pad_rows(tokens).astype(F32)

    def attend(block, x, picks, token, earlier=()):
        return attention_forward(
            x,
            attn_weights(block),
            picks,
            tie(vectors[block], token),
            qv[block],
            biases[block],
            masks[block % 2],
            live,
            local_heads,
            scale,
            earlier,
        )

    def feed(block, normed2, picks, token, earlier=()):
        return ffn_forward(
            normed2,
            ffn_weights(block),
            picks,
            hidden_biases[block],
            tie(vectors[block], token),
            live,
            earlier,
        )

    x0 = residual
    grad_rows = pad_rows(cotangent).astype(F32)
    token = (middle.held[0], biases[1], masks[1], grad_rows)
    saved_0, branch, normed_0 = attend(0, x0, first, token)
    a0.corner_end(0, branch)
    a0.core("corner")
    middle.sides_end(0, branch)
    middle.core("side", 0)
    middle.core("far", 0)
    middle.corner(0)
    middle.last_end(branch)
    middle.sides(1)
    f1.line(middle.held[1])
    f1.line_end()
    f1.last()
    token = (middle.held[1], f1.held[0])
    more, mixed_0, normed2_0 = attend(0, x0, second, token, (normed_0, branch))
    saved_0.update(more)
    middle.sides_end(1, mixed_0)
    middle.corner(1)
    f1.last_end(mixed_0)
    middle.held[1] = tie(middle.held[1], f1.held[1])
    middle.core("held", 1)
    middle.core("side", 1)
    middle.core("far", 1)
    middle.corner_end(0, mixed_0)
    middle.corner_end(1, mixed_0)
    middle.core("corner")
    f1.sides(0, middle.corners)
    f1.sides(1, middle.corners)
    hidden_0, x1 = feed(0, normed2_0, first + second, middle.corners, (mixed_0,))
    f1.sides_end(0, x1)
    f1.core("held")
    f1.core("side", 0)
    saved_1, branch, normed_1 = attend(1, x1, first, (f1.side[0], f1.far[0]))
    f1.sides_end(1, branch)
    f1.corner(0)
    f1.corner(1)
    f1.core("side", 1)
    f1.core("far")
    token = (f1.side, f1.far)
    more, mixed_1, normed2_1 = attend(1, x1, second, token, (normed_1, branch))
    saved_1.update(more)
    f1.corner_end(0, mixed_1)
    f1.corner_end(1, mixed_1)
    f1.core("corner")
    kept = [
        (x0, mixed_0, normed_0, normed2_0, saved_0, hidden_0),
        (x1, mixed_1, normed_1, normed2_1, saved_1, None),
    ]

    def feed_back(block, picks, layout, grad, token, mixed=None, earlier=()):
        _, _, _, normed2, _, hidden = kept[block]
        return ffn_backward(
            grad,
            hidden,
            normed2,
            ffn_weights(block),
            picks,
            layout,
            tie(vectors[block], token),
            live,
            mixed,
            earlier,
        )

    def attend_back(block, picks, layout, attn_grad, token, earlier=()):
        _, _, normed, _, saved, _ = kept[block]
        return attention_backward(
            attn_grad,
            normed,
            saved,
            attn_weights(block),
            picks,
            layout,
            tie(vectors[block], token),
            live,
            local_heads,
            scale,
            earlier,
        )

    def small_terms(block, attn, small_f, hidden_terms):
        scores_a, sums_a, scores_n, sums_n, small_a = attn

        def together(one, other):
            return ordered(jnp.stack([one[0], other[0], one[1], other[1]]), 0)

        table_grad = lax.dot_general(
            together(scores_n, scores_a).reshape(heads_total, -1),
            onehots[block % 2].astype(F32),
            (((1,), (1,)), ((), ())),
            precision=lax.Precision.HIGHEST,
            preferred_element_type=F32,
        )
        table_grad = jnp.pad(table_grad, ((0, 0), (0, table_lanes - rel_count)))
        qv_sums = together(sums_n, sums_a)[:, 0]
        items = [
            small_a[0:1],
            small_f[0:1],
            small_a[1:2],
            small_f[1:2],
            qv_sums[:, :local_width].reshape(1, width),
            qv_sums[:, 2 * local_width :].reshape(1, width),
            small_f[2:4],
            together(*hidden_terms)[:, 0],
            table_grad.reshape(-1, width),
        ]
        return jnp.concatenate(items)

    table_lanes = 2 * 128
    f1_sum, f0_sum = [Scatter(2, shard_rows, "xy") for _ in range(2)]
    a1_sum, a0_sum = [Scatter(1, shard_rows, "xy") for _ in range(2)]
    residual, mixed_grad, attn_grad, small_f, hidden_sums, outs = ffn_both(
        normed2_1,
        mixed_1,
        grad_rows,
        ffn_weights(1),
        away + near,
        f1_sum.both_layouts(),
        hidden_biases[1],
        tie(vectors[1], mixed_1),
        live,
    )
    count = len(f1_sum.away_layout[0])
    f1_sum.away(outs[:count])
    error, scores_a, sums_a, sent = attend_back(1, away, a1_sum.away_layout, attn_grad, None)
    f1_sum.near(outs[count:], error)
    f1_sum.corner()
    a1_sum.away(sent)
    grad_rows, scores_n, sums_n, small_a, outs = attend_back(
        1, near, a1_sum.near_layout, attn_grad, f1_sum.corners, (x1, mixed_grad, error)
    )
    late_terms = (scores_a, sums_a, scores_n, sums_n, small_a), small_f, hidden_sums
    token = f1_sum.corner_end(grad_rows)
    f1_sum.sides(part=0)
    a1_sum.near(outs, grad_rows)
    error, _, branch_grad, small_b, hidden_a, sent = feed_back(
        0, away, f0_sum.away_layout, grad_rows, (token, a1_sum.corners)
    )
    f0_sum.away(sent)
    token = f1_sum.sides_end(error, part=0)
    f1_sum.sides(token, part=1)
    a1_sum.corner(token)
    mixed_grad, attn_grad, _, small_f, hidden_n, outs = feed_back(
        0,
        near,
        f0_sum.near_layout,
        grad_rows,
        (error, token),
        mixed_0,
        (branch_grad, error),
    )
    small_f = jnp.concatenate([small_f[:3], small_b[3:4]])
    token = (f1_sum.sides_end(attn_grad, part=1), a1_sum.corner_end(attn_grad))
    f1_sum.last()
    a1_sum.sides()
    f0_sum.near(outs, attn_grad)
    f0_sum.corner()
    error, scores_a, sums_a, sent = attend_back(
        0, away, a0_sum.away_layout, attn_grad, (token, f0_sum.corners)
    )
    a0_sum.away(sent)
    token = (f0_sum.corner_end(error), a1_sum.sides_end(error), f1_sum.last_end(error))
    f0_sum.sides()
    a1_sum.last()
    f1_sum.line()
    grad_rows, scores_n, sums_n, small_a, outs = attend_back(
        0, near, a0_sum.near_layout, attn_grad, token, (x0, mixed_grad, error)
    )
    f0_sum.sides_end(grad_rows)
    f0_sum.last()
    a1_sum.last_end(grad_rows)
    a0_sum.near(outs, (grad_rows, f0_sum.held, a1_sum.held))
    a0_sum.corner()
    a1_sum.line()
    token = a0_sum.corner_end()
    a0_sum.sides()
    attn_terms = tie((scores_a, sums_a, scores_n, sums_n, small_a), token)
    small_0 = small_terms(0, attn_terms, small_f, (hidden_n, hidden_a))
    attn_terms, small_f, hidden_sums = tie(late_terms, token)
    small_1 = small_terms(1, attn_terms, small_f, (hidden_sums[2:], hidden_sums[:2]))
    small_sum = SmallSum(jnp.stack([small_0, small_1]))
    token = a0_sum.sides_end(at_once=True)
    residual, grad_rows = tie((residual, grad_rows), token)
    f0_sum.last_end(token)
    a0_sum.line((f0_sum.held, small_sum.total))
    f0_sum.line()
    a1_sum.line_end(token)
    f1_sum.line_end(token)
    small_sum.step()
    small_sum.step(token)
    while not small_sum.end():
        small_sum.step()
    a0_sum.line_end()
    f0_sum.line_end()
    shard_grads = [(a0_sum, f0_sum), (a1_sum, f1_sum)]
    shard_grads = [
        (attn.result, ffn.result[:shard_rows], ffn.result[shard_rows:])
        for attn, ffn in shard_grads
    ]

    totals = small_sum.result()

    def own(values):
        return lax.dynamic_slice_in_dim(values, dp_index * dp_width, dp_width, 2)

    small_grads = [own(totals[:, 2 * index : 2 * index + 2]) for index in range(4)]
    hidden_total = totals[:, 8 : 8 + pieces].reshape(BLOCKS, -1)
    fc1_bias_grad = lax.dynamic_slice_in_dim(hidden_total, dp_index * dp_hidden, dp_hidden, 1)
    table_total = totals[:, 8 + pieces :].reshape(BLOCKS, heads_total, table_lanes)
    bias_table_grad = lax.dynamic_slice_in_dim(
        table_total[:, :, :rel_count], head_index * local_heads, local_heads, 1
    )
    qkv_weight_grad = jnp.stack(
        [item[0][:, : 3 * local_width].reshape(-1, 3, local_width) for item in shard_grads]
    )
    proj_weight_grad = jnp.stack([item[0][:, 3 * local_width :].T for item in shard_grads])
    fc1_weight_grad = jnp.stack([item[1] for item in shard_grads])
    fc2_weight_grad = jnp.stack([item[2].T for item in shard_grads])
    return (
        drop_rows(residual),
        drop_rows(grad_rows),
        small_grads[0],
        small_grads[1],
        qkv_weight_grad,
        small_grads[2],
        bias_table_grad,
        proj_weight_grad,
        fc1_weight_grad,
        fc1_bias_grad,
        fc2_weight_grad,
        small_grads[3],
    )


def solution(mesh):
    placed = (
        P(("dp", "head"), None),
        P(("dp", "head"), None),
        P("dp"),
        P("dp", None),
        P("dp", None),
        P(),
        P(None, None, "dp"),
        P(None, None, "dp"),
        P(None, "dp", None, "head"),
        P(None, None, "dp"),
        P(None, "head", None),
        P(None, "head", "dp"),
        P(None, "dp", "head"),
        P(None, "dp"),
        P(None, "head", "dp"),
        P(None, None, "dp"),
    )
    return jax.shard_map(
        shards,
        mesh=mesh,
        in_specs=placed,
        out_specs=(
            P(("dp", "head"), None),
            P(("dp", "head"), None),
            P(None, None, "dp"),
            P(None, None, "dp"),
            P(None, "dp", None, "head"),
            P(None, None, "dp"),
            P(None, "head", None),
            P(None, "head", "dp"),
            P(None, "dp", "head"),
            P(None, "dp"),
            P(None, "head", "dp"),
            P(None, None, "dp"),
        ),
        check_vma=False,
    )
```
